32 devices in a mesh: clips: 2 (over x), tm: 8 (over z, y), cols: 2 (over core).
Axes of the slice: x: 2, y: 2, z: 4, core: 2. Of those that a mesh axis runs over, the one named last changes fastest.
Arguments:
- video: bfloat16 [64, 32, 32, 512], P(('clips', 'tm'), None, 'cols'), parts along dimension 0, may hold values from -6 to 6
- w_time: bfloat16 [3, 512, 512], replicated, may hold values from -0.15625 to 0.15625
- b_time: float32 [512], replicated, may hold values from -3 to 3
- w_down: bfloat16 [3, 512, 512], replicated, may hold values from -0.15625 to 0.15625
- b_down: float32 [512], replicated, may hold values from -3 to 3
- w_space: bfloat16 [9, 512, 512], replicated, may hold values from -0.09375 to 0.09375
- b_space: float32 [512], replicated, may hold values from -3 to 3
- gain: float32 [512], replicated, may hold values from 0.1 to 1.9
- w_query: bfloat16 [512, 512], replicated, may hold values from -30 to 30
- w_key: bfloat16 [512, 512], replicated, may hold values from -0.25 to 0.25
- w_value: bfloat16 [512, 512], replicated, may hold values from -0.25 to 0.25
- w_out: bfloat16 [512, 512], replicated, may hold values from -0.25 to 0.25
Outputs:
- encoded: bfloat16 [32, 32, 32, 512], P(('clips', 'tm'), None, 'cols'), parts along dimension 0
The draws below stay inside these ranges and needn't reach their ends.
There are 2 independent parts, one for each index of `clips`. The reference program is written for one: setup_inputs(seed, part) draws one part's arguments, and reference() takes and returns one part's arrays. A program takes and returns all parts, laid end to end along the dimension named above; an argument that names none is the same for every part. Nothing has to cross between parts.
All inputs are finite; a program needn't handle non-finite values.
Results may differ from the reference program's by a relative error of at most 0.019.
The reference program's roundings to bfloat16 on the way (of `lifted`, `reduced`, `spatial`, `normed`, `query`, `probs` and `context`) count: a program that leaves them out, or rounds other values in their place, can miss the bound.
Values may be sent and summed in bfloat16 or wider, within the bound.
No kernel may reach another device: no remote copies, remote signals or barrier semaphores. Data moves between devices by JAX's collectives and lax.ppermute only.
A program may use at most 64 MiB of HBM per device.

```python
import jax
import jax.numpy as jnp
from jax import lax

C = 512
H = 32
W = 32
FRAMES = 32


def draw_w_query(key, part):
    values = jax.random.truncated_normal(key, -4.0, 4.0, (C, C), jnp.float32) * C ** (-0.5)
    return values.astype(jnp.bfloat16)


def block_levels(stream_key, extent, shards, smallest, high):
    def one(position, parts):
        steps = jax.random.uniform(jax.random.fold_in(jax.random.fold_in(stream_key, 6), position), (parts,), jnp.float32, smallest / len(shards), high / len(shards))
        return jnp.repeat(jnp.exp(steps), extent[position] // parts).reshape((-1,) + (1,) * (len(extent) - position - 1))

    factor_of = one(*shards[0])
    for cut in shards[1:]:
        factor_of = factor_of * one(*cut)
    return factor_of


def gaussian(key, dims, scale, most, pieces=(), kind=jnp.bfloat16):
    entries = scale * jax.random.normal(key, dims, jnp.float32)
    if pieces:
        entries = entries * block_levels(key, dims, pieces, -0.22, 0.18)
    return jnp.clip(entries, -most, most).astype(kind)


def setup_inputs(seed: int = 0, part: int = 0) -> dict:
    streams_of = jax.random.split(jax.random.key(seed), 13)
    part_keys = jax.random.split(jax.random.fold_in(streams_of[12], part), 13)
    video = gaussian(part_keys[0], (FRAMES, H, W, C), 1.0, 6.0, ((0, 8), (2, 2)))
    w_time = gaussian(streams_of[1], (3, C, C), (3 * C) ** -0.5, 0.15625)
    b_time = gaussian(streams_of[2], (C,), 0.5, 3.0, (), jnp.float32)
    w_down = gaussian(streams_of[3], (3, C, C), (3 * C) ** -0.5, 0.15625)
    b_down = gaussian(streams_of[4], (C,), 0.5, 3.0, (), jnp.float32)
    w_space = gaussian(streams_of[5], (9, C, C), (9 * C) ** -0.5, 0.09375)
    b_space = gaussian(streams_of[6], (C,), 0.5, 3.0, (), jnp.float32)
    gain = jnp.clip(1.0 + 0.18 * jax.random.normal(streams_of[7], (C,), jnp.float32), 0.1, 1.9)
    w_query = draw_w_query(jax.random.fold_in(streams_of[12], 71), part)
    w_key = gaussian(streams_of[9], (C, C), C ** -0.5, 0.25)
    w_value = gaussian(streams_of[10], (C, C), C ** -0.5, 0.25)
    w_out = gaussian(streams_of[11], (C, C), C ** -0.5, 0.25)
    return {"video": video, "w_time": w_time, "b_time": b_time, "w_down": w_down, "b_down": b_down, "w_space": w_space, "b_space": b_space, "gain": gain, "w_query": w_query, "w_key": w_key, "w_value": w_value, "w_out": w_out}


epsilon = 1e-06

def attend(sequence, gain, w_query, w_key, w_value, w_out):
    frames, pixels, channels = sequence.shape
    wide = sequence.astype(jnp.float32)
    scale = lax.rsqrt(lax.optimization_barrier(jnp.mean(wide * wide, axis=-1, keepdims=True)) + epsilon)
    normed = (wide * scale * gain).astype(jnp.bfloat16).reshape(-1, channels)
    query = jnp.dot(normed, w_query, preferred_element_type=jnp.float32).astype(jnp.bfloat16).reshape(frames, pixels, channels)
    key = jnp.dot(normed, w_key, preferred_element_type=jnp.float32).astype(jnp.bfloat16).reshape(frames, pixels, channels)
    value = jnp.dot(normed, w_value, preferred_element_type=jnp.float32).astype(jnp.bfloat16).reshape(frames, pixels, channels)
    scores = jnp.einsum('spc,tpc->pst', query.astype(jnp.float32), key.astype(jnp.float32)) * channels ** (-0.5)
    steps = jnp.arange(frames)
    allowed = steps[None, :] <= steps[:, None]
    scores = jnp.where(allowed[None], scores, -1e+30)
    largest = lax.optimization_barrier(jnp.max(scores, axis=-1, keepdims=True))
    probs = jnp.exp(scores - largest)
    probs = probs / lax.optimization_barrier(jnp.sum(probs, axis=-1, keepdims=True))
    probs = probs.astype(jnp.bfloat16)
    context = jnp.einsum('pst,tpc->spc', probs.astype(jnp.float32), value.astype(jnp.float32)).astype(jnp.bfloat16)
    mixed = jnp.dot(context.reshape(-1, channels), w_out, preferred_element_type=jnp.float32).reshape(frames, pixels, channels)
    return (wide + mixed).astype(jnp.bfloat16)

def reference(video, w_time, b_time, w_down, b_down, w_space, b_space, gain, w_query, w_key, w_value, w_out):
    frames, height, columns, channels = video.shape
    shape = (frames, height, columns, channels)
    padded = jnp.concatenate([jnp.zeros((2, height, columns, channels), video.dtype), video], 0)
    summed = jnp.zeros((frames * height * columns, channels), jnp.float32) + b_time
    for offset in range(3):
        summed = summed + jnp.dot(padded[2 - offset:2 - offset + frames].reshape(-1, channels), w_time[offset], preferred_element_type=jnp.float32)
    lifted = (video.astype(jnp.float32) + jax.nn.silu(summed.reshape(shape))).astype(jnp.bfloat16)
    shifted = jnp.concatenate([jnp.zeros((1, height, columns, channels), lifted.dtype), lifted], 0)
    halves = frames // 2
    taps = [shifted[2:frames + 1:2], shifted[1:frames:2], shifted[0:frames - 1:2]]
    summed = jnp.zeros((halves * height * columns, channels), jnp.float32) + b_down
    for offset in range(3):
        summed = summed + jnp.dot(taps[offset].reshape(-1, channels), w_down[offset], preferred_element_type=jnp.float32)
    reduced = summed.reshape(halves, height, columns, channels).astype(jnp.bfloat16)
    framed = jnp.pad(reduced, ((0, 0), (1, 1), (1, 1), (0, 0)))
    summed = jnp.zeros((halves * height * columns, channels), jnp.float32) + b_space
    for row_tap in range(3):
        for col_tap in range(3):
            window = framed[:, row_tap:row_tap + height, col_tap:col_tap + columns]
            summed = summed + jnp.dot(window.reshape(-1, channels), w_space[3 * row_tap + col_tap], preferred_element_type=jnp.float32)
    spatial = (reduced.astype(jnp.float32) + jax.nn.silu(summed.reshape(halves, height, columns, channels))).astype(jnp.bfloat16)
    encoded = attend(spatial.reshape(halves, height * columns, channels), gain, w_query, w_key, w_value, w_out)
    return encoded.reshape(halves, height, columns, channels)
```

```python
from functools import partial

import jax
import jax.numpy as jnp
from jax import lax
from jax.experimental import pallas as pl
from jax.experimental.pallas import tpu as pltpu
from jax.sharding import PartitionSpec as P

epsilon = 1e-06
pair = 2
taps = 3
most_direct = 8
vmem_bytes = 48 * 1024 * 1024

VMEM = pl.BlockSpec(memory_space=pltpu.VMEM)
SMEM = pl.BlockSpec(memory_space=pltpu.SMEM)


def silu(v):
    return 0.5 * v * (1.0 + jnp.tanh(0.5 * v))


def dot32(a, b):
    return jnp.dot(a, b, preferred_element_type=jnp.float32)


def cost(flops, *arrays):
    size = sum(a.size * a.dtype.itemsize for a in arrays)
    return pl.CostEstimate(flops=flops, bytes_accessed=size, transcendentals=0)


def lift_kernel(flags, ext, w_time, b_time, w_down, b_down, out, odd, even):
    count, rows, width, channels = ext.shape
    pixels = rows * width
    frames = count - taps
    halves = frames // 2
    lifts = frames + 1
    group = 3 if lifts % 3 == 0 else 1

    def window(first):
        return ext[first : first + group].reshape(group * pixels, channels)

    for j in range(0, lifts, group):
        lhs = jnp.concatenate([window(j + 2 - k) for k in range(taps)], axis=1)
        acc = dot32(lhs, w_time[...]) + b_time[...]
        lifted = window(j + 2).astype(jnp.float32) + silu(acc)
        for g in range(group):
            piece = lifted[g * pixels : (g + 1) * pixels]
            if j + g == 0:
                piece = jnp.where(flags[0] > 0, piece, 0.0)
            (even if (j + g) % 2 else odd)[(j + g) // 2] = piece.astype(jnp.bfloat16)
    parts = [odd[1:], even[...], odd[:halves]]
    lhs = jnp.concatenate([p.reshape(halves * pixels, channels) for p in parts], axis=1)
    acc = dot32(lhs, w_down[...]) + b_down[...]
    out[...] = acc.reshape(halves, rows, width, channels).astype(jnp.bfloat16)

    @pl.when(flags[1] == 0)
    def _():
        out[:, 0] = jnp.zeros_like(out[:, 0])

    @pl.when(flags[2] == 0)
    def _():
        out[:, rows - 1] = jnp.zeros_like(out[:, rows - 1])


def lift(flags, ext, w_time, b_time, w_down, b_down):
    count, rows, width, channels = ext.shape
    frames = count - taps
    halves = frames // 2
    pixels = rows * width
    flops = 2 * taps * channels * channels * pixels * (frames + 1 + halves)
    return pl.pallas_call(
        lift_kernel,
        out_shape=jax.ShapeDtypeStruct((halves, rows, width, channels), jnp.bfloat16),
        in_specs=[SMEM] + [VMEM] * 5,
        out_specs=VMEM,
        scratch_shapes=[
            pltpu.VMEM((halves + 1, pixels, channels), jnp.bfloat16),
            pltpu.VMEM((halves, pixels, channels), jnp.bfloat16),
        ],
        compiler_params=pltpu.CompilerParams(vmem_limit_bytes=vmem_bytes),
        cost_estimate=cost(flops, ext, w_time, w_down),
        name="lift",
    )(flags, ext, w_time, b_time, w_down, b_down)


def space_kernel(left, middle, right, weights, bias, out):
    halves, rows, width, channels = out.shape
    pixels = halves * rows * width
    sources = (left, middle, right)

    def window(source, a):
        return source[:, a : a + rows].reshape(pixels, channels)

    lhs = jnp.concatenate([window(s, a) for a in range(3) for s in sources], axis=1)
    acc = dot32(lhs, weights[...]) + bias[...]
    result = window(middle, 1).astype(jnp.float32) + silu(acc)
    out[...] = result.astype(jnp.bfloat16).reshape(out.shape)


def space(left, middle, right, weights, bias):
    halves, rows, width, channels = middle.shape
    rows = rows - 2
    flops = 2 * 9 * channels * channels * halves * rows * width
    return pl.pallas_call(
        space_kernel,
        out_shape=jax.ShapeDtypeStruct((halves, rows, width, channels), jnp.bfloat16),
        in_specs=[VMEM] * 5,
        out_specs=VMEM,
        compiler_params=pltpu.CompilerParams(vmem_limit_bytes=vmem_bytes),
        cost_estimate=cost(flops, left, middle, right, weights),
        name="space",
    )(left, middle, right, weights, bias)


def attend_kernel(frames_per, lanes, count, first, *refs):
    blocks = refs[:count]
    gain, w_query, w_key, w_value, w_out = refs[count : count + 5]
    outs = refs[count + 5 :]
    channels = gain.shape[-1]
    flat = len(blocks[0].shape) == 2
    groups = 1 if flat else blocks[0].shape[1] // lanes
    each = frames_per * lanes
    size = count * each

    def piece(ref, g):
        if flat:
            return ref[...]
        return ref[:, g * lanes : (g + 1) * lanes].reshape(each, channels)

    def place(index):
        block = index // each
        frame = index // lanes % frames_per
        time = frame
        for j in range(count):
            time = time + jnp.where(block == j, first[j], 0)
        return time, index % lanes

    row_time, row_lane = place(lax.broadcasted_iota(jnp.int32, (size, 1), 0))
    col_time, col_lane = place(lax.broadcasted_iota(jnp.int32, (1, size), 1))
    allowed = (row_lane == col_lane) & (col_time <= row_time)
    x = jnp.concatenate([piece(b, g) for g in range(groups) for b in blocks], axis=0)
    wide = x.astype(jnp.float32)
    scale = lax.rsqrt(jnp.mean(wide * wide, axis=-1, keepdims=True) + epsilon)
    normed = (wide * scale * gain[...]).astype(jnp.bfloat16)
    query = dot32(normed, w_query[...]).astype(jnp.bfloat16)
    key = dot32(normed, w_key[...]).astype(jnp.bfloat16)
    value = dot32(normed, w_value[...]).astype(jnp.bfloat16)
    contexts = []
    for g in range(groups):
        part = slice(g * size, (g + 1) * size)
        scores = lax.dot_general(
            query[part], key[part], (((1,), (1,)), ((), ())), preferred_element_type=jnp.float32
        )
        scores = jnp.where(allowed, scores * channels ** (-0.5), -1e30)
        largest = jnp.max(scores, axis=-1, keepdims=True)
        probs = jnp.exp(scores - largest)
        probs = (probs / jnp.sum(probs, axis=-1, keepdims=True)).astype(jnp.bfloat16)
        contexts.append(dot32(probs, value[part]).astype(jnp.bfloat16))
    mixed = dot32(jnp.concatenate(contexts, axis=0), w_out[...])
    result = (wide + mixed).astype(jnp.bfloat16)
    for g in range(groups):
        for j, out in enumerate(outs):
            begin = g * size + j * each
            rows = result[begin : begin + each]
            if flat:
                out[...] = rows
            else:
                out[:, g * lanes : (g + 1) * lanes] = rows.reshape(frames_per, lanes, channels)


def attend(first, blocks, gain, w_query, w_key, w_value, w_out):
    frames_per, pixels, channels = blocks[0].shape
    lanes = 16 if pixels % 16 == 0 else pixels
    flat = pixels % 16 != 0
    if flat:
        blocks = [b.reshape(frames_per * pixels, channels) for b in blocks]
    count = len(blocks)
    rows = frames_per * pixels * count
    flops = 2 * rows * channels * (4 * channels + 2 * frames_per * count * lanes)
    outs = pl.pallas_call(
        partial(attend_kernel, frames_per, lanes, count),
        out_shape=[jax.ShapeDtypeStruct(b.shape, jnp.bfloat16) for b in blocks],
        in_specs=[SMEM] + [VMEM] * (count + 5),
        out_specs=[VMEM] * count,
        compiler_params=pltpu.CompilerParams(vmem_limit_bytes=vmem_bytes),
        cost_estimate=cost(flops, *blocks, w_query, w_key, w_value, w_out),
        name="attend",
    )(first, *blocks, gain, w_query, w_key, w_value, w_out)
    return [o.reshape(frames_per, pixels, channels) for o in outs]


def after(value, other):
    return lax.optimization_barrier((value, other))[0]


def per_device(
    video, w_time, b_time, w_down, b_down, w_space, b_space, gain, w_query, w_key, w_value, w_out
):
    frames, height, width, channels = video.shape
    devices = lax.axis_size("tm")
    levels = devices // pair
    columns = lax.axis_size("cols")
    place = lax.axis_index("tm")
    side = place % pair
    level = place // pair
    column = lax.axis_index("cols")
    half = height // pair
    halves = frames
    flags_of = lambda top, bottom: jnp.stack(
        [level, 1 if top is None else top, 1 if bottom is None else bottom]
    ).astype(jnp.int32)
    w_time = w_time.reshape(-1, channels)
    w_down = w_down.reshape(-1, channels)
    w_space = w_space.reshape(-1, channels)
    b_time, b_down, b_space, gain = (v.reshape(1, -1) for v in (b_time, b_down, b_space, gain))

    def swap(value):
        return lax.ppermute(value, "tm", [(i, i ^ 1) for i in range(devices)])

    def rows_of(owner, begin, end):
        low, high = owner * half + begin - 1, owner * half + end - 1
        body = video[:, max(low, 0) : min(high, height)]
        return jnp.pad(body, ((0, 0), (max(-low, 0), max(high - height, 0)), (0, 0), (0, 0)))

    def beside(value):
        last, first = value[:, :, -1:], value[:, :, :1]
        if columns == 2:
            other = lax.ppermute(jnp.where(column == 0, last, first), "cols", [(0, 1), (1, 0)])
            return jnp.where(column == 1, other, 0), jnp.where(column == 0, other, 0)
        up = [(i, i + 1) for i in range(columns - 1)]
        return lax.ppermute(last, "cols", up), lax.ppermute(
            first, "cols", [(j, i) for i, j in up]
        )

    if half % 4 == 0:
        sizes = (half // 4, half // 2, half // 4)
    else:
        sizes = (half,)
    direct = levels <= most_direct and levels & (levels - 1) == 0
    encoded = jnp.zeros((halves // pair, height * width, channels), jnp.bfloat16)
    previous = None
    previous_sent = None
    begin = 0
    for index, size in enumerate(sizes):
        end = begin + size
        first_row = 0 if index == 0 else begin + 2
        last_row = end + 2
        mine, others = (
            jnp.where(side == s, rows_of(0, first_row, last_row), rows_of(1, first_row, last_row))
            for s in (0, 1)
        )
        if previous_sent is not None:
            others = after(others, previous_sent)
        received = swap(others)
        previous_sent = received
        lower = jnp.where(side == 0, mine, received)
        upper = jnp.where(side == 0, received, mine)
        halo = lax.ppermute(
            upper[frames - taps :], "tm", [(i, i + pair) for i in range(devices - pair)]
        )
        ext = jnp.concatenate([halo, lower, upper], axis=0)
        flags = flags_of(side if index == 0 else None, 1 - side if end == half else None)
        reduced = lift(flags, ext, w_time, b_time, w_down, b_down)
        left, right = beside(reduced)
        pieces = (left, reduced, right)
        if previous is not None:
            pieces = tuple(jnp.concatenate(pq, axis=1) for pq in zip(previous, pieces))
        previous = tuple(p[:, -2:] for p in pieces)
        left, middle, right = pieces
        to_right = jnp.concatenate([left, middle[:, :, :-1]], axis=2)
        to_left = jnp.concatenate([middle[:, :, 1:], right], axis=2)
        spatial = space(to_right, middle, to_left, w_space, b_space)
        pixels = size * width // levels
        blocks = spatial.reshape(halves, levels, pixels, channels)
        if direct:
            gathered = []
            for j in range(levels):
                block = lax.dynamic_index_in_dim(blocks, level ^ j, 1, keepdims=False)
                if j:
                    route = [(i, (i // pair ^ j) * pair + i % pair) for i in range(devices)]
                    block = lax.ppermute(block, "tm", route)
                gathered.append(block)
            first = jnp.stack([(level ^ j) * halves for j in range(levels)]).astype(jnp.int32)
            results = attend(first, gathered, gain, w_query, w_key, w_value, w_out)
            returned = []
            for j in range(levels):
                block = results[j]
                if j:
                    route = [(i, (i // pair ^ j) * pair + i % pair) for i in range(devices)]
                    block = lax.ppermute(block, "tm", route)
                returned.append(block)
            whole = jnp.zeros((halves, levels, pixels, channels), jnp.bfloat16)
            for j in range(levels):
                whole = lax.dynamic_update_index_in_dim(whole, returned[j], level ^ j, 1)
        else:
            sets = [[s + pair * z for z in range(levels)] for s in range(pair)]
            gathered = lax.all_to_all(blocks, "tm", 1, 0, axis_index_groups=sets, tiled=True)
            gathered = gathered.reshape(halves * levels, pixels, channels)
            first = jnp.zeros((1,), jnp.int32)
            (result,) = attend(first, [gathered], gain, w_query, w_key, w_value, w_out)
            result = result.reshape(halves * levels, 1, pixels, channels)
            whole = lax.all_to_all(result, "tm", 0, 1, axis_index_groups=sets, tiled=True)
        whole = whole.reshape(pair, halves // pair, size * width, channels)
        kept = jnp.where(side == 0, whole[0], whole[1])
        other = swap(jnp.where(side == 0, whole[1], whole[0]))
        encoded = lax.dynamic_update_slice(
            encoded, kept, (0, (side * half + begin) * width, 0)
        )
        encoded = lax.dynamic_update_slice(
            encoded, other, (0, ((1 - side) * half + begin) * width, 0)
        )
        begin = end
    return encoded.reshape(halves // pair, height, width, channels)


def solution(mesh):
    spread = P(("clips", "tm"), None, "cols", None)
    return jax.shard_map(
        per_device,
        mesh=mesh,
        in_specs=(spread,) + (P(),) * 11,
        out_specs=spread,
        check_vma=False,
    )
```

```python
from functools import partial

import jax
import jax.numpy as jnp
from jax import lax
from jax.experimental import pallas as pl
from jax.experimental.pallas import tpu as pltpu
from jax.sharding import PartitionSpec as P

epsilon = 1e-06
parts = 2
taps = 3
vmem_bytes = 48 * 1024 * 1024

VMEM = pl.BlockSpec(memory_space=pltpu.VMEM)
SMEM = pl.BlockSpec(memory_space=pltpu.SMEM)


def silu(v):
    return 0.5 * v * (1.0 + jnp.tanh(0.5 * v))


def dot32(a, b):
    return jnp.dot(a, b, preferred_element_type=jnp.float32)


def cost(flops, *arrays):
    size = sum(a.size * a.dtype.itemsize for a in arrays)
    return pl.CostEstimate(flops=flops, bytes_accessed=size, transcendentals=0)


def lift_kernel(started, halo, video, w_time, b_time, w_down, b_down, out, lifted):
    frames, rows, width, channels = video.shape
    pixels = rows * width

    def frame(t):
        ref, index = (halo, t + taps) if t < 0 else (video, t)
        return ref[index].reshape(pixels, channels)

    for t in range(-1, frames):
        lhs = jnp.concatenate([frame(t - k) for k in range(taps)], axis=1)
        acc = dot32(lhs, w_time[...]) + b_time[...]
        result = frame(t).astype(jnp.float32) + silu(acc)
        if t < 0:
            result = jnp.where(started[0] > 0, result, 0.0)
        lifted[t + 1] = result.astype(jnp.bfloat16)
    for s in range(frames // 2):
        lhs = jnp.concatenate([lifted[2 * s + 2 - k] for k in range(taps)], axis=1)
        acc = dot32(lhs, w_down[...]) + b_down[...]
        out[s] = acc.astype(jnp.bfloat16).reshape(rows, width, channels)


def lift(started, halo, video, w_time, b_time, w_down, b_down):
    frames, rows, width, channels = video.shape
    pixels = rows * width
    flops = 2 * taps * channels * channels * pixels * (frames + 1 + frames // 2)
    return pl.pallas_call(
        lift_kernel,
        out_shape=jax.ShapeDtypeStruct((frames // 2, rows, width, channels), jnp.bfloat16),
        in_specs=[SMEM] + [VMEM] * 6,
        out_specs=VMEM,
        scratch_shapes=[pltpu.VMEM((frames + 1, pixels, channels), jnp.bfloat16)],
        compiler_params=pltpu.CompilerParams(vmem_limit_bytes=vmem_bytes),
        cost_estimate=cost(flops, halo, video, w_time, w_down),
        name="lift",
    )(started, halo, video, w_time, b_time, w_down, b_down)


def space_kernel(left, middle, right, weights, bias, out):
    halves, rows, width, channels = out.shape
    pixels = rows * width
    sources = (left, middle, right)
    for s in range(halves):

        def window(source, a):
            return source[s, a : a + rows].reshape(pixels, channels)

        lhs = jnp.concatenate([window(v, a) for a in range(3) for v in sources], axis=1)
        acc = dot32(lhs, weights[...]) + bias[...]
        result = window(middle, 1).astype(jnp.float32) + silu(acc)
        out[s] = result.astype(jnp.bfloat16).reshape(rows, width, channels)


def space(left, middle, right, weights, bias):
    halves, rows, width, channels = middle.shape
    rows = rows - 2
    flops = 2 * 9 * channels * channels * halves * rows * width
    return pl.pallas_call(
        space_kernel,
        out_shape=jax.ShapeDtypeStruct((halves, rows, width, channels), jnp.bfloat16),
        in_specs=[VMEM] * 5,
        out_specs=VMEM,
        compiler_params=pltpu.CompilerParams(vmem_limit_bytes=vmem_bytes),
        cost_estimate=cost(flops, left, middle, right, weights),
        name="space",
    )(left, middle, right, weights, bias)


def attend_kernel(frames_per, lanes, count, first, *refs):
    blocks = refs[:count]
    gain, w_query, w_key, w_value, w_out = refs[count : count + 5]
    outs = refs[count + 5 :]
    channels = gain.shape[-1]
    flat = len(blocks[0].shape) == 2
    groups = 1 if flat else blocks[0].shape[1] // lanes
    each = frames_per * lanes
    size = count * each

    def piece(ref, g):
        if flat:
            return ref[...]
        return ref[:, g * lanes : (g + 1) * lanes].reshape(each, channels)

    def place(index):
        block = index // each
        frame = index // lanes % frames_per
        time = frame
        for j in range(count):
            time = time + jnp.where(block == j, first[j], 0)
        return time, index % lanes

    row_time, row_lane = place(lax.broadcasted_iota(jnp.int32, (size, 1), 0))
    col_time, col_lane = place(lax.broadcasted_iota(jnp.int32, (1, size), 1))
    allowed = (row_lane == col_lane) & (col_time <= row_time)
    x = jnp.concatenate([piece(b, g) for g in range(groups) for b in blocks], axis=0)
    wide = x.astype(jnp.float32)
    scale = lax.rsqrt(jnp.mean(wide * wide, axis=-1, keepdims=True) + epsilon)
    normed = (wide * scale * gain[...]).astype(jnp.bfloat16)
    query = dot32(normed, w_query[...]).astype(jnp.bfloat16)
    key = dot32(normed, w_key[...]).astype(jnp.bfloat16)
    value = dot32(normed, w_value[...]).astype(jnp.bfloat16)
    contexts = []
    for g in range(groups):
        part = slice(g * size, (g + 1) * size)
        scores = lax.dot_general(
            query[part], key[part], (((1,), (1,)), ((), ())), preferred_element_type=jnp.float32
        )
        scores = jnp.where(allowed, scores * channels ** (-0.5), -1e30)
        largest = jnp.max(scores, axis=-1, keepdims=True)
        probs = jnp.exp(scores - largest)
        probs = (probs / jnp.sum(probs, axis=-1, keepdims=True)).astype(jnp.bfloat16)
        contexts.append(dot32(probs, value[part]).astype(jnp.bfloat16))
    mixed = dot32(jnp.concatenate(contexts, axis=0), w_out[...])
    result = (wide + mixed).astype(jnp.bfloat16)
    for g in range(groups):
        for j, out in enumerate(outs):
            begin = g * size + j * each
            rows = result[begin : begin + each]
            if flat:
                out[...] = rows
            else:
                out[:, g * lanes : (g + 1) * lanes] = rows.reshape(frames_per, lanes, channels)


def attend(first, blocks, gain, w_query, w_key, w_value, w_out):
    frames_per, pixels, channels = blocks[0].shape
    lanes = 16 if pixels % 16 == 0 else pixels
    flat = pixels % 16 != 0
    if flat:
        blocks = [b.reshape(frames_per * pixels, channels) for b in blocks]
    count = len(blocks)
    rows = frames_per * pixels * count
    flops = 2 * rows * channels * (4 * channels + 2 * frames_per * count * lanes)
    outs = pl.pallas_call(
        partial(attend_kernel, frames_per, lanes, count),
        out_shape=[jax.ShapeDtypeStruct(b.shape, jnp.bfloat16) for b in blocks],
        in_specs=[SMEM] + [VMEM] * (count + 5),
        out_specs=[VMEM] * count,
        compiler_params=pltpu.CompilerParams(vmem_limit_bytes=vmem_bytes),
        cost_estimate=cost(flops, *blocks, w_query, w_key, w_value, w_out),
        name="attend",
    )(first, *blocks, gain, w_query, w_key, w_value, w_out)
    return [o.reshape(frames_per, pixels, channels) for o in outs]


def after(value, other):
    return lax.optimization_barrier((value, other))[0]


def per_device(
    video, w_time, b_time, w_down, b_down, w_space, b_space, gain, w_query, w_key, w_value, w_out
):
    frames, height, width, channels = video.shape
    devices = lax.axis_size("tm")
    columns = lax.axis_size("cols")
    place = lax.axis_index("tm")
    column = lax.axis_index("cols")
    halves = frames // 2
    started = place.astype(jnp.int32).reshape(1)
    first = jnp.zeros((1,), jnp.int32)
    w_time = w_time.reshape(-1, channels)
    w_down = w_down.reshape(-1, channels)
    w_space = w_space.reshape(-1, channels)
    b_time, b_down, b_space, gain = (v.reshape(1, -1) for v in (b_time, b_down, b_space, gain))
    onward = [(i, i + 1) for i in range(devices - 1)]

    def beside(value):
        last, head = value[:, :, -1:], value[:, :, :1]
        if columns == 2:
            other = lax.ppermute(jnp.where(column == 0, last, head), "cols", [(0, 1), (1, 0)])
            return jnp.where(column == 1, other, 0), jnp.where(column == 0, other, 0)
        up = [(i, i + 1) for i in range(columns - 1)]
        return lax.ppermute(last, "cols", up), lax.ppermute(head, "cols", [(j, i) for i, j in up])

    chunks = parts if height % parts == 0 and height // parts * width % devices == 0 else 1
    size = height // chunks
    halos, newest = [], None
    for index in range(chunks):
        begin = index * size + (1 if index else 0)
        end = min((index + 1) * size + 1, height)
        sent = video[frames - taps :, begin:end]
        if newest is not None:
            sent = after(sent, newest)
        newest = lax.ppermute(sent, "tm", onward)
        halos.append((begin, end, newest))

    spatials, kept = [], None
    for index, (begin, end, halo) in enumerate(halos):
        own = video[:, begin:end]
        if spatials:
            own = after(own, spatials[-1])
        reduced = lift(started, halo, own, w_time, b_time, w_down, b_down)
        left, right = beside(reduced)
        pieces = (left, reduced, right)
        if kept is None:
            kept = tuple(jnp.zeros_like(p[:, :1]) for p in pieces)
        pieces = tuple(jnp.concatenate(pq, axis=1) for pq in zip(kept, pieces))
        if index == chunks - 1:
            pieces = tuple(jnp.pad(p, ((0, 0), (0, 1), (0, 0), (0, 0))) for p in pieces)
        kept = tuple(p[:, -2:] for p in pieces)
        left, middle, right = pieces
        to_right = jnp.concatenate([left, middle[:, :, :-1]], axis=2)
        to_left = jnp.concatenate([middle[:, :, 1:], right], axis=2)
        spatials.append(space(to_right, middle, to_left, w_space, b_space))

    gathers = [
        lax.all_to_all(s.reshape(halves, size * width, channels), "tm", 1, 0, tiled=True)
        for s in spatials
    ]
    returns, newest = [], spatials[-1]
    for block in gathers:
        block = after(block, newest)
        (newest,) = attend(first, [block], gain, w_query, w_key, w_value, w_out)
        returns.append(lax.all_to_all(newest, "tm", 0, 1, tiled=True))
    encoded = jnp.concatenate(returns, axis=1)
    return encoded.reshape(halves, height, width, channels)


def solution(mesh):
    spread = P(("clips", "tm"), None, "cols", None)
    return jax.shard_map(
        per_device,
        mesh=mesh,
        in_specs=(spread,) + (P(),) * 11,
        out_specs=spread,
        check_vma=False,
    )
```

```python
from functools import partial

import jax
import jax.numpy as jnp
from jax import lax
from jax.experimental import pallas as pl
from jax.experimental.pallas import tpu as pltpu
from jax.sharding import PartitionSpec as P

epsilon = 1e-06
parts = 2
taps = 3
most_direct = 8
vmem_bytes = 48 * 1024 * 1024

VMEM = pl.BlockSpec(memory_space=pltpu.VMEM)
SMEM = pl.BlockSpec(memory_space=pltpu.SMEM)
ANY = pl.BlockSpec(memory_space=pl.ANY)


def silu(v):
    return 0.5 * v * (1.0 + jnp.tanh(0.5 * v))


def dot32(a, b):
    return jnp.dot(a, b, preferred_element_type=jnp.float32)


def cost(flops, *arrays):
    size = sum(a.size * a.dtype.itemsize for a in arrays)
    return pl.CostEstimate(flops=flops, bytes_accessed=size, transcendentals=0)


def params():
    return pltpu.CompilerParams(vmem_limit_bytes=vmem_bytes)


def pick_kernel(first, begin, video, out, sem):
    count, rows = out.shape[:2]
    copy = pltpu.make_async_copy(video.at[first : first + count, begin : begin + rows], out, sem)
    copy.start()
    copy.wait()


def pick(video, first, begin, end):
    frames, _, width, channels = video.shape
    shape = (frames - first, end - begin, width, channels)
    return pl.pallas_call(
        partial(pick_kernel, first, begin),
        out_shape=jax.ShapeDtypeStruct(shape, video.dtype),
        in_specs=[ANY],
        out_specs=ANY,
        scratch_shapes=[pltpu.SemaphoreType.DMA],
        compiler_params=params(),
        name="pick",
    )(video)


def early_kernel(begin, video, w_time, b_time, w_down, b_down, own, part, rows_in, lifted, sem):
    frames, rows, width, channels = rows_in.shape
    pixels = rows * width
    copy = pltpu.make_async_copy(video.at[:, begin : begin + rows], rows_in, sem)
    copy.start()
    copy.wait()

    def frame(t):
        return rows_in[t].reshape(pixels, channels)

    for t in range(taps - 1, frames):
        lhs = jnp.concatenate([frame(t - k) for k in range(taps)], axis=1)
        acc = dot32(lhs, w_time[...]) + b_time[...]
        lifted[t] = (frame(t).astype(jnp.float32) + silu(acc)).astype(jnp.bfloat16)
    for s in range(1, frames // 2):
        known = [k for k in range(taps) if 2 * s + 1 - k >= taps - 1]
        lhs = jnp.concatenate([lifted[2 * s + 1 - k] for k in known], axis=1)
        part[s - 1] = dot32(lhs, w_down[: len(known) * channels]) + b_down[...]
    own[...] = rows_in[: taps - 1]


def early(video, begin, end, w_time, b_time, w_down, b_down):
    frames, _, width, channels = video.shape
    rows = end - begin
    pixels = rows * width
    flops = 2 * channels * channels * pixels * (taps * (frames - 2) + 2)
    return pl.pallas_call(
        partial(early_kernel, begin),
        out_shape=[
            jax.ShapeDtypeStruct((taps - 1, rows, width, channels), jnp.bfloat16),
            jax.ShapeDtypeStruct((frames // 2 - 1, pixels, channels), jnp.float32),
        ],
        in_specs=[ANY] + [VMEM] * 4,
        out_specs=[VMEM] * 2,
        scratch_shapes=[
            pltpu.VMEM((frames, rows, width, channels), jnp.bfloat16),
            pltpu.VMEM((frames, pixels, channels), jnp.bfloat16),
            pltpu.SemaphoreType.DMA,
        ],
        compiler_params=params(),
        cost_estimate=cost(flops, w_time, w_down),
        name="early",
    )(video, w_time, b_time, w_down, b_down)


def lift_kernel(started, halo, own, part, w_time, b_time, w_down, b_down, out, lifted):
    halves, rows, width, channels = out.shape
    pixels = rows * width

    def frame(t):
        ref, index = (halo, t + taps) if t < 0 else (own, t)
        return ref[index].reshape(pixels, channels)

    for t in range(-1, taps - 1):
        lhs = jnp.concatenate([frame(t - k) for k in range(taps)], axis=1)
        acc = dot32(lhs, w_time[...]) + b_time[...]
        result = frame(t).astype(jnp.float32) + silu(acc)
        if t < 0:
            result = jnp.where(started[0] > 0, result, 0.0)
        lifted[t + 1] = result.astype(jnp.bfloat16)
    for s in range(halves):
        late = [k for k in range(taps) if 2 * s + 1 - k < taps - 1]
        acc = b_down[...] if s == 0 else part[s - 1]
        if late:
            lhs = jnp.concatenate([lifted[2 * s + 2 - k] for k in late], axis=1)
            acc = dot32(lhs, w_down[late[0] * channels : (late[-1] + 1) * channels]) + acc
        out[s] = acc.astype(jnp.bfloat16).reshape(rows, width, channels)


def lift(started, halo, own, part, w_time, b_time, w_down, b_down):
    rows, width, channels = own.shape[1:]
    halves = part.shape[0] + 1
    pixels = rows * width
    flops = 2 * channels * channels * pixels * (taps * taps + 4)
    return pl.pallas_call(
        lift_kernel,
        out_shape=jax.ShapeDtypeStruct((halves, rows, width, channels), jnp.bfloat16),
        in_specs=[SMEM] + [VMEM] * 7,
        out_specs=VMEM,
        scratch_shapes=[pltpu.VMEM((taps, pixels, channels), jnp.bfloat16)],
        compiler_params=params(),
        cost_estimate=cost(flops, halo, own, part, w_time, w_down),
        name="lift",
    )(started, halo, own, part, w_time, b_time, w_down, b_down)


def space_kernel(owners, order, left, middle, right, weights, bias, *refs):
    outs, result = refs[:-1], refs[-1]
    halves, pixels, channels = result.shape
    rows = middle.shape[1] - 2
    sources = (left, middle, right)

    @pl.loop(0, halves)
    def _(s):
        def window(source, a):
            return source[s, a : a + rows].reshape(pixels, channels)

        lhs = jnp.concatenate([window(v, a) for a in range(3) for v in sources], axis=1)
        acc = dot32(lhs, weights[...]) + bias[...]
        value = window(middle, 1).astype(jnp.float32) + silu(acc)
        result[s] = value.astype(jnp.bfloat16)

    if owners == 1:
        outs[0][...] = result[...]
    else:
        each = pixels // owners
        for j, out in enumerate(outs):
            begin = pl.multiple_of(order[j] * each, each)
            out[...] = result[:, pl.ds(begin, each)]


def space(order, left, middle, right, weights, bias):
    halves, rows, width, channels = middle.shape
    owners = order.shape[0]
    pixels = (rows - 2) * width
    flops = 2 * 9 * channels * channels * halves * pixels
    block = jax.ShapeDtypeStruct((halves, pixels // owners, channels), jnp.bfloat16)
    return pl.pallas_call(
        partial(space_kernel, owners),
        out_shape=[block] * owners,
        in_specs=[SMEM] + [VMEM] * 5,
        out_specs=[VMEM] * owners,
        scratch_shapes=[pltpu.VMEM((halves, pixels, channels), jnp.bfloat16)],
        compiler_params=params(),
        cost_estimate=cost(flops, left, middle, right, weights),
        name="space",
    )(order, left, middle, right, weights, bias)


def attend_kernel(frames_per, lanes, count, first, *refs):
    blocks = refs[:count]
    gain, w_query, w_key, w_value, w_out = refs[count : count + 5]
    outs = refs[count + 5 :]
    channels = gain.shape[-1]
    flat = len(blocks[0].shape) == 2
    groups = 1 if flat else blocks[0].shape[1] // lanes
    each = frames_per * lanes
    size = count * each

    def piece(ref, g):
        if flat:
            return ref[...]
        return ref[:, g * lanes : (g + 1) * lanes].reshape(each, channels)

    def place(index):
        block = index // each
        frame = index // lanes % frames_per
        time = frame
        for j in range(count):
            time = time + jnp.where(block == j, first[j], 0)
        return time, index % lanes

    row_time, row_lane = place(lax.broadcasted_iota(jnp.int32, (size, 1), 0))
    col_time, col_lane = place(lax.broadcasted_iota(jnp.int32, (1, size), 1))
    allowed = (row_lane == col_lane) & (col_time <= row_time)
    x = jnp.concatenate([piece(b, g) for g in range(groups) for b in blocks], axis=0)
    wide = x.astype(jnp.float32)
    scale = lax.rsqrt(jnp.mean(wide * wide, axis=-1, keepdims=True) + epsilon)
    normed = (wide * scale * gain[...]).astype(jnp.bfloat16)
    query = dot32(normed, w_query[...]).astype(jnp.bfloat16)
    key = dot32(normed, w_key[...]).astype(jnp.bfloat16)
    value = dot32(normed, w_value[...]).astype(jnp.bfloat16)
    contexts = []
    for g in range(groups):
        part = slice(g * size, (g + 1) * size)
        scores = lax.dot_general(
            query[part], key[part], (((1,), (1,)), ((), ())), preferred_element_type=jnp.float32
        )
        scores = jnp.where(allowed, scores * channels ** (-0.5), -1e30)
        largest = jnp.max(scores, axis=-1, keepdims=True)
        probs = jnp.exp(scores - largest)
        probs = (probs / jnp.sum(probs, axis=-1, keepdims=True)).astype(jnp.bfloat16)
        contexts.append(dot32(probs, value[part]).astype(jnp.bfloat16))
    mixed = dot32(jnp.concatenate(contexts, axis=0), w_out[...])
    result = (wide + mixed).astype(jnp.bfloat16)
    for g in range(groups):
        for j, out in enumerate(outs):
            begin = g * size + j * each
            rows = result[begin : begin + each]
            if flat:
                out[...] = rows
            else:
                out[:, g * lanes : (g + 1) * lanes] = rows.reshape(frames_per, lanes, channels)


def attend(first, blocks, gain, w_query, w_key, w_value, w_out):
    frames_per, pixels, channels = blocks[0].shape
    lanes = 16 if pixels % 16 == 0 else pixels
    flat = pixels % 16 != 0
    if flat:
        blocks = [b.reshape(frames_per * pixels, channels) for b in blocks]
    count = len(blocks)
    rows = frames_per * pixels * count
    flops = 2 * rows * channels * (4 * channels + 2 * frames_per * count * lanes)
    outs = pl.pallas_call(
        partial(attend_kernel, frames_per, lanes, count),
        out_shape=[jax.ShapeDtypeStruct(b.shape, jnp.bfloat16) for b in blocks],
        in_specs=[SMEM] + [VMEM] * (count + 5),
        out_specs=[VMEM] * count,
        compiler_params=params(),
        cost_estimate=cost(flops, *blocks, w_query, w_key, w_value, w_out),
        name="attend",
    )(first, *blocks, gain, w_query, w_key, w_value, w_out)
    return [o.reshape(frames_per, pixels, channels) for o in outs]


def collect_kernel(count, base, order, *refs):
    blocks = refs[:count]
    out, sems = refs[-2:]
    copies = [
        pltpu.make_async_copy(block, out.at[:, base + order[j]], sems.at[j])
        for j, block in enumerate(blocks)
    ]
    for copy in copies:
        copy.start()
    for copy in copies:
        copy.wait()


def collect(order, blocks, chunk, chunks, whole):
    count = len(blocks)
    halves, pixels, channels = blocks[0].shape
    shape = (halves, chunks * count, pixels, channels)
    given = [] if whole is None else [whole]
    return pl.pallas_call(
        partial(collect_kernel, count, chunk * count),
        out_shape=jax.ShapeDtypeStruct(shape, jnp.bfloat16),
        in_specs=[SMEM] + [ANY] * (count + len(given)),
        out_specs=ANY,
        input_output_aliases={count + 1: 0} if given else {},
        scratch_shapes=[pltpu.SemaphoreType.DMA((count,))],
        compiler_params=params(),
        name="collect",
    )(order, *blocks, *given)


def after(value, other):
    return lax.optimization_barrier((value, other))[0]


def per_device(
    video, w_time, b_time, w_down, b_down, w_space, b_space, gain, w_query, w_key, w_value, w_out
):
    frames, height, width, channels = video.shape
    devices = lax.axis_size("tm")
    columns = lax.axis_size("cols")
    place = lax.axis_index("tm").astype(jnp.int32)
    column = lax.axis_index("cols")
    halves = frames // 2
    started = place.reshape(1)
    w_time = w_time.reshape(-1, channels)
    w_down = w_down.reshape(-1, channels)
    w_space = w_space.reshape(-1, channels)
    b_time, b_down, b_space, gain = (v.reshape(1, -1) for v in (b_time, b_down, b_space, gain))
    onward = [(i, i + 1) for i in range(devices - 1)]
    chunks = parts if height % parts == 0 and height // parts * width % devices == 0 else 1
    size = height // chunks
    each = size * width // devices
    direct = devices <= most_direct and devices & (devices - 1) == 0 and each % 16 == 0
    issue = sorted(range(1, devices), key=lambda j: -j)
    order = place ^ jnp.arange(devices, dtype=jnp.int32) if direct else jnp.zeros(1, jnp.int32)

    def beside(value):
        last, head = value[:, :, -1:], value[:, :, :1]
        if columns == 2:
            other = lax.ppermute(jnp.where(column == 0, last, head), "cols", [(0, 1), (1, 0)])
            return jnp.where(column == 1, other, 0), jnp.where(column == 0, other, 0)
        up = [(i, i + 1) for i in range(columns - 1)]
        return lax.ppermute(last, "cols", up), lax.ppermute(head, "cols", [(j, i) for i, j in up])

    def exchange(blocks):
        result = list(blocks)
        for j in issue:
            result[j] = lax.ppermute(blocks[j], "tm", [(i, i ^ j) for i in range(devices)])
        return result

    spans = [
        (k * size + (1 if k else 0), min((k + 1) * size + 1, height)) for k in range(chunks)
    ]
    halos, owns, sums = [], [], []
    for begin, end in spans:
        sent = pick(video, frames - taps, begin, end)
        if sums:
            sent = after(sent, sums[-1])
        halos.append(lax.ppermute(sent, "tm", onward))
        own, part = early(video, begin, end, w_time, b_time, w_down, b_down)
        owns.append(own)
        sums.append(part)

    spatials, kept = [], None
    for index in range(chunks):
        halo, own, part = halos[index], owns[index], sums[index]
        if spatials:
            own = after(own, spatials[-1][0])
        reduced = lift(started, halo, own, part, w_time, b_time, w_down, b_down)
        left, right = beside(reduced)
        pieces = (left, reduced, right)
        if kept is None:
            kept = tuple(jnp.zeros_like(p[:, :1]) for p in pieces)
        pieces = tuple(jnp.concatenate(pq, axis=1) for pq in zip(kept, pieces))
        if index == chunks - 1:
            pieces = tuple(jnp.pad(p, ((0, 0), (0, 1), (0, 0), (0, 0))) for p in pieces)
        kept = tuple(p[:, -2:] for p in pieces)
        left, middle, right = pieces
        to_right = jnp.concatenate([left, middle[:, :, :-1]], axis=2)
        to_left = jnp.concatenate([middle[:, :, 1:], right], axis=2)
        spatials.append(space(order, to_right, middle, to_left, w_space, b_space))

    newest = spatials[-1][0]
    if direct:
        whole = None
        returns = []
        for gathered in [exchange(blocks) for blocks in spatials]:
            gathered[0] = after(gathered[0], newest)
            results = attend(order * halves, gathered, gain, w_query, w_key, w_value, w_out)
            newest = results[0]
            returns.append(exchange(results))
        for index, blocks in enumerate(returns):
            whole = collect(order, blocks, index, chunks, whole)
        return whole.reshape(halves, height, width, channels)
    returns = []
    for (block,) in spatials:
        gathered = lax.all_to_all(block, "tm", 1, 0, tiled=True)
        (result,) = attend(order, [gathered], gain, w_query, w_key, w_value, w_out)
        returns.append(lax.all_to_all(result, "tm", 0, 1, tiled=True))
    return jnp.concatenate(returns, axis=1).reshape(halves, height, width, channels)


def solution(mesh):
    spread = P(("clips", "tm"), None, "cols", None)
    return jax.shard_map(
        per_device,
        mesh=mesh,
        in_specs=(spread,) + (P(),) * 11,
        out_specs=spread,
        check_vma=False,
    )
```

```python
from functools import partial

import jax
import jax.numpy as jnp
from jax import lax
from jax.experimental import pallas as pl
from jax.experimental.pallas import tpu as pltpu
from jax.sharding import PartitionSpec as P

epsilon = 1e-06
parts = 2
taps = 3
most_direct = 8
mebibyte = 1024 * 1024

VMEM = pl.BlockSpec(memory_space=pltpu.VMEM)
SMEM = pl.BlockSpec(memory_space=pltpu.SMEM)
ANY = pl.BlockSpec(memory_space=pl.ANY)


def silu(v):
    return 0.5 * v * (1.0 + jnp.tanh(0.5 * v))


def dot32(a, b):
    return jnp.dot(a, b, preferred_element_type=jnp.float32)


def cost(flops, *arrays):
    size = sum(a.size * a.dtype.itemsize for a in arrays)
    return pl.CostEstimate(flops=flops, bytes_accessed=size, transcendentals=0)


def params(mebibytes):
    return pltpu.CompilerParams(vmem_limit_bytes=mebibytes * mebibyte)


def pick_kernel(first, begin, video, out, sem):
    count, rows = out.shape[:2]
    copy = pltpu.make_async_copy(video.at[first : first + count, begin : begin + rows], out, sem)
    copy.start()
    copy.wait()


def pick(video, first, begin, end):
    frames, _, width, channels = video.shape
    shape = (frames - first, end - begin, width, channels)
    return pl.pallas_call(
        partial(pick_kernel, first, begin),
        out_shape=jax.ShapeDtypeStruct(shape, video.dtype),
        in_specs=[ANY],
        out_specs=ANY,
        scratch_shapes=[pltpu.SemaphoreType.DMA],
        compiler_params=params(56),
        name="pick",
    )(video)


def early_kernel(begin, video, w_time, b_time, w_down, b_down, own, part, rows_in, lifted, sem):
    frames, rows, width, channels = rows_in.shape
    pixels = rows * width
    copy = pltpu.make_async_copy(video.at[:, begin : begin + rows], rows_in, sem)
    copy.start()
    copy.wait()

    def frame(t):
        return rows_in[t].reshape(pixels, channels)

    for t in range(taps - 1, frames):
        lhs = jnp.concatenate([frame(t - k) for k in range(taps)], axis=1)
        acc = dot32(lhs, w_time[...]) + b_time[...]
        lifted[t] = (frame(t).astype(jnp.float32) + silu(acc)).astype(jnp.bfloat16)
    for s in range(1, frames // 2):
        known = [k for k in range(taps) if 2 * s + 1 - k >= taps - 1]
        lhs = jnp.concatenate([lifted[2 * s + 1 - k] for k in known], axis=1)
        part[s - 1] = dot32(lhs, w_down[: len(known) * channels]) + b_down[...]
    own[...] = rows_in[: taps - 1]


def early(video, begin, end, w_time, b_time, w_down, b_down):
    frames, _, width, channels = video.shape
    rows = end - begin
    pixels = rows * width
    flops = 2 * channels * channels * pixels * (taps * (frames - 2) + 2)
    return pl.pallas_call(
        partial(early_kernel, begin),
        out_shape=[
            jax.ShapeDtypeStruct((taps - 1, rows, width, channels), jnp.bfloat16),
            jax.ShapeDtypeStruct((frames // 2 - 1, pixels, channels), jnp.float32),
        ],
        in_specs=[ANY] + [VMEM] * 4,
        out_specs=[VMEM] * 2,
        scratch_shapes=[
            pltpu.VMEM((frames, rows, width, channels), jnp.bfloat16),
            pltpu.VMEM((frames, pixels, channels), jnp.bfloat16),
            pltpu.SemaphoreType.DMA,
        ],
        compiler_params=params(20),
        cost_estimate=cost(flops, w_time, w_down),
        name="early",
    )(video, w_time, b_time, w_down, b_down)


def lift_kernel(started, halo, own, part, w_time, b_time, w_down, b_down, out, lifted):
    halves, rows, width, channels = out.shape
    pixels = rows * width

    def frame(t):
        ref, index = (halo, t + taps) if t < 0 else (own, t)
        return ref[index].reshape(pixels, channels)

    for t in range(-1, taps - 1):
        lhs = jnp.concatenate([frame(t - k) for k in range(taps)], axis=1)
        acc = dot32(lhs, w_time[...]) + b_time[...]
        result = frame(t).astype(jnp.float32) + silu(acc)
        if t < 0:
            result = jnp.where(started[0] > 0, result, 0.0)
        lifted[t + 1] = result.astype(jnp.bfloat16)
    for s in range(halves):
        late = [k for k in range(taps) if 2 * s + 1 - k < taps - 1]
        acc = b_down[...] if s == 0 else part[s - 1]
        if late:
            lhs = jnp.concatenate([lifted[2 * s + 2 - k] for k in late], axis=1)
            acc = dot32(lhs, w_down[late[0] * channels : (late[-1] + 1) * channels]) + acc
        out[s] = acc.astype(jnp.bfloat16).reshape(rows, width, channels)


def lift(started, halo, own, part, w_time, b_time, w_down, b_down):
    rows, width, channels = own.shape[1:]
    halves = part.shape[0] + 1
    pixels = rows * width
    flops = 2 * channels * channels * pixels * (taps * taps + 4)
    return pl.pallas_call(
        lift_kernel,
        out_shape=jax.ShapeDtypeStruct((halves, rows, width, channels), jnp.bfloat16),
        in_specs=[SMEM] + [VMEM] * 7,
        out_specs=VMEM,
        scratch_shapes=[pltpu.VMEM((taps, pixels, channels), jnp.bfloat16)],
        compiler_params=params(20),
        cost_estimate=cost(flops, halo, own, part, w_time, w_down),
        name="lift",
    )(started, halo, own, part, w_time, b_time, w_down, b_down)


def space_kernel(owners, joined, order, left, middle, right, weights, bias, *refs):
    outs, result = refs[:-1], refs[-1]
    halves, pixels, channels = result.shape
    rows = middle.shape[1] - 2
    sources = (left, middle, right)

    @pl.loop(0, halves)
    def _(s):
        def window(source, a):
            return source[s, a : a + rows].reshape(pixels, channels)

        lhs = jnp.concatenate([window(v, a) for a in range(3) for v in sources], axis=1)
        acc = dot32(lhs, weights[...]) + bias[...]
        value = window(middle, 1).astype(jnp.float32) + silu(acc)
        result[s] = value.astype(jnp.bfloat16)

    each = pixels // owners
    if owners == 1:
        outs[0][...] = result[...]
    elif joined:
        for j in range(owners):
            outs[0][j] = result[:, j * each : (j + 1) * each]
    else:
        for j, out in enumerate(outs):
            begin = pl.multiple_of(order[j] * each, each)
            out[...] = result[:, pl.ds(begin, each)]


def space(joined, order, left, middle, right, weights, bias):
    halves, rows, width, channels = middle.shape
    owners = order.shape[0]
    pixels = (rows - 2) * width
    flops = 2 * 9 * channels * channels * halves * pixels
    block = (halves, pixels // owners, channels)
    shapes = [(owners,) + block] if joined else [block] * owners
    return pl.pallas_call(
        partial(space_kernel, owners, joined),
        out_shape=[jax.ShapeDtypeStruct(shape, jnp.bfloat16) for shape in shapes],
        in_specs=[SMEM] + [VMEM] * 5,
        out_specs=[VMEM] * len(shapes),
        scratch_shapes=[pltpu.VMEM((halves, pixels, channels), jnp.bfloat16)],
        compiler_params=params(20),
        cost_estimate=cost(flops, left, middle, right, weights),
        name="space",
    )(order, left, middle, right, weights, bias)


def attend_kernel(frames_per, lanes, count, first, *refs):
    blocks = refs[:count]
    gain, w_query, w_key, w_value, w_out = refs[count : count + 5]
    outs = refs[count + 5 :]
    channels = gain.shape[-1]
    flat = len(blocks[0].shape) == 2
    groups = 1 if flat else blocks[0].shape[1] // lanes
    each = frames_per * lanes
    size = count * each

    def piece(ref, g):
        if flat:
            return ref[...]
        return ref[:, g * lanes : (g + 1) * lanes].reshape(each, channels)

    def place(index):
        block = index // each
        frame = index // lanes % frames_per
        time = frame
        for j in range(count):
            time = time + jnp.where(block == j, first[j], 0)
        return time, index % lanes

    row_time, row_lane = place(lax.broadcasted_iota(jnp.int32, (size, 1), 0))
    col_time, col_lane = place(lax.broadcasted_iota(jnp.int32, (1, size), 1))
    allowed = (row_lane == col_lane) & (col_time <= row_time)
    x = jnp.concatenate([piece(b, g) for g in range(groups) for b in blocks], axis=0)
    wide = x.astype(jnp.float32)
    scale = lax.rsqrt(jnp.mean(wide * wide, axis=-1, keepdims=True) + epsilon)
    normed = (wide * scale * gain[...]).astype(jnp.bfloat16)
    query = dot32(normed, w_query[...]).astype(jnp.bfloat16)
    key = dot32(normed, w_key[...]).astype(jnp.bfloat16)
    value = dot32(normed, w_value[...]).astype(jnp.bfloat16)
    contexts = []
    for g in range(groups):
        part = slice(g * size, (g + 1) * size)
        scores = lax.dot_general(
            query[part], key[part], (((1,), (1,)), ((), ())), preferred_element_type=jnp.float32
        )
        scores = jnp.where(allowed, scores * channels ** (-0.5), -1e30)
        largest = jnp.max(scores, axis=-1, keepdims=True)
        probs = jnp.exp(scores - largest)
        probs = (probs / jnp.sum(probs, axis=-1, keepdims=True)).astype(jnp.bfloat16)
        contexts.append(dot32(probs, value[part]).astype(jnp.bfloat16))
    mixed = dot32(jnp.concatenate(contexts, axis=0), w_out[...])
    result = (wide + mixed).astype(jnp.bfloat16)
    for g in range(groups):
        for j, out in enumerate(outs):
            begin = g * size + j * each
            rows = result[begin : begin + each]
            if flat:
                out[...] = rows
            else:
                out[:, g * lanes : (g + 1) * lanes] = rows.reshape(frames_per, lanes, channels)


def attend(first, blocks, gain, w_query, w_key, w_value, w_out):
    frames_per, pixels, channels = blocks[0].shape
    lanes = 16 if pixels % 16 == 0 else pixels
    flat = pixels % 16 != 0
    if flat:
        blocks = [b.reshape(frames_per * pixels, channels) for b in blocks]
    count = len(blocks)
    rows = frames_per * pixels * count
    size = frames_per * count * lanes
    flops = 2 * rows * channels * (4 * channels + 2 * frames_per * count * lanes)
    outs = pl.pallas_call(
        partial(attend_kernel, frames_per, lanes, count),
        out_shape=[jax.ShapeDtypeStruct(b.shape, jnp.bfloat16) for b in blocks],
        in_specs=[SMEM] + [VMEM] * (count + 5),
        out_specs=[VMEM] * count,
        compiler_params=params(20 if 16 * size * size < 20 * mebibyte else 56),
        cost_estimate=cost(flops, *blocks, w_query, w_key, w_value, w_out),
        name="attend",
    )(first, *blocks, gain, w_query, w_key, w_value, w_out)
    return [o.reshape(frames_per, pixels, channels) for o in outs]


def collect_kernel(count, base, order, *refs):
    out, sems = refs[-2:]
    joined = len(refs[0].shape) == 4
    copies = []
    for j in range(count):
        block, owner = (refs[0].at[j], j) if joined else (refs[j], order[j])
        copies.append(pltpu.make_async_copy(block, out.at[:, base + owner], sems.at[j]))
    for copy in copies:
        copy.start()
    for copy in copies:
        copy.wait()


def collect(order, blocks, chunk, chunks, whole):
    count = order.shape[0]
    halves, pixels, channels = blocks[0].shape[-3:]
    shape = (halves, chunks * count, pixels, channels)
    given = [] if whole is None else [whole]
    return pl.pallas_call(
        partial(collect_kernel, count, chunk * count),
        out_shape=jax.ShapeDtypeStruct(shape, jnp.bfloat16),
        in_specs=[SMEM] + [ANY] * (len(blocks) + len(given)),
        out_specs=ANY,
        input_output_aliases={len(blocks) + 1: 0} if given else {},
        scratch_shapes=[pltpu.SemaphoreType.DMA((count,))],
        compiler_params=params(16),
        name="collect",
    )(order, *blocks, *given)


def after(value, other):
    return lax.optimization_barrier((value, other))[0]


def per_device(
    video, w_time, b_time, w_down, b_down, w_space, b_space, gain, w_query, w_key, w_value, w_out
):
    frames, height, width, channels = video.shape
    devices = lax.axis_size("tm")
    columns = lax.axis_size("cols")
    place = lax.axis_index("tm").astype(jnp.int32)
    column = lax.axis_index("cols")
    halves = frames // 2
    started = place.reshape(1)
    w_time = w_time.reshape(-1, channels)
    w_down = w_down.reshape(-1, channels)
    w_space = w_space.reshape(-1, channels)
    b_time, b_down, b_space, gain = (v.reshape(1, -1) for v in (b_time, b_down, b_space, gain))
    onward = [(i, i + 1) for i in range(devices - 1)]
    chunks = parts if height % parts == 0 and height // parts * width % devices == 0 else 1
    size = height // chunks
    each = size * width // devices
    direct = devices <= most_direct and devices & (devices - 1) == 0 and each % 16 == 0
    issue = sorted(range(1, devices), key=lambda j: -j)
    order = place ^ jnp.arange(devices, dtype=jnp.int32) if direct else jnp.zeros(1, jnp.int32)

    def beside(value):
        last, head = value[:, :, -1:], value[:, :, :1]
        if columns == 2:
            other = lax.ppermute(jnp.where(column == 0, last, head), "cols", [(0, 1), (1, 0)])
            return jnp.where(column == 1, other, 0), jnp.where(column == 0, other, 0)
        up = [(i, i + 1) for i in range(columns - 1)]
        return lax.ppermute(last, "cols", up), lax.ppermute(head, "cols", [(j, i) for i, j in up])

    def exchange(blocks):
        if len(blocks) == 1:
            shape = blocks[0].shape
            whole = blocks[0].reshape((devices, -1) + shape[-2:])
            return [lax.all_to_all(whole, "tm", 0, 0, tiled=True).reshape(shape)]
        result = list(blocks)
        for j in issue:
            result[j] = lax.ppermute(blocks[j], "tm", [(i, i ^ j) for i in range(devices)])
        return result

    spans = [
        (k * size + (1 if k else 0), min((k + 1) * size + 1, height)) for k in range(chunks)
    ]
    halos, owns, sums = [], [], []
    for begin, end in spans:
        sent = pick(video, frames - taps, begin, end)
        halos.append(lax.ppermute(sent, "tm", onward))
        own, part = early(video, begin, end, w_time, b_time, w_down, b_down)
        owns.append(own)
        sums.append(part)

    spatials, kept = [], None
    for index in range(chunks):
        halo, own, part = halos[index], owns[index], sums[index]
        if spatials:
            own = after(own, spatials[-1][0])
        reduced = lift(started, halo, own, part, w_time, b_time, w_down, b_down)
        left, right = beside(reduced)
        pieces = (left, reduced, right)
        if kept is None:
            kept = tuple(jnp.zeros_like(p[:, :1]) for p in pieces)
        pieces = tuple(jnp.concatenate(pq, axis=1) for pq in zip(kept, pieces))
        if index == chunks - 1:
            pieces = tuple(jnp.pad(p, ((0, 0), (0, 1), (0, 0), (0, 0))) for p in pieces)
        kept = tuple(p[:, -2:] for p in pieces)
        left, middle, right = pieces
        to_right = jnp.concatenate([left, middle[:, :, :-1]], axis=2)
        to_left = jnp.concatenate([middle[:, :, 1:], right], axis=2)
        joined = direct and index < chunks - 1
        spatials.append(space(joined, order, to_right, middle, to_left, w_space, b_space))

    newest = spatials[-1][0]
    if direct:
        whole = None
        returns = []
        for gathered in [exchange(blocks) for blocks in spatials]:
            gathered[0] = after(gathered[0], newest)
            starts = order * halves
            if len(gathered) == 1:
                gathered[0] = gathered[0].reshape(devices * halves, each, channels)
                starts = jnp.zeros(1, jnp.int32)
            results = attend(starts, gathered, gain, w_query, w_key, w_value, w_out)
            newest = results[0]
            if len(results) == 1:
                results = [results[0].reshape(devices, halves, each, channels)]
            returns.append(exchange(results))
        for index, blocks in enumerate(returns):
            whole = collect(order, blocks, index, chunks, whole)
        return whole.reshape(halves, height, width, channels)
    returns = []
    for (block,) in spatials:
        gathered = lax.all_to_all(block, "tm", 1, 0, tiled=True)
        (result,) = attend(order, [gathered], gain, w_query, w_key, w_value, w_out)
        returns.append(lax.all_to_all(result, "tm", 0, 1, tiled=True))
    return jnp.concatenate(returns, axis=1).reshape(halves, height, width, channels)


def solution(mesh):
    spread = P(("clips", "tm"), None, "cols", None)
    return jax.shard_map(
        per_device,
        mesh=mesh,
        in_specs=(spread,) + (P(),) * 11,
        out_specs=spread,
        check_vma=False,
    )
```

```python
from functools import partial

import jax
import jax.numpy as jnp
from jax import lax
from jax.experimental import pallas as pl
from jax.experimental.pallas import tpu as pltpu
from jax.sharding import PartitionSpec as P

epsilon = 1e-06
pair = 2
taps = 3
most_direct = 8
vmem_bytes = 48 * 1024 * 1024

VMEM = pl.BlockSpec(memory_space=pltpu.VMEM)
SMEM = pl.BlockSpec(memory_space=pltpu.SMEM)


def silu(v):
    return 0.5 * v * (1.0 + jnp.tanh(0.5 * v))


def dot32(a, b):
    return jnp.dot(a, b, preferred_element_type=jnp.float32)


def cost(flops, *arrays):
    size = sum(a.size * a.dtype.itemsize for a in arrays)
    return pl.CostEstimate(flops=flops, bytes_accessed=size, transcendentals=0)


def lift_kernel(flags, ext, w_time, b_time, w_down, b_down, out, odd, even):
    count, rows, width, channels = ext.shape
    pixels = rows * width
    frames = count - taps
    halves = frames // 2
    lifts = frames + 1
    group = 3 if lifts % 3 == 0 else 1

    def window(first):
        return ext[first : first + group].reshape(group * pixels, channels)

    for j in range(0, lifts, group):
        lhs = jnp.concatenate([window(j + 2 - k) for k in range(taps)], axis=1)
        acc = dot32(lhs, w_time[...]) + b_time[...]
        lifted = window(j + 2).astype(jnp.float32) + silu(acc)
        for g in range(group):
            piece = lifted[g * pixels : (g + 1) * pixels]
            if j + g == 0:
                piece = jnp.where(flags[0] > 0, piece, 0.0)
            (even if (j + g) % 2 else odd)[(j + g) // 2] = piece.astype(jnp.bfloat16)
    parts = [odd[1:], even[...], odd[:halves]]
    lhs = jnp.concatenate([p.reshape(halves * pixels, channels) for p in parts], axis=1)
    acc = dot32(lhs, w_down[...]) + b_down[...]
    out[...] = acc.reshape(halves, rows, width, channels).astype(jnp.bfloat16)

    @pl.when(flags[1] == 0)
    def _():
        out[:, 0] = jnp.zeros_like(out[:, 0])

    @pl.when(flags[2] == 0)
    def _():
        out[:, rows - 1] = jnp.zeros_like(out[:, rows - 1])


def lift(flags, ext, w_time, b_time, w_down, b_down):
    count, rows, width, channels = ext.shape
    frames = count - taps
    halves = frames // 2
    pixels = rows * width
    flops = 2 * taps * channels * channels * pixels * (frames + 1 + halves)
    return pl.pallas_call(
        lift_kernel,
        out_shape=jax.ShapeDtypeStruct((halves, rows, width, channels), jnp.bfloat16),
        in_specs=[SMEM] + [VMEM] * 5,
        out_specs=VMEM,
        scratch_shapes=[
            pltpu.VMEM((halves + 1, pixels, channels), jnp.bfloat16),
            pltpu.VMEM((halves, pixels, channels), jnp.bfloat16),
        ],
        compiler_params=pltpu.CompilerParams(vmem_limit_bytes=vmem_bytes),
        cost_estimate=cost(flops, ext, w_time, w_down),
        name="lift",
    )(flags, ext, w_time, b_time, w_down, b_down)


def space_kernel(left, middle, right, weights, bias, out):
    halves, rows, width, channels = out.shape
    pixels = halves * rows * width
    sources = (left, middle, right)

    def window(source, a):
        return source[:, a : a + rows].reshape(pixels, channels)

    lhs = jnp.concatenate([window(s, a) for a in range(3) for s in sources], axis=1)
    acc = dot32(lhs, weights[...]) + bias[...]
    result = window(middle, 1).astype(jnp.float32) + silu(acc)
    out[...] = result.astype(jnp.bfloat16).reshape(out.shape)


def space(left, middle, right, weights, bias):
    halves, rows, width, channels = middle.shape
    rows = rows - 2
    flops = 2 * 9 * channels * channels * halves * rows * width
    return pl.pallas_call(
        space_kernel,
        out_shape=jax.ShapeDtypeStruct((halves, rows, width, channels), jnp.bfloat16),
        in_specs=[VMEM] * 5,
        out_specs=VMEM,
        compiler_params=pltpu.CompilerParams(vmem_limit_bytes=vmem_bytes),
        cost_estimate=cost(flops, left, middle, right, weights),
        name="space",
    )(left, middle, right, weights, bias)


def attend_kernel(frames_per, lanes, count, first, *refs):
    blocks = refs[:count]
    gain, w_query, w_key, w_value, w_out = refs[count : count + 5]
    outs = refs[count + 5 :]
    channels = gain.shape[-1]
    flat = len(blocks[0].shape) == 2
    groups = 1 if flat else blocks[0].shape[1] // lanes
    each = frames_per * lanes
    size = count * each

    def piece(ref, g):
        if flat:
            return ref[...]
        return ref[:, g * lanes : (g + 1) * lanes].reshape(each, channels)

    def place(index):
        block = index // each
        frame = index // lanes % frames_per
        time = frame
        for j in range(count):
            time = time + jnp.where(block == j, first[j], 0)
        return time, index % lanes

    row_time, row_lane = place(lax.broadcasted_iota(jnp.int32, (size, 1), 0))
    col_time, col_lane = place(lax.broadcasted_iota(jnp.int32, (1, size), 1))
    allowed = (row_lane == col_lane) & (col_time <= row_time)
    x = jnp.concatenate([piece(b, g) for g in range(groups) for b in blocks], axis=0)
    wide = x.astype(jnp.float32)
    scale = lax.rsqrt(jnp.mean(wide * wide, axis=-1, keepdims=True) + epsilon)
    normed = (wide * scale * gain[...]).astype(jnp.bfloat16)
    query = dot32(normed, w_query[...]).astype(jnp.bfloat16)
    key = dot32(normed, w_key[...]).astype(jnp.bfloat16)
    value = dot32(normed, w_value[...]).astype(jnp.bfloat16)
    contexts = []
    for g in range(groups):
        part = slice(g * size, (g + 1) * size)
        scores = lax.dot_general(
            query[part], key[part], (((1,), (1,)), ((), ())), preferred_element_type=jnp.float32
        )
        scores = jnp.where(allowed, scores * channels ** (-0.5), -1e30)
        largest = jnp.max(scores, axis=-1, keepdims=True)
        probs = jnp.exp(scores - largest)
        probs = (probs / jnp.sum(probs, axis=-1, keepdims=True)).astype(jnp.bfloat16)
        contexts.append(dot32(probs, value[part]).astype(jnp.bfloat16))
    mixed = dot32(jnp.concatenate(contexts, axis=0), w_out[...])
    result = (wide + mixed).astype(jnp.bfloat16)
    for g in range(groups):
        for j, out in enumerate(outs):
            begin = g * size + j * each
            rows = result[begin : begin + each]
            if flat:
                out[...] = rows
            else:
                out[:, g * lanes : (g + 1) * lanes] = rows.reshape(frames_per, lanes, channels)


def attend(first, blocks, gain, w_query, w_key, w_value, w_out):
    frames_per, pixels, channels = blocks[0].shape
    lanes = 16 if pixels % 16 == 0 else pixels
    flat = pixels % 16 != 0
    if flat:
        blocks = [b.reshape(frames_per * pixels, channels) for b in blocks]
    count = len(blocks)
    rows = frames_per * pixels * count
    flops = 2 * rows * channels * (4 * channels + 2 * frames_per * count * lanes)
    outs = pl.pallas_call(
        partial(attend_kernel, frames_per, lanes, count),
        out_shape=[jax.ShapeDtypeStruct(b.shape, jnp.bfloat16) for b in blocks],
        in_specs=[SMEM] + [VMEM] * (count + 5),
        out_specs=[VMEM] * count,
        compiler_params=pltpu.CompilerParams(vmem_limit_bytes=vmem_bytes),
        cost_estimate=cost(flops, *blocks, w_query, w_key, w_value, w_out),
        name="attend",
    )(first, *blocks, gain, w_query, w_key, w_value, w_out)
    return [o.reshape(frames_per, pixels, channels) for o in outs]


def after(value, other):
    return lax.optimization_barrier((value, other))[0]


def per_device(
    video, w_time, b_time, w_down, b_down, w_space, b_space, gain, w_query, w_key, w_value, w_out
):
    frames, height, width, channels = video.shape
    devices = lax.axis_size("tm")
    levels = devices // pair
    columns = lax.axis_size("cols")
    place = lax.axis_index("tm")
    side = place % pair
    level = place // pair
    column = lax.axis_index("cols")
    half = height // pair
    halves = frames
    flags_of = lambda top, bottom: jnp.stack(
        [level, 1 if top is None else top, 1 if bottom is None else bottom]
    ).astype(jnp.int32)
    w_time = w_time.reshape(-1, channels)
    w_down = w_down.reshape(-1, channels)
    w_space = w_space.reshape(-1, channels)
    b_time, b_down, b_space, gain = (v.reshape(1, -1) for v in (b_time, b_down, b_space, gain))

    def exchange(value, bit):
        sets = [[i, i ^ bit] for i in range(devices) if i < i ^ bit]
        both = lax.all_gather(value, "tm", axis_index_groups=sets)
        return lax.dynamic_index_in_dim(both, (place < place ^ bit).astype(jnp.int32), keepdims=False)

    def swap(value):
        return exchange(value, 1)

    def rows_of(owner, begin, end):
        low, high = owner * half + begin - 1, owner * half + end - 1
        body = video[:, max(low, 0) : min(high, height)]
        return jnp.pad(body, ((0, 0), (max(-low, 0), max(high - height, 0)), (0, 0), (0, 0)))

    def beside(value):
        last, first = value[:, :, -1:], value[:, :, :1]
        if columns == 2:
            other = lax.ppermute(jnp.where(column == 0, last, first), "cols", [(0, 1), (1, 0)])
            return jnp.where(column == 1, other, 0), jnp.where(column == 0, other, 0)
        up = [(i, i + 1) for i in range(columns - 1)]
        return lax.ppermute(last, "cols", up), lax.ppermute(
            first, "cols", [(j, i) for i, j in up]
        )

    if half % 4 == 0:
        sizes = (half // 4, half // 2, half // 4)
    else:
        sizes = (half,)
    direct = levels <= most_direct and levels & (levels - 1) == 0
    encoded = jnp.zeros((halves // pair, height * width, channels), jnp.bfloat16)
    previous = None
    previous_sent = None
    begin = 0
    for index, size in enumerate(sizes):
        end = begin + size
        first_row = 0 if index == 0 else begin + 2
        last_row = end + 2
        mine, others = (
            jnp.where(side == s, rows_of(0, first_row, last_row), rows_of(1, first_row, last_row))
            for s in (0, 1)
        )
        if previous_sent is not None:
            others = after(others, previous_sent)
        received = swap(others)
        previous_sent = received
        lower = jnp.where(side == 0, mine, received)
        upper = jnp.where(side == 0, received, mine)
        halo = lax.ppermute(
            upper[frames - taps :], "tm", [(i, i + pair) for i in range(devices - pair)]
        )
        ext = jnp.concatenate([halo, lower, upper], axis=0)
        flags = flags_of(side if index == 0 else None, 1 - side if end == half else None)
        reduced = lift(flags, ext, w_time, b_time, w_down, b_down)
        left, right = beside(reduced)
        pieces = (left, reduced, right)
        if previous is not None:
            pieces = tuple(jnp.concatenate(pq, axis=1) for pq in zip(previous, pieces))
        previous = tuple(p[:, -2:] for p in pieces)
        left, middle, right = pieces
        to_right = jnp.concatenate([left, middle[:, :, :-1]], axis=2)
        to_left = jnp.concatenate([middle[:, :, 1:], right], axis=2)
        spatial = space(to_right, middle, to_left, w_space, b_space)
        pixels = size * width // levels
        blocks = spatial.reshape(halves, levels, pixels, channels)
        if direct:
            gathered = []
            for j in range(levels):
                block = lax.dynamic_index_in_dim(blocks, level ^ j, 1, keepdims=False)
                if j:
                    block = exchange(block, j * pair)
                gathered.append(block)
            first = jnp.stack([(level ^ j) * halves for j in range(levels)]).astype(jnp.int32)
            results = attend(first, gathered, gain, w_query, w_key, w_value, w_out)
            returned = []
            for j in range(levels):
                block = results[j]
                if j:
                    block = exchange(block, j * pair)
                returned.append(block)
            whole = jnp.zeros((halves, levels, pixels, channels), jnp.bfloat16)
            for j in range(levels):
                whole = lax.dynamic_update_index_in_dim(whole, returned[j], level ^ j, 1)
        else:
            sets = [[s + pair * z for z in range(levels)] for s in range(pair)]
            gathered = lax.all_to_all(blocks, "tm", 1, 0, axis_index_groups=sets, tiled=True)
            gathered = gathered.reshape(halves * levels, pixels, channels)
            first = jnp.zeros((1,), jnp.int32)
            (result,) = attend(first, [gathered], gain, w_query, w_key, w_value, w_out)
            result = result.reshape(halves * levels, 1, pixels, channels)
            whole = lax.all_to_all(result, "tm", 0, 1, axis_index_groups=sets, tiled=True)
        whole = whole.reshape(pair, halves // pair, size * width, channels)
        kept = jnp.where(side == 0, whole[0], whole[1])
        other = swap(jnp.where(side == 0, whole[1], whole[0]))
        encoded = lax.dynamic_update_slice(
            encoded, kept, (0, (side * half + begin) * width, 0)
        )
        encoded = lax.dynamic_update_slice(
            encoded, other, (0, ((1 - side) * half + begin) * width, 0)
        )
        begin = end
    return encoded.reshape(halves // pair, height, width, channels)


def solution(mesh):
    spread = P(("clips", "tm"), None, "cols", None)
    return jax.shard_map(
        per_device,
        mesh=mesh,
        in_specs=(spread,) + (P(),) * 11,
        out_specs=spread,
        check_vma=False,
    )
```

```python
from functools import partial

import jax
import jax.numpy as jnp
from jax import lax
from jax.experimental import pallas as pl
from jax.experimental.pallas import tpu as pltpu
from jax.sharding import PartitionSpec as P

epsilon = 1e-06
parts = 2
taps = 3
most_direct = 8
mebibyte = 1024 * 1024

VMEM = pl.BlockSpec(memory_space=pltpu.VMEM)
SMEM = pl.BlockSpec(memory_space=pltpu.SMEM)
ANY = pl.BlockSpec(memory_space=pl.ANY)


def silu(v):
    return 0.5 * v * (1.0 + jnp.tanh(0.5 * v))


def dot32(a, b):
    return jnp.dot(a, b, preferred_element_type=jnp.float32)


def cost(flops, *arrays):
    size = sum(a.size * a.dtype.itemsize for a in arrays)
    return pl.CostEstimate(flops=flops, bytes_accessed=size, transcendentals=0)


def params(mebibytes):
    return pltpu.CompilerParams(vmem_limit_bytes=mebibytes * mebibyte)


def pick_kernel(first, begin, video, out, sem):
    count, rows = out.shape[:2]
    copy = pltpu.make_async_copy(video.at[first : first + count, begin : begin + rows], out, sem)
    copy.start()
    copy.wait()


def pick(video, first, begin, end):
    frames, _, width, channels = video.shape
    shape = (frames - first, end - begin, width, channels)
    return pl.pallas_call(
        partial(pick_kernel, first, begin),
        out_shape=jax.ShapeDtypeStruct(shape, video.dtype),
        in_specs=[ANY],
        out_specs=VMEM,
        scratch_shapes=[pltpu.SemaphoreType.DMA],
        compiler_params=params(56),
        name="pick",
    )(video)


def early_kernel(begin, video, edge, w_time, b_time, w_down, b_down, own, part, rows_in, lifted, sem):
    frames, rows, width, channels = rows_in.shape
    pixels = rows * width
    copy = pltpu.make_async_copy(video.at[:, begin : begin + rows], rows_in, sem)
    copy.start()
    copy.wait()

    def frame(t):
        return jnp.concatenate([rows_in[t].reshape(pixels, channels), edge[t]], axis=0)

    for t in range(taps - 1, frames):
        lhs = jnp.concatenate([frame(t - k) for k in range(taps)], axis=1)
        acc = dot32(lhs, w_time[...]) + b_time[...]
        lifted[t] = (frame(t).astype(jnp.float32) + silu(acc)).astype(jnp.bfloat16)
    for s in range(1, frames // 2):
        known = [k for k in range(taps) if 2 * s + 1 - k >= taps - 1]
        lhs = jnp.concatenate([lifted[2 * s + 1 - k] for k in known], axis=1)
        part[s - 1] = dot32(lhs, w_down[: len(known) * channels]) + b_down[...]
    for t in range(taps - 1):
        own[t] = frame(t)


def early(video, edge, begin, end, w_time, b_time, w_down, b_down):
    frames, _, width, channels = video.shape
    rows = end - begin
    pixels = rows * width + edge.shape[1]
    flops = 2 * channels * channels * pixels * (taps * (frames - 2) + 2)
    return pl.pallas_call(
        partial(early_kernel, begin),
        out_shape=[
            jax.ShapeDtypeStruct((taps - 1, pixels, channels), jnp.bfloat16),
            jax.ShapeDtypeStruct((frames // 2 - 1, pixels, channels), jnp.float32),
        ],
        in_specs=[ANY] + [VMEM] * 5,
        out_specs=[VMEM] * 2,
        scratch_shapes=[
            pltpu.VMEM((frames, rows, width, channels), jnp.bfloat16),
            pltpu.VMEM((frames, pixels, channels), jnp.bfloat16),
            pltpu.SemaphoreType.DMA,
        ],
        compiler_params=params(24),
        cost_estimate=cost(flops, w_time, w_down),
        name="early",
    )(video, edge, w_time, b_time, w_down, b_down)


def conv_kernel(
    owners, size, fresh, last, scalars, halo, halo_edge, own, part, w_time, b_time, w_down, b_down,
    w_space, b_space, *refs
):
    refs = list(refs)
    kept = None if fresh else refs.pop(0)
    lifted, buffers, result, weights, sem = refs[-5:]
    outs = refs[:owners]
    keeps = None if last else refs[owners]
    _, rows, width, channels = halo.shape
    halves = result.shape[0]
    pixels = rows * width
    edges = halo_edge.shape[1]
    fetch = pltpu.make_async_copy(w_space, weights, sem)
    fetch.start()
    column = scalars[1]

    def frame(t):
        if t >= 0:
            return own[t]
        return jnp.concatenate([halo[t + taps].reshape(pixels, channels), halo_edge[t + taps]], 0)

    for t in range(-1, taps - 1):
        lhs = jnp.concatenate([frame(t - k) for k in range(taps)], axis=1)
        acc = dot32(lhs, w_time[...]) + b_time[...]
        value = frame(t).astype(jnp.float32) + silu(acc)
        if t < 0:
            value = jnp.where(scalars[0] > 0, value, 0.0)
        lifted[t + 1] = value.astype(jnp.bfloat16)

    top = 1 if fresh else 2
    row_of = lax.broadcasted_iota(jnp.int32, (pixels, edges), 0) // width
    spread = (row_of == lax.broadcasted_iota(jnp.int32, (pixels, edges), 1)).astype(jnp.bfloat16)
    across = lax.broadcasted_iota(jnp.int32, (pixels, channels), 0) % width
    for s in range(halves):
        late = [k for k in range(taps) if 2 * s + 1 - k < taps - 1]
        acc = b_down[...] if s == 0 else part[s - 1]
        if late:
            lhs = jnp.concatenate([lifted[2 * s + 2 - k] for k in late], axis=1)
            acc = dot32(lhs, w_down[late[0] * channels : (late[-1] + 1) * channels]) + acc
        reduced = acc.astype(jnp.bfloat16)
        wide = reduced[:pixels].astype(jnp.float32)
        beside = dot32(spread, reduced[pixels:])
        before = jnp.where(column == 1, beside, 0.0)
        behind = jnp.where(column == 0, beside, 0.0)
        shifted = (
            jnp.where(across == 0, before, pltpu.roll(wide, 1, 0)),
            wide,
            jnp.where(across == width - 1, behind, pltpu.roll(wide, pixels - 1, 0)),
        )
        for b in range(3):
            value = shifted[b].astype(jnp.bfloat16).reshape(rows, width, channels)
            buffers[b, s, top : top + rows] = value
    blank = jnp.zeros((3, halves, 1, width, channels), jnp.bfloat16)
    if fresh:
        buffers[:, :, :1] = blank
    else:
        buffers[:, :, :2] = kept[...]
    if last:
        buffers[:, :, size + 1 :] = blank
    else:
        keeps[...] = buffers[:, :, size:]
    fetch.wait()

    @pl.loop(0, halves)
    def _(s):
        def window(b, a):
            return buffers[b, s, a : a + size].reshape(size * width, channels)

        lhs = jnp.concatenate([window(b, a) for a in range(3) for b in range(3)], axis=1)
        acc = dot32(lhs, weights[...]) + b_space[...]
        value = window(1, 1).astype(jnp.float32) + silu(acc)
        result[s] = value.astype(jnp.bfloat16)

    each = size * width // owners
    if owners == 1:
        outs[0][...] = result[...]
    else:
        for j, out in enumerate(outs):
            begin = pl.multiple_of(scalars[2 + j] * each, each)
            out[...] = result[:, pl.ds(begin, each)]


def conv(
    owners, size, kept, last, scalars, halo, halo_edge, own, part, w_time, b_time, w_down, b_down,
    w_space, b_space
):
    _, rows, width, channels = halo.shape
    halves = part.shape[0] + 1
    pixels = own.shape[1]
    fresh = kept is None
    flops = 2 * channels * channels * (pixels * (taps * taps + 4) + 9 * halves * size * width)
    shapes = [(halves, size * width // owners, channels)] * owners
    if not last:
        shapes.append((3, halves, 2, width, channels))
    given = [] if fresh else [kept]
    return pl.pallas_call(
        partial(conv_kernel, owners, size, fresh, last),
        out_shape=[jax.ShapeDtypeStruct(shape, jnp.bfloat16) for shape in shapes],
        in_specs=[SMEM] + [VMEM] * 8 + [ANY] + [VMEM] * (1 + len(given)),
        out_specs=[VMEM] * len(shapes),
        scratch_shapes=[
            pltpu.VMEM((taps, pixels, channels), jnp.bfloat16),
            pltpu.VMEM((3, halves, size + 2, width, channels), jnp.bfloat16),
            pltpu.VMEM((halves, size * width, channels), jnp.bfloat16),
            pltpu.VMEM(w_space.shape, jnp.bfloat16),
            pltpu.SemaphoreType.DMA,
        ],
        compiler_params=params(36),
        cost_estimate=cost(flops, halo, own, part, w_time, w_down, w_space),
        name="conv",
    )(
        scalars, halo, halo_edge, own, part, w_time, b_time, w_down, b_down, w_space, b_space,
        *given
    )


def attend_kernel(frames_per, lanes, count, first, *refs):
    blocks = refs[:count]
    gain, w_query, w_key, w_value, w_out = refs[count : count + 5]
    outs = refs[count + 5 :]
    channels = gain.shape[-1]
    flat = len(blocks[0].shape) == 2
    groups = 1 if flat else blocks[0].shape[1] // lanes
    each = frames_per * lanes
    size = count * each

    def piece(ref, g):
        if flat:
            return ref[...]
        return ref[:, g * lanes : (g + 1) * lanes].reshape(each, channels)

    def place(index):
        block = index // each
        frame = index // lanes % frames_per
        time = frame
        for j in range(count):
            time = time + jnp.where(block == j, first[j], 0)
        return time, index % lanes

    row_time, row_lane = place(lax.broadcasted_iota(jnp.int32, (size, 1), 0))
    col_time, col_lane = place(lax.broadcasted_iota(jnp.int32, (1, size), 1))
    allowed = (row_lane == col_lane) & (col_time <= row_time)
    x = jnp.concatenate([piece(b, g) for g in range(groups) for b in blocks], axis=0)
    wide = x.astype(jnp.float32)
    scale = lax.rsqrt(jnp.mean(wide * wide, axis=-1, keepdims=True) + epsilon)
    normed = (wide * scale * gain[...]).astype(jnp.bfloat16)
    query = dot32(normed, w_query[...]).astype(jnp.bfloat16)
    key = dot32(normed, w_key[...]).astype(jnp.bfloat16)
    value = dot32(normed, w_value[...]).astype(jnp.bfloat16)
    contexts = []
    for g in range(groups):
        part = slice(g * size, (g + 1) * size)
        scores = lax.dot_general(
            query[part], key[part], (((1,), (1,)), ((), ())), preferred_element_type=jnp.float32
        )
        scores = jnp.where(allowed, scores * channels ** (-0.5), -1e30)
        largest = jnp.max(scores, axis=-1, keepdims=True)
        probs = jnp.exp(scores - largest)
        probs = (probs / jnp.sum(probs, axis=-1, keepdims=True)).astype(jnp.bfloat16)
        contexts.append(dot32(probs, value[part]).astype(jnp.bfloat16))
    mixed = dot32(jnp.concatenate(contexts, axis=0), w_out[...])
    result = (wide + mixed).astype(jnp.bfloat16)
    for g in range(groups):
        for j, out in enumerate(outs):
            begin = g * size + j * each
            rows = result[begin : begin + each]
            if flat:
                out[...] = rows
            else:
                out[:, g * lanes : (g + 1) * lanes] = rows.reshape(frames_per, lanes, channels)


def attend(first, blocks, gain, w_query, w_key, w_value, w_out):
    frames_per, pixels, channels = blocks[0].shape
    lanes = 16 if pixels % 16 == 0 else pixels
    flat = pixels % 16 != 0
    if flat:
        blocks = [b.reshape(frames_per * pixels, channels) for b in blocks]
    count = len(blocks)
    rows = frames_per * pixels * count
    size = frames_per * count * lanes
    flops = 2 * rows * channels * (4 * channels + 2 * frames_per * count * lanes)
    outs = pl.pallas_call(
        partial(attend_kernel, frames_per, lanes, count),
        out_shape=[jax.ShapeDtypeStruct(b.shape, jnp.bfloat16) for b in blocks],
        in_specs=[SMEM] + [VMEM] * (count + 5),
        out_specs=[VMEM] * count,
        compiler_params=params(20 if 16 * size * size < 20 * mebibyte else 56),
        cost_estimate=cost(flops, *blocks, w_query, w_key, w_value, w_out),
        name="attend",
    )(first, *blocks, gain, w_query, w_key, w_value, w_out)
    return [o.reshape(frames_per, pixels, channels) for o in outs]


def collect_kernel(count, base, order, *refs):
    blocks = refs[:count]
    out, sems = refs[-2:]
    copies = [
        pltpu.make_async_copy(block, out.at[:, base + order[j]], sems.at[j])
        for j, block in enumerate(blocks)
    ]
    for copy in copies:
        copy.start()
    for copy in copies:
        copy.wait()


def collect(order, blocks, chunk, chunks, whole):
    count = len(blocks)
    halves, pixels, channels = blocks[0].shape
    shape = (halves, chunks * count, pixels, channels)
    given = [] if whole is None else [whole]
    return pl.pallas_call(
        partial(collect_kernel, count, chunk * count),
        out_shape=jax.ShapeDtypeStruct(shape, jnp.bfloat16),
        in_specs=[SMEM] + [ANY] * (count + len(given)),
        out_specs=ANY,
        input_output_aliases={count + 1: 0} if given else {},
        scratch_shapes=[pltpu.SemaphoreType.DMA((count,))],
        compiler_params=params(16),
        name="collect",
    )(order, *blocks, *given)


def after(value, other):
    return lax.optimization_barrier((value, other))[0]


def per_device(
    video, w_time, b_time, w_down, b_down, w_space, b_space, gain, w_query, w_key, w_value, w_out
):
    frames, height, width, channels = video.shape
    devices = lax.axis_size("tm")
    columns = lax.axis_size("cols")
    assert columns == 2
    place = lax.axis_index("tm").astype(jnp.int32)
    column = lax.axis_index("cols").astype(jnp.int32)
    halves = frames // 2
    w_time = w_time.reshape(-1, channels)
    w_down = w_down.reshape(-1, channels)
    w_space = w_space.reshape(-1, channels)
    b_time, b_down, b_space, gain = (v.reshape(1, -1) for v in (b_time, b_down, b_space, gain))
    chunks = parts if height % parts == 0 and height // parts * width % devices == 0 else 1
    size = height // chunks
    each = size * width // devices
    direct = devices <= most_direct and devices & (devices - 1) == 0 and each % 16 == 0
    issue = sorted(range(1, devices), key=lambda j: -j)
    order = place ^ jnp.arange(devices, dtype=jnp.int32) if direct else jnp.zeros(1, jnp.int32)
    scalars = jnp.concatenate([jnp.stack([place, column]), order])
    owners = order.shape[0]

    def exchange(blocks):
        result = list(blocks)
        for j in issue:
            result[j] = lax.ppermute(blocks[j], "tm", [(i, i ^ j) for i in range(devices)])
        return result

    spans = [
        (k * size + (1 if k else 0), min((k + 1) * size + 1, height)) for k in range(chunks)
    ]
    onward = [(i, i + 1) for i in range(devices - 1)]
    aslant = [
        (i * columns + c, (i + 1) * columns + 1 - c)
        for i in range(devices - 1)
        for c in range(columns)
    ]
    sent = [pick(video, frames - taps, begin, end) for begin, end in spans]
    border = jnp.where(column == 0, video[:, :, -1], video[:, :, 0])
    border = after(border, sent[0])
    halos = [lax.ppermute(value, "tm", onward) for value in sent]
    own_edge = lax.ppermute(border, "cols", [(0, 1), (1, 0)])
    halo_edge = lax.ppermute(border[frames - taps :], ("tm", "cols"), aslant)

    def edge_rows(edge, begin, end):
        return jnp.pad(edge[:, begin:end], ((0, 0), (0, -(end - begin) % 16), (0, 0)))

    ahead = [
        early(video, edge_rows(own_edge, begin, end), begin, end, w_time, b_time, w_down, b_down)
        for begin, end in spans
    ]
    spatials, kept = [], None
    for index, (begin, end) in enumerate(spans):
        own, part = ahead[index]
        if spatials:
            own = after(own, spatials[-1][0])
        last = index == chunks - 1
        made = conv(
            owners, size, kept, last, scalars, halos[index], edge_rows(halo_edge, begin, end), own,
            part, w_time, b_time, w_down, b_down, w_space, b_space
        )
        spatials.append(made[:owners])
        kept = None if last else made[owners]

    newest = spatials[-1][0]
    if direct:
        whole = None
        returns = []
        for gathered in [exchange(blocks) for blocks in spatials]:
            gathered[0] = after(gathered[0], newest)
            results = attend(order * halves, gathered, gain, w_query, w_key, w_value, w_out)
            newest = results[0]
            returns.append(exchange(results))
        for index, blocks in enumerate(returns):
            whole = collect(order, blocks, index, chunks, whole)
        return whole.reshape(halves, height, width, channels)
    returns = []
    for (block,) in spatials:
        gathered = lax.all_to_all(block, "tm", 1, 0, tiled=True)
        (result,) = attend(order, [gathered], gain, w_query, w_key, w_value, w_out)
        returns.append(lax.all_to_all(result, "tm", 0, 1, tiled=True))
    return jnp.concatenate(returns, axis=1).reshape(halves, height, width, channels)


def solution(mesh):
    spread = P(("clips", "tm"), None, "cols", None)
    return jax.shard_map(
        per_device,
        mesh=mesh,
        in_specs=(spread,) + (P(),) * 11,
        out_specs=spread,
        check_vma=False,
    )
```

```python
from functools import partial

import jax
import jax.numpy as jnp
from jax import lax
from jax.experimental import pallas as pl
from jax.experimental.pallas import tpu as pltpu
from jax.sharding import PartitionSpec as P

epsilon = 1e-06
parts = 2
taps = 3
most_direct = 8
mebibyte = 1024 * 1024

VMEM = pl.BlockSpec(memory_space=pltpu.VMEM)
SMEM = pl.BlockSpec(memory_space=pltpu.SMEM)
HBM = pl.BlockSpec(memory_space=pltpu.HBM)
ANY = pl.BlockSpec(memory_space=pl.ANY)


def silu(v):
    return 0.5 * v * (1.0 + jnp.tanh(0.5 * v))


def dot32(a, b):
    return jnp.dot(a, b, preferred_element_type=jnp.float32)


def cost(flops, *arrays):
    size = sum(a.size * a.dtype.itemsize for a in arrays)
    return pl.CostEstimate(flops=flops, bytes_accessed=size, transcendentals=0)


def params(mebibytes):
    return pltpu.CompilerParams(vmem_limit_bytes=mebibytes * mebibyte)


def pick_kernel(first, begin, video, out, sem):
    count, rows = out.shape[:2]
    copies = [
        pltpu.make_async_copy(video.at[first + t, begin : begin + rows], out.at[t], sem.at[t])
        for t in range(count)
    ]
    for copy in copies:
        copy.start()
    for copy in copies:
        copy.wait()


def pick(video, first, begin, end):
    frames, _, width, channels = video.shape
    shape = (frames - first, end - begin, width, channels)
    return pl.pallas_call(
        partial(pick_kernel, first, begin),
        out_shape=jax.ShapeDtypeStruct(shape, video.dtype),
        in_specs=[HBM],
        out_specs=VMEM,
        scratch_shapes=[pltpu.SemaphoreType.DMA((frames - first,))],
        compiler_params=params(8),
        name="pick",
    )(video)


def early_kernel(begin, video, edge, w_time, b_time, w_down, b_down, own, part, rows_in, lifted, sem):
    frames, rows, width, channels = rows_in.shape
    pixels = rows * width
    copies = [
        pltpu.make_async_copy(video.at[t, begin : begin + rows], rows_in.at[t], sem.at[t])
        for t in range(frames)
    ]
    for copy in copies:
        copy.start()
    for copy in copies:
        copy.wait()

    def frame(t):
        return jnp.concatenate([rows_in[t].reshape(pixels, channels), edge[t]], axis=0)

    for t in range(taps - 1, frames):
        lhs = jnp.concatenate([frame(t - k) for k in range(taps)], axis=1)
        acc = dot32(lhs, w_time[...]) + b_time[...]
        lifted[t] = (frame(t).astype(jnp.float32) + silu(acc)).astype(jnp.bfloat16)
    for s in range(1, frames // 2):
        known = [k for k in range(taps) if 2 * s + 1 - k >= taps - 1]
        lhs = jnp.concatenate([lifted[2 * s + 1 - k] for k in known], axis=1)
        part[s - 1] = dot32(lhs, w_down[: len(known) * channels]) + b_down[...]
    for t in range(taps - 1):
        own[t] = frame(t)


def early(video, edge, begin, end, w_time, b_time, w_down, b_down):
    frames, _, width, channels = video.shape
    rows = end - begin
    pixels = rows * width + edge.shape[1]
    flops = 2 * channels * channels * pixels * (taps * (frames - 2) + 2)
    return pl.pallas_call(
        partial(early_kernel, begin),
        out_shape=[
            jax.ShapeDtypeStruct((taps - 1, pixels, channels), jnp.bfloat16),
            jax.ShapeDtypeStruct((frames // 2 - 1, pixels, channels), jnp.float32),
        ],
        in_specs=[HBM] + [VMEM] * 5,
        out_specs=[VMEM] * 2,
        scratch_shapes=[
            pltpu.VMEM((frames, rows, width, channels), jnp.bfloat16),
            pltpu.VMEM((frames, pixels, channels), jnp.bfloat16),
            pltpu.SemaphoreType.DMA((frames,)),
        ],
        compiler_params=params(16),
        cost_estimate=cost(flops, w_time, w_down),
        name="early",
    )(video, edge, w_time, b_time, w_down, b_down)


def conv_kernel(
    owners, size, fresh, last, scalars, halo, halo_edge, own, part, w_time, b_time, w_down, b_down,
    w_space, b_space, *refs
):
    refs = list(refs)
    kept = None if fresh else refs.pop(0)
    lifted, buffers, result, weights, sem = refs[-5:]
    outs = refs[:owners]
    keeps = None if last else refs[owners]
    _, rows, width, channels = halo.shape
    halves = result.shape[0]
    pixels = rows * width
    edges = halo_edge.shape[1]
    fetches = [
        pltpu.make_async_copy(w_space.at[tap], weights.at[tap], sem.at[tap])
        for tap in range(w_space.shape[0])
    ]
    for fetch in fetches:
        fetch.start()
    column = scalars[1]

    def frame(t):
        if t >= 0:
            return own[t]
        return jnp.concatenate([halo[t + taps].reshape(pixels, channels), halo_edge[t + taps]], 0)

    for t in range(-1, taps - 1):
        lhs = jnp.concatenate([frame(t - k) for k in range(taps)], axis=1)
        acc = dot32(lhs, w_time[...]) + b_time[...]
        value = frame(t).astype(jnp.float32) + silu(acc)
        if t < 0:
            value = jnp.where(scalars[0] > 0, value, 0.0)
        lifted[t + 1] = value.astype(jnp.bfloat16)

    top = 1 if fresh else 2
    row_of = lax.broadcasted_iota(jnp.int32, (pixels, edges), 0) // width
    spread = (row_of == lax.broadcasted_iota(jnp.int32, (pixels, edges), 1)).astype(jnp.bfloat16)
    across = lax.broadcasted_iota(jnp.int32, (pixels, channels), 0) % width
    for s in range(halves):
        late = [k for k in range(taps) if 2 * s + 1 - k < taps - 1]
        acc = b_down[...] if s == 0 else part[s - 1]
        if late:
            lhs = jnp.concatenate([lifted[2 * s + 2 - k] for k in late], axis=1)
            acc = dot32(lhs, w_down[late[0] * channels : (late[-1] + 1) * channels]) + acc
        reduced = acc.astype(jnp.bfloat16)
        wide = reduced[:pixels].astype(jnp.float32)
        beside = dot32(spread, reduced[pixels:])
        before = jnp.where(column == 1, beside, 0.0)
        behind = jnp.where(column == 0, beside, 0.0)
        shifted = (
            jnp.where(across == 0, before, pltpu.roll(wide, 1, 0)),
            wide,
            jnp.where(across == width - 1, behind, pltpu.roll(wide, pixels - 1, 0)),
        )
        for b in range(3):
            value = shifted[b].astype(jnp.bfloat16).reshape(rows, width, channels)
            buffers[b, s, top : top + rows] = value
    blank = jnp.zeros((3, halves, 1, width, channels), jnp.bfloat16)
    if fresh:
        buffers[:, :, :1] = blank
    else:
        buffers[:, :, :2] = kept[...]
    if last:
        buffers[:, :, size + 1 :] = blank
    else:
        keeps[...] = buffers[:, :, size:]
    for fetch in fetches:
        fetch.wait()

    @pl.loop(0, halves)
    def _(s):
        def window(b, a):
            return buffers[b, s, a : a + size].reshape(size * width, channels)

        lhs = jnp.concatenate([window(b, a) for a in range(3) for b in range(3)], axis=1)
        acc = dot32(lhs, weights[...].reshape(-1, channels)) + b_space[...]
        value = window(1, 1).astype(jnp.float32) + silu(acc)
        result[s] = value.astype(jnp.bfloat16)

    each = size * width // owners
    if owners == 1:
        outs[0][...] = result[...]
    else:
        for j, out in enumerate(outs):
            begin = pl.multiple_of(scalars[2 + j] * each, each)
            out[...] = result[:, pl.ds(begin, each)]


def conv(
    owners, size, kept, last, scalars, halo, halo_edge, own, part, w_time, b_time, w_down, b_down,
    w_space, b_space
):
    _, rows, width, channels = halo.shape
    halves = part.shape[0] + 1
    pixels = own.shape[1]
    fresh = kept is None
    flops = 2 * channels * channels * (pixels * (taps * taps + 4) + 9 * halves * size * width)
    shapes = [(halves, size * width // owners, channels)] * owners
    if not last:
        shapes.append((3, halves, 2, width, channels))
    given = [] if fresh else [kept]
    return pl.pallas_call(
        partial(conv_kernel, owners, size, fresh, last),
        out_shape=[jax.ShapeDtypeStruct(shape, jnp.bfloat16) for shape in shapes],
        in_specs=[SMEM] + [VMEM] * 8 + [HBM] + [VMEM] * (1 + len(given)),
        out_specs=[VMEM] * len(shapes),
        scratch_shapes=[
            pltpu.VMEM((taps, pixels, channels), jnp.bfloat16),
            pltpu.VMEM((3, halves, size + 2, width, channels), jnp.bfloat16),
            pltpu.VMEM((halves, size * width, channels), jnp.bfloat16),
            pltpu.VMEM(w_space.shape, jnp.bfloat16),
            pltpu.SemaphoreType.DMA(w_space.shape[:1]),
        ],
        compiler_params=params(24),
        cost_estimate=cost(flops, halo, own, part, w_time, w_down, w_space),
        name="conv",
    )(
        scalars, halo, halo_edge, own, part, w_time, b_time, w_down, b_down, w_space, b_space,
        *given
    )


def attend_kernel(frames_per, lanes, count, first, *refs):
    blocks = refs[:count]
    gain, w_query, w_key, w_value, w_out = refs[count : count + 5]
    outs = refs[count + 5 :]
    channels = gain.shape[-1]
    flat = len(blocks[0].shape) == 2
    groups = 1 if flat else blocks[0].shape[1] // lanes
    each = frames_per * lanes
    size = count * each

    def piece(ref, g):
        if flat:
            return ref[...]
        return ref[:, g * lanes : (g + 1) * lanes].reshape(each, channels)

    def place(index):
        block = index // each
        frame = index // lanes % frames_per
        time = frame
        for j in range(count):
            time = time + jnp.where(block == j, first[j], 0)
        return time, index % lanes

    row_time, row_lane = place(lax.broadcasted_iota(jnp.int32, (size, 1), 0))
    col_time, col_lane = place(lax.broadcasted_iota(jnp.int32, (1, size), 1))
    allowed = (row_lane == col_lane) & (col_time <= row_time)
    x = jnp.concatenate([piece(b, g) for g in range(groups) for b in blocks], axis=0)
    wide = x.astype(jnp.float32)
    scale = lax.rsqrt(jnp.mean(wide * wide, axis=-1, keepdims=True) + epsilon)
    normed = (wide * scale * gain[...]).astype(jnp.bfloat16)
    query = dot32(normed, w_query[...]).astype(jnp.bfloat16)
    key = dot32(normed, w_key[...]).astype(jnp.bfloat16)
    value = dot32(normed, w_value[...]).astype(jnp.bfloat16)
    contexts = []
    for g in range(groups):
        part = slice(g * size, (g + 1) * size)
        scores = lax.dot_general(
            query[part], key[part], (((1,), (1,)), ((), ())), preferred_element_type=jnp.float32
        )
        scores = jnp.where(allowed, scores * channels ** (-0.5), -1e30)
        largest = jnp.max(scores, axis=-1, keepdims=True)
        probs = jnp.exp(scores - largest)
        probs = (probs / jnp.sum(probs, axis=-1, keepdims=True)).astype(jnp.bfloat16)
        contexts.append(dot32(probs, value[part]).astype(jnp.bfloat16))
    mixed = dot32(jnp.concatenate(contexts, axis=0), w_out[...])
    result = (wide + mixed).astype(jnp.bfloat16)
    for g in range(groups):
        for j, out in enumerate(outs):
            begin = g * size + j * each
            rows = result[begin : begin + each]
            if flat:
                out[...] = rows
            else:
                out[:, g * lanes : (g + 1) * lanes] = rows.reshape(frames_per, lanes, channels)


def attend(first, blocks, gain, w_query, w_key, w_value, w_out):
    frames_per, pixels, channels = blocks[0].shape
    lanes = 16 if pixels % 16 == 0 else pixels
    flat = pixels % 16 != 0
    if flat:
        blocks = [b.reshape(frames_per * pixels, channels) for b in blocks]
    count = len(blocks)
    rows = frames_per * pixels * count
    size = frames_per * count * lanes
    flops = 2 * rows * channels * (4 * channels + 2 * frames_per * count * lanes)
    outs = pl.pallas_call(
        partial(attend_kernel, frames_per, lanes, count),
        out_shape=[jax.ShapeDtypeStruct(b.shape, jnp.bfloat16) for b in blocks],
        in_specs=[SMEM] + [VMEM] * (count + 5),
        out_specs=[VMEM] * count,
        compiler_params=params(20 if 16 * size * size < 20 * mebibyte else 56),
        cost_estimate=cost(flops, *blocks, w_query, w_key, w_value, w_out),
        name="attend",
    )(first, *blocks, gain, w_query, w_key, w_value, w_out)
    return [o.reshape(frames_per, pixels, channels) for o in outs]


def collect_kernel(count, base, order, *refs):
    blocks = refs[:count]
    out, sems = refs[-2:]
    copies = [
        pltpu.make_async_copy(block, out.at[:, base + order[j]], sems.at[j])
        for j, block in enumerate(blocks)
    ]
    for copy in copies:
        copy.start()
    for copy in copies:
        copy.wait()


def collect(order, blocks, chunk, chunks, whole):
    count = len(blocks)
    halves, pixels, channels = blocks[0].shape
    shape = (halves, chunks * count, pixels, channels)
    given = [] if whole is None else [whole]
    return pl.pallas_call(
        partial(collect_kernel, count, chunk * count),
        out_shape=jax.ShapeDtypeStruct(shape, jnp.bfloat16),
        in_specs=[SMEM] + [ANY] * (count + len(given)),
        out_specs=ANY,
        input_output_aliases={count + 1: 0} if given else {},
        scratch_shapes=[pltpu.SemaphoreType.DMA((count,))],
        compiler_params=params(16),
        name="collect",
    )(order, *blocks, *given)


def after(value, other):
    return lax.optimization_barrier((value, other))[0]


def per_device(
    video, w_time, b_time, w_down, b_down, w_space, b_space, gain, w_query, w_key, w_value, w_out
):
    frames, height, width, channels = video.shape
    devices = lax.axis_size("tm")
    columns = lax.axis_size("cols")
    assert columns == 2
    place = lax.axis_index("tm").astype(jnp.int32)
    column = lax.axis_index("cols").astype(jnp.int32)
    halves = frames // 2
    w_time = w_time.reshape(-1, channels)
    w_down = w_down.reshape(-1, channels)
    b_time, b_down, b_space, gain = (v.reshape(1, -1) for v in (b_time, b_down, b_space, gain))
    chunks = parts if height % parts == 0 and height // parts * width % devices == 0 else 1
    size = height // chunks
    each = size * width // devices
    direct = devices <= most_direct and devices & (devices - 1) == 0 and each % 16 == 0
    issue = sorted(range(1, devices), key=lambda j: -j)
    order = place ^ jnp.arange(devices, dtype=jnp.int32) if direct else jnp.zeros(1, jnp.int32)
    scalars = jnp.concatenate([jnp.stack([place, column]), order])
    owners = order.shape[0]

    def exchange(blocks):
        result = list(blocks)
        for j in issue:
            result[j] = lax.ppermute(blocks[j], "tm", [(i, i ^ j) for i in range(devices)])
        return result

    spans = [
        (k * size + (1 if k else 0), min((k + 1) * size + 1, height)) for k in range(chunks)
    ]
    onward = [(i, i + 1) for i in range(devices - 1)]
    aslant = [
        (i * columns + c, (i + 1) * columns + 1 - c)
        for i in range(devices - 1)
        for c in range(columns)
    ]
    sent = [pick(video, frames - taps, begin, end) for begin, end in spans]
    border = jnp.where(column == 0, video[:, :, -1], video[:, :, 0])
    border = after(border, sent[0])
    halos = [lax.ppermute(value, "tm", onward) for value in sent]
    own_edge = lax.ppermute(border, "cols", [(0, 1), (1, 0)])
    halo_edge = lax.ppermute(border[frames - taps :], ("tm", "cols"), aslant)

    def edge_rows(edge, begin, end):
        return jnp.pad(edge[:, begin:end], ((0, 0), (0, -(end - begin) % 16), (0, 0)))

    ahead = [
        early(video, edge_rows(own_edge, begin, end), begin, end, w_time, b_time, w_down, b_down)
        for begin, end in spans
    ]
    halo_edge = after(halo_edge, [part for _, part in ahead])
    spatials, kept = [], None
    for index, (begin, end) in enumerate(spans):
        own, part = ahead[index]
        if spatials:
            own = after(own, spatials[-1][0])
        last = index == chunks - 1
        made = conv(
            owners, size, kept, last, scalars, halos[index], edge_rows(halo_edge, begin, end), own,
            part, w_time, b_time, w_down, b_down, w_space, b_space
        )
        spatials.append(made[:owners])
        kept = None if last else made[owners]

    newest = spatials[-1][0]
    if direct:
        whole = None
        returns = []
        for gathered in [exchange(blocks) for blocks in spatials]:
            gathered[0] = after(gathered[0], newest)
            results = attend(order * halves, gathered, gain, w_query, w_key, w_value, w_out)
            newest = results[0]
            returns.append(exchange(results))
        for index, blocks in enumerate(returns):
            whole = collect(order, blocks, index, chunks, whole)
        return whole.reshape(halves, height, width, channels)
    returns = []
    for (block,) in spatials:
        gathered = lax.all_to_all(block, "tm", 1, 0, tiled=True)
        (result,) = attend(order, [gathered], gain, w_query, w_key, w_value, w_out)
        returns.append(lax.all_to_all(result, "tm", 0, 1, tiled=True))
    return jnp.concatenate(returns, axis=1).reshape(halves, height, width, channels)


def solution(mesh):
    spread = P(("clips", "tm"), None, "cols", None)
    return jax.shard_map(
        per_device,
        mesh=mesh,
        in_specs=(spread,) + (P(),) * 11,
        out_specs=spread,
        check_vma=False,
    )
```

```python
from functools import partial

import jax
import jax.numpy as jnp
from jax import lax
from jax.experimental import pallas as pl
from jax.experimental.pallas import tpu as pltpu
from jax.sharding import PartitionSpec as P

epsilon = 1e-06
parts = 2
taps = 3
most_direct = 8
mebibyte = 1024 * 1024

VMEM = pl.BlockSpec(memory_space=pltpu.VMEM)
SMEM = pl.BlockSpec(memory_space=pltpu.SMEM)
ANY = pl.BlockSpec(memory_space=pl.ANY)


def silu(v):
    return 0.5 * v * (1.0 + jnp.tanh(0.5 * v))


def dot32(a, b):
    return jnp.dot(a, b, preferred_element_type=jnp.float32)


def cost(flops, *arrays):
    size = sum(a.size * a.dtype.itemsize for a in arrays)
    return pl.CostEstimate(flops=flops, bytes_accessed=size, transcendentals=0)


def params(mebibytes):
    return pltpu.CompilerParams(vmem_limit_bytes=mebibytes * mebibyte)


def pick_kernel(first, spans, video, *refs):
    outs, sem = refs[:-1], refs[-1]
    copies = []
    for (begin, end), out in zip(spans, outs):
        for t in range(out.shape[0]):
            source = video.at[first + t, begin:end]
            copies.append(pltpu.make_async_copy(source, out.at[t], sem.at[len(copies)]))
    for copy in copies:
        copy.start()
    for copy in copies:
        copy.wait()


def pick(video, first, spans):
    frames, _, width, channels = video.shape
    shapes = [(frames - first, end - begin, width, channels) for begin, end in spans]
    return pl.pallas_call(
        partial(pick_kernel, first, spans),
        out_shape=[jax.ShapeDtypeStruct(shape, video.dtype) for shape in shapes],
        in_specs=[ANY],
        out_specs=[VMEM] * len(shapes),
        scratch_shapes=[pltpu.SemaphoreType.DMA((len(spans) * (frames - first),))],
        compiler_params=params(8),
        name="pick",
    )(video)


def early_kernel(
    begin, video, edge, w_time, b_time, w_down, b_down, own, part, rows_in, lifted, sem
):
    frames, rows, width, channels = rows_in.shape
    pixels = rows * width
    copies = [
        pltpu.make_async_copy(video.at[t, begin : begin + rows], rows_in.at[t], sem.at[t])
        for t in range(frames)
    ]
    for copy in copies:
        copy.start()
    for copy in copies:
        copy.wait()

    def frame(t):
        return jnp.concatenate([rows_in[t].reshape(pixels, channels), edge[t]], axis=0)

    for t in range(taps - 1, frames):
        lhs = jnp.concatenate([frame(t - k) for k in range(taps)], axis=1)
        acc = dot32(lhs, w_time[...]) + b_time[...]
        lifted[t] = (frame(t).astype(jnp.float32) + silu(acc)).astype(jnp.bfloat16)
    for s in range(1, frames // 2):
        known = [k for k in range(taps) if 2 * s + 1 - k >= taps - 1]
        lhs = jnp.concatenate([lifted[2 * s + 1 - k] for k in known], axis=1)
        part[s - 1] = dot32(lhs, w_down[: len(known) * channels]) + b_down[...]
    for t in range(taps - 1):
        own[t] = frame(t)


def early(video, edge, begin, end, w_time, b_time, w_down, b_down):
    frames, _, width, channels = video.shape
    rows = end - begin
    pixels = rows * width + edge.shape[1]
    flops = 2 * channels * channels * pixels * (taps * (frames - 2) + 2)
    return pl.pallas_call(
        partial(early_kernel, begin),
        out_shape=[
            jax.ShapeDtypeStruct((taps - 1, pixels, channels), jnp.bfloat16),
            jax.ShapeDtypeStruct((frames // 2 - 1, pixels, channels), jnp.float32),
        ],
        in_specs=[ANY] + [VMEM] * 5,
        out_specs=[VMEM] * 2,
        scratch_shapes=[
            pltpu.VMEM((frames, rows, width, channels), jnp.bfloat16),
            pltpu.VMEM((frames, pixels, channels), jnp.bfloat16),
            pltpu.SemaphoreType.DMA((frames,)),
        ],
        compiler_params=params(16),
        cost_estimate=cost(flops, w_time, w_down),
        name="early",
    )(video, edge, w_time, b_time, w_down, b_down)


def conv_kernel(
    owners, joined, size, fresh, last, scalars, halo, halo_edge, own, part, w_time, b_time, w_down, b_down,
    w_space, b_space, *refs
):
    refs = list(refs)
    kept = None if fresh else refs.pop(0)
    lifted, buffers, result = refs[-3:]
    outs = refs[: 1 if joined else owners]
    keeps = None if last else refs[-4]
    _, rows, width, channels = halo.shape
    halves = result.shape[0]
    pixels = rows * width
    edges = halo_edge.shape[1]
    column = scalars[1]

    def frame(t):
        if t >= 0:
            return own[t]
        return jnp.concatenate([halo[t + taps].reshape(pixels, channels), halo_edge[t + taps]], 0)

    for t in range(-1, taps - 1):
        lhs = jnp.concatenate([frame(t - k) for k in range(taps)], axis=1)
        acc = dot32(lhs, w_time[...]) + b_time[...]
        value = frame(t).astype(jnp.float32) + silu(acc)
        if t < 0:
            value = jnp.where(scalars[0] > 0, value, 0.0)
        lifted[t + 1] = value.astype(jnp.bfloat16)

    top = 1 if fresh else 2
    row_of = lax.broadcasted_iota(jnp.int32, (pixels, edges), 0) // width
    spread = (row_of == lax.broadcasted_iota(jnp.int32, (pixels, edges), 1)).astype(jnp.bfloat16)
    across = lax.broadcasted_iota(jnp.int32, (pixels, channels), 0) % width
    for s in range(halves):
        late = [k for k in range(taps) if 2 * s + 1 - k < taps - 1]
        acc = b_down[...] if s == 0 else part[s - 1]
        if late:
            lhs = jnp.concatenate([lifted[2 * s + 2 - k] for k in late], axis=1)
            acc = dot32(lhs, w_down[late[0] * channels : (late[-1] + 1) * channels]) + acc
        reduced = acc.astype(jnp.bfloat16)
        wide = reduced[:pixels].astype(jnp.float32)
        beside = dot32(spread, reduced[pixels:])
        before = jnp.where(column == 1, beside, 0.0)
        behind = jnp.where(column == 0, beside, 0.0)
        shifted = (
            jnp.where(across == 0, before, pltpu.roll(wide, 1, 0)),
            wide,
            jnp.where(across == width - 1, behind, pltpu.roll(wide, pixels - 1, 0)),
        )
        for b in range(3):
            value = shifted[b].astype(jnp.bfloat16).reshape(rows, width, channels)
            buffers[b, s, top : top + rows] = value
    blank = jnp.zeros((3, halves, 1, width, channels), jnp.bfloat16)
    if fresh:
        buffers[:, :, :1] = blank
    else:
        buffers[:, :, :2] = kept[...]
    if last:
        buffers[:, :, size + 1 :] = blank
    else:
        keeps[...] = buffers[:, :, size:]

    @pl.loop(0, halves)
    def _(s):
        def window(b, a):
            return buffers[b, s, a : a + size].reshape(size * width, channels)

        lhs = jnp.concatenate([window(b, a) for a in range(3) for b in range(3)], axis=1)
        acc = dot32(lhs, w_space[...].reshape(-1, channels)) + b_space[...]
        value = window(1, 1).astype(jnp.float32) + silu(acc)
        result[s] = value.astype(jnp.bfloat16)

    each = size * width // owners
    if owners == 1:
        outs[0][...] = result[...]
    elif joined:
        for j in range(owners):
            outs[0][j] = result[:, j * each : (j + 1) * each]
    else:
        for j, out in enumerate(outs):
            begin = pl.multiple_of(scalars[2 + j] * each, each)
            out[...] = result[:, pl.ds(begin, each)]


def conv(
    owners, joined, size, kept, last, scalars, halo, halo_edge, own, part, w_time, b_time, w_down, b_down,
    w_space, b_space
):
    _, rows, width, channels = halo.shape
    halves = part.shape[0] + 1
    pixels = own.shape[1]
    fresh = kept is None
    flops = 2 * channels * channels * (pixels * (taps * taps + 4) + 9 * halves * size * width)
    block = (halves, size * width // owners, channels)
    shapes = [(owners,) + block] if joined else [block] * owners
    if not last:
        shapes.append((3, halves, 2, width, channels))
    given = [] if fresh else [kept]
    return pl.pallas_call(
        partial(conv_kernel, owners, joined, size, fresh, last),
        out_shape=[jax.ShapeDtypeStruct(shape, jnp.bfloat16) for shape in shapes],
        in_specs=[SMEM] + [VMEM] * 9 + [VMEM] * (1 + len(given)),
        out_specs=[VMEM] * len(shapes),
        scratch_shapes=[
            pltpu.VMEM((taps, pixels, channels), jnp.bfloat16),
            pltpu.VMEM((3, halves, size + 2, width, channels), jnp.bfloat16),
            pltpu.VMEM((halves, size * width, channels), jnp.bfloat16),
        ],
        compiler_params=params(24),
        cost_estimate=cost(flops, halo, own, part, w_time, w_down, w_space),
        name="conv",
    )(
        scalars, halo, halo_edge, own, part, w_time, b_time, w_down, b_down, w_space, b_space,
        *given
    )


def attend_kernel(frames_per, lanes, count, taken, order, *refs):
    blocks = refs[:taken]
    gain, w_query, w_key, w_value, w_out = refs[taken : taken + 5]
    outs = refs[taken + 5 :]
    channels = gain.shape[-1]
    flat = len(blocks[0].shape) == 2
    groups = 1 if flat else blocks[0].shape[-2] // lanes
    each = frames_per * lanes
    size = count * each

    def piece(j, g):
        if flat:
            return blocks[0][...]
        part = slice(g * lanes, (g + 1) * lanes)
        rows = blocks[j][:, part] if taken == count else blocks[0][order[j], :, part]
        return rows.reshape(each, channels)

    def place(index):
        block = index // each
        time = index // lanes % frames_per
        for j in range(count):
            time = time + jnp.where(block == j, order[j] * frames_per, 0)
        return time, index % lanes

    row_time, row_lane = place(lax.broadcasted_iota(jnp.int32, (size, 1), 0))
    col_time, col_lane = place(lax.broadcasted_iota(jnp.int32, (1, size), 1))
    allowed = (row_lane == col_lane) & (col_time <= row_time)
    x = jnp.concatenate([piece(j, g) for g in range(groups) for j in range(count)], axis=0)
    wide = x.astype(jnp.float32)
    scale = lax.rsqrt(jnp.mean(wide * wide, axis=-1, keepdims=True) + epsilon)
    normed = (wide * scale * gain[...]).astype(jnp.bfloat16)
    query = dot32(normed, w_query[...]).astype(jnp.bfloat16)
    key = dot32(normed, w_key[...]).astype(jnp.bfloat16)
    value = dot32(normed, w_value[...]).astype(jnp.bfloat16)
    contexts = []
    for g in range(groups):
        part = slice(g * size, (g + 1) * size)
        scores = lax.dot_general(
            query[part], key[part], (((1,), (1,)), ((), ())), preferred_element_type=jnp.float32
        )
        scores = jnp.where(allowed, scores * channels ** (-0.5), -1e30)
        largest = jnp.max(scores, axis=-1, keepdims=True)
        probs = jnp.exp(scores - largest)
        probs = (probs / jnp.sum(probs, axis=-1, keepdims=True)).astype(jnp.bfloat16)
        contexts.append(dot32(probs, value[part]).astype(jnp.bfloat16))
    mixed = dot32(jnp.concatenate(contexts, axis=0), w_out[...])
    result = (wide + mixed).astype(jnp.bfloat16)
    if flat:
        outs[0][...] = result
        return
    for g in range(groups):
        part = slice(g * lanes, (g + 1) * lanes)
        for j in range(count):
            begin = g * size + j * each
            rows = result[begin : begin + each].reshape(frames_per, lanes, channels)
            if len(outs) == count:
                outs[j][:, part] = rows
            else:
                outs[0][order[j], :, part] = rows


def attend(order, joined, blocks, gain, w_query, w_key, w_value, w_out):
    count = order.shape[0]
    frames_per, pixels, channels = blocks[0].shape[-3:]
    flat = pixels % 16 != 0
    lanes = pixels if flat else 16
    if flat:
        blocks = [b.reshape(frames_per * pixels, channels) for b in blocks]
    size = frames_per * count * lanes
    block = (frames_per, pixels, channels)
    shapes = [blocks[0].shape] if flat else [(count,) + block] if joined else [block] * count
    flops = 2 * frames_per * pixels * count * channels * (4 * channels + 2 * size)
    outs = pl.pallas_call(
        partial(attend_kernel, frames_per, lanes, count, len(blocks)),
        out_shape=[jax.ShapeDtypeStruct(shape, jnp.bfloat16) for shape in shapes],
        in_specs=[SMEM] + [VMEM] * (len(blocks) + 5),
        out_specs=[VMEM] * len(shapes),
        compiler_params=params(20 if 16 * size * size < 20 * mebibyte else 56),
        cost_estimate=cost(flops, *blocks, w_query, w_key, w_value, w_out),
        name="attend",
    )(order, *blocks, gain, w_query, w_key, w_value, w_out)
    return [o.reshape(block) for o in outs] if flat else outs


def collect_kernel(base, joined, order, *refs):
    out, sems = refs[-2:]
    copies = []
    for j in range(sems.shape[0]):
        block, owner = (refs[0].at[j], j) if joined else (refs[j], order[j])
        copies.append(pltpu.make_async_copy(block, out.at[:, base + owner], sems.at[j]))
    for copy in copies:
        copy.start()
    for copy in copies:
        copy.wait()


def collect(order, blocks, chunk, chunks, whole):
    count = order.shape[0]
    halves, pixels, channels = blocks[0].shape[-3:]
    shape = (halves, chunks * count, pixels, channels)
    given = [] if whole is None else [whole]
    return pl.pallas_call(
        partial(collect_kernel, chunk * count, len(blocks) != count),
        out_shape=jax.ShapeDtypeStruct(shape, jnp.bfloat16),
        in_specs=[SMEM] + [ANY] * (len(blocks) + len(given)),
        out_specs=ANY,
        input_output_aliases={len(blocks) + 1: 0} if given else {},
        scratch_shapes=[pltpu.SemaphoreType.DMA((count,))],
        compiler_params=params(16),
        name="collect",
    )(order, *blocks, *given)


def after(value, other):
    return lax.optimization_barrier((value, other))[0]


def per_device(
    video, w_time, b_time, w_down, b_down, w_space, b_space, gain, w_query, w_key, w_value, w_out
):
    frames, height, width, channels = video.shape
    devices = lax.axis_size("tm")
    columns = lax.axis_size("cols")
    assert columns == 2
    place = lax.axis_index("tm").astype(jnp.int32)
    column = lax.axis_index("cols").astype(jnp.int32)
    halves = frames // 2
    w_time = w_time.reshape(-1, channels)
    w_down = w_down.reshape(-1, channels)
    b_time, b_down, b_space, gain = (v.reshape(1, -1) for v in (b_time, b_down, b_space, gain))
    chunks = parts if height % parts == 0 and height // parts * width % devices == 0 else 1
    size = height // chunks
    each = size * width // devices
    direct = devices <= most_direct and devices & (devices - 1) == 0 and each % 16 == 0
    issue = sorted(range(1, devices), key=lambda j: -j)
    order = place ^ jnp.arange(devices, dtype=jnp.int32) if direct else jnp.zeros(1, jnp.int32)
    scalars = jnp.concatenate([jnp.stack([place, column]), order])
    owners = order.shape[0]

    def exchange(blocks):
        if len(blocks) == 1:
            return [lax.all_to_all(blocks[0], "tm", 0, 0, tiled=True)]
        result = list(blocks)
        for j in issue:
            result[j] = lax.ppermute(blocks[j], "tm", [(i, i ^ j) for i in range(devices)])
        return result

    spans = [
        (k * size + (1 if k else 0), min((k + 1) * size + 1, height)) for k in range(chunks)
    ]
    onward = [(i, i + 1) for i in range(devices - 1)]
    aslant = [
        (i * columns + c, (i + 1) * columns + 1 - c)
        for i in range(devices - 1)
        for c in range(columns)
    ]
    sent = pick(video, frames - taps, spans)
    border = jnp.where(column == 0, video[:, :, -1], video[:, :, 0])
    border = after(border, sent[0])
    halos = [lax.ppermute(value, "tm", onward) for value in sent]
    own_edge = lax.ppermute(border, "cols", [(0, 1), (1, 0)])
    halo_edge = lax.ppermute(border[frames - taps :], ("tm", "cols"), aslant)

    def edge_rows(edge, begin, end):
        return jnp.pad(edge[:, begin:end], ((0, 0), (0, -(end - begin) % 16), (0, 0)))

    ahead = [
        early(video, edge_rows(own_edge, begin, end), begin, end, w_time, b_time, w_down, b_down)
        for begin, end in spans
    ]
    w_space = jnp.where(after(place, own_edge) >= 0, w_space, 0)
    halo_edge = after(halo_edge, [w_space] + [part for _, part in ahead])
    spatials, kept = [], None
    for index, (begin, end) in enumerate(spans):
        own, part = ahead[index]
        if spatials:
            own = after(own, spatials[-1][0])
        last = index == chunks - 1
        joined = direct and index == 0 and chunks > 1
        made = conv(
            owners, joined, size, kept, last, scalars, halos[index], edge_rows(halo_edge, begin, end), own,
            part, w_time, b_time, w_down, b_down, w_space, b_space
        )
        spatials.append(made if last else made[:-1])
        kept = None if last else made[-1]

    newest = spatials[-1][0]
    if direct:
        whole = None
        returns = []
        for gathered in [exchange(blocks) for blocks in spatials]:
            gathered[0] = after(gathered[0], newest)
            joined = len(returns) == chunks - 1
            results = attend(order, joined, gathered, gain, w_query, w_key, w_value, w_out)
            newest = results[0]
            returns.append(exchange(results))
        for index, blocks in enumerate(returns):
            whole = collect(order, blocks, index, chunks, whole)
        return whole.reshape(halves, height, width, channels)
    returns = []
    for (block,) in spatials:
        gathered = lax.all_to_all(block, "tm", 1, 0, tiled=True)
        (result,) = attend(order, True, [gathered], gain, w_query, w_key, w_value, w_out)
        returns.append(lax.all_to_all(result, "tm", 0, 1, tiled=True))
    return jnp.concatenate(returns, axis=1).reshape(halves, height, width, channels)


def solution(mesh):
    spread = P(("clips", "tm"), None, "cols", None)
    return jax.shard_map(
        per_device,
        mesh=mesh,
        in_specs=(spread,) + (P(),) * 11,
        out_specs=spread,
        check_vma=False,
    )
```

```python
from functools import partial

import jax
import jax.numpy as jnp
from jax import lax
from jax.experimental import pallas as pl
from jax.experimental.pallas import tpu as pltpu
from jax.sharding import PartitionSpec as P

epsilon = 1e-06
parts = 2
pair = 2
taps = 3
most_direct = 8
mebibyte = 1024 * 1024

VMEM = pl.BlockSpec(memory_space=pltpu.VMEM)
SMEM = pl.BlockSpec(memory_space=pltpu.SMEM)
ANY = pl.BlockSpec(memory_space=pl.ANY)


def silu(v):
    return 0.5 * v * (1.0 + jnp.tanh(0.5 * v))


def dot32(a, b):
    return jnp.dot(a, b, preferred_element_type=jnp.float32)


def cost(flops, *arrays):
    size = sum(a.size * a.dtype.itemsize for a in arrays)
    return pl.CostEstimate(flops=flops, bytes_accessed=size, transcendentals=0)


def params(mebibytes):
    return pltpu.CompilerParams(vmem_limit_bytes=mebibytes * mebibyte)


def rows_of(owner, begin, end, half, height):
    low, high = max(begin, 1), min(end, half + 1)
    pieces = [(owner * half + low - 1, low - begin, high - low)]
    if begin == 0:
        pieces.append((jnp.maximum(owner * half - 1, 0), 0, 1))
    if end == half + 2:
        pieces.append((jnp.minimum((owner + 1) * half, height - 1), end - 1 - begin, 1))
    return pieces


def run(copies):
    for copy in copies:
        copy.start()
    for copy in copies:
        copy.wait()


def send_kernel(spans, half, scalars, video, *refs):
    outs, sems = refs[:-1], refs[-1]
    frames, height = video.shape[:2]
    copies = []
    for (begin, end), out in zip(spans, outs):
        for source, here, count in rows_of(1 - scalars[0], begin, end, half, height):
            copies.append(
                pltpu.make_async_copy(
                    video.at[:, pl.ds(source, count)],
                    out.at[:, here : here + count],
                    sems.at[len(copies)],
                )
            )
    run(copies)


def send(scalars, video, spans, half):
    frames, _, width, channels = video.shape
    shapes = [(frames, end - begin, width, channels) for begin, end in spans]
    return pl.pallas_call(
        partial(send_kernel, spans, half),
        out_shape=[jax.ShapeDtypeStruct(shape, video.dtype) for shape in shapes],
        in_specs=[SMEM, ANY],
        out_specs=[VMEM] * len(shapes),
        scratch_shapes=[pltpu.SemaphoreType.DMA((3 * len(spans),))],
        compiler_params=params(8),
        name="send",
    )(scalars, video)


def join_kernel(begin, end, half, scalars, video, received, own_edge, other_edge, first, last, sems):
    frames, height = video.shape[:2]
    rows = end - begin
    split = first.shape[0]

    def at(f):
        return first.at[f] if f < split else last.at[f - split]

    def copies(side):
        made = []

        def add(source, target):
            made.append(pltpu.make_async_copy(source, target, sems.at[len(made)]))

        for t in range(frames):
            mine, others = at(side * frames + t), at((1 - side) * frames + t)
            for source, here, count in rows_of(side, begin, end, half, height):
                add(video.at[t, pl.ds(source, count)], mine.at[here : here + count])
            add(received.at[t], others.at[:rows])
            add(own_edge.at[t], mine.at[rows:])
            add(other_edge.at[t], others.at[rows:])
        return made

    for side in range(pair):

        @pl.when(scalars[0] == side)
        def _():
            run(copies(side))


def join(scalars, video, received, own_edge, other_edge, begin, end, half):
    frames, _, width, channels = video.shape
    rows = end - begin + own_edge.shape[1]
    lasting = pair * frames - taps
    return pl.pallas_call(
        partial(join_kernel, begin, end, half),
        out_shape=[
            jax.ShapeDtypeStruct((count, rows, width, channels), jnp.bfloat16)
            for count in (lasting, taps)
        ],
        in_specs=[SMEM] + [ANY] * 4,
        out_specs=[VMEM] * 2,
        scratch_shapes=[pltpu.SemaphoreType.DMA((6 * frames,))],
        compiler_params=params(8),
        name="join",
    )(scalars, video, received, own_edge, other_edge)


def place_rows(buffers, index, top, reduced, rows, width, column):
    pixels, channels = rows * width, reduced.shape[-1]
    edges = reduced.shape[0] - pixels
    row_of = lax.broadcasted_iota(jnp.int32, (pixels, edges), 0) // width
    spread = (row_of == lax.broadcasted_iota(jnp.int32, (pixels, edges), 1)).astype(jnp.bfloat16)
    across = lax.broadcasted_iota(jnp.int32, (pixels, channels), 0) % width
    wide = reduced[:pixels].astype(jnp.float32)
    beside = dot32(spread, reduced[pixels:])
    before = jnp.where(column == 1, beside, 0.0)
    behind = jnp.where(column == 0, beside, 0.0)
    shifted = (
        jnp.where(across == 0, before, pltpu.roll(wide, 1, 0)),
        wide,
        jnp.where(across == width - 1, behind, pltpu.roll(wide, pixels - 1, 0)),
    )
    for b in range(3):
        value = shifted[b].astype(jnp.bfloat16).reshape(rows, width, channels)
        buffers[b, index, top : top + rows] = value


def convolve(buffers, fresh, last, side, kept, keeps, w_space, b_space):
    _, frames, rows, width, channels = buffers.shape
    size = rows - 2
    if fresh:

        @pl.when(side == 0)
        def _():
            buffers[:, :, :1] = jnp.zeros((3, frames, 1, width, channels), jnp.bfloat16)

    else:
        buffers[:, :, :2] = kept[...]
    if last:

        @pl.when(side == pair - 1)
        def _():
            buffers[:, :, size + 1 :] = jnp.zeros((3, frames, 1, width, channels), jnp.bfloat16)

    else:
        keeps[...] = buffers[:, :, size:]

    def window(b, a):
        return buffers[b, :, a : a + size].reshape(frames * size * width, channels)

    lhs = jnp.concatenate([window(b, a) for a in range(3) for b in range(3)], axis=1)
    acc = dot32(lhs, w_space[...].reshape(-1, channels)) + b_space[...]
    value = window(1, 1).astype(jnp.float32) + silu(acc)
    return value.astype(jnp.bfloat16).reshape(frames, size * width, channels)


def early_kernel(
    fresh, final, rows, scalars, first, last, w_time, b_time, w_down, b_down, w_space, b_space, *refs
):
    refs = list(refs)
    kept = None if fresh else refs.pop(0)
    part, spatial = refs[:2]
    keeps = None if final else refs[2]
    lifted, buffers = refs[-2:]
    split, depth, width, channels = first.shape
    count = split + taps
    halves = count // 2
    pixels = depth * width

    def frame(t):
        return (first[t] if t < split else last[t - split]).reshape(pixels, channels)

    starts = list(range(taps - 1, count))
    for low in range(0, len(starts), 3):
        group = starts[low : low + 3]
        lhs = jnp.concatenate(
            [jnp.concatenate([frame(t - k) for t in group], axis=0) for k in range(taps)], axis=1
        )
        acc = dot32(lhs, w_time[...]) + b_time[...]
        held = jnp.concatenate([frame(t) for t in group], axis=0).astype(jnp.float32)
        value = (held + silu(acc)).astype(jnp.bfloat16)
        for g, t in enumerate(group):
            lifted[t] = value[g * pixels : (g + 1) * pixels]
    lhs = jnp.concatenate([lifted[3], lifted[2]], axis=1)
    part[...] = dot32(lhs, w_down[: 2 * channels]) + b_down[...]
    whole = range(2, halves)
    lhs = jnp.concatenate(
        [jnp.concatenate([lifted[2 * s + 1 - k] for s in whole], axis=0) for k in range(taps)],
        axis=1,
    )
    reduced = (dot32(lhs, w_down[...]) + b_down[...]).astype(jnp.bfloat16)
    for index in range(len(whole)):
        value = reduced[index * pixels : (index + 1) * pixels]
        place_rows(buffers, index, 0 if fresh else 2, value, rows, width, scalars[1])
    spatial[...] = convolve(buffers, fresh, final, scalars[0], kept, keeps, w_space, b_space)


def early(scalars, first, last, kept, final, size, rows, *weights):
    split, depth, width, channels = first.shape
    halves = (split + taps) // 2
    pixels = depth * width
    later = halves - 2
    given = [] if kept is None else [kept]
    shapes = [
        jax.ShapeDtypeStruct((pixels, channels), jnp.float32),
        jax.ShapeDtypeStruct((later, size * width, channels), jnp.bfloat16),
    ]
    if not final:
        shapes.append(jax.ShapeDtypeStruct((3, later, 2, width, channels), jnp.bfloat16))
    flops = 2 * channels * channels * (pixels * 26 + 9 * later * size * width)
    return pl.pallas_call(
        partial(early_kernel, kept is None, final, rows),
        out_shape=shapes,
        in_specs=[SMEM] + [VMEM] * (2 + len(weights) + len(given)),
        out_specs=[VMEM] * len(shapes),
        scratch_shapes=[
            pltpu.VMEM((2 * halves, pixels, channels), jnp.bfloat16),
            pltpu.VMEM((3, later, size + 2, width, channels), jnp.bfloat16),
        ],
        compiler_params=params(24),
        cost_estimate=cost(flops, first, last, *weights),
        name="early",
    )(scalars, first, last, *weights, *given)


def late_kernel(
    owners, fresh, final, rows, scalars, halo, first, part, spatial, w_time, b_time, w_down, b_down,
    w_space, b_space, *refs
):
    refs = list(refs)
    kept = None if fresh else refs.pop(0)
    outs = refs[:owners]
    keeps = None if final else refs[owners]
    lifted, buffers, result = refs[-3:]
    _, depth, width, channels = first.shape
    pixels = depth * width

    def frame(t):
        return (halo[t + taps] if t < 0 else first[t]).reshape(pixels, channels)

    group = range(-1, taps - 1)
    lhs = jnp.concatenate(
        [jnp.concatenate([frame(t - k) for t in group], axis=0) for k in range(taps)], axis=1
    )
    acc = dot32(lhs, w_time[...]) + b_time[...]
    held = jnp.concatenate([frame(t) for t in group], axis=0).astype(jnp.float32)
    value = held + silu(acc)
    for index in range(taps):
        piece = value[index * pixels : (index + 1) * pixels]
        if index == 0:
            piece = jnp.where(scalars[2] > 0, piece, 0.0)
        lifted[index] = piece.astype(jnp.bfloat16)
    lhs = jnp.concatenate([lifted[2], lifted[1], lifted[0]], axis=1)
    reduced = (
        dot32(lhs, w_down[...]) + b_down[...],
        dot32(lifted[2], w_down[2 * channels :]) + part[...],
    )
    for index, value in enumerate(reduced):
        value = value.astype(jnp.bfloat16)
        place_rows(buffers, index, 0 if fresh else 2, value, rows, width, scalars[1])
    result[:2] = convolve(buffers, fresh, final, scalars[0], kept, keeps, w_space, b_space)
    result[2:] = spatial[...]
    each = result.shape[1] // owners
    if owners == 1:
        outs[0][...] = result[...]
    else:
        for j, out in enumerate(outs):
            begin = pl.multiple_of((scalars[2] ^ j) * each, each)
            out[...] = result[:, pl.ds(begin, each)]


def late(owners, scalars, halo, first, part, spatial, kept, final, rows, *weights):
    _, depth, width, channels = first.shape
    later, pixels = spatial.shape[:2]
    halves = later + 2
    size = pixels // width
    given = [] if kept is None else [kept]
    shapes = [(halves, pixels // owners, channels)] * owners
    if not final:
        shapes.append((3, 2, 2, width, channels))
    flops = 2 * channels * channels * (depth * width * 13 + 18 * pixels)
    return pl.pallas_call(
        partial(late_kernel, owners, kept is None, final, rows),
        out_shape=[jax.ShapeDtypeStruct(shape, jnp.bfloat16) for shape in shapes],
        in_specs=[SMEM] + [VMEM] * (4 + len(weights) + len(given)),
        out_specs=[VMEM] * len(shapes),
        scratch_shapes=[
            pltpu.VMEM((taps, depth * width, channels), jnp.bfloat16),
            pltpu.VMEM((3, 2, size + 2, width, channels), jnp.bfloat16),
            pltpu.VMEM((halves, pixels, channels), jnp.bfloat16),
        ],
        compiler_params=params(24),
        cost_estimate=cost(flops, halo, first, part, *weights),
        name="late",
    )(scalars, halo, first, part, spatial, *weights, *given)


def attend_kernel(frames_per, lanes, count, scalars, *refs):
    blocks = refs[:count]
    gain, w_query, w_key, w_value, w_out = refs[count : count + 5]
    outs = refs[count + 5 :]
    channels = gain.shape[-1]
    flat = len(blocks[0].shape) == 2
    groups = 1 if flat else blocks[0].shape[1] // lanes
    each = frames_per * lanes
    size = count * each

    def piece(j, g):
        if flat:
            return blocks[0][...]
        return blocks[j][:, g * lanes : (g + 1) * lanes].reshape(each, channels)

    def place(index):
        block = index // each
        time = index // lanes % frames_per
        for j in range(count):
            level = 0 if flat else scalars[2] ^ j
            time = time + jnp.where(block == j, level * frames_per, 0)
        return time, index % lanes

    row_time, row_lane = place(lax.broadcasted_iota(jnp.int32, (size, 1), 0))
    col_time, col_lane = place(lax.broadcasted_iota(jnp.int32, (1, size), 1))
    allowed = (row_lane == col_lane) & (col_time <= row_time)
    x = jnp.concatenate([piece(j, g) for g in range(groups) for j in range(count)], axis=0)
    wide = x.astype(jnp.float32)
    scale = lax.rsqrt(jnp.mean(wide * wide, axis=-1, keepdims=True) + epsilon)
    normed = (wide * scale * gain[...]).astype(jnp.bfloat16)
    query = dot32(normed, w_query[...]).astype(jnp.bfloat16)
    key = dot32(normed, w_key[...]).astype(jnp.bfloat16)
    value = dot32(normed, w_value[...]).astype(jnp.bfloat16)
    contexts = []
    for g in range(groups):
        part = slice(g * size, (g + 1) * size)
        scores = lax.dot_general(
            query[part], key[part], (((1,), (1,)), ((), ())), preferred_element_type=jnp.float32
        )
        scores = jnp.where(allowed, scores * channels ** (-0.5), -1e30)
        largest = jnp.max(scores, axis=-1, keepdims=True)
        probs = jnp.exp(scores - largest)
        probs = (probs / jnp.sum(probs, axis=-1, keepdims=True)).astype(jnp.bfloat16)
        contexts.append(dot32(probs, value[part]).astype(jnp.bfloat16))
    mixed = dot32(jnp.concatenate(contexts, axis=0), w_out[...])
    result = (wide + mixed).astype(jnp.bfloat16)
    if flat:
        outs[0][...] = result
        return
    short = frames_per // pair
    for g in range(groups):
        for j in range(count):
            begin = g * size + j * each
            rows = result[begin : begin + each].reshape(pair, short, lanes, channels)
            for side in range(pair):

                @pl.when(scalars[0] == side)
                def _():
                    for x in range(pair):
                        outs[pair * j + x][:, g * lanes : (g + 1) * lanes] = rows[side ^ x]


def attend(scalars, blocks, gain, w_query, w_key, w_value, w_out):
    frames_per, pixels, channels = blocks[0].shape
    flat = pixels % 16 != 0
    lanes = pixels if flat else 16
    if flat:
        blocks = [b.reshape(frames_per * pixels, channels) for b in blocks]
    count = len(blocks)
    size = frames_per * count * lanes
    shapes = [(frames_per // pair, pixels, channels)] * (pair * count)
    if flat:
        shapes = [blocks[0].shape]
    flops = 2 * frames_per * pixels * count * channels * (4 * channels + 2 * size)
    outs = pl.pallas_call(
        partial(attend_kernel, frames_per, lanes, count),
        out_shape=[jax.ShapeDtypeStruct(shape, jnp.bfloat16) for shape in shapes],
        in_specs=[SMEM] + [VMEM] * (count + 5),
        out_specs=[VMEM] * len(shapes),
        compiler_params=params(20 if 16 * size * size < 20 * mebibyte else 56),
        cost_estimate=cost(flops, *blocks, w_query, w_key, w_value, w_out),
        name="attend",
    )(scalars, *blocks, gain, w_query, w_key, w_value, w_out)
    return [o.reshape(frames_per, pixels, channels) for o in outs] if flat else outs


def collect_kernel(base, stride, scalars, *refs):
    out, sems = refs[-2:]
    copies = []
    for m in range(sems.shape[0]):
        index = base + (scalars[0] ^ m % pair) * stride + (scalars[2] ^ m // pair)
        copies.append(pltpu.make_async_copy(refs[m], out.at[:, index], sems.at[m]))
    run(copies)


def collect(scalars, blocks, chunk, chunks, whole):
    count = len(blocks)
    halves, pixels, channels = blocks[0].shape
    levels = count // pair
    given = [] if whole is None else [whole]
    return pl.pallas_call(
        partial(collect_kernel, chunk * levels, chunks * levels),
        out_shape=jax.ShapeDtypeStruct((halves, chunks * count, pixels, channels), jnp.bfloat16),
        in_specs=[SMEM] + [ANY] * (count + len(given)),
        out_specs=ANY,
        input_output_aliases={count + 1: 0} if given else {},
        scratch_shapes=[pltpu.SemaphoreType.DMA((count,))],
        compiler_params=params(16),
        name="collect",
    )(scalars, *blocks, *given)


def after(value, other):
    return lax.optimization_barrier((value, other))[0]


def per_device(
    video, w_time, b_time, w_down, b_down, w_space, b_space, gain, w_query, w_key, w_value, w_out
):
    frames, height, width, channels = video.shape
    devices = lax.axis_size("tm")
    levels = devices // pair
    columns = lax.axis_size("cols")
    assert columns == 2 and devices % pair == 0 and height % pair == 0 and frames >= taps
    place = lax.axis_index("tm").astype(jnp.int32)
    column = lax.axis_index("cols").astype(jnp.int32)
    side, level = place % pair, place // pair
    scalars = jnp.stack([side, column, level])
    half = height // pair
    gain = gain.reshape(1, -1)
    weights = [
        w_time.reshape(-1, channels), b_time.reshape(1, -1), w_down.reshape(-1, channels),
        b_down.reshape(1, -1), w_space, b_space.reshape(1, -1),
    ]
    attention = [gain, w_query, w_key, w_value, w_out]
    chunks = parts if half % parts == 0 and half // parts * width % levels == 0 else 1
    size = half // chunks
    each = size * width // levels
    direct = devices <= most_direct and levels & (levels - 1) == 0 and each % 16 == 0
    spans = [
        (k * size + (2 if k else 0), (k + 1) * size + 2) for k in range(chunks)
    ]

    def tm_permute(value, move):
        return lax.ppermute(value, "tm", [(i, move(i)) for i in range(devices) if move(i) < devices])

    sent = send(scalars, video, spans, half)
    received = [tm_permute(value, lambda i: i ^ 1) for value in sent]
    border = jnp.where(column == 0, video[:, :, -1], video[:, :, 0])
    border = jnp.pad(after(border, sent[0]), ((0, 0), (1, 1), (0, 0)))
    own_edge, other_edge = (
        lax.dynamic_slice_in_dim(border, s * half, half + 2, axis=1) for s in (side, 1 - side)
    )
    own_edge = lax.ppermute(own_edge, "cols", [(0, 1), (1, 0)])
    aslant = [
        (i * columns + c, (i ^ 1) * columns + 1 - c)
        for i in range(devices)
        for c in range(columns)
    ]
    other_edge = lax.ppermute(other_edge, ("tm", "cols"), aslant)

    def edge_rows(edge, begin, end):
        cut = jnp.pad(edge[:, begin:end], ((0, 0), (0, -(end - begin) % width), (0, 0)))
        return cut.reshape(frames, -1, width, channels)

    ahead, halos = [], []
    kept = None
    for k, (begin, end) in enumerate(spans):
        arrived = after(received[k], ahead[-1][1]) if ahead else received[k]
        first, last = join(
            scalars, video, arrived, edge_rows(own_edge, begin, end),
            edge_rows(other_edge, begin, end), begin, end, half
        )
        halos.append(tm_permute(last, lambda i: i + pair))
        final = k == chunks - 1
        made = early(scalars, first, last, kept, final, size, end - begin, *weights)
        kept = None if final else made[2]
        ahead.append((first, made[0], made[1]))

    spatials = []
    kept = None
    owners = levels if direct else 1
    for k, (begin, end) in enumerate(spans):
        first, part, spatial = ahead[k]
        if spatials:
            part = after(part, spatials[-1][0])
        final = k == chunks - 1
        made = late(
            owners, scalars, halos[k], first, part, spatial, kept, final, end - begin, *weights
        )
        spatials.append(made[:owners])
        kept = None if final else made[owners]

    newest = spatials[-1][0]
    if direct:
        gathers = [
            [blocks[0]]
            + [tm_permute(blocks[j], lambda i: i ^ (pair * j)) for j in range(1, levels)]
            for blocks in spatials
        ]
        returns = []
        for gathered in gathers:
            gathered[0] = after(gathered[0], newest)
            results = attend(scalars, gathered, *attention)
            newest = results[0]
            returns.append(
                [results[0]]
                + [tm_permute(results[m], lambda i: i ^ m) for m in range(1, devices)]
            )
        whole = None
        for k, blocks in enumerate(returns):
            whole = collect(scalars, blocks, k, chunks, whole)
        return whole.reshape(frames // 2, height, width, channels)
    sets = [[pair * z + s for z in range(levels)] for s in range(pair)]
    returns = []
    for (block,) in spatials:
        gathered = lax.all_to_all(block, "tm", 1, 0, axis_index_groups=sets, tiled=True)
        (result,) = attend(scalars, [gathered], *attention)
        result = lax.all_to_all(result, "tm", 0, 1, tiled=True)
        result = result.reshape(frames // 2, levels, pair, each, channels)
        returns.append(result.transpose(0, 2, 1, 3, 4).reshape(frames // 2, pair, -1, channels))
    return jnp.concatenate(returns, axis=2).reshape(frames // 2, height, width, channels)


def solution(mesh):
    spread = P(("clips", "tm"), None, "cols", None)
    return jax.shard_map(
        per_device,
        mesh=mesh,
        in_specs=(spread,) + (P(),) * 11,
        out_specs=spread,
        check_vma=False,
    )
```

```python
from functools import partial

import jax
import jax.numpy as jnp
from jax import lax
from jax.experimental import pallas as pl
from jax.experimental.pallas import tpu as pltpu
from jax.sharding import PartitionSpec as P

epsilon = 1e-06
parts = 2
pair = 2
taps = 3
most_direct = 8
mebibyte = 1024 * 1024

VMEM = pl.BlockSpec(memory_space=pltpu.VMEM)
SMEM = pl.BlockSpec(memory_space=pltpu.SMEM)
ANY = pl.BlockSpec(memory_space=pl.ANY)


def silu(v):
    return 0.5 * v * (1.0 + jnp.tanh(0.5 * v))


def dot32(a, b):
    return jnp.dot(a, b, preferred_element_type=jnp.float32)


def cost(flops, *arrays):
    size = sum(a.size * a.dtype.itemsize for a in arrays)
    return pl.CostEstimate(flops=flops, bytes_accessed=size, transcendentals=0)


def params(mebibytes):
    return pltpu.CompilerParams(vmem_limit_bytes=mebibytes * mebibyte)


def rows_of(owner, begin, end, half, height):
    low, high = max(begin, 1), min(end, half + 1)
    pieces = [(owner * half + low - 1, low - begin, high - low)]
    if begin == 0:
        pieces.append((jnp.maximum(owner * half - 1, 0), 0, 1))
    if end == half + 2:
        pieces.append((jnp.minimum((owner + 1) * half, height - 1), end - 1 - begin, 1))
    return pieces


def run(copies):
    for copy in copies:
        copy.start()
    for copy in copies:
        copy.wait()


def cut(target, video, frame, owner, begin, end, half):
    for source, here, count in rows_of(owner, begin, end, half, video.shape[1]):
        target[here : here + count] = video[frame, pl.ds(source, count)]


def send_kernel(spans, half, scalars, video, *outs):
    frames = video.shape[0]
    rest = frames - taps
    for k, (begin, end) in enumerate(spans):
        for t in range(frames):
            if k == 0:
                target = outs[0].at[t - rest] if t >= rest else outs[1].at[t]
            else:
                target = outs[k + 1].at[t]
            cut(target, video, t, 1 - scalars[0], begin, end, half)


def send(scalars, video, spans, half):
    frames, _, width, channels = video.shape
    counts = [taps, frames - taps] + [frames] * (len(spans) - 1)
    shapes = [
        (count, end - begin, width, channels)
        for count, (begin, end) in zip(counts, spans[:1] + spans)
    ]
    return pl.pallas_call(
        partial(send_kernel, spans, half),
        out_shape=[jax.ShapeDtypeStruct(shape, video.dtype) for shape in shapes],
        in_specs=[SMEM, VMEM],
        out_specs=[VMEM] * len(shapes),
        compiler_params=params(12),
        name="send",
    )(scalars, video)


def join_last_kernel(begin, end, half, scalars, video, received, own_edge, other_edge, out):
    frames, rows = video.shape[0], end - begin

    @pl.when(scalars[0] == 0)
    def _():
        out[:, :rows] = received[received.shape[0] - taps :]
        out[:, rows:] = other_edge[frames - taps :]

    @pl.when(scalars[0] == 1)
    def _():
        for t in range(taps):
            cut(out.at[t], video, frames - taps + t, 1, begin, end, half)
        out[:, rows:] = own_edge[frames - taps :]


def join_first_kernel(
    begin, end, half, scalars, video, received, others, own_edge, other_edge, out
):
    frames, rows = video.shape[0], end - begin
    rest = frames - taps

    @pl.when(scalars[0] == 0)
    def _():
        for t in range(frames):
            cut(out.at[t], video, t, 0, begin, end, half)
        out[:frames, rows:] = own_edge[...]
        out[frames:, :rows] = others[:rest]
        out[frames:, rows:] = other_edge[:rest]

    @pl.when(scalars[0] == 1)
    def _():
        out[:rest, :rows] = others[:rest]
        out[rest:frames, :rows] = received[received.shape[0] - taps :]
        out[:frames, rows:] = other_edge[...]
        for t in range(rest):
            cut(out.at[frames + t], video, t, 1, begin, end, half)
        out[frames:, rows:] = own_edge[:rest]


def join(kernel, count, name, begin, end, half, scalars, video, *parts):
    _, _, width, channels = video.shape
    rows = end - begin + parts[-1].shape[1]
    return pl.pallas_call(
        partial(kernel, begin, end, half),
        out_shape=jax.ShapeDtypeStruct((count, rows, width, channels), jnp.bfloat16),
        in_specs=[SMEM] + [VMEM] * (1 + len(parts)),
        out_specs=VMEM,
        compiler_params=params(12),
        name=name,
    )(scalars, video, *parts)


def place_rows(buffers, index, top, reduced, rows, width, column):
    pixels, channels = rows * width, reduced.shape[-1]
    edges = reduced.shape[0] - pixels
    row_of = lax.broadcasted_iota(jnp.int32, (pixels, edges), 0) // width
    spread = (row_of == lax.broadcasted_iota(jnp.int32, (pixels, edges), 1)).astype(jnp.bfloat16)
    across = lax.broadcasted_iota(jnp.int32, (pixels, channels), 0) % width
    wide = reduced[:pixels].astype(jnp.float32)
    beside = dot32(spread, reduced[pixels:])
    before = jnp.where(column == 1, beside, 0.0)
    behind = jnp.where(column == 0, beside, 0.0)
    shifted = (
        jnp.where(across == 0, before, pltpu.roll(wide, 1, 0)),
        wide,
        jnp.where(across == width - 1, behind, pltpu.roll(wide, pixels - 1, 0)),
    )
    for b in range(3):
        value = shifted[b].astype(jnp.bfloat16).reshape(rows, width, channels)
        buffers[b, index, top : top + rows] = value


def convolve(buffers, fresh, last, side, kept, keeps, w_space, b_space):
    _, frames, rows, width, channels = buffers.shape
    size = rows - 2
    if fresh:

        @pl.when(side == 0)
        def _():
            buffers[:, :, :1] = jnp.zeros((3, frames, 1, width, channels), jnp.bfloat16)

    else:
        buffers[:, :, :2] = kept[...]
    if last:

        @pl.when(side == pair - 1)
        def _():
            buffers[:, :, size + 1 :] = jnp.zeros((3, frames, 1, width, channels), jnp.bfloat16)

    else:
        keeps[...] = buffers[:, :, size:]

    def window(b, a):
        return buffers[b, :, a : a + size].reshape(frames * size * width, channels)

    lhs = jnp.concatenate([window(b, a) for a in range(3) for b in range(3)], axis=1)
    acc = dot32(lhs, w_space[...].reshape(-1, channels)) + b_space[...]
    value = window(1, 1).astype(jnp.float32) + silu(acc)
    return value.astype(jnp.bfloat16).reshape(frames, size * width, channels)


def early_kernel(
    fresh, final, rows, scalars, first, last, w_time, b_time, w_down, b_down, w_space, b_space, *refs
):
    refs = list(refs)
    kept = None if fresh else refs.pop(0)
    part, spatial = refs[:2]
    keeps = None if final else refs[2]
    lifted, buffers = refs[-2:]
    split, depth, width, channels = first.shape
    count = split + taps
    halves = count // 2
    pixels = depth * width

    def frame(t):
        return (first[t] if t < split else last[t - split]).reshape(pixels, channels)

    starts = list(range(taps - 1, count))
    for low in range(0, len(starts), 3):
        group = starts[low : low + 3]
        lhs = jnp.concatenate(
            [jnp.concatenate([frame(t - k) for t in group], axis=0) for k in range(taps)], axis=1
        )
        acc = dot32(lhs, w_time[...]) + b_time[...]
        held = jnp.concatenate([frame(t) for t in group], axis=0).astype(jnp.float32)
        value = (held + silu(acc)).astype(jnp.bfloat16)
        for g, t in enumerate(group):
            lifted[t] = value[g * pixels : (g + 1) * pixels]
    lhs = jnp.concatenate([lifted[3], lifted[2]], axis=1)
    part[...] = dot32(lhs, w_down[: 2 * channels]) + b_down[...]
    whole = range(2, halves)
    lhs = jnp.concatenate(
        [jnp.concatenate([lifted[2 * s + 1 - k] for s in whole], axis=0) for k in range(taps)],
        axis=1,
    )
    reduced = (dot32(lhs, w_down[...]) + b_down[...]).astype(jnp.bfloat16)
    for index in range(len(whole)):
        value = reduced[index * pixels : (index + 1) * pixels]
        place_rows(buffers, index, 0 if fresh else 2, value, rows, width, scalars[1])
    spatial[...] = convolve(buffers, fresh, final, scalars[0], kept, keeps, w_space, b_space)


def early(scalars, first, last, kept, final, size, rows, *weights):
    split, depth, width, channels = first.shape
    halves = (split + taps) // 2
    pixels = depth * width
    later = halves - 2
    given = [] if kept is None else [kept]
    shapes = [
        jax.ShapeDtypeStruct((pixels, channels), jnp.float32),
        jax.ShapeDtypeStruct((later, size * width, channels), jnp.bfloat16),
    ]
    if not final:
        shapes.append(jax.ShapeDtypeStruct((3, later, 2, width, channels), jnp.bfloat16))
    flops = 2 * channels * channels * (pixels * 26 + 9 * later * size * width)
    return pl.pallas_call(
        partial(early_kernel, kept is None, final, rows),
        out_shape=shapes,
        in_specs=[SMEM] + [VMEM] * (2 + len(weights) + len(given)),
        out_specs=[VMEM] * len(shapes),
        scratch_shapes=[
            pltpu.VMEM((2 * halves, pixels, channels), jnp.bfloat16),
            pltpu.VMEM((3, later, size + 2, width, channels), jnp.bfloat16),
        ],
        compiler_params=params(24),
        cost_estimate=cost(flops, first, last, *weights),
        name="early",
    )(scalars, first, last, *weights, *given)


def late_kernel(
    owners, fresh, final, rows, scalars, halo, first, part, spatial, w_time, b_time, w_down, b_down,
    w_space, b_space, *refs
):
    refs = list(refs)
    kept = None if fresh else refs.pop(0)
    outs = refs[:owners]
    keeps = None if final else refs[owners]
    lifted, buffers, result = refs[-3:]
    _, depth, width, channels = first.shape
    pixels = depth * width

    def frame(t):
        return (halo[t + taps] if t < 0 else first[t]).reshape(pixels, channels)

    group = range(-1, taps - 1)
    lhs = jnp.concatenate(
        [jnp.concatenate([frame(t - k) for t in group], axis=0) for k in range(taps)], axis=1
    )
    acc = dot32(lhs, w_time[...]) + b_time[...]
    held = jnp.concatenate([frame(t) for t in group], axis=0).astype(jnp.float32)
    value = held + silu(acc)
    for index in range(taps):
        piece = value[index * pixels : (index + 1) * pixels]
        if index == 0:
            piece = jnp.where(scalars[2] > 0, piece, 0.0)
        lifted[index] = piece.astype(jnp.bfloat16)
    lhs = jnp.concatenate([lifted[2], lifted[1], lifted[0]], axis=1)
    reduced = (
        dot32(lhs, w_down[...]) + b_down[...],
        dot32(lifted[2], w_down[2 * channels :]) + part[...],
    )
    for index, value in enumerate(reduced):
        value = value.astype(jnp.bfloat16)
        place_rows(buffers, index, 0 if fresh else 2, value, rows, width, scalars[1])
    result[:2] = convolve(buffers, fresh, final, scalars[0], kept, keeps, w_space, b_space)
    result[2:] = spatial[...]
    each = result.shape[1] // owners
    if owners == 1:
        outs[0][...] = result[...]
    else:
        for j, out in enumerate(outs):
            begin = pl.multiple_of((scalars[2] ^ j) * each, each)
            out[...] = result[:, pl.ds(begin, each)]


def late(owners, scalars, halo, first, part, spatial, kept, final, rows, *weights):
    _, depth, width, channels = first.shape
    later, pixels = spatial.shape[:2]
    halves = later + 2
    size = pixels // width
    given = [] if kept is None else [kept]
    shapes = [(halves, pixels // owners, channels)] * owners
    if not final:
        shapes.append((3, 2, 2, width, channels))
    flops = 2 * channels * channels * (depth * width * 13 + 18 * pixels)
    return pl.pallas_call(
        partial(late_kernel, owners, kept is None, final, rows),
        out_shape=[jax.ShapeDtypeStruct(shape, jnp.bfloat16) for shape in shapes],
        in_specs=[SMEM] + [VMEM] * (4 + len(weights) + len(given)),
        out_specs=[VMEM] * len(shapes),
        scratch_shapes=[
            pltpu.VMEM((taps, depth * width, channels), jnp.bfloat16),
            pltpu.VMEM((3, 2, size + 2, width, channels), jnp.bfloat16),
            pltpu.VMEM((halves, pixels, channels), jnp.bfloat16),
        ],
        compiler_params=params(24),
        cost_estimate=cost(flops, halo, first, part, *weights),
        name="late",
    )(scalars, halo, first, part, spatial, *weights, *given)


def attend_kernel(frames_per, lanes, count, scalars, *refs):
    blocks = refs[:count]
    gain, w_query, w_key, w_value, w_out = refs[count : count + 5]
    outs = refs[count + 5 :]
    channels = gain.shape[-1]
    flat = len(blocks[0].shape) == 2
    groups = 1 if flat else blocks[0].shape[1] // lanes
    each = frames_per * lanes
    size = count * each

    def piece(j, g):
        if flat:
            return blocks[0][...]
        return blocks[j][:, g * lanes : (g + 1) * lanes].reshape(each, channels)

    def place(index):
        block = index // each
        time = index // lanes % frames_per
        for j in range(count):
            level = 0 if flat else scalars[2] ^ j
            time = time + jnp.where(block == j, level * frames_per, 0)
        return time, index % lanes

    row_time, row_lane = place(lax.broadcasted_iota(jnp.int32, (size, 1), 0))
    col_time, col_lane = place(lax.broadcasted_iota(jnp.int32, (1, size), 1))
    allowed = (row_lane == col_lane) & (col_time <= row_time)
    x = jnp.concatenate([piece(j, g) for g in range(groups) for j in range(count)], axis=0)
    wide = x.astype(jnp.float32)
    scale = lax.rsqrt(jnp.mean(wide * wide, axis=-1, keepdims=True) + epsilon)
    normed = (wide * scale * gain[...]).astype(jnp.bfloat16)
    query = dot32(normed, w_query[...]).astype(jnp.bfloat16)
    key = dot32(normed, w_key[...]).astype(jnp.bfloat16)
    value = dot32(normed, w_value[...]).astype(jnp.bfloat16)
    contexts = []
    for g in range(groups):
        part = slice(g * size, (g + 1) * size)
        scores = lax.dot_general(
            query[part], key[part], (((1,), (1,)), ((), ())), preferred_element_type=jnp.float32
        )
        scores = jnp.where(allowed, scores * channels ** (-0.5), -1e30)
        largest = jnp.max(scores, axis=-1, keepdims=True)
        probs = jnp.exp(scores - largest)
        probs = (probs / jnp.sum(probs, axis=-1, keepdims=True)).astype(jnp.bfloat16)
        contexts.append(dot32(probs, value[part]).astype(jnp.bfloat16))
    mixed = dot32(jnp.concatenate(contexts, axis=0), w_out[...])
    result = (wide + mixed).astype(jnp.bfloat16)
    if flat:
        outs[0][...] = result
        return
    short = frames_per // pair
    for g in range(groups):
        for j in range(count):
            begin = g * size + j * each
            rows = result[begin : begin + each].reshape(pair, short, lanes, channels)
            for side in range(pair):

                @pl.when(scalars[0] == side)
                def _():
                    for x in range(pair):
                        outs[pair * j + x][:, g * lanes : (g + 1) * lanes] = rows[side ^ x]


def attend(scalars, blocks, gain, w_query, w_key, w_value, w_out):
    frames_per, pixels, channels = blocks[0].shape
    flat = pixels % 16 != 0
    lanes = pixels if flat else 16
    if flat:
        blocks = [b.reshape(frames_per * pixels, channels) for b in blocks]
    count = len(blocks)
    size = frames_per * count * lanes
    shapes = [(frames_per // pair, pixels, channels)] * (pair * count)
    if flat:
        shapes = [blocks[0].shape]
    flops = 2 * frames_per * pixels * count * channels * (4 * channels + 2 * size)
    outs = pl.pallas_call(
        partial(attend_kernel, frames_per, lanes, count),
        out_shape=[jax.ShapeDtypeStruct(shape, jnp.bfloat16) for shape in shapes],
        in_specs=[SMEM] + [VMEM] * (count + 5),
        out_specs=[VMEM] * len(shapes),
        compiler_params=params(20 if 16 * size * size < 20 * mebibyte else 56),
        cost_estimate=cost(flops, *blocks, w_query, w_key, w_value, w_out),
        name="attend",
    )(scalars, *blocks, gain, w_query, w_key, w_value, w_out)
    return [o.reshape(frames_per, pixels, channels) for o in outs] if flat else outs


def collect_kernel(base, stride, scalars, *refs):
    out, sems = refs[-2:]
    copies = []
    for m in range(sems.shape[0]):
        index = base + (scalars[0] ^ m % pair) * stride + (scalars[2] ^ m // pair)
        copies.append(pltpu.make_async_copy(refs[m], out.at[:, index], sems.at[m]))
    run(copies)


def collect(scalars, blocks, chunk, chunks, whole):
    count = len(blocks)
    halves, pixels, channels = blocks[0].shape
    levels = count // pair
    given = [] if whole is None else [whole]
    return pl.pallas_call(
        partial(collect_kernel, chunk * levels, chunks * levels),
        out_shape=jax.ShapeDtypeStruct((halves, chunks * count, pixels, channels), jnp.bfloat16),
        in_specs=[SMEM] + [ANY] * (count + len(given)),
        out_specs=ANY,
        input_output_aliases={count + 1: 0} if given else {},
        scratch_shapes=[pltpu.SemaphoreType.DMA((count,))],
        compiler_params=params(16),
        name="collect",
    )(scalars, *blocks, *given)


def after(value, other):
    return lax.optimization_barrier((value, other))[0]


def per_device(
    video, w_time, b_time, w_down, b_down, w_space, b_space, gain, w_query, w_key, w_value, w_out
):
    frames, height, width, channels = video.shape
    devices = lax.axis_size("tm")
    levels = devices // pair
    columns = lax.axis_size("cols")
    assert columns == 2 and devices % pair == 0 and height % pair == 0 and frames >= taps
    place = lax.axis_index("tm").astype(jnp.int32)
    column = lax.axis_index("cols").astype(jnp.int32)
    side, level = place % pair, place // pair
    scalars = jnp.stack([side, column, level])
    half = height // pair
    gain = gain.reshape(1, -1)
    w_space = jnp.where(after(place, video) >= 0, w_space, 0)
    weights = [
        w_time.reshape(-1, channels), b_time.reshape(1, -1), w_down.reshape(-1, channels),
        b_down.reshape(1, -1), w_space, b_space.reshape(1, -1),
    ]
    attention = [gain, w_query, w_key, w_value, w_out]
    chunks = parts if half % parts == 0 and half // parts * width % levels == 0 else 1
    size = half // chunks
    each = size * width // levels
    direct = devices <= most_direct and levels & (levels - 1) == 0 and each % 16 == 0
    spans = [
        (k * size + (2 if k else 0), (k + 1) * size + 2) for k in range(chunks)
    ]

    def tm_permute(value, move):
        return lax.ppermute(value, "tm", [(i, move(i)) for i in range(devices) if move(i) < devices])

    sent = send(scalars, video, spans, half)
    received = [tm_permute(value, lambda i: i ^ 1) for value in sent]
    border = jnp.where(column == 0, video[:, :, -1], video[:, :, 0])
    border = jnp.pad(after(border, sent[0]), ((0, 0), (1, 1), (0, 0)))
    own_edge, other_edge = (
        lax.dynamic_slice_in_dim(border, s * half, half + 2, axis=1) for s in (side, 1 - side)
    )
    own_edge = lax.ppermute(own_edge, "cols", [(0, 1), (1, 0)])
    aslant = [
        (i * columns + c, (i ^ 1) * columns + 1 - c)
        for i in range(devices)
        for c in range(columns)
    ]
    other_edge = lax.ppermute(other_edge, ("tm", "cols"), aslant)

    def edge_rows(edge, begin, end):
        cut = jnp.pad(edge[:, begin:end], ((0, 0), (0, -(end - begin) % width), (0, 0)))
        return cut.reshape(frames, -1, width, channels)

    ahead, halos = [], []
    kept = None
    for k, (begin, end) in enumerate(spans):
        edges = [edge_rows(edge, begin, end) for edge in (own_edge, other_edge)]
        arrived, others = received[:2] if k == 0 else (received[k + 1], received[k + 1])
        arrived = after(arrived, ahead[-1][1] if ahead else w_space)
        place_of = (begin, end, half, scalars, video)
        last = join(join_last_kernel, taps, "join_last", *place_of, arrived, *edges)
        others = after(others, last) if k == 0 else arrived
        first = join(
            join_first_kernel, pair * frames - taps, "join_first", *place_of, arrived, others, *edges
        )
        halos.append(tm_permute(last, lambda i: i + pair))
        final = k == chunks - 1
        made = early(scalars, first, last, kept, final, size, end - begin, *weights)
        kept = None if final else made[2]
        ahead.append((first, made[0], made[1]))

    spatials = []
    kept = None
    owners = levels if direct else 1
    for k, (begin, end) in enumerate(spans):
        first, part, spatial = ahead[k]
        if spatials:
            part = after(part, spatials[-1][0])
        final = k == chunks - 1
        made = late(
            owners, scalars, halos[k], first, part, spatial, kept, final, end - begin, *weights
        )
        spatials.append(made[:owners])
        kept = None if final else made[owners]

    newest = spatials[-1][0]
    if direct:
        gathers = [
            [blocks[0]]
            + [tm_permute(blocks[j], lambda i: i ^ (pair * j)) for j in range(1, levels)]
            for blocks in spatials
        ]
        returns = []
        for gathered in gathers:
            gathered[0] = after(gathered[0], newest)
            results = attend(scalars, gathered, *attention)
            newest = results[0]
            returns.append(
                [results[0]]
                + [tm_permute(results[m], lambda i: i ^ m) for m in range(1, devices)]
            )
        whole = None
        for k, blocks in enumerate(returns):
            whole = collect(scalars, blocks, k, chunks, whole)
        return whole.reshape(frames // 2, height, width, channels)
    sets = [[pair * z + s for z in range(levels)] for s in range(pair)]
    returns = []
    for (block,) in spatials:
        gathered = lax.all_to_all(block, "tm", 1, 0, axis_index_groups=sets, tiled=True)
        (result,) = attend(scalars, [gathered], *attention)
        result = lax.all_to_all(result, "tm", 0, 1, tiled=True)
        result = result.reshape(frames // 2, levels, pair, each, channels)
        returns.append(result.transpose(0, 2, 1, 3, 4).reshape(frames // 2, pair, -1, channels))
    return jnp.concatenate(returns, axis=2).reshape(frames // 2, height, width, channels)


def solution(mesh):
    spread = P(("clips", "tm"), None, "cols", None)
    return jax.shard_map(
        per_device,
        mesh=mesh,
        in_specs=(spread,) + (P(),) * 11,
        out_specs=spread,
        check_vma=False,
    )
```

```python
from functools import partial

import jax
import jax.numpy as jnp
from jax import lax
from jax.experimental import pallas as pl
from jax.experimental.pallas import tpu as pltpu
from jax.sharding import PartitionSpec as P

epsilon = 1e-06
parts = 2
pair = 2
taps = 3
most_direct = 8
mebibyte = 1024 * 1024

VMEM = pl.BlockSpec(memory_space=pltpu.VMEM)
SMEM = pl.BlockSpec(memory_space=pltpu.SMEM)
ANY = pl.BlockSpec(memory_space=pl.ANY)


def silu(v):
    return 0.5 * v * (1.0 + jnp.tanh(0.5 * v))


def dot32(a, b):
    return jnp.dot(a, b, preferred_element_type=jnp.float32)


def cost(flops, *arrays):
    size = sum(a.size * a.dtype.itemsize for a in arrays)
    return pl.CostEstimate(flops=flops, bytes_accessed=size, transcendentals=0)


def params(mebibytes):
    return pltpu.CompilerParams(vmem_limit_bytes=mebibytes * mebibyte)


def rows_of(owner, begin, end, half, height):
    low, high = max(begin, 1), min(end, half + 1)
    pieces = [(owner * half + low - 1, low - begin, high - low)]
    if begin == 0:
        pieces.append((jnp.maximum(owner * half - 1, 0), 0, 1))
    if end == half + 2:
        pieces.append((jnp.minimum((owner + 1) * half, height - 1), end - 1 - begin, 1))
    return pieces


def run(copies):
    for copy in copies:
        copy.start()
    for copy in copies:
        copy.wait()


def cut(target, video, frame, owner, begin, end, half):
    for source, here, count in rows_of(owner, begin, end, half, video.shape[1]):
        target[here : here + count] = video[frame, pl.ds(source, count)]


def send_kernel(spans, half, scalars, video, *outs):
    frames = video.shape[0]
    rest = frames - taps
    for k, (begin, end) in enumerate(spans):
        for t in range(frames):
            target = outs[k].at[t - rest] if t >= rest else outs[len(spans) + k].at[t]
            cut(target, video, t, 1 - scalars[0], begin, end, half)


def send(scalars, video, spans, half):
    frames, _, width, channels = video.shape
    shapes = [
        (count, end - begin, width, channels)
        for count in (taps, frames - taps)
        for begin, end in spans
    ]
    return pl.pallas_call(
        partial(send_kernel, spans, half),
        out_shape=[jax.ShapeDtypeStruct(shape, video.dtype) for shape in shapes],
        in_specs=[SMEM, VMEM],
        out_specs=[VMEM] * len(shapes),
        compiler_params=params(12),
        name="send",
    )(scalars, video)


def join_last_kernel(begin, end, half, scalars, video, received, own_edge, other_edge, out):
    frames, rows = video.shape[0], end - begin

    @pl.when(scalars[0] == 0)
    def _():
        out[:, :rows] = received[...]
        out[:, rows:] = other_edge[frames - taps :]

    @pl.when(scalars[0] == 1)
    def _():
        for t in range(taps):
            cut(out.at[t], video, frames - taps + t, 1, begin, end, half)
        out[:, rows:] = own_edge[frames - taps :]


def join_first_kernel(
    begin, end, half, scalars, video, received, others, own_edge, other_edge, out
):
    frames, rows = video.shape[0], end - begin
    rest = frames - taps

    @pl.when(scalars[0] == 0)
    def _():
        for t in range(frames):
            cut(out.at[t], video, t, 0, begin, end, half)
        out[:frames, rows:] = own_edge[...]
        out[frames:, :rows] = others[...]
        out[frames:, rows:] = other_edge[:rest]

    @pl.when(scalars[0] == 1)
    def _():
        out[:rest, :rows] = others[...]
        out[rest:frames, :rows] = received[...]
        out[:frames, rows:] = other_edge[...]
        for t in range(rest):
            cut(out.at[frames + t], video, t, 1, begin, end, half)
        out[frames:, rows:] = own_edge[:rest]


def join(kernel, count, name, begin, end, half, scalars, video, *parts):
    _, _, width, channels = video.shape
    rows = end - begin + parts[-1].shape[1]
    return pl.pallas_call(
        partial(kernel, begin, end, half),
        out_shape=jax.ShapeDtypeStruct((count, rows, width, channels), jnp.bfloat16),
        in_specs=[SMEM] + [VMEM] * (1 + len(parts)),
        out_specs=VMEM,
        compiler_params=params(12),
        name=name,
    )(scalars, video, *parts)


def place_rows(buffers, index, top, reduced, rows, width, column):
    pixels, channels = rows * width, reduced.shape[-1]
    edges = reduced.shape[0] - pixels
    row_of = lax.broadcasted_iota(jnp.int32, (pixels, edges), 0) // width
    spread = (row_of == lax.broadcasted_iota(jnp.int32, (pixels, edges), 1)).astype(jnp.bfloat16)
    across = lax.broadcasted_iota(jnp.int32, (pixels, channels), 0) % width
    wide = reduced[:pixels].astype(jnp.float32)
    beside = dot32(spread, reduced[pixels:])
    before = jnp.where(column == 1, beside, 0.0)
    behind = jnp.where(column == 0, beside, 0.0)
    shifted = (
        jnp.where(across == 0, before, pltpu.roll(wide, 1, 0)),
        wide,
        jnp.where(across == width - 1, behind, pltpu.roll(wide, pixels - 1, 0)),
    )
    for b in range(3):
        value = shifted[b].astype(jnp.bfloat16).reshape(rows, width, channels)
        buffers[b, index, top : top + rows] = value


def convolve(buffers, fresh, last, side, kept, keeps, w_space, b_space):
    _, frames, rows, width, channels = buffers.shape
    size = rows - 2
    if fresh:

        @pl.when(side == 0)
        def _():
            buffers[:, :, :1] = jnp.zeros((3, frames, 1, width, channels), jnp.bfloat16)

    else:
        buffers[:, :, :2] = kept
    if last:

        @pl.when(side == pair - 1)
        def _():
            buffers[:, :, size + 1 :] = jnp.zeros((3, frames, 1, width, channels), jnp.bfloat16)

    else:
        keeps(buffers[:, :, size:])

    def window(b, a):
        return buffers[b, :, a : a + size].reshape(frames * size * width, channels)

    lhs = jnp.concatenate([window(b, a) for a in range(3) for b in range(3)], axis=1)
    acc = dot32(lhs, w_space[...].reshape(-1, channels)) + b_space[...]
    value = window(1, 1).astype(jnp.float32) + silu(acc)
    return value.astype(jnp.bfloat16).reshape(frames, size * width, channels)


def early_kernel(
    final, rows, scalars, first, last, w_time, b_time, w_down, b_down, w_space, b_space, *refs
):
    part, spatial = refs[:2]
    lifted, buffers = refs[-2:]
    keeps = None if final else (lambda value: refs[2].__setitem__(..., value))
    split, depth, width, channels = first.shape
    count = split + taps
    halves = count // 2
    pixels = depth * width

    def frame(t):
        return (first[t] if t < split else last[t - split]).reshape(pixels, channels)

    starts = list(range(taps - 1, count))
    for low in range(0, len(starts), 3):
        group = starts[low : low + 3]
        lhs = jnp.concatenate(
            [jnp.concatenate([frame(t - k) for t in group], axis=0) for k in range(taps)], axis=1
        )
        acc = dot32(lhs, w_time[...]) + b_time[...]
        held = jnp.concatenate([frame(t) for t in group], axis=0).astype(jnp.float32)
        value = (held + silu(acc)).astype(jnp.bfloat16)
        for g, t in enumerate(group):
            lifted[t] = value[g * pixels : (g + 1) * pixels]
    lhs = jnp.concatenate([lifted[3], lifted[2]], axis=1)
    part[...] = dot32(lhs, w_down[: 2 * channels]) + b_down[...]
    whole = range(2, halves)
    lhs = jnp.concatenate(
        [jnp.concatenate([lifted[2 * s + 1 - k] for s in whole], axis=0) for k in range(taps)],
        axis=1,
    )
    reduced = (dot32(lhs, w_down[...]) + b_down[...]).astype(jnp.bfloat16)
    for index in range(len(whole)):
        value = reduced[index * pixels : (index + 1) * pixels]
        place_rows(buffers, index, 0, value, rows, width, scalars[1])
    spatial[...] = convolve(buffers, True, final, scalars[0], None, keeps, w_space, b_space)


def early(scalars, first, last, final, size, rows, *weights):
    split, depth, width, channels = first.shape
    halves = (split + taps) // 2
    pixels = depth * width
    later = halves - 2
    shapes = [
        jax.ShapeDtypeStruct((pixels, channels), jnp.float32),
        jax.ShapeDtypeStruct((later, size * width, channels), jnp.bfloat16),
    ]
    if not final:
        shapes.append(jax.ShapeDtypeStruct((3, later, 2, width, channels), jnp.bfloat16))
    flops = 2 * channels * channels * (pixels * 26 + 9 * later * size * width)
    return pl.pallas_call(
        partial(early_kernel, final, rows),
        out_shape=shapes,
        in_specs=[SMEM] + [VMEM] * (2 + len(weights)),
        out_specs=[VMEM] * len(shapes),
        scratch_shapes=[
            pltpu.VMEM((2 * halves, pixels, channels), jnp.bfloat16),
            pltpu.VMEM((3, later, size + 2, width, channels), jnp.bfloat16),
        ],
        compiler_params=params(24),
        cost_estimate=cost(flops, first, last, *weights),
        name="early",
    )(scalars, first, last, *weights)


def full_kernel(
    owners, final, rows, scalars, halo, first, last, kept_late, kept_early, w_time, b_time, w_down,
    b_down, w_space, b_space, *refs
):
    outs = refs[:owners]
    keeps = None if final else refs[owners : owners + 2]
    lifted, buffers = refs[-2:]
    split, depth, width, channels = first.shape
    count = split + taps
    halves = count // 2
    pixels = depth * width

    def frame(t):
        if t < 0:
            value = halo[t + taps].reshape(pixels, channels)
            return jnp.where(scalars[2] > 0, value, jnp.zeros_like(value))
        return (first[t] if t < split else last[t - split]).reshape(pixels, channels)

    starts = list(range(-1, count))
    for low in range(0, len(starts), 3):
        group = starts[low : low + 3]
        lhs = jnp.concatenate(
            [jnp.concatenate([frame(t - k) for t in group], axis=0) for k in range(taps)], axis=1
        )
        acc = dot32(lhs, w_time[...]) + b_time[...]
        held = jnp.concatenate([frame(t) for t in group], axis=0).astype(jnp.float32)
        value = held + silu(acc)
        for g, t in enumerate(group):
            piece = value[g * pixels : (g + 1) * pixels]
            if t < 0:
                piece = jnp.where(scalars[2] > 0, piece, 0.0)
            lifted[t + 1] = piece.astype(jnp.bfloat16)
    lhs = jnp.concatenate(
        [
            jnp.concatenate([lifted[2 * s + 2 - k] for s in range(halves)], axis=0)
            for k in range(taps)
        ],
        axis=1,
    )
    reduced = (dot32(lhs, w_down[...]) + b_down[...]).astype(jnp.bfloat16)
    for index in range(halves):
        value = reduced[index * pixels : (index + 1) * pixels]
        place_rows(buffers, index, 2, value, rows, width, scalars[1])
    kept = jnp.concatenate([kept_late[...], kept_early[...]], axis=1)
    keep = None if final else (lambda value: keep_both(keeps, value))
    result = convolve(buffers, False, final, scalars[0], kept, keep, w_space, b_space)
    each = result.shape[1] // owners
    if owners == 1:
        outs[0][...] = result
    else:
        for j in range(owners):
            part = result[:, j * each : (j + 1) * each]
            for m in range(owners):

                @pl.when((scalars[2] ^ m) == j)
                def _():
                    outs[m][...] = part


def keep_both(keeps, value):
    keeps[0][...] = value[:, :2]
    keeps[1][...] = value[:, 2:]


def full(owners, scalars, halo, first, last, kept, final, size, rows, *weights):
    split, depth, width, channels = first.shape
    halves = (split + taps) // 2
    pixels = depth * width
    shapes = [(halves, size * width // owners, channels)] * owners
    if not final:
        shapes += [(3, count, 2, width, channels) for count in (2, halves - 2)]
    flops = 2 * channels * channels * (pixels * 39 + 9 * halves * size * width)
    return pl.pallas_call(
        partial(full_kernel, owners, final, rows),
        out_shape=[jax.ShapeDtypeStruct(shape, jnp.bfloat16) for shape in shapes],
        in_specs=[SMEM] + [VMEM] * (5 + len(weights)),
        out_specs=[VMEM] * len(shapes),
        scratch_shapes=[
            pltpu.VMEM((2 * halves + 1, pixels, channels), jnp.bfloat16),
            pltpu.VMEM((3, halves, size + 2, width, channels), jnp.bfloat16),
        ],
        compiler_params=params(28),
        cost_estimate=cost(flops, halo, first, last, *weights),
        name="full",
    )(scalars, halo, first, last, *kept, *weights)


def late_kernel(
    owners, final, rows, scalars, halo, first, part, spatial, w_time, b_time, w_down, b_down,
    w_space, b_space, *refs
):
    outs = refs[:owners]
    keeps = None if final else (lambda value: refs[owners].__setitem__(..., value))
    lifted, buffers, result = refs[-3:]
    _, depth, width, channels = first.shape
    pixels = depth * width

    def frame(t):
        if t < 0:
            value = halo[t + taps].reshape(pixels, channels)
            return jnp.where(scalars[2] > 0, value, jnp.zeros_like(value))
        return first[t].reshape(pixels, channels)

    group = range(-1, taps - 1)
    lhs = jnp.concatenate(
        [jnp.concatenate([frame(t - k) for t in group], axis=0) for k in range(taps)], axis=1
    )
    acc = dot32(lhs, w_time[...]) + b_time[...]
    held = jnp.concatenate([frame(t) for t in group], axis=0).astype(jnp.float32)
    value = held + silu(acc)
    for index in range(taps):
        piece = value[index * pixels : (index + 1) * pixels]
        if index == 0:
            piece = jnp.where(scalars[2] > 0, piece, 0.0)
        lifted[index] = piece.astype(jnp.bfloat16)
    lhs = jnp.concatenate([lifted[2], lifted[1], lifted[0]], axis=1)
    reduced = (
        dot32(lhs, w_down[...]) + b_down[...],
        dot32(lifted[2], w_down[2 * channels :]) + part[...],
    )
    for index, value in enumerate(reduced):
        value = value.astype(jnp.bfloat16)
        place_rows(buffers, index, 0, value, rows, width, scalars[1])
    result[:2] = convolve(buffers, True, final, scalars[0], None, keeps, w_space, b_space)
    result[2:] = spatial[...]
    each = result.shape[1] // owners
    if owners == 1:
        outs[0][...] = result[...]
    else:
        for j, out in enumerate(outs):
            begin = pl.multiple_of((scalars[2] ^ j) * each, each)
            out[...] = result[:, pl.ds(begin, each)]


def late(owners, scalars, halo, first, part, spatial, final, rows, *weights):
    _, depth, width, channels = first.shape
    later, pixels = spatial.shape[:2]
    halves = later + 2
    size = pixels // width
    shapes = [(halves, pixels // owners, channels)] * owners
    if not final:
        shapes.append((3, 2, 2, width, channels))
    flops = 2 * channels * channels * (depth * width * 13 + 18 * pixels)
    return pl.pallas_call(
        partial(late_kernel, owners, final, rows),
        out_shape=[jax.ShapeDtypeStruct(shape, jnp.bfloat16) for shape in shapes],
        in_specs=[SMEM] + [VMEM] * (4 + len(weights)),
        out_specs=[VMEM] * len(shapes),
        scratch_shapes=[
            pltpu.VMEM((taps, depth * width, channels), jnp.bfloat16),
            pltpu.VMEM((3, 2, size + 2, width, channels), jnp.bfloat16),
            pltpu.VMEM((halves, pixels, channels), jnp.bfloat16),
        ],
        compiler_params=params(24),
        cost_estimate=cost(flops, halo, first, part, *weights),
        name="late",
    )(scalars, halo, first, part, spatial, *weights)


def attend_kernel(frames_per, lanes, count, scalars, *refs):
    blocks = refs[:count]
    gain, w_query, w_key, w_value, w_out = refs[count : count + 5]
    outs = refs[count + 5 :]
    channels = gain.shape[-1]
    flat = len(blocks[0].shape) == 2
    groups = 1 if flat else blocks[0].shape[1] // lanes
    each = frames_per * lanes
    size = count * each

    def piece(j, g):
        if flat:
            return blocks[0][...]
        return blocks[j][:, g * lanes : (g + 1) * lanes].reshape(each, channels)

    def place(index):
        block = index // each
        time = index // lanes % frames_per
        for j in range(count):
            level = 0 if flat else scalars[2] ^ j
            time = time + jnp.where(block == j, level * frames_per, 0)
        return time, index % lanes

    row_time, row_lane = place(lax.broadcasted_iota(jnp.int32, (size, 1), 0))
    col_time, col_lane = place(lax.broadcasted_iota(jnp.int32, (1, size), 1))
    allowed = (row_lane == col_lane) & (col_time <= row_time)
    x = jnp.concatenate([piece(j, g) for g in range(groups) for j in range(count)], axis=0)
    wide = x.astype(jnp.float32)
    scale = lax.rsqrt(jnp.mean(wide * wide, axis=-1, keepdims=True) + epsilon)
    normed = (wide * scale * gain[...]).astype(jnp.bfloat16)
    query = dot32(normed, w_query[...]).astype(jnp.bfloat16)
    key = dot32(normed, w_key[...]).astype(jnp.bfloat16)
    value = dot32(normed, w_value[...]).astype(jnp.bfloat16)
    contexts = []
    for g in range(groups):
        part = slice(g * size, (g + 1) * size)
        scores = lax.dot_general(
            query[part], key[part], (((1,), (1,)), ((), ())), preferred_element_type=jnp.float32
        )
        scores = jnp.where(allowed, scores * channels ** (-0.5), -1e30)
        largest = jnp.max(scores, axis=-1, keepdims=True)
        probs = jnp.exp(scores - largest)
        probs = (probs / jnp.sum(probs, axis=-1, keepdims=True)).astype(jnp.bfloat16)
        contexts.append(dot32(probs, value[part]).astype(jnp.bfloat16))
    mixed = dot32(jnp.concatenate(contexts, axis=0), w_out[...])
    result = (wide + mixed).astype(jnp.bfloat16)
    if flat:
        outs[0][...] = result
        return
    short = frames_per // pair
    for g in range(groups):
        for j in range(count):
            begin = g * size + j * each
            rows = result[begin : begin + each].reshape(pair, short, lanes, channels)
            for side in range(pair):

                @pl.when(scalars[0] == side)
                def _():
                    for x in range(pair):
                        outs[pair * j + x][:, g * lanes : (g + 1) * lanes] = rows[side ^ x]


def attend(scalars, blocks, gain, w_query, w_key, w_value, w_out):
    frames_per, pixels, channels = blocks[0].shape
    flat = pixels % 16 != 0
    lanes = pixels if flat else 16
    if flat:
        blocks = [b.reshape(frames_per * pixels, channels) for b in blocks]
    count = len(blocks)
    size = frames_per * count * lanes
    shapes = [(frames_per // pair, pixels, channels)] * (pair * count)
    if flat:
        shapes = [blocks[0].shape]
    flops = 2 * frames_per * pixels * count * channels * (4 * channels + 2 * size)
    outs = pl.pallas_call(
        partial(attend_kernel, frames_per, lanes, count),
        out_shape=[jax.ShapeDtypeStruct(shape, jnp.bfloat16) for shape in shapes],
        in_specs=[SMEM] + [VMEM] * (count + 5),
        out_specs=[VMEM] * len(shapes),
        compiler_params=params(20 if 16 * size * size < 20 * mebibyte else 56),
        cost_estimate=cost(flops, *blocks, w_query, w_key, w_value, w_out),
        name="attend",
    )(scalars, *blocks, gain, w_query, w_key, w_value, w_out)
    return [o.reshape(frames_per, pixels, channels) for o in outs] if flat else outs


def collect_kernel(base, stride, scalars, *refs):
    out, sems = refs[-2:]
    copies = []
    for m in range(sems.shape[0]):
        index = base + (scalars[0] ^ m % pair) * stride + (scalars[2] ^ m // pair)
        copies.append(pltpu.make_async_copy(refs[m], out.at[:, index], sems.at[m]))
    run(copies)


def collect(scalars, blocks, chunk, chunks, whole):
    count = len(blocks)
    halves, pixels, channels = blocks[0].shape
    levels = count // pair
    given = [] if whole is None else [whole]
    return pl.pallas_call(
        partial(collect_kernel, chunk * levels, chunks * levels),
        out_shape=jax.ShapeDtypeStruct((halves, chunks * count, pixels, channels), jnp.bfloat16),
        in_specs=[SMEM] + [ANY] * (count + len(given)),
        out_specs=ANY,
        input_output_aliases={count + 1: 0} if given else {},
        scratch_shapes=[pltpu.SemaphoreType.DMA((count,))],
        compiler_params=params(16),
        name="collect",
    )(scalars, *blocks, *given)


def after(value, other):
    return lax.optimization_barrier((value, other))[0]


def per_device(
    video, w_time, b_time, w_down, b_down, w_space, b_space, gain, w_query, w_key, w_value, w_out
):
    frames, height, width, channels = video.shape
    devices = lax.axis_size("tm")
    levels = devices // pair
    columns = lax.axis_size("cols")
    assert columns == 2 and devices % pair == 0 and height % pair == 0 and frames >= taps
    place = lax.axis_index("tm").astype(jnp.int32)
    column = lax.axis_index("cols").astype(jnp.int32)
    side, level = place % pair, place // pair
    scalars = jnp.stack([side, column, level])
    half = height // pair
    gain = gain.reshape(1, -1)
    w_space = jnp.where(after(place, video) >= 0, w_space, 0)
    weights = [
        w_time.reshape(-1, channels), b_time.reshape(1, -1), w_down.reshape(-1, channels),
        b_down.reshape(1, -1), w_space, b_space.reshape(1, -1),
    ]
    attention = [gain, w_query, w_key, w_value, w_out]
    chunks = parts if half % parts == 0 and half // parts * width % levels == 0 else 1
    size = half // chunks
    each = size * width // levels
    direct = devices <= most_direct and levels & (levels - 1) == 0 and each % 16 == 0
    spans = [
        (k * size + (2 if k else 0), (k + 1) * size + 2) for k in range(chunks)
    ]

    def tm_permute(value, move):
        return lax.ppermute(value, "tm", [(i, move(i)) for i in range(devices) if move(i) < devices])

    sent = send(scalars, video, spans, half)
    received = [tm_permute(value, lambda i: i ^ 1) for value in sent]
    border = jnp.where(column == 0, video[:, :, -1], video[:, :, 0])
    border = jnp.pad(after(border, sent[0]), ((0, 0), (1, 1), (0, 0)))
    own_edge, other_edge = (
        lax.dynamic_slice_in_dim(border, s * half, half + 2, axis=1) for s in (side, 1 - side)
    )
    own_edge = lax.ppermute(own_edge, "cols", [(0, 1), (1, 0)])
    aslant = [
        (i * columns + c, (i ^ 1) * columns + 1 - c)
        for i in range(devices)
        for c in range(columns)
    ]
    other_edge = lax.ppermute(other_edge, ("tm", "cols"), aslant)

    def edge_rows(edge, begin, end):
        cut = jnp.pad(edge[:, begin:end], ((0, 0), (0, -(end - begin) % width), (0, 0)))
        return cut.reshape(frames, -1, width, channels)

    owners = levels if direct else 1
    edges = [[edge_rows(e, begin, end) for e in (own_edge, other_edge)] for begin, end in spans]
    lasts, halos = [], []
    newest = w_space
    for k, (begin, end) in enumerate(spans):
        newest = join(
            join_last_kernel, taps, "join_last", begin, end, half, scalars, video,
            after(received[k], newest), *edges[k]
        )
        lasts.append(newest)
        halos.append(tm_permute(newest, lambda i: (i + pair) % devices))

    spatials = []
    kept = None
    for k, (begin, end) in enumerate(spans):
        rows, final = end - begin, k == chunks - 1
        others = after(received[chunks + k], newest)
        first = join(
            join_first_kernel, pair * frames - taps, "join_first", begin, end, half, scalars,
            video, received[k], others, *edges[k]
        )
        if k == 0:
            part, spatial, *kept = early(scalars, first, lasts[k], final, size, rows, *weights)
            made = late(
                owners, scalars, halos[k], first, part, spatial, final, rows, *weights
            )
            kept = [*made[owners:], *kept]
        else:
            made = full(
                owners, scalars, halos[k], first, lasts[k], kept, final, size, rows, *weights
            )
            kept = made[owners:]
        spatials.append(made[:owners])
        newest = made[0]

    newest = spatials[-1][0]
    if direct:
        gathers = [
            [blocks[0]]
            + [tm_permute(blocks[j], lambda i: i ^ (pair * j)) for j in range(1, levels)]
            for blocks in spatials
        ]
        returns = []
        for gathered in gathers:
            gathered[0] = after(gathered[0], newest)
            results = attend(scalars, gathered, *attention)
            newest = results[0]
            returns.append(
                [results[0]]
                + [tm_permute(results[m], lambda i: i ^ m) for m in range(1, devices)]
            )
        whole = None
        for k, blocks in enumerate(returns):
            whole = collect(scalars, blocks, k, chunks, whole)
        return whole.reshape(frames // 2, height, width, channels)
    sets = [[pair * z + s for z in range(levels)] for s in range(pair)]
    returns = []
    for (block,) in spatials:
        gathered = lax.all_to_all(block, "tm", 1, 0, axis_index_groups=sets, tiled=True)
        (result,) = attend(scalars, [gathered], *attention)
        result = lax.all_to_all(result, "tm", 0, 1, tiled=True)
        result = result.reshape(frames // 2, levels, pair, each, channels)
        returns.append(result.transpose(0, 2, 1, 3, 4).reshape(frames // 2, pair, -1, channels))
    return jnp.concatenate(returns, axis=2).reshape(frames // 2, height, width, channels)


def solution(mesh):
    spread = P(("clips", "tm"), None, "cols", None)
    return jax.shard_map(
        per_device,
        mesh=mesh,
        in_specs=(spread,) + (P(),) * 11,
        out_specs=spread,
        check_vma=False,
    )
```

```python
from functools import partial

import jax
import jax.numpy as jnp
from jax import lax
from jax.experimental import pallas as pl
from jax.experimental.pallas import tpu as pltpu
from jax.sharding import PartitionSpec as P

epsilon = 1e-06
parts = 2
pair = 2
taps = 3
most_direct = 8
mebibyte = 1024 * 1024

VMEM = pl.BlockSpec(memory_space=pltpu.VMEM)
SMEM = pl.BlockSpec(memory_space=pltpu.SMEM)
ANY = pl.BlockSpec(memory_space=pl.ANY)


def silu(v):
    return 0.5 * v * (1.0 + jnp.tanh(0.5 * v))


def dot32(a, b):
    return jnp.dot(a, b, preferred_element_type=jnp.float32)


def cost(flops, *arrays):
    size = sum(a.size * a.dtype.itemsize for a in arrays)
    return pl.CostEstimate(flops=flops, bytes_accessed=size, transcendentals=0)


def params(mebibytes):
    return pltpu.CompilerParams(vmem_limit_bytes=mebibytes * mebibyte)


def rows_of(owner, begin, end, half, height):
    low, high = max(begin, 1), min(end, half + 1)
    pieces = [(owner * half + low - 1, low - begin, high - low)]
    if begin == 0:
        pieces.append((jnp.maximum(owner * half - 1, 0), 0, 1))
    if end == half + 2:
        pieces.append((jnp.minimum((owner + 1) * half, height - 1), end - 1 - begin, 1))
    return pieces


def run(copies):
    for copy in copies:
        copy.start()
    for copy in copies:
        copy.wait()


def cut(target, video, frame, owner, begin, end, half):
    for source, here, count in rows_of(owner, begin, end, half, video.shape[1]):
        target[here : here + count] = video[frame, pl.ds(source, count)]


def send_kernel(spans, half, scalars, video, *outs):
    frames = video.shape[0]
    rest = frames - taps
    for k, (begin, end) in enumerate(spans):
        for t in range(frames):
            target = outs[k].at[t - rest] if t >= rest else outs[len(spans) + k].at[t]
            cut(target, video, t, 1 - scalars[0], begin, end, half)


def send(scalars, video, spans, half):
    frames, _, width, channels = video.shape
    shapes = [
        (count, end - begin, width, channels)
        for count in (taps, frames - taps)
        for begin, end in spans
    ]
    return pl.pallas_call(
        partial(send_kernel, spans, half),
        out_shape=[jax.ShapeDtypeStruct(shape, video.dtype) for shape in shapes],
        in_specs=[SMEM, VMEM],
        out_specs=[VMEM] * len(shapes),
        compiler_params=params(12),
        name="send",
    )(scalars, video)


def join_last_kernel(begin, end, half, scalars, video, received, own_edge, other_edge, out):
    frames, rows = video.shape[0], end - begin

    @pl.when(scalars[0] == 0)
    def _():
        out[:, :rows] = received[...]
        out[:, rows:] = other_edge[frames - taps :]

    @pl.when(scalars[0] == 1)
    def _():
        for t in range(taps):
            cut(out.at[t], video, frames - taps + t, 1, begin, end, half)
        out[:, rows:] = own_edge[frames - taps :]


def join_first_kernel(
    begin, end, half, scalars, video, received, others, own_edge, other_edge, out
):
    frames, rows = video.shape[0], end - begin
    rest = frames - taps

    @pl.when(scalars[0] == 0)
    def _():
        for t in range(frames):
            cut(out.at[t], video, t, 0, begin, end, half)
        out[:frames, rows:] = own_edge[...]
        out[frames:, :rows] = others[...]
        out[frames:, rows:] = other_edge[:rest]

    @pl.when(scalars[0] == 1)
    def _():
        out[:rest, :rows] = others[...]
        out[rest:frames, :rows] = received[...]
        out[:frames, rows:] = other_edge[...]
        for t in range(rest):
            cut(out.at[frames + t], video, t, 1, begin, end, half)
        out[frames:, rows:] = own_edge[:rest]


def join(kernel, count, name, begin, end, half, scalars, video, *parts):
    _, _, width, channels = video.shape
    rows = end - begin + parts[-1].shape[1]
    return pl.pallas_call(
        partial(kernel, begin, end, half),
        out_shape=jax.ShapeDtypeStruct((count, rows, width, channels), jnp.bfloat16),
        in_specs=[SMEM] + [VMEM] * (1 + len(parts)),
        out_specs=VMEM,
        compiler_params=params(12),
        name=name,
    )(scalars, video, *parts)


def place_rows(buffers, index, top, reduced, rows, width, column):
    pixels, channels = rows * width, reduced.shape[-1]
    edges = reduced.shape[0] - pixels
    row_of = lax.broadcasted_iota(jnp.int32, (pixels, edges), 0) // width
    spread = (row_of == lax.broadcasted_iota(jnp.int32, (pixels, edges), 1)).astype(jnp.bfloat16)
    across = lax.broadcasted_iota(jnp.int32, (pixels, channels), 0) % width
    wide = reduced[:pixels].astype(jnp.float32)
    beside = dot32(spread, reduced[pixels:])
    before = jnp.where(column == 1, beside, 0.0)
    behind = jnp.where(column == 0, beside, 0.0)
    shifted = (
        jnp.where(across == 0, before, pltpu.roll(wide, 1, 0)),
        wide,
        jnp.where(across == width - 1, behind, pltpu.roll(wide, pixels - 1, 0)),
    )
    for b in range(3):
        value = shifted[b].astype(jnp.bfloat16).reshape(rows, width, channels)
        buffers[b, index, top : top + rows] = value


def convolve(buffers, fresh, last, side, kept, keeps, w_space, b_space):
    _, frames, rows, width, channels = buffers.shape
    size = rows - 2
    if fresh:

        @pl.when(side == 0)
        def _():
            buffers[:, :, :1] = jnp.zeros((3, frames, 1, width, channels), jnp.bfloat16)

    else:
        buffers[:, :, :2] = kept
    if last:

        @pl.when(side == pair - 1)
        def _():
            buffers[:, :, size + 1 :] = jnp.zeros((3, frames, 1, width, channels), jnp.bfloat16)

    else:
        keeps(buffers[:, :, size:])

    def window(b, a):
        return buffers[b, :, a : a + size].reshape(frames * size * width, channels)

    lhs = jnp.concatenate([window(b, a) for a in range(3) for b in range(3)], axis=1)
    acc = dot32(lhs, w_space[...].reshape(-1, channels)) + b_space[...]
    value = window(1, 1).astype(jnp.float32) + silu(acc)
    return value.astype(jnp.bfloat16).reshape(frames, size * width, channels)


def early_kernel(
    final, rows, scalars, first, last, w_time, b_time, w_down, b_down, w_space, b_space, *refs
):
    part, spatial = refs[:2]
    lifted, buffers = refs[-2:]
    keeps = None if final else (lambda value: refs[2].__setitem__(..., value))
    split, depth, width, channels = first.shape
    count = split + taps
    halves = count // 2
    pixels = depth * width

    def frame(t):
        return (first[t] if t < split else last[t - split]).reshape(pixels, channels)

    starts = list(range(taps - 1, count))
    for low in range(0, len(starts), 3):
        group = starts[low : low + 3]
        lhs = jnp.concatenate(
            [jnp.concatenate([frame(t - k) for t in group], axis=0) for k in range(taps)], axis=1
        )
        acc = dot32(lhs, w_time[...]) + b_time[...]
        held = jnp.concatenate([frame(t) for t in group], axis=0).astype(jnp.float32)
        value = (held + silu(acc)).astype(jnp.bfloat16)
        for g, t in enumerate(group):
            lifted[t] = value[g * pixels : (g + 1) * pixels]
    lhs = jnp.concatenate([lifted[3], lifted[2]], axis=1)
    part[...] = dot32(lhs, w_down[: 2 * channels]) + b_down[...]
    whole = range(2, halves)
    lhs = jnp.concatenate(
        [jnp.concatenate([lifted[2 * s + 1 - k] for s in whole], axis=0) for k in range(taps)],
        axis=1,
    )
    reduced = (dot32(lhs, w_down[...]) + b_down[...]).astype(jnp.bfloat16)
    for index in range(len(whole)):
        value = reduced[index * pixels : (index + 1) * pixels]
        place_rows(buffers, index, 0, value, rows, width, scalars[1])
    spatial[...] = convolve(buffers, True, final, scalars[0], None, keeps, w_space, b_space)


def early(scalars, first, last, final, size, rows, *weights):
    split, depth, width, channels = first.shape
    halves = (split + taps) // 2
    pixels = depth * width
    later = halves - 2
    shapes = [
        jax.ShapeDtypeStruct((pixels, channels), jnp.float32),
        jax.ShapeDtypeStruct((later, size * width, channels), jnp.bfloat16),
    ]
    if not final:
        shapes.append(jax.ShapeDtypeStruct((3, later, 2, width, channels), jnp.bfloat16))
    flops = 2 * channels * channels * (pixels * 26 + 9 * later * size * width)
    return pl.pallas_call(
        partial(early_kernel, final, rows),
        out_shape=shapes,
        in_specs=[SMEM] + [VMEM] * (2 + len(weights)),
        out_specs=[VMEM] * len(shapes),
        scratch_shapes=[
            pltpu.VMEM((2 * halves, pixels, channels), jnp.bfloat16),
            pltpu.VMEM((3, later, size + 2, width, channels), jnp.bfloat16),
        ],
        compiler_params=params(24),
        cost_estimate=cost(flops, first, last, *weights),
        name="early",
    )(scalars, first, last, *weights)


def full_kernel(
    owners, final, rows, scalars, halo, first, last, kept_late, kept_early, w_time, b_time, w_down,
    b_down, w_space, b_space, *refs
):
    outs = refs[:owners]
    keeps = None if final else refs[owners : owners + 2]
    lifted, buffers = refs[-2:]
    split, depth, width, channels = first.shape
    count = split + taps
    halves = count // 2
    pixels = depth * width

    def frame(t):
        if t < 0:
            value = halo[t + taps].reshape(pixels, channels)
            return jnp.where(scalars[2] > 0, value, jnp.zeros_like(value))
        return (first[t] if t < split else last[t - split]).reshape(pixels, channels)

    starts = list(range(-1, count))
    for low in range(0, len(starts), 3):
        group = starts[low : low + 3]
        lhs = jnp.concatenate(
            [jnp.concatenate([frame(t - k) for t in group], axis=0) for k in range(taps)], axis=1
        )
        acc = dot32(lhs, w_time[...]) + b_time[...]
        held = jnp.concatenate([frame(t) for t in group], axis=0).astype(jnp.float32)
        value = held + silu(acc)
        for g, t in enumerate(group):
            piece = value[g * pixels : (g + 1) * pixels]
            if t < 0:
                piece = jnp.where(scalars[2] > 0, piece, 0.0)
            lifted[t + 1] = piece.astype(jnp.bfloat16)
    lhs = jnp.concatenate(
        [
            jnp.concatenate([lifted[2 * s + 2 - k] for s in range(halves)], axis=0)
            for k in range(taps)
        ],
        axis=1,
    )
    reduced = (dot32(lhs, w_down[...]) + b_down[...]).astype(jnp.bfloat16)
    for index in range(halves):
        value = reduced[index * pixels : (index + 1) * pixels]
        place_rows(buffers, index, 2, value, rows, width, scalars[1])
    kept = jnp.concatenate([kept_late[...], kept_early[...]], axis=1)
    keep = None if final else (lambda value: keep_both(keeps, value))
    result = convolve(buffers, False, final, scalars[0], kept, keep, w_space, b_space)
    each = result.shape[1] // owners
    if owners == 1:
        outs[0][...] = result
    else:
        for j in range(owners):
            part = result[:, j * each : (j + 1) * each]
            for m in range(owners):

                @pl.when((scalars[2] ^ m) == j)
                def _():
                    outs[m][...] = part


def keep_both(keeps, value):
    keeps[0][...] = value[:, :2]
    keeps[1][...] = value[:, 2:]


def full(owners, scalars, halo, first, last, kept, final, size, rows, *weights):
    split, depth, width, channels = first.shape
    halves = (split + taps) // 2
    pixels = depth * width
    shapes = [(halves, size * width // owners, channels)] * owners
    if not final:
        shapes += [(3, count, 2, width, channels) for count in (2, halves - 2)]
    flops = 2 * channels * channels * (pixels * 39 + 9 * halves * size * width)
    return pl.pallas_call(
        partial(full_kernel, owners, final, rows),
        out_shape=[jax.ShapeDtypeStruct(shape, jnp.bfloat16) for shape in shapes],
        in_specs=[SMEM] + [VMEM] * (5 + len(weights)),
        out_specs=[VMEM] * len(shapes),
        scratch_shapes=[
            pltpu.VMEM((2 * halves + 1, pixels, channels), jnp.bfloat16),
            pltpu.VMEM((3, halves, size + 2, width, channels), jnp.bfloat16),
        ],
        compiler_params=params(28),
        cost_estimate=cost(flops, halo, first, last, *weights),
        name="full",
    )(scalars, halo, first, last, *kept, *weights)


def late_kernel(
    owners, final, rows, scalars, halo, first, part, spatial, w_time, b_time, w_down, b_down,
    w_space, b_space, *refs
):
    outs = refs[:owners]
    keeps = None if final else (lambda value: refs[owners].__setitem__(..., value))
    lifted, buffers, result = refs[-3:]
    _, depth, width, channels = first.shape
    pixels = depth * width

    def frame(t):
        if t < 0:
            value = halo[t + taps].reshape(pixels, channels)
            return jnp.where(scalars[2] > 0, value, jnp.zeros_like(value))
        return first[t].reshape(pixels, channels)

    group = range(-1, taps - 1)
    lhs = jnp.concatenate(
        [jnp.concatenate([frame(t - k) for t in group], axis=0) for k in range(taps)], axis=1
    )
    acc = dot32(lhs, w_time[...]) + b_time[...]
    held = jnp.concatenate([frame(t) for t in group], axis=0).astype(jnp.float32)
    value = held + silu(acc)
    for index in range(taps):
        piece = value[index * pixels : (index + 1) * pixels]
        if index == 0:
            piece = jnp.where(scalars[2] > 0, piece, 0.0)
        lifted[index] = piece.astype(jnp.bfloat16)
    lhs = jnp.concatenate([lifted[2], lifted[1], lifted[0]], axis=1)
    reduced = (
        dot32(lhs, w_down[...]) + b_down[...],
        dot32(lifted[2], w_down[2 * channels :]) + part[...],
    )
    for index, value in enumerate(reduced):
        value = value.astype(jnp.bfloat16)
        place_rows(buffers, index, 0, value, rows, width, scalars[1])
    result[:2] = convolve(buffers, True, final, scalars[0], None, keeps, w_space, b_space)
    result[2:] = spatial[...]
    each = result.shape[1] // owners
    if owners == 1:
        outs[0][...] = result[...]
    else:
        for j, out in enumerate(outs):
            begin = pl.multiple_of((scalars[2] ^ j) * each, each)
            out[...] = result[:, pl.ds(begin, each)]


def late(owners, scalars, halo, first, part, spatial, final, rows, *weights):
    _, depth, width, channels = first.shape
    later, pixels = spatial.shape[:2]
    halves = later + 2
    size = pixels // width
    shapes = [(halves, pixels // owners, channels)] * owners
    if not final:
        shapes.append((3, 2, 2, width, channels))
    flops = 2 * channels * channels * (depth * width * 13 + 18 * pixels)
    return pl.pallas_call(
        partial(late_kernel, owners, final, rows),
        out_shape=[jax.ShapeDtypeStruct(shape, jnp.bfloat16) for shape in shapes],
        in_specs=[SMEM] + [VMEM] * (4 + len(weights)),
        out_specs=[VMEM] * len(shapes),
        scratch_shapes=[
            pltpu.VMEM((taps, depth * width, channels), jnp.bfloat16),
            pltpu.VMEM((3, 2, size + 2, width, channels), jnp.bfloat16),
            pltpu.VMEM((halves, pixels, channels), jnp.bfloat16),
        ],
        compiler_params=params(24),
        cost_estimate=cost(flops, halo, first, part, *weights),
        name="late",
    )(scalars, halo, first, part, spatial, *weights)


def attend_kernel(frames_per, lanes, turns, scalars, *refs):
    count = len(turns)
    blocks = refs[:count]
    gain, w_query, w_key, w_value, w_out = refs[count : count + 5]
    outs = refs[count + 5 :]
    channels = gain.shape[-1]
    flat = len(blocks[0].shape) == 2
    groups = 1 if flat else blocks[0].shape[1] // lanes
    each = frames_per * lanes
    size = count * each

    def piece(j, g):
        if flat:
            return blocks[0][...]
        return blocks[j][:, g * lanes : (g + 1) * lanes].reshape(each, channels)

    def place(index):
        block = index // each
        time = index // lanes % frames_per
        for j, turn in enumerate(turns):
            level = 0 if flat else scalars[2] ^ turn
            time = time + jnp.where(block == j, level * frames_per, 0)
        return time, index % lanes

    row_time, row_lane = place(lax.broadcasted_iota(jnp.int32, (size, 1), 0))
    col_time, col_lane = place(lax.broadcasted_iota(jnp.int32, (1, size), 1))
    allowed = (row_lane == col_lane) & (col_time <= row_time)
    x = jnp.concatenate([piece(j, g) for g in range(groups) for j in range(count)], axis=0)
    wide = x.astype(jnp.float32)
    scale = lax.rsqrt(jnp.mean(wide * wide, axis=-1, keepdims=True) + epsilon)
    normed = (wide * scale * gain[...]).astype(jnp.bfloat16)
    query = dot32(normed, w_query[...]).astype(jnp.bfloat16)
    key = dot32(normed, w_key[...]).astype(jnp.bfloat16)
    value = dot32(normed, w_value[...]).astype(jnp.bfloat16)
    contexts = []
    for g in range(groups):
        part = slice(g * size, (g + 1) * size)
        scores = lax.dot_general(
            query[part], key[part], (((1,), (1,)), ((), ())), preferred_element_type=jnp.float32
        )
        scores = jnp.where(allowed, scores * channels ** (-0.5), -1e30)
        largest = jnp.max(scores, axis=-1, keepdims=True)
        probs = jnp.exp(scores - largest)
        probs = (probs / jnp.sum(probs, axis=-1, keepdims=True)).astype(jnp.bfloat16)
        contexts.append(dot32(probs, value[part]).astype(jnp.bfloat16))
    mixed = dot32(jnp.concatenate(contexts, axis=0), w_out[...])
    result = (wide + mixed).astype(jnp.bfloat16)
    if flat:
        outs[0][...] = result
        return
    short = frames_per // pair
    for g in range(groups):
        for j in range(count):
            begin = g * size + j * each
            rows = result[begin : begin + each].reshape(pair, short, lanes, channels)
            for side in range(pair):

                @pl.when(scalars[0] == side)
                def _():
                    for x in range(pair):
                        outs[pair * j + x][:, g * lanes : (g + 1) * lanes] = rows[side ^ x]


def attend(scalars, turns, blocks, gain, w_query, w_key, w_value, w_out):
    frames_per, pixels, channels = blocks[0].shape
    flat = pixels % 16 != 0
    lanes = pixels if flat else 16
    if flat:
        blocks = [b.reshape(frames_per * pixels, channels) for b in blocks]
    count = len(blocks)
    size = frames_per * count * lanes
    shapes = [(frames_per // pair, pixels, channels)] * (pair * count)
    if flat:
        shapes = [blocks[0].shape]
    flops = 2 * frames_per * pixels * count * channels * (4 * channels + 2 * size)
    outs = pl.pallas_call(
        partial(attend_kernel, frames_per, lanes, turns),
        out_shape=[jax.ShapeDtypeStruct(shape, jnp.bfloat16) for shape in shapes],
        in_specs=[SMEM] + [VMEM] * (count + 5),
        out_specs=[VMEM] * len(shapes),
        compiler_params=params(20 if 16 * size * size < 20 * mebibyte else 56),
        cost_estimate=cost(flops, *blocks, w_query, w_key, w_value, w_out),
        name="attend",
    )(scalars, *blocks, gain, w_query, w_key, w_value, w_out)
    return [o.reshape(frames_per, pixels, channels) for o in outs] if flat else outs


def collect_kernel(base, stride, turns, scalars, *refs):
    out, sems = refs[-2:]
    copies = []
    for j, level in enumerate(turns):
        for x in range(pair):
            block = refs[pair * j + x]
            index = base + (scalars[0] ^ x) * stride + (scalars[2] ^ level)
            copies.append(pltpu.make_async_copy(block, out.at[:, index], sems.at[len(copies)]))
    run(copies)


def collect(scalars, turns, blocks, chunk, chunks, whole):
    levels = len(turns)
    count = pair * levels
    halves, pixels, channels = blocks[0].shape
    given = [] if whole is None else [whole]
    return pl.pallas_call(
        partial(collect_kernel, chunk * levels, chunks * levels, turns),
        out_shape=jax.ShapeDtypeStruct((halves, chunks * count, pixels, channels), jnp.bfloat16),
        in_specs=[SMEM] + [ANY] * (len(blocks) + len(given)),
        out_specs=ANY,
        input_output_aliases={len(blocks) + 1: 0} if given else {},
        scratch_shapes=[pltpu.SemaphoreType.DMA((count,))],
        compiler_params=params(16),
        name="collect",
    )(scalars, *blocks, *given)


def after(value, other):
    return lax.optimization_barrier((value, other))[0]


def per_device(
    video, w_time, b_time, w_down, b_down, w_space, b_space, gain, w_query, w_key, w_value, w_out
):
    frames, height, width, channels = video.shape
    devices = lax.axis_size("tm")
    levels = devices // pair
    columns = lax.axis_size("cols")
    assert columns == 2 and devices % pair == 0 and height % pair == 0 and frames >= taps
    place = lax.axis_index("tm").astype(jnp.int32)
    column = lax.axis_index("cols").astype(jnp.int32)
    side, level = place % pair, place // pair
    scalars = jnp.stack([side, column, level])
    half = height // pair
    gain = gain.reshape(1, -1)
    w_space = jnp.where(after(place, video) >= 0, w_space, 0)
    weights = [
        w_time.reshape(-1, channels), b_time.reshape(1, -1), w_down.reshape(-1, channels),
        b_down.reshape(1, -1), w_space, b_space.reshape(1, -1),
    ]
    attention = [gain, w_query, w_key, w_value, w_out]
    chunks = parts if half % parts == 0 and half // parts * width % levels == 0 else 1
    size = half // chunks
    each = size * width // levels
    direct = devices <= most_direct and levels & (levels - 1) == 0 and each % 16 == 0
    spans = [
        (k * size + (2 if k else 0), (k + 1) * size + 2) for k in range(chunks)
    ]

    def tm_permute(value, move):
        return lax.ppermute(value, "tm", [(i, move(i)) for i in range(devices) if move(i) < devices])

    sent = send(scalars, video, spans, half)
    received = [tm_permute(value, lambda i: i ^ 1) for value in sent]
    border = jnp.where(column == 0, video[:, :, -1], video[:, :, 0])
    border = jnp.pad(after(border, sent[0]), ((0, 0), (1, 1), (0, 0)))
    own_edge, other_edge = (
        lax.dynamic_slice_in_dim(border, s * half, half + 2, axis=1) for s in (side, 1 - side)
    )
    own_edge = lax.ppermute(own_edge, "cols", [(0, 1), (1, 0)])
    aslant = [
        (i * columns + c, (i ^ 1) * columns + 1 - c)
        for i in range(devices)
        for c in range(columns)
    ]
    other_edge = lax.ppermute(other_edge, ("tm", "cols"), aslant)

    def edge_rows(edge, begin, end):
        cut = jnp.pad(edge[:, begin:end], ((0, 0), (0, -(end - begin) % width), (0, 0)))
        return cut.reshape(frames, -1, width, channels)

    owners = levels if direct else 1
    edges = [[edge_rows(e, begin, end) for e in (own_edge, other_edge)] for begin, end in spans]
    lasts, halos = [], []
    newest = w_space
    for k, (begin, end) in enumerate(spans):
        newest = join(
            join_last_kernel, taps, "join_last", begin, end, half, scalars, video,
            after(received[k], newest), *edges[k]
        )
        lasts.append(newest)
        halos.append(tm_permute(newest, lambda i: (i + pair) % devices))

    spatials = []
    kept = None
    for k, (begin, end) in enumerate(spans):
        rows, final = end - begin, k == chunks - 1
        others = after(received[chunks + k], newest)
        first = join(
            join_first_kernel, pair * frames - taps, "join_first", begin, end, half, scalars,
            video, received[k], others, *edges[k]
        )
        if k == 0:
            part, spatial, *kept = early(scalars, first, lasts[k], final, size, rows, *weights)
            made = late(
                owners, scalars, halos[k], first, part, spatial, final, rows, *weights
            )
            kept = [*made[owners:], *kept]
        else:
            made = full(
                owners, scalars, halos[k], first, lasts[k], kept, final, size, rows, *weights
            )
            kept = made[owners:]
        spatials.append(made[:owners])
        newest = made[0]

    newest = spatials[-1][0]
    if direct:
        turns = tuple(range(levels // 2, levels)) + tuple(range(levels // 2))[::-1]

        def exchange(blocks, moves):
            return [
                tm_permute(block, lambda i: i ^ move) if move else block
                for block, move in zip(blocks, moves)
            ]

        gathers = [
            exchange([blocks[j] for j in turns], [pair * j for j in turns]) for blocks in spatials
        ]
        returns = []
        for gathered in gathers:
            gathered[-1] = after(gathered[-1], newest)
            results = attend(scalars, turns, gathered, *attention)
            newest = results[0]
            moves = [pair * j + x for j in turns for x in range(pair)]
            returns.append(exchange(results, moves))
        whole = None
        for k, blocks in enumerate(returns):
            whole = collect(scalars, turns, blocks, k, chunks, whole)
        return whole.reshape(frames // 2, height, width, channels)
    sets = [[pair * z + s for z in range(levels)] for s in range(pair)]
    returns = []
    for (block,) in spatials:
        gathered = lax.all_to_all(block, "tm", 1, 0, axis_index_groups=sets, tiled=True)
        (result,) = attend(scalars, (0,), [gathered], *attention)
        result = lax.all_to_all(result, "tm", 0, 1, tiled=True)
        result = result.reshape(frames // 2, levels, pair, each, channels)
        returns.append(result.transpose(0, 2, 1, 3, 4).reshape(frames // 2, pair, -1, channels))
    return jnp.concatenate(returns, axis=2).reshape(frames // 2, height, width, channels)


def solution(mesh):
    spread = P(("clips", "tm"), None, "cols", None)
    return jax.shard_map(
        per_device,
        mesh=mesh,
        in_specs=(spread,) + (P(),) * 11,
        out_specs=spread,
        check_vma=False,
    )
```

```python
from functools import partial

import jax
import jax.numpy as jnp
from jax import lax
from jax.experimental import pallas as pl
from jax.experimental.pallas import tpu as pltpu
from jax.sharding import PartitionSpec as P

epsilon = 1e-06
parts = 2
pair = 2
taps = 3
most_direct = 8
mebibyte = 1024 * 1024

VMEM = pl.BlockSpec(memory_space=pltpu.VMEM)
SMEM = pl.BlockSpec(memory_space=pltpu.SMEM)
ANY = pl.BlockSpec(memory_space=pl.ANY)


def silu(v):
    return 0.5 * v * (1.0 + jnp.tanh(0.5 * v))


def dot32(a, b):
    return jnp.dot(a, b, preferred_element_type=jnp.float32)


def cost(flops, *arrays):
    size = sum(a.size * a.dtype.itemsize for a in arrays)
    return pl.CostEstimate(flops=flops, bytes_accessed=size, transcendentals=0)


def params(mebibytes):
    return pltpu.CompilerParams(vmem_limit_bytes=mebibytes * mebibyte)


def rows_of(owner, begin, end, half, height):
    low, high = max(begin, 1), min(end, half + 1)
    pieces = [(owner * half + low - 1, low - begin, high - low)]
    if begin == 0:
        pieces.append((jnp.maximum(owner * half - 1, 0), 0, 1))
    if end == half + 2:
        pieces.append((jnp.minimum((owner + 1) * half, height - 1), end - 1 - begin, 1))
    return pieces


def run(copies):
    for copy in copies:
        copy.start()
    for copy in copies:
        copy.wait()


def cut(target, video, frame, owner, begin, end, half):
    for source, here, count in rows_of(owner, begin, end, half, video.shape[1]):
        target[here : here + count] = video[frame, pl.ds(source, count)]


def send_kernel(spans, half, scalars, video, *outs):
    frames = video.shape[0]
    rest = frames - taps
    for k, (begin, end) in enumerate(spans):
        for t in range(frames):
            target = outs[2 * k].at[t - rest] if t >= rest else outs[2 * k + 1].at[t]
            cut(target, video, t, 1 - scalars[0], begin, end, half)


def send(scalars, video, spans, half):
    frames, _, width, channels = video.shape
    shapes = [
        (count, end - begin, width, channels)
        for begin, end in spans
        for count in (taps, frames - taps)
    ]
    return pl.pallas_call(
        partial(send_kernel, spans, half),
        out_shape=[jax.ShapeDtypeStruct(shape, video.dtype) for shape in shapes],
        in_specs=[SMEM, VMEM],
        out_specs=[VMEM] * len(shapes),
        compiler_params=params(12),
        name="send",
    )(scalars, video)


def join_last_kernel(begin, end, half, scalars, video, received, own_edge, other_edge, out):
    frames, rows = video.shape[0], end - begin

    @pl.when(scalars[0] == 0)
    def _():
        out[:, :rows] = received[...]
        out[:, rows:] = other_edge[frames - taps :]

    @pl.when(scalars[0] == 1)
    def _():
        for t in range(taps):
            cut(out.at[t], video, frames - taps + t, 1, begin, end, half)
        out[:, rows:] = own_edge[frames - taps :]


def join_first_kernel(
    begin, end, half, scalars, video, received, others, own_edge, other_edge, out
):
    frames, rows = video.shape[0], end - begin
    rest = frames - taps

    @pl.when(scalars[0] == 0)
    def _():
        for t in range(frames):
            cut(out.at[t], video, t, 0, begin, end, half)
        out[:frames, rows:] = own_edge[...]
        out[frames:, :rows] = others[...]
        out[frames:, rows:] = other_edge[:rest]

    @pl.when(scalars[0] == 1)
    def _():
        out[:rest, :rows] = others[...]
        out[rest:frames, :rows] = received[...]
        out[:frames, rows:] = other_edge[...]
        for t in range(rest):
            cut(out.at[frames + t], video, t, 1, begin, end, half)
        out[frames:, rows:] = own_edge[:rest]


def join(kernel, count, name, begin, end, half, scalars, video, *parts):
    _, _, width, channels = video.shape
    rows = end - begin + parts[-1].shape[1]
    return pl.pallas_call(
        partial(kernel, begin, end, half),
        out_shape=jax.ShapeDtypeStruct((count, rows, width, channels), jnp.bfloat16),
        in_specs=[SMEM] + [VMEM] * (1 + len(parts)),
        out_specs=VMEM,
        compiler_params=params(12),
        name=name,
    )(scalars, video, *parts)


def place_rows(buffers, index, top, reduced, rows, width, column):
    pixels, channels = rows * width, reduced.shape[-1]
    edges = reduced.shape[0] - pixels
    row_of = lax.broadcasted_iota(jnp.int32, (pixels, edges), 0) // width
    spread = (row_of == lax.broadcasted_iota(jnp.int32, (pixels, edges), 1)).astype(jnp.bfloat16)
    across = lax.broadcasted_iota(jnp.int32, (pixels, channels), 0) % width
    wide = reduced[:pixels].astype(jnp.float32)
    beside = dot32(spread, reduced[pixels:])
    before = jnp.where(column == 1, beside, 0.0)
    behind = jnp.where(column == 0, beside, 0.0)
    shifted = (
        jnp.where(across == 0, before, pltpu.roll(wide, 1, 0)),
        wide,
        jnp.where(across == width - 1, behind, pltpu.roll(wide, pixels - 1, 0)),
    )
    for b in range(3):
        value = shifted[b].astype(jnp.bfloat16).reshape(rows, width, channels)
        buffers[b, index, top : top + rows] = value


def convolve(buffers, fresh, last, side, kept, keeps, w_space, b_space):
    _, frames, rows, width, channels = buffers.shape
    size = rows - 2
    if fresh:

        @pl.when(side == 0)
        def _():
            buffers[:, :, :1] = jnp.zeros((3, frames, 1, width, channels), jnp.bfloat16)

    else:
        buffers[:, :, :2] = kept
    if last:

        @pl.when(side == pair - 1)
        def _():
            buffers[:, :, size + 1 :] = jnp.zeros((3, frames, 1, width, channels), jnp.bfloat16)

    else:
        keeps(buffers[:, :, size:])

    def window(b, a):
        return buffers[b, :, a : a + size].reshape(frames * size * width, channels)

    lhs = jnp.concatenate([window(b, a) for a in range(3) for b in range(3)], axis=1)
    acc = dot32(lhs, w_space[...].reshape(-1, channels)) + b_space[...]
    value = window(1, 1).astype(jnp.float32) + silu(acc)
    return value.astype(jnp.bfloat16).reshape(frames, size * width, channels)


def early_kernel(
    final, rows, scalars, first, last, w_time, b_time, w_down, b_down, w_space, b_space, *refs
):
    part, spatial = refs[:2]
    lifted, buffers = refs[-2:]
    keeps = None if final else (lambda value: refs[2].__setitem__(..., value))
    split, depth, width, channels = first.shape
    count = split + taps
    halves = count // 2
    pixels = depth * width

    def frame(t):
        return (first[t] if t < split else last[t - split]).reshape(pixels, channels)

    starts = list(range(taps - 1, count))
    for low in range(0, len(starts), 3):
        group = starts[low : low + 3]
        lhs = jnp.concatenate(
            [jnp.concatenate([frame(t - k) for t in group], axis=0) for k in range(taps)], axis=1
        )
        acc = dot32(lhs, w_time[...]) + b_time[...]
        held = jnp.concatenate([frame(t) for t in group], axis=0).astype(jnp.float32)
        value = (held + silu(acc)).astype(jnp.bfloat16)
        for g, t in enumerate(group):
            lifted[t] = value[g * pixels : (g + 1) * pixels]
    lhs = jnp.concatenate([lifted[3], lifted[2]], axis=1)
    part[...] = dot32(lhs, w_down[: 2 * channels]) + b_down[...]
    whole = range(2, halves)
    lhs = jnp.concatenate(
        [jnp.concatenate([lifted[2 * s + 1 - k] for s in whole], axis=0) for k in range(taps)],
        axis=1,
    )
    reduced = (dot32(lhs, w_down[...]) + b_down[...]).astype(jnp.bfloat16)
    for index in range(len(whole)):
        value = reduced[index * pixels : (index + 1) * pixels]
        place_rows(buffers, index, 0, value, rows, width, scalars[1])
    spatial[...] = convolve(buffers, True, final, scalars[0], None, keeps, w_space, b_space)


def early(scalars, first, last, final, size, rows, *weights):
    split, depth, width, channels = first.shape
    halves = (split + taps) // 2
    pixels = depth * width
    later = halves - 2
    shapes = [
        jax.ShapeDtypeStruct((pixels, channels), jnp.float32),
        jax.ShapeDtypeStruct((later, size * width, channels), jnp.bfloat16),
    ]
    if not final:
        shapes.append(jax.ShapeDtypeStruct((3, later, 2, width, channels), jnp.bfloat16))
    flops = 2 * channels * channels * (pixels * 26 + 9 * later * size * width)
    return pl.pallas_call(
        partial(early_kernel, final, rows),
        out_shape=shapes,
        in_specs=[SMEM] + [VMEM] * (2 + len(weights)),
        out_specs=[VMEM] * len(shapes),
        scratch_shapes=[
            pltpu.VMEM((2 * halves, pixels, channels), jnp.bfloat16),
            pltpu.VMEM((3, later, size + 2, width, channels), jnp.bfloat16),
        ],
        compiler_params=params(24),
        cost_estimate=cost(flops, first, last, *weights),
        name="early",
    )(scalars, first, last, *weights)


def full_kernel(
    owners, final, rows, scalars, halo, first, last, kept_late, kept_early, w_time, b_time, w_down,
    b_down, w_space, b_space, *refs
):
    outs = refs[:owners]
    keeps = None if final else refs[owners : owners + 2]
    lifted, buffers = refs[-2:]
    split, depth, width, channels = first.shape
    count = split + taps
    halves = count // 2
    pixels = depth * width

    def frame(t):
        if t < 0:
            value = halo[t + taps].reshape(pixels, channels)
            return jnp.where(scalars[2] > 0, value, jnp.zeros_like(value))
        return (first[t] if t < split else last[t - split]).reshape(pixels, channels)

    starts = list(range(-1, count))
    for low in range(0, len(starts), 3):
        group = starts[low : low + 3]
        lhs = jnp.concatenate(
            [jnp.concatenate([frame(t - k) for t in group], axis=0) for k in range(taps)], axis=1
        )
        acc = dot32(lhs, w_time[...]) + b_time[...]
        held = jnp.concatenate([frame(t) for t in group], axis=0).astype(jnp.float32)
        value = held + silu(acc)
        for g, t in enumerate(group):
            piece = value[g * pixels : (g + 1) * pixels]
            if t < 0:
                piece = jnp.where(scalars[2] > 0, piece, 0.0)
            lifted[t + 1] = piece.astype(jnp.bfloat16)
    lhs = jnp.concatenate(
        [
            jnp.concatenate([lifted[2 * s + 2 - k] for s in range(halves)], axis=0)
            for k in range(taps)
        ],
        axis=1,
    )
    reduced = (dot32(lhs, w_down[...]) + b_down[...]).astype(jnp.bfloat16)
    for index in range(halves):
        value = reduced[index * pixels : (index + 1) * pixels]
        place_rows(buffers, index, 2, value, rows, width, scalars[1])
    kept = jnp.concatenate([kept_late[...], kept_early[...]], axis=1)
    keep = None if final else (lambda value: keep_both(keeps, value))
    result = convolve(buffers, False, final, scalars[0], kept, keep, w_space, b_space)
    each = result.shape[1] // owners
    if owners == 1:
        outs[0][...] = result
    else:
        for j in range(owners):
            part = result[:, j * each : (j + 1) * each]
            for m in range(owners):

                @pl.when((scalars[2] ^ m) == j)
                def _():
                    outs[m][...] = part


def keep_both(keeps, value):
    keeps[0][...] = value[:, :2]
    keeps[1][...] = value[:, 2:]


def full(owners, scalars, halo, first, last, kept, final, size, rows, *weights):
    split, depth, width, channels = first.shape
    halves = (split + taps) // 2
    pixels = depth * width
    shapes = [(halves, size * width // owners, channels)] * owners
    if not final:
        shapes += [(3, count, 2, width, channels) for count in (2, halves - 2)]
    flops = 2 * channels * channels * (pixels * 39 + 9 * halves * size * width)
    return pl.pallas_call(
        partial(full_kernel, owners, final, rows),
        out_shape=[jax.ShapeDtypeStruct(shape, jnp.bfloat16) for shape in shapes],
        in_specs=[SMEM] + [VMEM] * (5 + len(weights)),
        out_specs=[VMEM] * len(shapes),
        scratch_shapes=[
            pltpu.VMEM((2 * halves + 1, pixels, channels), jnp.bfloat16),
            pltpu.VMEM((3, halves, size + 2, width, channels), jnp.bfloat16),
        ],
        compiler_params=params(28),
        cost_estimate=cost(flops, halo, first, last, *weights),
        name="full",
    )(scalars, halo, first, last, *kept, *weights)


def late_kernel(
    owners, final, rows, scalars, halo, first, part, spatial, w_time, b_time, w_down, b_down,
    w_space, b_space, *refs
):
    outs = refs[:owners]
    keeps = None if final else (lambda value: refs[owners].__setitem__(..., value))
    lifted, buffers, result = refs[-3:]
    _, depth, width, channels = first.shape
    pixels = depth * width

    def frame(t):
        if t < 0:
            value = halo[t + taps].reshape(pixels, channels)
            return jnp.where(scalars[2] > 0, value, jnp.zeros_like(value))
        return first[t].reshape(pixels, channels)

    group = range(-1, taps - 1)
    lhs = jnp.concatenate(
        [jnp.concatenate([frame(t - k) for t in group], axis=0) for k in range(taps)], axis=1
    )
    acc = dot32(lhs, w_time[...]) + b_time[...]
    held = jnp.concatenate([frame(t) for t in group], axis=0).astype(jnp.float32)
    value = held + silu(acc)
    for index in range(taps):
        piece = value[index * pixels : (index + 1) * pixels]
        if index == 0:
            piece = jnp.where(scalars[2] > 0, piece, 0.0)
        lifted[index] = piece.astype(jnp.bfloat16)
    lhs = jnp.concatenate([lifted[2], lifted[1], lifted[0]], axis=1)
    reduced = (
        dot32(lhs, w_down[...]) + b_down[...],
        dot32(lifted[2], w_down[2 * channels :]) + part[...],
    )
    for index, value in enumerate(reduced):
        value = value.astype(jnp.bfloat16)
        place_rows(buffers, index, 0, value, rows, width, scalars[1])
    result[:2] = convolve(buffers, True, final, scalars[0], None, keeps, w_space, b_space)
    result[2:] = spatial[...]
    each = result.shape[1] // owners
    if owners == 1:
        outs[0][...] = result[...]
    else:
        for j, out in enumerate(outs):
            begin = pl.multiple_of((scalars[2] ^ j) * each, each)
            out[...] = result[:, pl.ds(begin, each)]


def late(owners, scalars, halo, first, part, spatial, final, rows, *weights):
    _, depth, width, channels = first.shape
    later, pixels = spatial.shape[:2]
    halves = later + 2
    size = pixels // width
    shapes = [(halves, pixels // owners, channels)] * owners
    if not final:
        shapes.append((3, 2, 2, width, channels))
    flops = 2 * channels * channels * (depth * width * 13 + 18 * pixels)
    return pl.pallas_call(
        partial(late_kernel, owners, final, rows),
        out_shape=[jax.ShapeDtypeStruct(shape, jnp.bfloat16) for shape in shapes],
        in_specs=[SMEM] + [VMEM] * (4 + len(weights)),
        out_specs=[VMEM] * len(shapes),
        scratch_shapes=[
            pltpu.VMEM((taps, depth * width, channels), jnp.bfloat16),
            pltpu.VMEM((3, 2, size + 2, width, channels), jnp.bfloat16),
            pltpu.VMEM((halves, pixels, channels), jnp.bfloat16),
        ],
        compiler_params=params(24),
        cost_estimate=cost(flops, halo, first, part, *weights),
        name="late",
    )(scalars, halo, first, part, spatial, *weights)


def attend_kernel(frames_per, lanes, count, scalars, *refs):
    blocks = refs[:count]
    gain, w_query, w_key, w_value, w_out = refs[count : count + 5]
    outs = refs[count + 5 :]
    channels = gain.shape[-1]
    flat = len(blocks[0].shape) == 2
    groups = 1 if flat else blocks[0].shape[1] // lanes
    each = frames_per * lanes
    size = count * each

    def piece(j, g):
        if flat:
            return blocks[0][...]
        return blocks[j][:, g * lanes : (g + 1) * lanes].reshape(each, channels)

    def place(index):
        block = index // each
        time = index // lanes % frames_per
        for j in range(count):
            level = 0 if flat else scalars[2] ^ j
            time = time + jnp.where(block == j, level * frames_per, 0)
        return time, index % lanes

    row_time, row_lane = place(lax.broadcasted_iota(jnp.int32, (size, 1), 0))
    col_time, col_lane = place(lax.broadcasted_iota(jnp.int32, (1, size), 1))
    allowed = (row_lane == col_lane) & (col_time <= row_time)
    x = jnp.concatenate([piece(j, g) for g in range(groups) for j in range(count)], axis=0)
    wide = x.astype(jnp.float32)
    scale = lax.rsqrt(jnp.mean(wide * wide, axis=-1, keepdims=True) + epsilon)
    normed = (wide * scale * gain[...]).astype(jnp.bfloat16)
    query = dot32(normed, w_query[...]).astype(jnp.bfloat16)
    key = dot32(normed, w_key[...]).astype(jnp.bfloat16)
    value = dot32(normed, w_value[...]).astype(jnp.bfloat16)
    contexts = []
    for g in range(groups):
        part = slice(g * size, (g + 1) * size)
        scores = lax.dot_general(
            query[part], key[part], (((1,), (1,)), ((), ())), preferred_element_type=jnp.float32
        )
        scores = jnp.where(allowed, scores * channels ** (-0.5), -1e30)
        largest = jnp.max(scores, axis=-1, keepdims=True)
        probs = jnp.exp(scores - largest)
        probs = (probs / jnp.sum(probs, axis=-1, keepdims=True)).astype(jnp.bfloat16)
        contexts.append(dot32(probs, value[part]).astype(jnp.bfloat16))
    mixed = dot32(jnp.concatenate(contexts, axis=0), w_out[...])
    result = (wide + mixed).astype(jnp.bfloat16)
    if flat:
        outs[0][...] = result
        return
    short = frames_per // pair
    for g in range(groups):
        for j in range(count):
            begin = g * size + j * each
            rows = result[begin : begin + each].reshape(pair, short, lanes, channels)
            for side in range(pair):

                @pl.when(scalars[0] == side)
                def _():
                    for x in range(pair):
                        outs[pair * j + x][:, g * lanes : (g + 1) * lanes] = rows[side ^ x]


def attend(scalars, blocks, gain, w_query, w_key, w_value, w_out):
    frames_per, pixels, channels = blocks[0].shape
    flat = pixels % 16 != 0
    lanes = pixels if flat else 16
    if flat:
        blocks = [b.reshape(frames_per * pixels, channels) for b in blocks]
    count = len(blocks)
    size = frames_per * count * lanes
    shapes = [(frames_per // pair, pixels, channels)] * (pair * count)
    if flat:
        shapes = [blocks[0].shape]
    flops = 2 * frames_per * pixels * count * channels * (4 * channels + 2 * size)
    outs = pl.pallas_call(
        partial(attend_kernel, frames_per, lanes, count),
        out_shape=[jax.ShapeDtypeStruct(shape, jnp.bfloat16) for shape in shapes],
        in_specs=[SMEM] + [VMEM] * (count + 5),
        out_specs=[VMEM] * len(shapes),
        compiler_params=params(20 if 16 * size * size < 20 * mebibyte else 56),
        cost_estimate=cost(flops, *blocks, w_query, w_key, w_value, w_out),
        name="attend",
    )(scalars, *blocks, gain, w_query, w_key, w_value, w_out)
    return [o.reshape(frames_per, pixels, channels) for o in outs] if flat else outs


def collect_kernel(base, stride, scalars, *refs):
    out, sems = refs[-2:]
    copies = []
    for m in range(sems.shape[0]):
        index = base + (scalars[0] ^ m % pair) * stride + (scalars[2] ^ m // pair)
        copies.append(pltpu.make_async_copy(refs[m], out.at[:, index], sems.at[m]))
    run(copies)


def collect(scalars, blocks, chunk, chunks, whole):
    count = len(blocks)
    halves, pixels, channels = blocks[0].shape
    levels = count // pair
    given = [] if whole is None else [whole]
    return pl.pallas_call(
        partial(collect_kernel, chunk * levels, chunks * levels),
        out_shape=jax.ShapeDtypeStruct((halves, chunks * count, pixels, channels), jnp.bfloat16),
        in_specs=[SMEM] + [ANY] * (count + len(given)),
        out_specs=ANY,
        input_output_aliases={count + 1: 0} if given else {},
        scratch_shapes=[pltpu.SemaphoreType.DMA((count,))],
        compiler_params=params(16),
        name="collect",
    )(scalars, *blocks, *given)


def after(value, other):
    return lax.optimization_barrier((value, other))[0]


def per_device(
    video, w_time, b_time, w_down, b_down, w_space, b_space, gain, w_query, w_key, w_value, w_out
):
    frames, height, width, channels = video.shape
    devices = lax.axis_size("tm")
    levels = devices // pair
    columns = lax.axis_size("cols")
    assert columns == 2 and devices % pair == 0 and height % pair == 0 and frames >= taps
    place = lax.axis_index("tm").astype(jnp.int32)
    column = lax.axis_index("cols").astype(jnp.int32)
    side, level = place % pair, place // pair
    scalars = jnp.stack([side, column, level])
    half = height // pair
    gain = gain.reshape(1, -1)
    w_space = jnp.where(after(place, video) >= 0, w_space, 0)
    weights = [
        w_time.reshape(-1, channels), b_time.reshape(1, -1), w_down.reshape(-1, channels),
        b_down.reshape(1, -1), w_space, b_space.reshape(1, -1),
    ]
    attention = [gain, w_query, w_key, w_value, w_out]
    chunks = parts if half % parts == 0 and half // parts * width % levels == 0 else 1
    size = half // chunks
    each = size * width // levels
    direct = devices <= most_direct and levels & (levels - 1) == 0 and each % 16 == 0
    spans = [
        (k * size + (2 if k else 0), (k + 1) * size + 2) for k in range(chunks)
    ]

    def tm_permute(value, move):
        return lax.ppermute(value, "tm", [(i, move(i)) for i in range(devices) if move(i) < devices])

    sent = send(scalars, video, spans, half)
    received = [tm_permute(value, lambda i: i ^ 1) for value in sent]
    border = jnp.where(column == 0, video[:, :, -1], video[:, :, 0])
    border = jnp.pad(after(border, sent[0]), ((0, 0), (1, 1), (0, 0)))
    own_edge, other_edge = (
        lax.dynamic_slice_in_dim(border, s * half, half + 2, axis=1) for s in (side, 1 - side)
    )
    own_edge = lax.ppermute(own_edge, "cols", [(0, 1), (1, 0)])
    aslant = [
        (i * columns + c, (i ^ 1) * columns + 1 - c)
        for i in range(devices)
        for c in range(columns)
    ]
    other_edge = lax.ppermute(other_edge, ("tm", "cols"), aslant)

    def edge_rows(edge, begin, end):
        cut = jnp.pad(edge[:, begin:end], ((0, 0), (0, -(end - begin) % width), (0, 0)))
        return cut.reshape(frames, -1, width, channels)

    owners = levels if direct else 1
    edges = [[edge_rows(e, begin, end) for e in (own_edge, other_edge)] for begin, end in spans]
    lasts, firsts, halos = [], [], []
    newest = w_space
    for k, (begin, end) in enumerate(spans):
        span = (begin, end, half, scalars, video)
        arrived = after(received[2 * k], newest)
        last = join(join_last_kernel, taps, "join_last", *span, arrived, *edges[k])
        lasts.append(last)
        halos.append(tm_permute(last, lambda i: (i + pair) % devices))
        if k == 0:
            others = after(received[1], last)
            firsts.append(join(
                join_first_kernel, pair * frames - taps, "join_first", *span, arrived, others,
                *edges[k]
            ))
            part, spatial, *kept = early(
                scalars, firsts[0], last, chunks == 1, size, end - begin, *weights
            )
            newest = part

    spatials = []
    for k, (begin, end) in enumerate(spans):
        rows, final = end - begin, k == chunks - 1
        if k == 0:
            part = after(part, lasts[-1])
            made = late(
                owners, scalars, halos[k], firsts[0], part, spatial, final, rows, *weights
            )
            kept = [*made[owners:], *kept]
        else:
            span = (begin, end, half, scalars, video)
            others = after(received[2 * k + 1], spatials[-1][0])
            first = join(
                join_first_kernel, pair * frames - taps, "join_first", *span, received[2 * k],
                others, *edges[k]
            )
            made = full(
                owners, scalars, halos[k], first, lasts[k], kept, final, size, rows, *weights
            )
            kept = made[owners:]
        spatials.append(made[:owners])

    newest = spatials[-1][0]
    if direct:
        gathers = [
            [blocks[0]]
            + [tm_permute(blocks[j], lambda i: i ^ (pair * j)) for j in range(1, levels)]
            for blocks in spatials
        ]
        returns = []
        for gathered in gathers:
            gathered[0] = after(gathered[0], newest)
            results = attend(scalars, gathered, *attention)
            newest = results[0]
            returns.append(
                [results[0]]
                + [tm_permute(results[m], lambda i: i ^ m) for m in range(1, devices)]
            )
        whole = None
        for k, blocks in enumerate(returns):
            whole = collect(scalars, blocks, k, chunks, whole)
        return whole.reshape(frames // 2, height, width, channels)
    sets = [[pair * z + s for z in range(levels)] for s in range(pair)]
    returns = []
    for (block,) in spatials:
        gathered = lax.all_to_all(block, "tm", 1, 0, axis_index_groups=sets, tiled=True)
        (result,) = attend(scalars, [gathered], *attention)
        result = lax.all_to_all(result, "tm", 0, 1, tiled=True)
        result = result.reshape(frames // 2, levels, pair, each, channels)
        returns.append(result.transpose(0, 2, 1, 3, 4).reshape(frames // 2, pair, -1, channels))
    return jnp.concatenate(returns, axis=2).reshape(frames // 2, height, width, channels)


def solution(mesh):
    spread = P(("clips", "tm"), None, "cols", None)
    return jax.shard_map(
        per_device,
        mesh=mesh,
        in_specs=(spread,) + (P(),) * 11,
        out_specs=spread,
        check_vma=False,
    )
```

```python
from functools import partial

import jax
import jax.numpy as jnp
from jax import lax
from jax.experimental import pallas as pl
from jax.experimental.pallas import tpu as pltpu
from jax.sharding import PartitionSpec as P

epsilon = 1e-06
parts = 2
pair = 2
taps = 3
most_direct = 8
mebibyte = 1024 * 1024

VMEM = pl.BlockSpec(memory_space=pltpu.VMEM)
SMEM = pl.BlockSpec(memory_space=pltpu.SMEM)
ANY = pl.BlockSpec(memory_space=pl.ANY)


def silu(v):
    return 0.5 * v * (1.0 + jnp.tanh(0.5 * v))


def dot32(a, b):
    return jnp.dot(a, b, preferred_element_type=jnp.float32)


def cost(flops, *arrays):
    size = sum(a.size * a.dtype.itemsize for a in arrays)
    return pl.CostEstimate(flops=flops, bytes_accessed=size, transcendentals=0)


def params(mebibytes):
    return pltpu.CompilerParams(vmem_limit_bytes=mebibytes * mebibyte)


def rows_of(owner, begin, end, half, height):
    low, high = max(begin, 1), min(end, half + 1)
    pieces = [(owner * half + low - 1, low - begin, high - low)]
    if begin == 0:
        pieces.append((jnp.maximum(owner * half - 1, 0), 0, 1))
    if end == half + 2:
        pieces.append((jnp.minimum((owner + 1) * half, height - 1), end - 1 - begin, 1))
    return pieces


def run(copies):
    for copy in copies:
        copy.start()
    for copy in copies:
        copy.wait()


def cut(target, video, frame, owner, begin, end, half):
    for source, here, count in rows_of(owner, begin, end, half, video.shape[1]):
        target[here : here + count] = video[frame, pl.ds(source, count)]


def cuts(k, frames):
    first = frames - taps
    return ((first + 1, frames), (first, first + 1)) if k == 0 else ((first, frames),)


def frame_of(refs, pieces, t):
    for ref, (low, high) in zip(refs, pieces):
        if low <= t < high:
            return ref[t - low]


def send_kernel(spans, pieces, half, scalars, video, *outs):
    for out, (k, low, high) in zip(outs, pieces):
        begin, end = spans[k]
        for t in range(low, high):
            cut(out.at[t - low], video, t, 1 - scalars[0], begin, end, half)


def send(scalars, video, spans, pieces, half):
    width, channels = video.shape[2:]
    shapes = [
        (high - low, spans[k][1] - spans[k][0], width, channels) for k, low, high in pieces
    ]
    return pl.pallas_call(
        partial(send_kernel, spans, pieces, half),
        out_shape=[jax.ShapeDtypeStruct(shape, video.dtype) for shape in shapes],
        in_specs=[SMEM, VMEM],
        out_specs=[VMEM] * len(shapes),
        compiler_params=params(12),
        name="send",
    )(scalars, video)


def join_last_kernel(begin, end, half, pieces, scalars, video, received, own_edge, other_edge, out):
    rows = end - begin
    ((low, high),) = pieces

    @pl.when(scalars[0] == 0)
    def _():
        out[:, :rows] = received[...]
        out[:, rows:] = other_edge[low:high]

    @pl.when(scalars[0] == 1)
    def _():
        for t in range(low, high):
            cut(out.at[t - low], video, t, 1, begin, end, half)
        out[:, rows:] = own_edge[low:high]


def join_first_kernel(begin, end, half, pieces, scalars, video, *refs):
    received, others = refs[: len(pieces)], refs[len(pieces)]
    own_edge, other_edge, out = refs[-3:]
    frames, rows = video.shape[0], end - begin
    rest = frames - taps

    @pl.when(scalars[0] == 0)
    def _():
        for t in range(frames):
            cut(out.at[t], video, t, 0, begin, end, half)
        out[:frames, rows:] = own_edge[...]
        out[frames:, :rows] = others[...]
        out[frames:, rows:] = other_edge[:rest]

    @pl.when(scalars[0] == 1)
    def _():
        out[:rest, :rows] = others[...]
        for ref, (low, high) in zip(received, pieces):
            out[low:high, :rows] = ref[...]
        out[:frames, rows:] = other_edge[...]
        for t in range(rest):
            cut(out.at[frames + t], video, t, 1, begin, end, half)
        out[frames:, rows:] = own_edge[:rest]


def join(kernel, count, name, begin, end, half, pieces, scalars, video, *parts):
    width, channels = video.shape[2:]
    rows = end - begin + parts[-1].shape[1]
    return pl.pallas_call(
        partial(kernel, begin, end, half, pieces),
        out_shape=jax.ShapeDtypeStruct((count, rows, width, channels), jnp.bfloat16),
        in_specs=[SMEM] + [VMEM] * (1 + len(parts)),
        out_specs=VMEM,
        compiler_params=params(12),
        name=name,
    )(scalars, video, *parts)


def place_rows(buffers, index, top, reduced, rows, width, column):
    pixels, channels = rows * width, reduced.shape[-1]
    edges = reduced.shape[0] - pixels
    row_of = lax.broadcasted_iota(jnp.int32, (pixels, edges), 0) // width
    spread = (row_of == lax.broadcasted_iota(jnp.int32, (pixels, edges), 1)).astype(jnp.bfloat16)
    across = lax.broadcasted_iota(jnp.int32, (pixels, channels), 0) % width
    wide = reduced[:pixels].astype(jnp.float32)
    beside = dot32(spread, reduced[pixels:])
    before = jnp.where(column == 1, beside, 0.0)
    behind = jnp.where(column == 0, beside, 0.0)
    shifted = (
        jnp.where(across == 0, before, pltpu.roll(wide, 1, 0)),
        wide,
        jnp.where(across == width - 1, behind, pltpu.roll(wide, pixels - 1, 0)),
    )
    for b in range(3):
        value = shifted[b].astype(jnp.bfloat16).reshape(rows, width, channels)
        buffers[b, index, top : top + rows] = value


def convolve(buffers, fresh, last, side, kept, keeps, w_space, b_space):
    _, frames, rows, width, channels = buffers.shape
    size = rows - 2
    if fresh:

        @pl.when(side == 0)
        def _():
            buffers[:, :, :1] = jnp.zeros((3, frames, 1, width, channels), jnp.bfloat16)

    else:
        buffers[:, :, :2] = kept
    if last:

        @pl.when(side == pair - 1)
        def _():
            buffers[:, :, size + 1 :] = jnp.zeros((3, frames, 1, width, channels), jnp.bfloat16)

    else:
        keeps(buffers[:, :, size:])

    def window(b, a):
        return buffers[b, :, a : a + size].reshape(frames * size * width, channels)

    lhs = jnp.concatenate([window(b, a) for a in range(3) for b in range(3)], axis=1)
    acc = dot32(lhs, w_space[...].reshape(-1, channels)) + b_space[...]
    value = window(1, 1).astype(jnp.float32) + silu(acc)
    return value.astype(jnp.bfloat16).reshape(frames, size * width, channels)


def early_kernel(
    final, rows, pieces, scalars, first, *refs
):
    lasts, refs = refs[: len(pieces)], refs[len(pieces) :]
    w_time, b_time, w_down, b_down, w_space, b_space = refs[:6]
    refs = refs[6:]
    part, spatial = refs[:2]
    lifted, buffers = refs[-2:]
    keeps = None if final else (lambda value: refs[2].__setitem__(..., value))
    split, depth, width, channels = first.shape
    count = split + taps
    halves = count // 2
    pixels = depth * width

    def frame(t):
        return (first[t] if t < split else frame_of(lasts, pieces, t - halves)).reshape(pixels, channels)

    starts = list(range(taps - 1, count))
    for low in range(0, len(starts), 3):
        group = starts[low : low + 3]
        lhs = jnp.concatenate(
            [jnp.concatenate([frame(t - k) for t in group], axis=0) for k in range(taps)], axis=1
        )
        acc = dot32(lhs, w_time[...]) + b_time[...]
        held = jnp.concatenate([frame(t) for t in group], axis=0).astype(jnp.float32)
        value = (held + silu(acc)).astype(jnp.bfloat16)
        for g, t in enumerate(group):
            lifted[t] = value[g * pixels : (g + 1) * pixels]
    lhs = jnp.concatenate([lifted[3], lifted[2]], axis=1)
    part[...] = dot32(lhs, w_down[: 2 * channels]) + b_down[...]
    whole = range(2, halves)
    lhs = jnp.concatenate(
        [jnp.concatenate([lifted[2 * s + 1 - k] for s in whole], axis=0) for k in range(taps)],
        axis=1,
    )
    reduced = (dot32(lhs, w_down[...]) + b_down[...]).astype(jnp.bfloat16)
    for index in range(len(whole)):
        value = reduced[index * pixels : (index + 1) * pixels]
        place_rows(buffers, index, 0, value, rows, width, scalars[1])
    spatial[...] = convolve(buffers, True, final, scalars[0], None, keeps, w_space, b_space)


def early(scalars, first, lasts, pieces, final, size, rows, *weights):
    split, depth, width, channels = first.shape
    halves = (split + taps) // 2
    pixels = depth * width
    later = halves - 2
    shapes = [
        jax.ShapeDtypeStruct((pixels, channels), jnp.float32),
        jax.ShapeDtypeStruct((later, size * width, channels), jnp.bfloat16),
    ]
    if not final:
        shapes.append(jax.ShapeDtypeStruct((3, later, 2, width, channels), jnp.bfloat16))
    flops = 2 * channels * channels * (pixels * 26 + 9 * later * size * width)
    return pl.pallas_call(
        partial(early_kernel, final, rows, pieces),
        out_shape=shapes,
        in_specs=[SMEM] + [VMEM] * (1 + len(lasts) + len(weights)),
        out_specs=[VMEM] * len(shapes),
        scratch_shapes=[
            pltpu.VMEM((2 * halves, pixels, channels), jnp.bfloat16),
            pltpu.VMEM((3, later, size + 2, width, channels), jnp.bfloat16),
        ],
        compiler_params=params(24),
        cost_estimate=cost(flops, first, *lasts, *weights),
        name="early",
    )(scalars, first, *lasts, *weights)


def full_kernel(
    owners, final, rows, pieces, scalars, halo, first, last, kept_late, kept_early, w_time, b_time,
    w_down, b_down, w_space, b_space, *refs
):
    outs = refs[:owners]
    keeps = None if final else refs[owners : owners + 2]
    lifted, buffers = refs[-2:]
    split, depth, width, channels = first.shape
    count = split + taps
    halves = count // 2
    pixels = depth * width

    def frame(t):
        if t < 0:
            value = frame_of([halo], pieces, halves + t).reshape(pixels, channels)
            return jnp.where(scalars[2] > 0, value, jnp.zeros_like(value))
        return (first[t] if t < split else frame_of([last], pieces, t - halves)).reshape(pixels, channels)

    starts = list(range(-1, count))
    for low in range(0, len(starts), 3):
        group = starts[low : low + 3]
        lhs = jnp.concatenate(
            [jnp.concatenate([frame(t - k) for t in group], axis=0) for k in range(taps)], axis=1
        )
        acc = dot32(lhs, w_time[...]) + b_time[...]
        held = jnp.concatenate([frame(t) for t in group], axis=0).astype(jnp.float32)
        value = held + silu(acc)
        for g, t in enumerate(group):
            piece = value[g * pixels : (g + 1) * pixels]
            if t < 0:
                piece = jnp.where(scalars[2] > 0, piece, 0.0)
            lifted[t + 1] = piece.astype(jnp.bfloat16)
    lhs = jnp.concatenate(
        [
            jnp.concatenate([lifted[2 * s + 2 - k] for s in range(halves)], axis=0)
            for k in range(taps)
        ],
        axis=1,
    )
    reduced = (dot32(lhs, w_down[...]) + b_down[...]).astype(jnp.bfloat16)
    for index in range(halves):
        value = reduced[index * pixels : (index + 1) * pixels]
        place_rows(buffers, index, 2, value, rows, width, scalars[1])
    kept = jnp.concatenate([kept_late[...], kept_early[...]], axis=1)
    keep = None if final else (lambda value: keep_both(keeps, value))
    result = convolve(buffers, False, final, scalars[0], kept, keep, w_space, b_space)
    each = result.shape[1] // owners
    if owners == 1:
        outs[0][...] = result
    else:
        for j in range(owners):
            part = result[:, j * each : (j + 1) * each]
            for m in range(owners):

                @pl.when((scalars[2] ^ m) == j)
                def _():
                    outs[m][...] = part


def keep_both(keeps, value):
    keeps[0][...] = value[:, :2]
    keeps[1][...] = value[:, 2:]


def full(owners, scalars, halo, first, last, pieces, kept, final, size, rows, *weights):
    split, depth, width, channels = first.shape
    halves = (split + taps) // 2
    pixels = depth * width
    shapes = [(halves, size * width // owners, channels)] * owners
    if not final:
        shapes += [(3, count, 2, width, channels) for count in (2, halves - 2)]
    flops = 2 * channels * channels * (pixels * 39 + 9 * halves * size * width)
    return pl.pallas_call(
        partial(full_kernel, owners, final, rows, pieces),
        out_shape=[jax.ShapeDtypeStruct(shape, jnp.bfloat16) for shape in shapes],
        in_specs=[SMEM] + [VMEM] * (5 + len(weights)),
        out_specs=[VMEM] * len(shapes),
        scratch_shapes=[
            pltpu.VMEM((2 * halves + 1, pixels, channels), jnp.bfloat16),
            pltpu.VMEM((3, halves, size + 2, width, channels), jnp.bfloat16),
        ],
        compiler_params=params(28),
        cost_estimate=cost(flops, halo, first, last, *weights),
        name="full",
    )(scalars, halo, first, last, *kept, *weights)


def late_kernel(
    owners, final, rows, pieces, scalars, *refs
):
    halos, refs = refs[: len(pieces)], refs[len(pieces) :]
    first, part, spatial, w_time, b_time, w_down, b_down, w_space, b_space = refs[:9]
    refs = refs[9:]
    outs = refs[:owners]
    keeps = None if final else (lambda value: refs[owners].__setitem__(..., value))
    lifted, buffers, result = refs[-3:]
    _, depth, width, channels = first.shape
    pixels = depth * width

    def frame(t):
        if t < 0:
            value = frame_of(halos, pieces, result.shape[0] + t).reshape(pixels, channels)
            return jnp.where(scalars[2] > 0, value, jnp.zeros_like(value))
        return first[t].reshape(pixels, channels)

    group = range(-1, taps - 1)
    lhs = jnp.concatenate(
        [jnp.concatenate([frame(t - k) for t in group], axis=0) for k in range(taps)], axis=1
    )
    acc = dot32(lhs, w_time[...]) + b_time[...]
    held = jnp.concatenate([frame(t) for t in group], axis=0).astype(jnp.float32)
    value = held + silu(acc)
    for index in range(taps):
        piece = value[index * pixels : (index + 1) * pixels]
        if index == 0:
            piece = jnp.where(scalars[2] > 0, piece, 0.0)
        lifted[index] = piece.astype(jnp.bfloat16)
    lhs = jnp.concatenate([lifted[2], lifted[1], lifted[0]], axis=1)
    reduced = (
        dot32(lhs, w_down[...]) + b_down[...],
        dot32(lifted[2], w_down[2 * channels :]) + part[...],
    )
    for index, value in enumerate(reduced):
        value = value.astype(jnp.bfloat16)
        place_rows(buffers, index, 0, value, rows, width, scalars[1])
    result[:2] = convolve(buffers, True, final, scalars[0], None, keeps, w_space, b_space)
    result[2:] = spatial[...]
    each = result.shape[1] // owners
    if owners == 1:
        outs[0][...] = result[...]
    else:
        for j, out in enumerate(outs):
            begin = pl.multiple_of((scalars[2] ^ j) * each, each)
            out[...] = result[:, pl.ds(begin, each)]


def late(owners, scalars, halos, pieces, first, part, spatial, final, rows, *weights):
    _, depth, width, channels = first.shape
    later, pixels = spatial.shape[:2]
    halves = later + 2
    size = pixels // width
    shapes = [(halves, pixels // owners, channels)] * owners
    if not final:
        shapes.append((3, 2, 2, width, channels))
    flops = 2 * channels * channels * (depth * width * 13 + 18 * pixels)
    return pl.pallas_call(
        partial(late_kernel, owners, final, rows, pieces),
        out_shape=[jax.ShapeDtypeStruct(shape, jnp.bfloat16) for shape in shapes],
        in_specs=[SMEM] + [VMEM] * (3 + len(halos) + len(weights)),
        out_specs=[VMEM] * len(shapes),
        scratch_shapes=[
            pltpu.VMEM((taps, depth * width, channels), jnp.bfloat16),
            pltpu.VMEM((3, 2, size + 2, width, channels), jnp.bfloat16),
            pltpu.VMEM((halves, pixels, channels), jnp.bfloat16),
        ],
        compiler_params=params(24),
        cost_estimate=cost(flops, *halos, first, part, *weights),
        name="late",
    )(scalars, *halos, first, part, spatial, *weights)


def attend_kernel(frames_per, lanes, count, scalars, *refs):
    blocks = refs[:count]
    gain, w_query, w_key, w_value, w_out = refs[count : count + 5]
    outs = refs[count + 5 :]
    channels = gain.shape[-1]
    flat = len(blocks[0].shape) == 2
    groups = 1 if flat else blocks[0].shape[1] // lanes
    each = frames_per * lanes
    size = count * each

    def piece(j, g):
        if flat:
            return blocks[0][...]
        return blocks[j][:, g * lanes : (g + 1) * lanes].reshape(each, channels)

    def place(index):
        block = index // each
        time = index // lanes % frames_per
        for j in range(count):
            level = 0 if flat else scalars[2] ^ j
            time = time + jnp.where(block == j, level * frames_per, 0)
        return time, index % lanes

    row_time, row_lane = place(lax.broadcasted_iota(jnp.int32, (size, 1), 0))
    col_time, col_lane = place(lax.broadcasted_iota(jnp.int32, (1, size), 1))
    allowed = (row_lane == col_lane) & (col_time <= row_time)
    x = jnp.concatenate([piece(j, g) for g in range(groups) for j in range(count)], axis=0)
    wide = x.astype(jnp.float32)
    scale = lax.rsqrt(jnp.mean(wide * wide, axis=-1, keepdims=True) + epsilon)
    normed = (wide * scale * gain[...]).astype(jnp.bfloat16)
    query = dot32(normed, w_query[...]).astype(jnp.bfloat16)
    key = dot32(normed, w_key[...]).astype(jnp.bfloat16)
    value = dot32(normed, w_value[...]).astype(jnp.bfloat16)
    contexts = []
    for g in range(groups):
        part = slice(g * size, (g + 1) * size)
        scores = lax.dot_general(
            query[part], key[part], (((1,), (1,)), ((), ())), preferred_element_type=jnp.float32
        )
        scores = jnp.where(allowed, scores * channels ** (-0.5), -1e30)
        largest = jnp.max(scores, axis=-1, keepdims=True)
        probs = jnp.exp(scores - largest)
        probs = (probs / jnp.sum(probs, axis=-1, keepdims=True)).astype(jnp.bfloat16)
        contexts.append(dot32(probs, value[part]).astype(jnp.bfloat16))
    mixed = dot32(jnp.concatenate(contexts, axis=0), w_out[...])
    result = (wide + mixed).astype(jnp.bfloat16)
    if flat:
        outs[0][...] = result
        return
    short = frames_per // pair
    for g in range(groups):
        for j in range(count):
            begin = g * size + j * each
            rows = result[begin : begin + each].reshape(pair, short, lanes, channels)
            for side in range(pair):

                @pl.when(scalars[0] == side)
                def _():
                    for x in range(pair):
                        outs[pair * j + x][:, g * lanes : (g + 1) * lanes] = rows[side ^ x]


def attend(scalars, blocks, gain, w_query, w_key, w_value, w_out):
    frames_per, pixels, channels = blocks[0].shape
    flat = pixels % 16 != 0
    lanes = pixels if flat else 16
    if flat:
        blocks = [b.reshape(frames_per * pixels, channels) for b in blocks]
    count = len(blocks)
    size = frames_per * count * lanes
    shapes = [(frames_per // pair, pixels, channels)] * (pair * count)
    if flat:
        shapes = [blocks[0].shape]
    flops = 2 * frames_per * pixels * count * channels * (4 * channels + 2 * size)
    outs = pl.pallas_call(
        partial(attend_kernel, frames_per, lanes, count),
        out_shape=[jax.ShapeDtypeStruct(shape, jnp.bfloat16) for shape in shapes],
        in_specs=[SMEM] + [VMEM] * (count + 5),
        out_specs=[VMEM] * len(shapes),
        compiler_params=params(20 if 16 * size * size < 20 * mebibyte else 56),
        cost_estimate=cost(flops, *blocks, w_query, w_key, w_value, w_out),
        name="attend",
    )(scalars, *blocks, gain, w_query, w_key, w_value, w_out)
    return [o.reshape(frames_per, pixels, channels) for o in outs] if flat else outs


def collect_kernel(base, stride, scalars, *refs):
    out, sems = refs[-2:]
    copies = []
    for m in range(sems.shape[0]):
        index = base + (scalars[0] ^ m % pair) * stride + (scalars[2] ^ m // pair)
        copies.append(pltpu.make_async_copy(refs[m], out.at[:, index], sems.at[m]))
    run(copies)


def collect(scalars, blocks, chunk, chunks, whole):
    count = len(blocks)
    halves, pixels, channels = blocks[0].shape
    levels = count // pair
    given = [] if whole is None else [whole]
    return pl.pallas_call(
        partial(collect_kernel, chunk * levels, chunks * levels),
        out_shape=jax.ShapeDtypeStruct((halves, chunks * count, pixels, channels), jnp.bfloat16),
        in_specs=[SMEM] + [ANY] * (count + len(given)),
        out_specs=ANY,
        input_output_aliases={count + 1: 0} if given else {},
        scratch_shapes=[pltpu.SemaphoreType.DMA((count,))],
        compiler_params=params(16),
        name="collect",
    )(scalars, *blocks, *given)


def after(value, other):
    return lax.optimization_barrier((value, other))[0]


def per_device(
    video, w_time, b_time, w_down, b_down, w_space, b_space, gain, w_query, w_key, w_value, w_out
):
    frames, height, width, channels = video.shape
    devices = lax.axis_size("tm")
    levels = devices // pair
    columns = lax.axis_size("cols")
    assert columns == 2 and devices % pair == 0 and height % pair == 0 and frames >= taps
    place = lax.axis_index("tm").astype(jnp.int32)
    column = lax.axis_index("cols").astype(jnp.int32)
    side, level = place % pair, place // pair
    scalars = jnp.stack([side, column, level])
    half = height // pair
    gain = gain.reshape(1, -1)
    w_space = jnp.where(after(place, video) >= 0, w_space, 0)
    weights = [
        w_time.reshape(-1, channels), b_time.reshape(1, -1), w_down.reshape(-1, channels),
        b_down.reshape(1, -1), w_space, b_space.reshape(1, -1),
    ]
    attention = [gain, w_query, w_key, w_value, w_out]
    chunks = parts if half % parts == 0 and half // parts * width % levels == 0 else 1
    size = half // chunks
    each = size * width // levels
    direct = devices <= most_direct and levels & (levels - 1) == 0 and each % 16 == 0
    spans = [
        (k * size + (2 if k else 0), (k + 1) * size + 2) for k in range(chunks)
    ]

    def tm_permute(value, move):
        return lax.ppermute(value, "tm", [(i, move(i)) for i in range(devices) if move(i) < devices])

    rest = frames - taps
    pieces = [(k, low, high) for k in range(chunks) for low, high in cuts(k, frames)]
    pieces += [(k, 0, rest) for k in range(chunks)]
    sent = send(scalars, video, spans, pieces, half)
    received = {}
    for key, value in zip(pieces, sent):
        if key[2] == rest and key[1] == 0:
            value = after(value, received[(key[0],) + cuts(key[0], frames)[0]])
        received[key] = tm_permute(value, lambda i: i ^ 1)
    border = jnp.where(column == 0, video[:, :, -1], video[:, :, 0])
    border = jnp.pad(after(border, sent[0]), ((0, 0), (1, 1), (0, 0)))
    own_edge, other_edge = (
        lax.dynamic_slice_in_dim(border, s * half, half + 2, axis=1) for s in (side, 1 - side)
    )
    own_edge = lax.ppermute(own_edge, "cols", [(0, 1), (1, 0)])
    aslant = [
        (i * columns + c, (i ^ 1) * columns + 1 - c)
        for i in range(devices)
        for c in range(columns)
    ]
    other_edge = lax.ppermute(other_edge, ("tm", "cols"), aslant)

    def edge_rows(edge, begin, end):
        cut = jnp.pad(edge[:, begin:end], ((0, 0), (0, -(end - begin) % width), (0, 0)))
        return cut.reshape(frames, -1, width, channels)

    owners = levels if direct else 1
    edges = [[edge_rows(e, begin, end) for e in (own_edge, other_edge)] for begin, end in spans]
    lasts, halos = {}, {}
    newest = w_space
    for k, low, high in pieces[: len(pieces) - chunks]:
        begin, end = spans[k]
        newest = join(
            join_last_kernel, high - low, "join_last", begin, end, half, ((low, high),), scalars,
            video, after(received[k, low, high], newest), *edges[k]
        )
        lasts[k, low, high] = newest
        halos[k, low, high] = tm_permute(newest, lambda i: (i + pair) % devices)

    spatials = []
    kept = None
    for k, (begin, end) in enumerate(spans):
        rows, final = end - begin, k == chunks - 1
        ranges = cuts(k, frames)
        keys = [(k,) + piece for piece in ranges]
        first = join(
            join_first_kernel, pair * frames - taps, "join_first", begin, end, half, ranges, scalars,
            video, *[received[key] for key in keys], after(received[k, 0, rest], newest), *edges[k]
        )
        if k == 0:
            part, spatial, *kept = early(
                scalars, first, [lasts[key] for key in keys], ranges, final, size, rows, *weights
            )
            made = late(
                owners, scalars, [halos[key] for key in keys], ranges, first, part, spatial, final,
                rows, *weights
            )
            kept = [*made[owners:], *kept]
        else:
            (key,) = keys
            made = full(
                owners, scalars, halos[key], first, lasts[key], ranges, kept, final, size, rows,
                *weights
            )
            kept = made[owners:]
        spatials.append(made[:owners])
        newest = made[0]

    newest = spatials[-1][0]
    if direct:
        gathers = [
            [blocks[0]]
            + [tm_permute(blocks[j], lambda i: i ^ (pair * j)) for j in range(1, levels)]
            for blocks in spatials
        ]
        returns = []
        for gathered in gathers:
            gathered[0] = after(gathered[0], newest)
            results = attend(scalars, gathered, *attention)
            newest = results[0]
            returns.append(
                [results[0]]
                + [tm_permute(results[m], lambda i: i ^ m) for m in range(1, devices)]
            )
        whole = None
        for k, blocks in enumerate(returns):
            whole = collect(scalars, blocks, k, chunks, whole)
        return whole.reshape(frames // 2, height, width, channels)
    sets = [[pair * z + s for z in range(levels)] for s in range(pair)]
    returns = []
    for (block,) in spatials:
        gathered = lax.all_to_all(block, "tm", 1, 0, axis_index_groups=sets, tiled=True)
        (result,) = attend(scalars, [gathered], *attention)
        result = lax.all_to_all(result, "tm", 0, 1, tiled=True)
        result = result.reshape(frames // 2, levels, pair, each, channels)
        returns.append(result.transpose(0, 2, 1, 3, 4).reshape(frames // 2, pair, -1, channels))
    return jnp.concatenate(returns, axis=2).reshape(frames // 2, height, width, channels)


def solution(mesh):
    spread = P(("clips", "tm"), None, "cols", None)
    return jax.shard_map(
        per_device,
        mesh=mesh,
        in_specs=(spread,) + (P(),) * 11,
        out_specs=spread,
        check_vma=False,
    )
```

```python
from functools import partial

import jax
import jax.numpy as jnp
from jax import lax
from jax.experimental import pallas as pl
from jax.experimental.pallas import tpu as pltpu
from jax.sharding import PartitionSpec as P

epsilon = 1e-06
parts = 2
pair = 2
taps = 3
most_direct = 8
mebibyte = 1024 * 1024

VMEM = pl.BlockSpec(memory_space=pltpu.VMEM)
SMEM = pl.BlockSpec(memory_space=pltpu.SMEM)
ANY = pl.BlockSpec(memory_space=pl.ANY)


def silu(v):
    return 0.5 * v * (1.0 + jnp.tanh(0.5 * v))


def dot32(a, b):
    return jnp.dot(a, b, preferred_element_type=jnp.float32)


def cost(flops, *arrays):
    size = sum(a.size * a.dtype.itemsize for a in arrays)
    return pl.CostEstimate(flops=flops, bytes_accessed=size, transcendentals=0)


def params(mebibytes):
    return pltpu.CompilerParams(vmem_limit_bytes=mebibytes * mebibyte)


def rows_of(owner, begin, end, half, height):
    low, high = max(begin, 1), min(end, half + 1)
    pieces = [(owner * half + low - 1, low - begin, high - low)]
    if begin == 0:
        pieces.append((jnp.maximum(owner * half - 1, 0), 0, 1))
    if end == half + 2:
        pieces.append((jnp.minimum((owner + 1) * half, height - 1), end - 1 - begin, 1))
    return pieces


def run(copies):
    for copy in copies:
        copy.start()
    for copy in copies:
        copy.wait()


def cut(target, video, frame, owner, begin, end, half):
    for source, here, count in rows_of(owner, begin, end, half, video.shape[1]):
        target[here : here + count] = video[frame, pl.ds(source, count)]


def send_kernel(spans, half, scalars, video, *outs):
    frames = video.shape[0]
    rest = frames - taps
    for k, (begin, end) in enumerate(spans):
        for t in range(frames):
            target = outs[2 * k].at[t - rest] if t >= rest else outs[2 * k + 1].at[t]
            cut(target, video, t, 1 - scalars[0], begin, end, half)


def send(scalars, video, spans, half):
    frames, _, width, channels = video.shape
    shapes = [
        (count, end - begin, width, channels)
        for begin, end in spans
        for count in (taps, frames - taps)
    ]
    return pl.pallas_call(
        partial(send_kernel, spans, half),
        out_shape=[jax.ShapeDtypeStruct(shape, video.dtype) for shape in shapes],
        in_specs=[SMEM, VMEM],
        out_specs=[VMEM] * len(shapes),
        compiler_params=params(12),
        name="send",
    )(scalars, video)


def join_last_kernel(begin, end, half, scalars, video, received, own_edge, other_edge, out):
    frames, rows = video.shape[0], end - begin

    @pl.when(scalars[0] == 0)
    def _():
        out[:, :rows] = received[...]
        out[:, rows:] = other_edge[frames - taps :]

    @pl.when(scalars[0] == 1)
    def _():
        for t in range(taps):
            cut(out.at[t], video, frames - taps + t, 1, begin, end, half)
        out[:, rows:] = own_edge[frames - taps :]


def join_first_kernel(
    begin, end, half, scalars, video, received, others, own_edge, other_edge, out
):
    frames, rows = video.shape[0], end - begin
    rest = frames - taps

    @pl.when(scalars[0] == 0)
    def _():
        for t in range(frames):
            cut(out.at[t], video, t, 0, begin, end, half)
        out[:frames, rows:] = own_edge[...]
        out[frames:, :rows] = others[...]
        out[frames:, rows:] = other_edge[:rest]

    @pl.when(scalars[0] == 1)
    def _():
        out[:rest, :rows] = others[...]
        out[rest:frames, :rows] = received[...]
        out[:frames, rows:] = other_edge[...]
        for t in range(rest):
            cut(out.at[frames + t], video, t, 1, begin, end, half)
        out[frames:, rows:] = own_edge[:rest]


def join(kernel, count, name, begin, end, half, scalars, video, *parts):
    _, _, width, channels = video.shape
    rows = end - begin + parts[-1].shape[1]
    return pl.pallas_call(
        partial(kernel, begin, end, half),
        out_shape=jax.ShapeDtypeStruct((count, rows, width, channels), jnp.bfloat16),
        in_specs=[SMEM] + [VMEM] * (1 + len(parts)),
        out_specs=VMEM,
        compiler_params=params(12),
        name=name,
    )(scalars, video, *parts)


def place_rows(buffers, index, top, reduced, rows, width, column):
    pixels, channels = rows * width, reduced.shape[-1]
    edges = reduced.shape[0] - pixels
    row_of = lax.broadcasted_iota(jnp.int32, (pixels, edges), 0) // width
    spread = (row_of == lax.broadcasted_iota(jnp.int32, (pixels, edges), 1)).astype(jnp.bfloat16)
    across = lax.broadcasted_iota(jnp.int32, (pixels, channels), 0) % width
    wide = reduced[:pixels].astype(jnp.float32)
    beside = dot32(spread, reduced[pixels:])
    before = jnp.where(column == 1, beside, 0.0)
    behind = jnp.where(column == 0, beside, 0.0)
    shifted = (
        jnp.where(across == 0, before, pltpu.roll(wide, 1, 0)),
        wide,
        jnp.where(across == width - 1, behind, pltpu.roll(wide, pixels - 1, 0)),
    )
    for b in range(3):
        value = shifted[b].astype(jnp.bfloat16).reshape(rows, width, channels)
        buffers[b, index, top : top + rows] = value


def convolve(buffers, fresh, last, side, kept, keeps, w_space, b_space):
    _, frames, rows, width, channels = buffers.shape
    size = rows - 2
    if fresh:

        @pl.when(side == 0)
        def _():
            buffers[:, :, :1] = jnp.zeros((3, frames, 1, width, channels), jnp.bfloat16)

    else:
        buffers[:, :, :2] = kept
    if last:

        @pl.when(side == pair - 1)
        def _():
            buffers[:, :, size + 1 :] = jnp.zeros((3, frames, 1, width, channels), jnp.bfloat16)

    else:
        keeps(buffers[:, :, size:])

    def window(b, a):
        return buffers[b, :, a : a + size].reshape(frames * size * width, channels)

    lhs = jnp.concatenate([window(b, a) for a in range(3) for b in range(3)], axis=1)
    acc = dot32(lhs, w_space[...].reshape(-1, channels)) + b_space[...]
    value = window(1, 1).astype(jnp.float32) + silu(acc)
    return value.astype(jnp.bfloat16).reshape(frames, size * width, channels)


def early_kernel(
    final, rows, scalars, first, last, w_time, b_time, w_down, b_down, w_space, b_space, *refs
):
    part, spatial = refs[:2]
    lifted, buffers = refs[-2:]
    keeps = None if final else (lambda value: refs[2].__setitem__(..., value))
    split, depth, width, channels = first.shape
    count = split + taps
    halves = count // 2
    pixels = depth * width

    def frame(t):
        return (first[t] if t < split else last[t - split]).reshape(pixels, channels)

    starts = list(range(taps - 1, count))
    for low in range(0, len(starts), 3):
        group = starts[low : low + 3]
        lhs = jnp.concatenate(
            [jnp.concatenate([frame(t - k) for t in group], axis=0) for k in range(taps)], axis=1
        )
        acc = dot32(lhs, w_time[...]) + b_time[...]
        held = jnp.concatenate([frame(t) for t in group], axis=0).astype(jnp.float32)
        value = (held + silu(acc)).astype(jnp.bfloat16)
        for g, t in enumerate(group):
            lifted[t] = value[g * pixels : (g + 1) * pixels]
    lhs = jnp.concatenate([lifted[3], lifted[2]], axis=1)
    part[...] = dot32(lhs, w_down[: 2 * channels]) + b_down[...]
    whole = range(2, halves)
    lhs = jnp.concatenate(
        [jnp.concatenate([lifted[2 * s + 1 - k] for s in whole], axis=0) for k in range(taps)],
        axis=1,
    )
    reduced = (dot32(lhs, w_down[...]) + b_down[...]).astype(jnp.bfloat16)
    for index in range(len(whole)):
        value = reduced[index * pixels : (index + 1) * pixels]
        place_rows(buffers, index, 0, value, rows, width, scalars[1])
    spatial[...] = convolve(buffers, True, final, scalars[0], None, keeps, w_space, b_space)


def early(scalars, first, last, final, size, rows, *weights):
    split, depth, width, channels = first.shape
    halves = (split + taps) // 2
    pixels = depth * width
    later = halves - 2
    shapes = [
        jax.ShapeDtypeStruct((pixels, channels), jnp.float32),
        jax.ShapeDtypeStruct((later, size * width, channels), jnp.bfloat16),
    ]
    if not final:
        shapes.append(jax.ShapeDtypeStruct((3, later, 2, width, channels), jnp.bfloat16))
    flops = 2 * channels * channels * (pixels * 26 + 9 * later * size * width)
    return pl.pallas_call(
        partial(early_kernel, final, rows),
        out_shape=shapes,
        in_specs=[SMEM] + [VMEM] * (2 + len(weights)),
        out_specs=[VMEM] * len(shapes),
        scratch_shapes=[
            pltpu.VMEM((2 * halves, pixels, channels), jnp.bfloat16),
            pltpu.VMEM((3, later, size + 2, width, channels), jnp.bfloat16),
        ],
        compiler_params=params(24),
        cost_estimate=cost(flops, first, last, *weights),
        name="early",
    )(scalars, first, last, *weights)


def full_kernel(
    owners, final, rows, scalars, halo, first, last, kept_late, kept_early, w_time, b_time, w_down,
    b_down, w_space, b_space, *refs
):
    outs = refs[:owners]
    keeps = None if final else refs[owners : owners + 2]
    lifted, buffers = refs[-2:]
    split, depth, width, channels = first.shape
    count = split + taps
    halves = count // 2
    pixels = depth * width

    def frame(t):
        if t < 0:
            value = halo[t + taps].reshape(pixels, channels)
            return jnp.where(scalars[2] > 0, value, jnp.zeros_like(value))
        return (first[t] if t < split else last[t - split]).reshape(pixels, channels)

    starts = list(range(-1, count))
    for low in range(0, len(starts), 3):
        group = starts[low : low + 3]
        lhs = jnp.concatenate(
            [jnp.concatenate([frame(t - k) for t in group], axis=0) for k in range(taps)], axis=1
        )
        acc = dot32(lhs, w_time[...]) + b_time[...]
        held = jnp.concatenate([frame(t) for t in group], axis=0).astype(jnp.float32)
        value = held + silu(acc)
        for g, t in enumerate(group):
            piece = value[g * pixels : (g + 1) * pixels]
            if t < 0:
                piece = jnp.where(scalars[2] > 0, piece, 0.0)
            lifted[t + 1] = piece.astype(jnp.bfloat16)
    lhs = jnp.concatenate(
        [
            jnp.concatenate([lifted[2 * s + 2 - k] for s in range(halves)], axis=0)
            for k in range(taps)
        ],
        axis=1,
    )
    reduced = (dot32(lhs, w_down[...]) + b_down[...]).astype(jnp.bfloat16)
    for index in range(halves):
        value = reduced[index * pixels : (index + 1) * pixels]
        place_rows(buffers, index, 2, value, rows, width, scalars[1])
    kept = jnp.concatenate([kept_late[...], kept_early[...]], axis=1)
    keep = None if final else (lambda value: keep_both(keeps, value))
    result = convolve(buffers, False, final, scalars[0], kept, keep, w_space, b_space)
    each = result.shape[1] // owners
    if owners == 1:
        outs[0][...] = result
    else:
        for j in range(owners):
            part = result[:, j * each : (j + 1) * each]
            for m in range(owners):

                @pl.when((scalars[2] ^ m) == j)
                def _():
                    outs[m][...] = part


def keep_both(keeps, value):
    keeps[0][...] = value[:, :2]
    keeps[1][...] = value[:, 2:]


def full(owners, scalars, halo, first, last, kept, final, size, rows, *weights):
    split, depth, width, channels = first.shape
    halves = (split + taps) // 2
    pixels = depth * width
    shapes = [(halves, size * width // owners, channels)] * owners
    if not final:
        shapes += [(3, count, 2, width, channels) for count in (2, halves - 2)]
    flops = 2 * channels * channels * (pixels * 39 + 9 * halves * size * width)
    return pl.pallas_call(
        partial(full_kernel, owners, final, rows),
        out_shape=[jax.ShapeDtypeStruct(shape, jnp.bfloat16) for shape in shapes],
        in_specs=[SMEM] + [VMEM] * (5 + len(weights)),
        out_specs=[VMEM] * len(shapes),
        scratch_shapes=[
            pltpu.VMEM((2 * halves + 1, pixels, channels), jnp.bfloat16),
            pltpu.VMEM((3, halves, size + 2, width, channels), jnp.bfloat16),
        ],
        compiler_params=params(28),
        cost_estimate=cost(flops, halo, first, last, *weights),
        name="full",
    )(scalars, halo, first, last, *kept, *weights)


def late_kernel(
    owners, final, rows, scalars, halo, first, part, spatial, w_time, b_time, w_down, b_down,
    w_space, b_space, *refs
):
    outs = refs[:owners]
    keeps = None if final else (lambda value: refs[owners].__setitem__(..., value))
    lifted, buffers, result = refs[-3:]
    _, depth, width, channels = first.shape
    pixels = depth * width

    def frame(t):
        if t < 0:
            value = halo[t + taps].reshape(pixels, channels)
            return jnp.where(scalars[2] > 0, value, jnp.zeros_like(value))
        return first[t].reshape(pixels, channels)

    group = range(-1, taps - 1)
    lhs = jnp.concatenate(
        [jnp.concatenate([frame(t - k) for t in group], axis=0) for k in range(taps)], axis=1
    )
    acc = dot32(lhs, w_time[...]) + b_time[...]
    held = jnp.concatenate([frame(t) for t in group], axis=0).astype(jnp.float32)
    value = held + silu(acc)
    for index in range(taps):
        piece = value[index * pixels : (index + 1) * pixels]
        if index == 0:
            piece = jnp.where(scalars[2] > 0, piece, 0.0)
        lifted[index] = piece.astype(jnp.bfloat16)
    lhs = jnp.concatenate([lifted[2], lifted[1], lifted[0]], axis=1)
    reduced = (
        dot32(lhs, w_down[...]) + b_down[...],
        dot32(lifted[2], w_down[2 * channels :]) + part[...],
    )
    for index, value in enumerate(reduced):
        value = value.astype(jnp.bfloat16)
        place_rows(buffers, index, 0, value, rows, width, scalars[1])
    result[:2] = convolve(buffers, True, final, scalars[0], None, keeps, w_space, b_space)
    result[2:] = spatial[...]
    each = result.shape[1] // owners
    if owners == 1:
        outs[0][...] = result[...]
    else:
        for j, out in enumerate(outs):
            begin = pl.multiple_of((scalars[2] ^ j) * each, each)
            out[...] = result[:, pl.ds(begin, each)]


def late(owners, scalars, halo, first, part, spatial, final, rows, *weights):
    _, depth, width, channels = first.shape
    later, pixels = spatial.shape[:2]
    halves = later + 2
    size = pixels // width
    shapes = [(halves, pixels // owners, channels)] * owners
    if not final:
        shapes.append((3, 2, 2, width, channels))
    flops = 2 * channels * channels * (depth * width * 13 + 18 * pixels)
    return pl.pallas_call(
        partial(late_kernel, owners, final, rows),
        out_shape=[jax.ShapeDtypeStruct(shape, jnp.bfloat16) for shape in shapes],
        in_specs=[SMEM] + [VMEM] * (4 + len(weights)),
        out_specs=[VMEM] * len(shapes),
        scratch_shapes=[
            pltpu.VMEM((taps, depth * width, channels), jnp.bfloat16),
            pltpu.VMEM((3, 2, size + 2, width, channels), jnp.bfloat16),
            pltpu.VMEM((halves, pixels, channels), jnp.bfloat16),
        ],
        compiler_params=params(24),
        cost_estimate=cost(flops, halo, first, part, *weights),
        name="late",
    )(scalars, halo, first, part, spatial, *weights)


def attend_kernel(frames_per, lanes, count, near, chunks, scalars, *refs):
    blocks, refs = refs[:count], refs[count:]
    gain, w_query, w_key, w_value, w_out = refs[:5]
    waiting, outs = refs[5 : 5 + near * (chunks - 1)], refs[5 + near * (chunks - 1) :]
    for index, block in enumerate(waiting):
        outs[1 + index % near][index // near] = block[...]
    channels = gain.shape[-1]
    flat = len(blocks[0].shape) == 2
    groups = 1 if flat else blocks[0].shape[1] // lanes
    each = frames_per * lanes
    size = count * each

    def piece(j, g):
        if flat:
            return blocks[0][...]
        return blocks[j][:, g * lanes : (g + 1) * lanes].reshape(each, channels)

    def place(index):
        block = index // each
        time = index // lanes % frames_per
        for j in range(count):
            level = 0 if flat else scalars[2] ^ j
            time = time + jnp.where(block == j, level * frames_per, 0)
        return time, index % lanes

    row_time, row_lane = place(lax.broadcasted_iota(jnp.int32, (size, 1), 0))
    col_time, col_lane = place(lax.broadcasted_iota(jnp.int32, (1, size), 1))
    allowed = (row_lane == col_lane) & (col_time <= row_time)
    x = jnp.concatenate([piece(j, g) for g in range(groups) for j in range(count)], axis=0)
    wide = x.astype(jnp.float32)
    scale = lax.rsqrt(jnp.mean(wide * wide, axis=-1, keepdims=True) + epsilon)
    normed = (wide * scale * gain[...]).astype(jnp.bfloat16)
    query = dot32(normed, w_query[...]).astype(jnp.bfloat16)
    key = dot32(normed, w_key[...]).astype(jnp.bfloat16)
    value = dot32(normed, w_value[...]).astype(jnp.bfloat16)
    contexts = []
    for g in range(groups):
        part = slice(g * size, (g + 1) * size)
        scores = lax.dot_general(
            query[part], key[part], (((1,), (1,)), ((), ())), preferred_element_type=jnp.float32
        )
        scores = jnp.where(allowed, scores * channels ** (-0.5), -1e30)
        largest = jnp.max(scores, axis=-1, keepdims=True)
        probs = jnp.exp(scores - largest)
        probs = (probs / jnp.sum(probs, axis=-1, keepdims=True)).astype(jnp.bfloat16)
        contexts.append(dot32(probs, value[part]).astype(jnp.bfloat16))
    mixed = dot32(jnp.concatenate(contexts, axis=0), w_out[...])
    result = (wide + mixed).astype(jnp.bfloat16)
    if flat:
        outs[0][...] = result
        return
    short = frames_per // pair
    for g in range(groups):
        for j in range(count):
            begin = g * size + j * each
            rows = result[begin : begin + each].reshape(pair, short, lanes, channels)
            for side in range(pair):

                @pl.when(scalars[0] == side)
                def _():
                    part = slice(g * lanes, (g + 1) * lanes)
                    for x in range(pair):
                        m = pair * j + x
                        if 0 < m <= near:
                            outs[m][chunks - 1, :, part] = rows[side ^ x]
                        else:
                            outs[m][:, part] = rows[side ^ x]


def attend(scalars, blocks, near, waiting, gain, w_query, w_key, w_value, w_out):
    frames_per, pixels, channels = blocks[0].shape
    flat = pixels % 16 != 0
    lanes = pixels if flat else 16
    if flat:
        blocks = [b.reshape(frames_per * pixels, channels) for b in blocks]
    count = len(blocks)
    size = frames_per * count * lanes
    block = (frames_per // pair, pixels, channels)
    chunks = 1 + len(waiting) // near if near else 1
    shapes = [
        (chunks,) + block if 0 < m <= near else block for m in range(pair * count)
    ]
    if flat:
        shapes = [blocks[0].shape]
    flops = 2 * frames_per * pixels * count * channels * (4 * channels + 2 * size)
    outs = pl.pallas_call(
        partial(attend_kernel, frames_per, lanes, count, near, chunks),
        out_shape=[jax.ShapeDtypeStruct(shape, jnp.bfloat16) for shape in shapes],
        in_specs=[SMEM] + [VMEM] * (count + 5 + len(waiting)),
        out_specs=[VMEM] * len(shapes),
        compiler_params=params(20 if 16 * size * size < 20 * mebibyte else 56),
        cost_estimate=cost(flops, *blocks, w_query, w_key, w_value, w_out),
        name="attend",
    )(scalars, *blocks, gain, w_query, w_key, w_value, w_out, *waiting)
    return [o.reshape(frames_per, pixels, channels) for o in outs] if flat else outs


def collect_kernel(entries, levels, chunks, scalars, *refs):
    out, sems = refs[-2:]
    copies = []
    for index, (ref, sub, k, m) in enumerate(entries):
        block = refs[ref] if sub is None else refs[ref].at[sub]
        place = ((scalars[0] ^ m % pair) * chunks + k) * levels + (scalars[2] ^ m // pair)
        copies.append(pltpu.make_async_copy(block, out.at[:, place], sems.at[index]))
    run(copies)


def collect(scalars, blocks, entries, levels, chunks, whole):
    halves, pixels, channels = blocks[0].shape[-3:]
    given = [] if whole is None else [whole]
    shape = (halves, chunks * pair * levels, pixels, channels)
    return pl.pallas_call(
        partial(collect_kernel, entries, levels, chunks),
        out_shape=jax.ShapeDtypeStruct(shape, jnp.bfloat16),
        in_specs=[SMEM] + [ANY] * (len(blocks) + len(given)),
        out_specs=ANY,
        input_output_aliases={len(blocks) + 1: 0} if given else {},
        scratch_shapes=[pltpu.SemaphoreType.DMA((len(entries),))],
        compiler_params=params(16),
        name="collect",
    )(scalars, *blocks, *given)


def after(value, other):
    return lax.optimization_barrier((value, other))[0]


def per_device(
    video, w_time, b_time, w_down, b_down, w_space, b_space, gain, w_query, w_key, w_value, w_out
):
    frames, height, width, channels = video.shape
    devices = lax.axis_size("tm")
    levels = devices // pair
    columns = lax.axis_size("cols")
    assert columns == 2 and devices % pair == 0 and height % pair == 0 and frames >= taps
    place = lax.axis_index("tm").astype(jnp.int32)
    column = lax.axis_index("cols").astype(jnp.int32)
    side, level = place % pair, place // pair
    scalars = jnp.stack([side, column, level])
    half = height // pair
    gain = gain.reshape(1, -1)
    w_space = jnp.where(after(place, video) >= 0, w_space, 0)
    weights = [
        w_time.reshape(-1, channels), b_time.reshape(1, -1), w_down.reshape(-1, channels),
        b_down.reshape(1, -1), w_space, b_space.reshape(1, -1),
    ]
    attention = [gain, w_query, w_key, w_value, w_out]
    chunks = parts if half % parts == 0 and half // parts * width % levels == 0 else 1
    size = half // chunks
    each = size * width // levels
    direct = devices <= most_direct and levels & (levels - 1) == 0 and each % 16 == 0
    spans = [
        (k * size + (2 if k else 0), (k + 1) * size + 2) for k in range(chunks)
    ]

    def tm_permute(value, move):
        return lax.ppermute(value, "tm", [(i, move(i)) for i in range(devices) if move(i) < devices])

    sent = send(scalars, video, spans, half)
    received = [tm_permute(value, lambda i: i ^ 1) for value in sent]
    border = jnp.where(column == 0, video[:, :, -1], video[:, :, 0])
    border = jnp.pad(after(border, sent[0]), ((0, 0), (1, 1), (0, 0)))
    own_edge, other_edge = (
        lax.dynamic_slice_in_dim(border, s * half, half + 2, axis=1) for s in (side, 1 - side)
    )
    own_edge = lax.ppermute(own_edge, "cols", [(0, 1), (1, 0)])
    aslant = [
        (i * columns + c, (i ^ 1) * columns + 1 - c)
        for i in range(devices)
        for c in range(columns)
    ]
    other_edge = lax.ppermute(other_edge, ("tm", "cols"), aslant)

    def edge_rows(edge, begin, end):
        cut = jnp.pad(edge[:, begin:end], ((0, 0), (0, -(end - begin) % width), (0, 0)))
        return cut.reshape(frames, -1, width, channels)

    owners = levels if direct else 1
    edges = [[edge_rows(e, begin, end) for e in (own_edge, other_edge)] for begin, end in spans]
    lasts, firsts, halos = [], [], []
    newest = w_space
    for k, (begin, end) in enumerate(spans):
        span = (begin, end, half, scalars, video)
        arrived = after(received[2 * k], newest)
        last = join(join_last_kernel, taps, "join_last", *span, arrived, *edges[k])
        lasts.append(last)
        halos.append(tm_permute(last, lambda i: (i + pair) % devices))
        if k == 0:
            others = after(received[1], last)
            firsts.append(join(
                join_first_kernel, pair * frames - taps, "join_first", *span, arrived, others,
                *edges[k]
            ))
            part, spatial, *kept = early(
                scalars, firsts[0], last, chunks == 1, size, end - begin, *weights
            )
            newest = part

    spatials = []
    for k, (begin, end) in enumerate(spans):
        rows, final = end - begin, k == chunks - 1
        if k == 0:
            part = after(part, lasts[-1])
            made = late(
                owners, scalars, halos[k], firsts[0], part, spatial, final, rows, *weights
            )
            kept = [*made[owners:], *kept]
        else:
            span = (begin, end, half, scalars, video)
            others = after(received[2 * k + 1], spatials[-1][0])
            first = join(
                join_first_kernel, pair * frames - taps, "join_first", *span, received[2 * k],
                others, *edges[k]
            )
            made = full(
                owners, scalars, halos[k], first, lasts[k], kept, final, size, rows, *weights
            )
            kept = made[owners:]
        spatials.append(made[:owners])

    newest = spatials[-1][0]
    if direct:
        gathers = [
            [blocks[0]]
            + [tm_permute(blocks[j], lambda i: i ^ (pair * j)) for j in range(1, levels)]
            for blocks in spatials
        ]
        far = devices // 2
        near = far - 1
        whole, waiting = None, []
        for k, gathered in enumerate(gathers):
            gathered[0] = after(gathered[0], newest)
            final = k == chunks - 1
            results = attend(
                scalars, gathered, near if final else 0, waiting if final else [], *attention
            )
            newest = results[0]
            blocks = [tm_permute(results[m], lambda i: i ^ m) for m in range(far, devices)]
            entries = [(m - far, None, k, m) for m in range(far, devices)]
            if final:
                for m in range(1, far):
                    entries += [(len(blocks), c, c, m) for c in range(chunks)]
                    blocks.append(tm_permute(results[m], lambda i: i ^ m))
            else:
                waiting += results[1:far]
            entries.append((len(blocks), None, k, 0))
            blocks.append(results[0])
            whole = collect(scalars, blocks, entries, levels, chunks, whole)
        return whole.reshape(frames // 2, height, width, channels)
    sets = [[pair * z + s for z in range(levels)] for s in range(pair)]
    returns = []
    for (block,) in spatials:
        gathered = lax.all_to_all(block, "tm", 1, 0, axis_index_groups=sets, tiled=True)
        (result,) = attend(scalars, [gathered], 0, [], *attention)
        result = lax.all_to_all(result, "tm", 0, 1, tiled=True)
        result = result.reshape(frames // 2, levels, pair, each, channels)
        returns.append(result.transpose(0, 2, 1, 3, 4).reshape(frames // 2, pair, -1, channels))
    return jnp.concatenate(returns, axis=2).reshape(frames // 2, height, width, channels)


def solution(mesh):
    spread = P(("clips", "tm"), None, "cols", None)
    return jax.shard_map(
        per_device,
        mesh=mesh,
        in_specs=(spread,) + (P(),) * 11,
        out_specs=spread,
        check_vma=False,
    )
```

```python
from functools import partial

import jax
import jax.numpy as jnp
from jax import lax
from jax.experimental import pallas as pl
from jax.experimental.pallas import tpu as pltpu
from jax.sharding import PartitionSpec as P

epsilon = 1e-06
parts = 2
pair = 2
taps = 3
most_direct = 8
mebibyte = 1024 * 1024

VMEM = pl.BlockSpec(memory_space=pltpu.VMEM)
SMEM = pl.BlockSpec(memory_space=pltpu.SMEM)
ANY = pl.BlockSpec(memory_space=pl.ANY)


def silu(v):
    return 0.5 * v * (1.0 + jnp.tanh(0.5 * v))


def dot32(a, b):
    return jnp.dot(a, b, preferred_element_type=jnp.float32)


def cost(flops, *arrays):
    size = sum(a.size * a.dtype.itemsize for a in arrays)
    return pl.CostEstimate(flops=flops, bytes_accessed=size, transcendentals=0)


def params(mebibytes):
    return pltpu.CompilerParams(vmem_limit_bytes=mebibytes * mebibyte)


def rows_of(owner, begin, end, half, height):
    low, high = max(begin, 1), min(end, half + 1)
    pieces = [(owner * half + low - 1, low - begin, high - low)]
    if begin == 0:
        pieces.append((jnp.maximum(owner * half - 1, 0), 0, 1))
    if end == half + 2:
        pieces.append((jnp.minimum((owner + 1) * half, height - 1), end - 1 - begin, 1))
    return pieces


def run(copies):
    for copy in copies:
        copy.start()
    for copy in copies:
        copy.wait()


def cut(target, video, frame, owner, begin, end, half):
    for source, here, count in rows_of(owner, begin, end, half, video.shape[1]):
        target[here : here + count] = video[frame, pl.ds(source, count)]


def send_kernel(spans, half, scalars, video, *outs):
    frames = pl.num_programs(0)
    rest = frames - taps
    step = pl.program_id(0)
    for k, (begin, end) in enumerate(spans):

        @pl.when(step < rest)
        def _():
            cut(outs[2 * k + 1].at[step], video, 0, 1 - scalars[0], begin, end, half)

        @pl.when(step >= rest)
        def _():
            cut(outs[2 * k].at[step - rest], video, 0, 1 - scalars[0], begin, end, half)


def send(scalars, video, spans, half):
    frames, height, width, channels = video.shape
    shapes = [
        (count, end - begin, width, channels)
        for begin, end in spans
        for count in (taps, frames - taps)
    ]
    return pl.pallas_call(
        partial(send_kernel, spans, half),
        grid=(frames,),
        out_shape=[jax.ShapeDtypeStruct(shape, video.dtype) for shape in shapes],
        in_specs=[
            SMEM,
            pl.BlockSpec((1, height, width, channels), lambda t: (t, 0, 0, 0)),
        ],
        out_specs=[pl.BlockSpec(shape, lambda t: (0, 0, 0, 0)) for shape in shapes],
        compiler_params=params(56),
        name="send",
    )(scalars, video)


def join_last_kernel(begin, end, half, scalars, video, received, own_edge, other_edge, out):
    frames, rows = video.shape[0], end - begin

    @pl.when(scalars[0] == 0)
    def _():
        out[:, :rows] = received[...]
        out[:, rows:] = other_edge[frames - taps :]

    @pl.when(scalars[0] == 1)
    def _():
        for t in range(taps):
            cut(out.at[t], video, frames - taps + t, 1, begin, end, half)
        out[:, rows:] = own_edge[frames - taps :]


def join_first_kernel(
    begin, end, half, scalars, video, received, others, own_edge, other_edge, out
):
    frames, rows = video.shape[0], end - begin
    rest = frames - taps

    @pl.when(scalars[0] == 0)
    def _():
        for t in range(frames):
            cut(out.at[t], video, t, 0, begin, end, half)
        out[:frames, rows:] = own_edge[...]
        out[frames:, :rows] = others[...]
        out[frames:, rows:] = other_edge[:rest]

    @pl.when(scalars[0] == 1)
    def _():
        out[:rest, :rows] = others[...]
        out[rest:frames, :rows] = received[...]
        out[:frames, rows:] = other_edge[...]
        for t in range(rest):
            cut(out.at[frames + t], video, t, 1, begin, end, half)
        out[frames:, rows:] = own_edge[:rest]


def join(kernel, count, name, begin, end, half, scalars, video, *parts):
    _, _, width, channels = video.shape
    rows = end - begin + parts[-1].shape[1]
    return pl.pallas_call(
        partial(kernel, begin, end, half),
        out_shape=jax.ShapeDtypeStruct((count, rows, width, channels), jnp.bfloat16),
        in_specs=[SMEM] + [VMEM] * (1 + len(parts)),
        out_specs=VMEM,
        compiler_params=params(12),
        name=name,
    )(scalars, video, *parts)


def place_rows(buffers, index, top, reduced, rows, width, column):
    pixels, channels = rows * width, reduced.shape[-1]
    edges = reduced.shape[0] - pixels
    row_of = lax.broadcasted_iota(jnp.int32, (pixels, edges), 0) // width
    spread = (row_of == lax.broadcasted_iota(jnp.int32, (pixels, edges), 1)).astype(jnp.bfloat16)
    across = lax.broadcasted_iota(jnp.int32, (pixels, channels), 0) % width
    wide = reduced[:pixels].astype(jnp.float32)
    beside = dot32(spread, reduced[pixels:])
    before = jnp.where(column == 1, beside, 0.0)
    behind = jnp.where(column == 0, beside, 0.0)
    shifted = (
        jnp.where(across == 0, before, pltpu.roll(wide, 1, 0)),
        wide,
        jnp.where(across == width - 1, behind, pltpu.roll(wide, pixels - 1, 0)),
    )
    for b in range(3):
        value = shifted[b].astype(jnp.bfloat16).reshape(rows, width, channels)
        buffers[b, index, top : top + rows] = value


def convolve(buffers, fresh, last, side, kept, keeps, w_space, b_space):
    _, frames, rows, width, channels = buffers.shape
    size = rows - 2
    if fresh:

        @pl.when(side == 0)
        def _():
            buffers[:, :, :1] = jnp.zeros((3, frames, 1, width, channels), jnp.bfloat16)

    else:
        buffers[:, :, :2] = kept
    if last:

        @pl.when(side == pair - 1)
        def _():
            buffers[:, :, size + 1 :] = jnp.zeros((3, frames, 1, width, channels), jnp.bfloat16)

    else:
        keeps(buffers[:, :, size:])

    def window(b, a):
        return buffers[b, :, a : a + size].reshape(frames * size * width, channels)

    lhs = jnp.concatenate([window(b, a) for a in range(3) for b in range(3)], axis=1)
    acc = dot32(lhs, w_space[...].reshape(-1, channels)) + b_space[...]
    value = window(1, 1).astype(jnp.float32) + silu(acc)
    return value.astype(jnp.bfloat16).reshape(frames, size * width, channels)


def early_kernel(
    final, rows, scalars, first, last, w_time, b_time, w_down, b_down, w_space, b_space, *refs
):
    part, spatial = refs[:2]
    lifted, buffers = refs[-2:]
    keeps = None if final else (lambda value: refs[2].__setitem__(..., value))
    split, depth, width, channels = first.shape
    count = split + taps
    halves = count // 2
    pixels = depth * width

    def frame(t):
        return (first[t] if t < split else last[t - split]).reshape(pixels, channels)

    starts = list(range(taps - 1, count))
    for low in range(0, len(starts), 3):
        group = starts[low : low + 3]
        lhs = jnp.concatenate(
            [jnp.concatenate([frame(t - k) for t in group], axis=0) for k in range(taps)], axis=1
        )
        acc = dot32(lhs, w_time[...]) + b_time[...]
        held = jnp.concatenate([frame(t) for t in group], axis=0).astype(jnp.float32)
        value = (held + silu(acc)).astype(jnp.bfloat16)
        for g, t in enumerate(group):
            lifted[t] = value[g * pixels : (g + 1) * pixels]
    lhs = jnp.concatenate([lifted[3], lifted[2]], axis=1)
    part[...] = dot32(lhs, w_down[: 2 * channels]) + b_down[...]
    whole = range(2, halves)
    lhs = jnp.concatenate(
        [jnp.concatenate([lifted[2 * s + 1 - k] for s in whole], axis=0) for k in range(taps)],
        axis=1,
    )
    reduced = (dot32(lhs, w_down[...]) + b_down[...]).astype(jnp.bfloat16)
    for index in range(len(whole)):
        value = reduced[index * pixels : (index + 1) * pixels]
        place_rows(buffers, index, 0, value, rows, width, scalars[1])
    spatial[...] = convolve(buffers, True, final, scalars[0], None, keeps, w_space, b_space)


def early(scalars, first, last, final, size, rows, *weights):
    split, depth, width, channels = first.shape
    halves = (split + taps) // 2
    pixels = depth * width
    later = halves - 2
    shapes = [
        jax.ShapeDtypeStruct((pixels, channels), jnp.float32),
        jax.ShapeDtypeStruct((later, size * width, channels), jnp.bfloat16),
    ]
    if not final:
        shapes.append(jax.ShapeDtypeStruct((3, later, 2, width, channels), jnp.bfloat16))
    flops = 2 * channels * channels * (pixels * 26 + 9 * later * size * width)
    return pl.pallas_call(
        partial(early_kernel, final, rows),
        out_shape=shapes,
        in_specs=[SMEM] + [VMEM] * (2 + len(weights)),
        out_specs=[VMEM] * len(shapes),
        scratch_shapes=[
            pltpu.VMEM((2 * halves, pixels, channels), jnp.bfloat16),
            pltpu.VMEM((3, later, size + 2, width, channels), jnp.bfloat16),
        ],
        compiler_params=params(24),
        cost_estimate=cost(flops, first, last, *weights),
        name="early",
    )(scalars, first, last, *weights)


def full_kernel(
    owners, final, rows, scalars, halo, first, last, kept_late, kept_early, w_time, b_time, w_down,
    b_down, w_space, b_space, *refs
):
    outs = refs[:owners]
    keeps = None if final else refs[owners : owners + 2]
    lifted, buffers = refs[-2:]
    split, depth, width, channels = first.shape
    count = split + taps
    halves = count // 2
    pixels = depth * width

    def frame(t):
        if t < 0:
            value = halo[t + taps].reshape(pixels, channels)
            return jnp.where(scalars[2] > 0, value, jnp.zeros_like(value))
        return (first[t] if t < split else last[t - split]).reshape(pixels, channels)

    starts = list(range(-1, count))
    for low in range(0, len(starts), 3):
        group = starts[low : low + 3]
        lhs = jnp.concatenate(
            [jnp.concatenate([frame(t - k) for t in group], axis=0) for k in range(taps)], axis=1
        )
        acc = dot32(lhs, w_time[...]) + b_time[...]
        held = jnp.concatenate([frame(t) for t in group], axis=0).astype(jnp.float32)
        value = held + silu(acc)
        for g, t in enumerate(group):
            piece = value[g * pixels : (g + 1) * pixels]
            if t < 0:
                piece = jnp.where(scalars[2] > 0, piece, 0.0)
            lifted[t + 1] = piece.astype(jnp.bfloat16)
    lhs = jnp.concatenate(
        [
            jnp.concatenate([lifted[2 * s + 2 - k] for s in range(halves)], axis=0)
            for k in range(taps)
        ],
        axis=1,
    )
    reduced = (dot32(lhs, w_down[...]) + b_down[...]).astype(jnp.bfloat16)
    for index in range(halves):
        value = reduced[index * pixels : (index + 1) * pixels]
        place_rows(buffers, index, 2, value, rows, width, scalars[1])
    kept = jnp.concatenate([kept_late[...], kept_early[...]], axis=1)
    keep = None if final else (lambda value: keep_both(keeps, value))
    result = convolve(buffers, False, final, scalars[0], kept, keep, w_space, b_space)
    each = result.shape[1] // owners
    if owners == 1:
        outs[0][...] = result
    else:
        for j in range(owners):
            part = result[:, j * each : (j + 1) * each]
            for m in range(owners):

                @pl.when((scalars[2] ^ m) == j)
                def _():
                    outs[m][...] = part


def keep_both(keeps, value):
    keeps[0][...] = value[:, :2]
    keeps[1][...] = value[:, 2:]


def full(owners, scalars, halo, first, last, kept, final, size, rows, *weights):
    split, depth, width, channels = first.shape
    halves = (split + taps) // 2
    pixels = depth * width
    shapes = [(halves, size * width // owners, channels)] * owners
    if not final:
        shapes += [(3, count, 2, width, channels) for count in (2, halves - 2)]
    flops = 2 * channels * channels * (pixels * 39 + 9 * halves * size * width)
    return pl.pallas_call(
        partial(full_kernel, owners, final, rows),
        out_shape=[jax.ShapeDtypeStruct(shape, jnp.bfloat16) for shape in shapes],
        in_specs=[SMEM] + [VMEM] * (5 + len(weights)),
        out_specs=[VMEM] * len(shapes),
        scratch_shapes=[
            pltpu.VMEM((2 * halves + 1, pixels, channels), jnp.bfloat16),
            pltpu.VMEM((3, halves, size + 2, width, channels), jnp.bfloat16),
        ],
        compiler_params=params(28),
        cost_estimate=cost(flops, halo, first, last, *weights),
        name="full",
    )(scalars, halo, first, last, *kept, *weights)


def late_kernel(
    owners, final, rows, scalars, halo, first, part, spatial, w_time, b_time, w_down, b_down,
    w_space, b_space, *refs
):
    outs = refs[:owners]
    keeps = None if final else (lambda value: refs[owners].__setitem__(..., value))
    lifted, buffers, result = refs[-3:]
    _, depth, width, channels = first.shape
    pixels = depth * width

    def frame(t):
        if t < 0:
            value = halo[t + taps].reshape(pixels, channels)
            return jnp.where(scalars[2] > 0, value, jnp.zeros_like(value))
        return first[t].reshape(pixels, channels)

    group = range(-1, taps - 1)
    lhs = jnp.concatenate(
        [jnp.concatenate([frame(t - k) for t in group], axis=0) for k in range(taps)], axis=1
    )
    acc = dot32(lhs, w_time[...]) + b_time[...]
    held = jnp.concatenate([frame(t) for t in group], axis=0).astype(jnp.float32)
    value = held + silu(acc)
    for index in range(taps):
        piece = value[index * pixels : (index + 1) * pixels]
        if index == 0:
            piece = jnp.where(scalars[2] > 0, piece, 0.0)
        lifted[index] = piece.astype(jnp.bfloat16)
    lhs = jnp.concatenate([lifted[2], lifted[1], lifted[0]], axis=1)
    reduced = (
        dot32(lhs, w_down[...]) + b_down[...],
        dot32(lifted[2], w_down[2 * channels :]) + part[...],
    )
    for index, value in enumerate(reduced):
        value = value.astype(jnp.bfloat16)
        place_rows(buffers, index, 0, value, rows, width, scalars[1])
    result[:2] = convolve(buffers, True, final, scalars[0], None, keeps, w_space, b_space)
    result[2:] = spatial[...]
    each = result.shape[1] // owners
    if owners == 1:
        outs[0][...] = result[...]
    else:
        for j, out in enumerate(outs):
            begin = pl.multiple_of((scalars[2] ^ j) * each, each)
            out[...] = result[:, pl.ds(begin, each)]


def late(owners, scalars, halo, first, part, spatial, final, rows, *weights):
    _, depth, width, channels = first.shape
    later, pixels = spatial.shape[:2]
    halves = later + 2
    size = pixels // width
    shapes = [(halves, pixels // owners, channels)] * owners
    if not final:
        shapes.append((3, 2, 2, width, channels))
    flops = 2 * channels * channels * (depth * width * 13 + 18 * pixels)
    return pl.pallas_call(
        partial(late_kernel, owners, final, rows),
        out_shape=[jax.ShapeDtypeStruct(shape, jnp.bfloat16) for shape in shapes],
        in_specs=[SMEM] + [VMEM] * (4 + len(weights)),
        out_specs=[VMEM] * len(shapes),
        scratch_shapes=[
            pltpu.VMEM((taps, depth * width, channels), jnp.bfloat16),
            pltpu.VMEM((3, 2, size + 2, width, channels), jnp.bfloat16),
            pltpu.VMEM((halves, pixels, channels), jnp.bfloat16),
        ],
        compiler_params=params(24),
        cost_estimate=cost(flops, halo, first, part, *weights),
        name="late",
    )(scalars, halo, first, part, spatial, *weights)


def attend_kernel(frames_per, lanes, count, near, chunks, scalars, *refs):
    blocks, refs = refs[:count], refs[count:]
    gain, w_query, w_key, w_value, w_out = refs[:5]
    waiting, outs = refs[5 : 5 + near * (chunks - 1)], refs[5 + near * (chunks - 1) :]
    for index, block in enumerate(waiting):
        outs[1 + index % near][index // near] = block[...]
    channels = gain.shape[-1]
    flat = len(blocks[0].shape) == 2
    groups = 1 if flat else blocks[0].shape[1] // lanes
    each = frames_per * lanes
    size = count * each

    def piece(j, g):
        if flat:
            return blocks[0][...]
        return blocks[j][:, g * lanes : (g + 1) * lanes].reshape(each, channels)

    def place(index):
        block = index // each
        time = index // lanes % frames_per
        for j in range(count):
            level = 0 if flat else scalars[2] ^ j
            time = time + jnp.where(block == j, level * frames_per, 0)
        return time, index % lanes

    row_time, row_lane = place(lax.broadcasted_iota(jnp.int32, (size, 1), 0))
    col_time, col_lane = place(lax.broadcasted_iota(jnp.int32, (1, size), 1))
    allowed = (row_lane == col_lane) & (col_time <= row_time)
    x = jnp.concatenate([piece(j, g) for g in range(groups) for j in range(count)], axis=0)
    wide = x.astype(jnp.float32)
    scale = lax.rsqrt(jnp.mean(wide * wide, axis=-1, keepdims=True) + epsilon)
    normed = (wide * scale * gain[...]).astype(jnp.bfloat16)
    query = dot32(normed, w_query[...]).astype(jnp.bfloat16)
    key = dot32(normed, w_key[...]).astype(jnp.bfloat16)
    value = dot32(normed, w_value[...]).astype(jnp.bfloat16)
    contexts = []
    for g in range(groups):
        part = slice(g * size, (g + 1) * size)
        scores = lax.dot_general(
            query[part], key[part], (((1,), (1,)), ((), ())), preferred_element_type=jnp.float32
        )
        scores = jnp.where(allowed, scores * channels ** (-0.5), -1e30)
        largest = jnp.max(scores, axis=-1, keepdims=True)
        probs = jnp.exp(scores - largest)
        probs = (probs / jnp.sum(probs, axis=-1, keepdims=True)).astype(jnp.bfloat16)
        contexts.append(dot32(probs, value[part]).astype(jnp.bfloat16))
    mixed = dot32(jnp.concatenate(contexts, axis=0), w_out[...])
    result = (wide + mixed).astype(jnp.bfloat16)
    if flat:
        outs[0][...] = result
        return
    short = frames_per // pair
    for g in range(groups):
        for j in range(count):
            begin = g * size + j * each
            rows = result[begin : begin + each].reshape(pair, short, lanes, channels)
            for side in range(pair):

                @pl.when(scalars[0] == side)
                def _():
                    part = slice(g * lanes, (g + 1) * lanes)
                    for x in range(pair):
                        m = pair * j + x
                        if 0 < m <= near:
                            outs[m][chunks - 1, :, part] = rows[side ^ x]
                        else:
                            outs[m][:, part] = rows[side ^ x]


def attend(scalars, blocks, near, waiting, gain, w_query, w_key, w_value, w_out):
    frames_per, pixels, channels = blocks[0].shape
    flat = pixels % 16 != 0
    lanes = pixels if flat else 16
    if flat:
        blocks = [b.reshape(frames_per * pixels, channels) for b in blocks]
    count = len(blocks)
    size = frames_per * count * lanes
    block = (frames_per // pair, pixels, channels)
    chunks = 1 + len(waiting) // near if near else 1
    shapes = [
        (chunks,) + block if 0 < m <= near else block for m in range(pair * count)
    ]
    if flat:
        shapes = [blocks[0].shape]
    flops = 2 * frames_per * pixels * count * channels * (4 * channels + 2 * size)
    outs = pl.pallas_call(
        partial(attend_kernel, frames_per, lanes, count, near, chunks),
        out_shape=[jax.ShapeDtypeStruct(shape, jnp.bfloat16) for shape in shapes],
        in_specs=[SMEM] + [VMEM] * (count + 5 + len(waiting)),
        out_specs=[VMEM] * len(shapes),
        compiler_params=params(20 if 16 * size * size < 20 * mebibyte else 56),
        cost_estimate=cost(flops, *blocks, w_query, w_key, w_value, w_out),
        name="attend",
    )(scalars, *blocks, gain, w_query, w_key, w_value, w_out, *waiting)
    return [o.reshape(frames_per, pixels, channels) for o in outs] if flat else outs


def collect_kernel(entries, levels, chunks, scalars, *refs):
    out, sems = refs[-2:]
    copies = []
    for index, (ref, sub, k, m) in enumerate(entries):
        block = refs[ref] if sub is None else refs[ref].at[sub]
        place = ((scalars[0] ^ m % pair) * chunks + k) * levels + (scalars[2] ^ m // pair)
        copies.append(pltpu.make_async_copy(block, out.at[:, place], sems.at[index]))
    run(copies)


def collect(scalars, blocks, entries, levels, chunks, whole):
    halves, pixels, channels = blocks[0].shape[-3:]
    given = [] if whole is None else [whole]
    shape = (halves, chunks * pair * levels, pixels, channels)
    return pl.pallas_call(
        partial(collect_kernel, entries, levels, chunks),
        out_shape=jax.ShapeDtypeStruct(shape, jnp.bfloat16),
        in_specs=[SMEM] + [ANY] * (len(blocks) + len(given)),
        out_specs=ANY,
        input_output_aliases={len(blocks) + 1: 0} if given else {},
        scratch_shapes=[pltpu.SemaphoreType.DMA((len(entries),))],
        compiler_params=params(16),
        name="collect",
    )(scalars, *blocks, *given)


def after(value, other):
    return lax.optimization_barrier((value, other))[0]


def per_device(
    video, w_time, b_time, w_down, b_down, w_space, b_space, gain, w_query, w_key, w_value, w_out
):
    frames, height, width, channels = video.shape
    devices = lax.axis_size("tm")
    levels = devices // pair
    columns = lax.axis_size("cols")
    assert columns == 2 and devices % pair == 0 and height % pair == 0 and frames >= taps
    place = lax.axis_index("tm").astype(jnp.int32)
    column = lax.axis_index("cols").astype(jnp.int32)
    side, level = place % pair, place // pair
    scalars = jnp.stack([side, column, level])
    half = height // pair
    gain = gain.reshape(1, -1)
    w_space = jnp.where(after(place, video) >= 0, w_space, 0)
    weights = [
        w_time.reshape(-1, channels), b_time.reshape(1, -1), w_down.reshape(-1, channels),
        b_down.reshape(1, -1), w_space, b_space.reshape(1, -1),
    ]
    attention = [gain, w_query, w_key, w_value, w_out]
    chunks = parts if half % parts == 0 and half // parts * width % levels == 0 else 1
    size = half // chunks
    each = size * width // levels
    direct = devices <= most_direct and levels & (levels - 1) == 0 and each % 16 == 0
    spans = [
        (k * size + (2 if k else 0), (k + 1) * size + 2) for k in range(chunks)
    ]

    def tm_permute(value, move):
        return lax.ppermute(value, "tm", [(i, move(i)) for i in range(devices) if move(i) < devices])

    sent = send(scalars, video, spans, half)
    received = [tm_permute(value, lambda i: i ^ 1) for value in sent]
    border = jnp.where(column == 0, video[:, :, -1], video[:, :, 0])
    border = jnp.pad(after(border, sent[0]), ((0, 0), (1, 1), (0, 0)))
    own_edge, other_edge = (
        lax.dynamic_slice_in_dim(border, s * half, half + 2, axis=1) for s in (side, 1 - side)
    )
    own_edge = lax.ppermute(own_edge, "cols", [(0, 1), (1, 0)])
    aslant = [
        (i * columns + c, (i ^ 1) * columns + 1 - c)
        for i in range(devices)
        for c in range(columns)
    ]
    other_edge = lax.ppermute(other_edge, ("tm", "cols"), aslant)

    def edge_rows(edge, begin, end):
        cut = jnp.pad(edge[:, begin:end], ((0, 0), (0, -(end - begin) % width), (0, 0)))
        return cut.reshape(frames, -1, width, channels)

    owners = levels if direct else 1
    edges = [[edge_rows(e, begin, end) for e in (own_edge, other_edge)] for begin, end in spans]
    lasts, firsts, halos = [], [], []
    newest = w_space
    for k, (begin, end) in enumerate(spans):
        span = (begin, end, half, scalars, video)
        arrived = after(received[2 * k], newest)
        last = join(join_last_kernel, taps, "join_last", *span, arrived, *edges[k])
        lasts.append(last)
        halos.append(tm_permute(last, lambda i: (i + pair) % devices))
        if k == 0:
            others = after(received[1], last)
            firsts.append(join(
                join_first_kernel, pair * frames - taps, "join_first", *span, arrived, others,
                *edges[k]
            ))
            part, spatial, *kept = early(
                scalars, firsts[0], last, chunks == 1, size, end - begin, *weights
            )
            newest = part

    spatials = []
    for k, (begin, end) in enumerate(spans):
        rows, final = end - begin, k == chunks - 1
        if k == 0:
            part = after(part, lasts[-1])
            made = late(
                owners, scalars, halos[k], firsts[0], part, spatial, final, rows, *weights
            )
            kept = [*made[owners:], *kept]
        else:
            span = (begin, end, half, scalars, video)
            others = after(received[2 * k + 1], spatials[-1][0])
            first = join(
                join_first_kernel, pair * frames - taps, "join_first", *span, received[2 * k],
                others, *edges[k]
            )
            made = full(
                owners, scalars, halos[k], first, lasts[k], kept, final, size, rows, *weights
            )
            kept = made[owners:]
        spatials.append(made[:owners])

    newest = spatials[-1][0]
    if direct:
        gathers = [
            [blocks[0]]
            + [tm_permute(blocks[j], lambda i: i ^ (pair * j)) for j in range(1, levels)]
            for blocks in spatials
        ]
        far = devices // 2
        near = far - 1
        whole, waiting = None, []
        for k, gathered in enumerate(gathers):
            gathered[0] = after(gathered[0], newest)
            final = k == chunks - 1
            results = attend(
                scalars, gathered, near if final else 0, waiting if final else [], *attention
            )
            newest = results[0]
            blocks = [tm_permute(results[m], lambda i: i ^ m) for m in range(far, devices)]
            entries = [(m - far, None, k, m) for m in range(far, devices)]
            if final:
                for m in range(1, far):
                    entries += [(len(blocks), c, c, m) for c in range(chunks)]
                    blocks.append(tm_permute(results[m], lambda i: i ^ m))
            else:
                waiting += results[1:far]
            entries.append((len(blocks), None, k, 0))
            blocks.append(results[0])
            whole = collect(scalars, blocks, entries, levels, chunks, whole)
        return whole.reshape(frames // 2, height, width, channels)
    sets = [[pair * z + s for z in range(levels)] for s in range(pair)]
    returns = []
    for (block,) in spatials:
        gathered = lax.all_to_all(block, "tm", 1, 0, axis_index_groups=sets, tiled=True)
        (result,) = attend(scalars, [gathered], 0, [], *attention)
        result = lax.all_to_all(result, "tm", 0, 1, tiled=True)
        result = result.reshape(frames // 2, levels, pair, each, channels)
        returns.append(result.transpose(0, 2, 1, 3, 4).reshape(frames // 2, pair, -1, channels))
    return jnp.concatenate(returns, axis=2).reshape(frames // 2, height, width, channels)


def solution(mesh):
    spread = P(("clips", "tm"), None, "cols", None)
    return jax.shard_map(
        per_device,
        mesh=mesh,
        in_specs=(spread,) + (P(),) * 11,
        out_specs=spread,
        check_vma=False,
    )
```

```python
from functools import partial

import jax
import jax.numpy as jnp
from jax import lax
from jax.experimental import pallas as pl
from jax.experimental.pallas import tpu as pltpu
from jax.sharding import PartitionSpec as P

epsilon = 1e-06
parts = 2
pair = 2
taps = 3
most_direct = 8
mebibyte = 1024 * 1024

VMEM = pl.BlockSpec(memory_space=pltpu.VMEM)
SMEM = pl.BlockSpec(memory_space=pltpu.SMEM)
ANY = pl.BlockSpec(memory_space=pl.ANY)


def silu(v):
    return 0.5 * v * (1.0 + jnp.tanh(0.5 * v))


def dot32(a, b):
    return jnp.dot(a, b, preferred_element_type=jnp.float32)


def cost(flops, *arrays):
    size = sum(a.size * a.dtype.itemsize for a in arrays)
    return pl.CostEstimate(flops=flops, bytes_accessed=size, transcendentals=0)


def params(mebibytes):
    return pltpu.CompilerParams(vmem_limit_bytes=mebibytes * mebibyte)


def rows_of(owner, begin, end, half, height):
    low, high = max(begin, 1), min(end, half + 1)
    pieces = [(owner * half + low - 1, low - begin, high - low)]
    if begin == 0:
        pieces.append((jnp.maximum(owner * half - 1, 0), 0, 1))
    if end == half + 2:
        pieces.append((jnp.minimum((owner + 1) * half, height - 1), end - 1 - begin, 1))
    return pieces


def run(copies):
    for copy in copies:
        copy.start()
    for copy in copies:
        copy.wait()


def cut(target, video, frame, owner, begin, end, half):
    for source, here, count in rows_of(owner, begin, end, half, video.shape[1]):
        target[here : here + count] = video[frame, pl.ds(source, count)]


def send_kernel(spans, half, scalars, video, *outs):
    frames = video.shape[0]
    rest = frames - taps
    for k, (begin, end) in enumerate(spans):
        for t in range(frames):
            target = outs[2 * k].at[t - rest] if t >= rest else outs[2 * k + 1].at[t]
            cut(target, video, t, 1 - scalars[0], begin, end, half)


def send(scalars, video, spans, half):
    frames, _, width, channels = video.shape
    shapes = [
        (count, end - begin, width, channels)
        for begin, end in spans
        for count in (taps, frames - taps)
    ]
    return pl.pallas_call(
        partial(send_kernel, spans, half),
        out_shape=[jax.ShapeDtypeStruct(shape, video.dtype) for shape in shapes],
        in_specs=[SMEM, VMEM],
        out_specs=[VMEM] * len(shapes),
        compiler_params=params(12),
        name="send",
    )(scalars, video)


def join_last_kernel(begin, end, half, scalars, video, received, own_edge, other_edge, out):
    frames, rows = video.shape[0], end - begin

    @pl.when(scalars[0] == 0)
    def _():
        out[:, :rows] = received[...]
        out[:, rows:] = other_edge[frames - taps :]

    @pl.when(scalars[0] == 1)
    def _():
        for t in range(taps):
            cut(out.at[t], video, frames - taps + t, 1, begin, end, half)
        out[:, rows:] = own_edge[frames - taps :]


def join_first_kernel(
    begin, end, half, scalars, video, received, others, own_edge, other_edge, out
):
    frames, rows = video.shape[0], end - begin
    rest = frames - taps

    @pl.when(scalars[0] == 0)
    def _():
        for t in range(frames):
            cut(out.at[t], video, t, 0, begin, end, half)
        out[:frames, rows:] = own_edge[...]
        out[frames:, :rows] = others[...]
        out[frames:, rows:] = other_edge[:rest]

    @pl.when(scalars[0] == 1)
    def _():
        out[:rest, :rows] = others[...]
        out[rest:frames, :rows] = received[...]
        out[:frames, rows:] = other_edge[...]
        for t in range(rest):
            cut(out.at[frames + t], video, t, 1, begin, end, half)
        out[frames:, rows:] = own_edge[:rest]


def join(kernel, count, name, begin, end, half, scalars, video, *parts):
    _, _, width, channels = video.shape
    rows = end - begin + parts[-1].shape[1]
    return pl.pallas_call(
        partial(kernel, begin, end, half),
        out_shape=jax.ShapeDtypeStruct((count, rows, width, channels), jnp.bfloat16),
        in_specs=[SMEM] + [VMEM] * (1 + len(parts)),
        out_specs=VMEM,
        compiler_params=params(12),
        name=name,
    )(scalars, video, *parts)


def place_rows(buffers, index, top, reduced, rows, width, column):
    pixels, channels = rows * width, reduced.shape[-1]
    edges = reduced.shape[0] - pixels
    row_of = lax.broadcasted_iota(jnp.int32, (pixels, edges), 0) // width
    spread = (row_of == lax.broadcasted_iota(jnp.int32, (pixels, edges), 1)).astype(jnp.bfloat16)
    across = lax.broadcasted_iota(jnp.int32, (pixels, channels), 0) % width
    wide = reduced[:pixels].astype(jnp.float32)
    beside = dot32(spread, reduced[pixels:])
    before = jnp.where(column == 1, beside, 0.0)
    behind = jnp.where(column == 0, beside, 0.0)
    shifted = (
        jnp.where(across == 0, before, pltpu.roll(wide, 1, 0)),
        wide,
        jnp.where(across == width - 1, behind, pltpu.roll(wide, pixels - 1, 0)),
    )
    for b in range(3):
        value = shifted[b].astype(jnp.bfloat16).reshape(rows, width, channels)
        buffers[b, index, top : top + rows] = value


def convolve(buffers, fresh, last, side, kept, keeps, w_space, b_space):
    _, frames, rows, width, channels = buffers.shape
    size = rows - 2
    if fresh:

        @pl.when(side == 0)
        def _():
            buffers[:, :, :1] = jnp.zeros((3, frames, 1, width, channels), jnp.bfloat16)

    else:
        buffers[:, :, :2] = kept
    if last:

        @pl.when(side == pair - 1)
        def _():
            buffers[:, :, size + 1 :] = jnp.zeros((3, frames, 1, width, channels), jnp.bfloat16)

    else:
        keeps(buffers[:, :, size:])

    def window(b, a):
        return buffers[b, :, a : a + size].reshape(frames * size * width, channels)

    lhs = jnp.concatenate([window(b, a) for a in range(3) for b in range(3)], axis=1)
    acc = dot32(lhs, w_space[...].reshape(-1, channels)) + b_space[...]
    value = window(1, 1).astype(jnp.float32) + silu(acc)
    return value.astype(jnp.bfloat16).reshape(frames, size * width, channels)


def early_kernel(
    final, rows, scalars, first, last, w_time, b_time, w_down, b_down, w_space, b_space, *refs
):
    part, spatial = refs[:2]
    lifted, buffers = refs[-2:]
    keeps = None if final else (lambda value: refs[2].__setitem__(..., value))
    split, depth, width, channels = first.shape
    count = split + taps
    halves = count // 2
    pixels = depth * width

    def frame(t):
        return (first[t] if t < split else last[t - split]).reshape(pixels, channels)

    starts = list(range(taps - 1, count))
    for low in range(0, len(starts), 3):
        group = starts[low : low + 3]
        lhs = jnp.concatenate(
            [jnp.concatenate([frame(t - k) for t in group], axis=0) for k in range(taps)], axis=1
        )
        acc = dot32(lhs, w_time[...]) + b_time[...]
        held = jnp.concatenate([frame(t) for t in group], axis=0).astype(jnp.float32)
        value = (held + silu(acc)).astype(jnp.bfloat16)
        for g, t in enumerate(group):
            lifted[t] = value[g * pixels : (g + 1) * pixels]
    lhs = jnp.concatenate([lifted[3], lifted[2]], axis=1)
    part[...] = dot32(lhs, w_down[: 2 * channels]) + b_down[...]
    whole = range(2, halves)
    lhs = jnp.concatenate(
        [jnp.concatenate([lifted[2 * s + 1 - k] for s in whole], axis=0) for k in range(taps)],
        axis=1,
    )
    reduced = (dot32(lhs, w_down[...]) + b_down[...]).astype(jnp.bfloat16)
    for index in range(len(whole)):
        value = reduced[index * pixels : (index + 1) * pixels]
        place_rows(buffers, index, 0, value, rows, width, scalars[1])
    spatial[...] = convolve(buffers, True, final, scalars[0], None, keeps, w_space, b_space)


def early(scalars, first, last, final, size, rows, *weights):
    split, depth, width, channels = first.shape
    halves = (split + taps) // 2
    pixels = depth * width
    later = halves - 2
    shapes = [
        jax.ShapeDtypeStruct((pixels, channels), jnp.float32),
        jax.ShapeDtypeStruct((later, size * width, channels), jnp.bfloat16),
    ]
    if not final:
        shapes.append(jax.ShapeDtypeStruct((3, later, 2, width, channels), jnp.bfloat16))
    flops = 2 * channels * channels * (pixels * 26 + 9 * later * size * width)
    return pl.pallas_call(
        partial(early_kernel, final, rows),
        out_shape=shapes,
        in_specs=[SMEM] + [VMEM] * (2 + len(weights)),
        out_specs=[VMEM] * len(shapes),
        scratch_shapes=[
            pltpu.VMEM((2 * halves, pixels, channels), jnp.bfloat16),
            pltpu.VMEM((3, later, size + 2, width, channels), jnp.bfloat16),
        ],
        compiler_params=params(24),
        cost_estimate=cost(flops, first, last, *weights),
        name="early",
    )(scalars, first, last, *weights)


def full_kernel(
    owners, final, rows, scalars, halo, first, last, kept_late, kept_early, w_time, b_time, w_down,
    b_down, w_space, b_space, *refs
):
    outs = refs[:owners]
    keeps = None if final else refs[owners : owners + 2]
    lifted, buffers = refs[-2:]
    split, depth, width, channels = first.shape
    count = split + taps
    halves = count // 2
    pixels = depth * width

    def frame(t):
        if t < 0:
            value = halo[t + taps].reshape(pixels, channels)
            return jnp.where(scalars[2] > 0, value, jnp.zeros_like(value))
        return (first[t] if t < split else last[t - split]).reshape(pixels, channels)

    starts = list(range(-1, count))
    for low in range(0, len(starts), 3):
        group = starts[low : low + 3]
        lhs = jnp.concatenate(
            [jnp.concatenate([frame(t - k) for t in group], axis=0) for k in range(taps)], axis=1
        )
        acc = dot32(lhs, w_time[...]) + b_time[...]
        held = jnp.concatenate([frame(t) for t in group], axis=0).astype(jnp.float32)
        value = held + silu(acc)
        for g, t in enumerate(group):
            piece = value[g * pixels : (g + 1) * pixels]
            if t < 0:
                piece = jnp.where(scalars[2] > 0, piece, 0.0)
            lifted[t + 1] = piece.astype(jnp.bfloat16)
    lhs = jnp.concatenate(
        [
            jnp.concatenate([lifted[2 * s + 2 - k] for s in range(halves)], axis=0)
            for k in range(taps)
        ],
        axis=1,
    )
    reduced = (dot32(lhs, w_down[...]) + b_down[...]).astype(jnp.bfloat16)
    for index in range(halves):
        value = reduced[index * pixels : (index + 1) * pixels]
        place_rows(buffers, index, 2, value, rows, width, scalars[1])
    kept = jnp.concatenate([kept_late[...], kept_early[...]], axis=1)
    keep = None if final else (lambda value: keep_both(keeps, value))
    result = convolve(buffers, False, final, scalars[0], kept, keep, w_space, b_space)
    each = result.shape[1] // owners
    if owners == 1:
        outs[0][...] = result
    else:
        for j in range(owners):
            part = result[:, j * each : (j + 1) * each]
            for m in range(owners):

                @pl.when((scalars[2] ^ m) == j)
                def _():
                    outs[m][...] = part


def keep_both(keeps, value):
    keeps[0][...] = value[:, :2]
    keeps[1][...] = value[:, 2:]


def full(owners, scalars, halo, first, last, kept, final, size, rows, *weights):
    split, depth, width, channels = first.shape
    halves = (split + taps) // 2
    pixels = depth * width
    shapes = [(halves, size * width // owners, channels)] * owners
    if not final:
        shapes += [(3, count, 2, width, channels) for count in (2, halves - 2)]
    flops = 2 * channels * channels * (pixels * 39 + 9 * halves * size * width)
    return pl.pallas_call(
        partial(full_kernel, owners, final, rows),
        out_shape=[jax.ShapeDtypeStruct(shape, jnp.bfloat16) for shape in shapes],
        in_specs=[SMEM] + [VMEM] * (5 + len(weights)),
        out_specs=[VMEM] * len(shapes),
        scratch_shapes=[
            pltpu.VMEM((2 * halves + 1, pixels, channels), jnp.bfloat16),
            pltpu.VMEM((3, halves, size + 2, width, channels), jnp.bfloat16),
        ],
        compiler_params=params(28),
        cost_estimate=cost(flops, halo, first, last, *weights),
        name="full",
    )(scalars, halo, first, last, *kept, *weights)


def late_kernel(
    owners, final, rows, scalars, halo, first, part, spatial, w_time, b_time, w_down, b_down,
    w_space, b_space, *refs
):
    outs = refs[:owners]
    keeps = None if final else (lambda value: refs[owners].__setitem__(..., value))
    lifted, buffers, result = refs[-3:]
    _, depth, width, channels = first.shape
    pixels = depth * width

    def frame(t):
        if t < 0:
            value = halo[t + taps].reshape(pixels, channels)
            return jnp.where(scalars[2] > 0, value, jnp.zeros_like(value))
        return first[t].reshape(pixels, channels)

    group = range(-1, taps - 1)
    lhs = jnp.concatenate(
        [jnp.concatenate([frame(t - k) for t in group], axis=0) for k in range(taps)], axis=1
    )
    acc = dot32(lhs, w_time[...]) + b_time[...]
    held = jnp.concatenate([frame(t) for t in group], axis=0).astype(jnp.float32)
    value = held + silu(acc)
    for index in range(taps):
        piece = value[index * pixels : (index + 1) * pixels]
        if index == 0:
            piece = jnp.where(scalars[2] > 0, piece, 0.0)
        lifted[index] = piece.astype(jnp.bfloat16)
    lhs = jnp.concatenate([lifted[2], lifted[1], lifted[0]], axis=1)
    reduced = (
        dot32(lhs, w_down[...]) + b_down[...],
        dot32(lifted[2], w_down[2 * channels :]) + part[...],
    )
    for index, value in enumerate(reduced):
        value = value.astype(jnp.bfloat16)
        place_rows(buffers, index, 0, value, rows, width, scalars[1])
    result[:2] = convolve(buffers, True, final, scalars[0], None, keeps, w_space, b_space)
    result[2:] = spatial[...]
    each = result.shape[1] // owners
    if owners == 1:
        outs[0][...] = result[...]
    else:
        for j, out in enumerate(outs):
            begin = pl.multiple_of((scalars[2] ^ j) * each, each)
            out[...] = result[:, pl.ds(begin, each)]


def late(owners, scalars, halo, first, part, spatial, final, rows, *weights):
    _, depth, width, channels = first.shape
    later, pixels = spatial.shape[:2]
    halves = later + 2
    size = pixels // width
    shapes = [(halves, pixels // owners, channels)] * owners
    if not final:
        shapes.append((3, 2, 2, width, channels))
    flops = 2 * channels * channels * (depth * width * 13 + 18 * pixels)
    return pl.pallas_call(
        partial(late_kernel, owners, final, rows),
        out_shape=[jax.ShapeDtypeStruct(shape, jnp.bfloat16) for shape in shapes],
        in_specs=[SMEM] + [VMEM] * (4 + len(weights)),
        out_specs=[VMEM] * len(shapes),
        scratch_shapes=[
            pltpu.VMEM((taps, depth * width, channels), jnp.bfloat16),
            pltpu.VMEM((3, 2, size + 2, width, channels), jnp.bfloat16),
            pltpu.VMEM((halves, pixels, channels), jnp.bfloat16),
        ],
        compiler_params=params(24),
        cost_estimate=cost(flops, halo, first, part, *weights),
        name="late",
    )(scalars, halo, first, part, spatial, *weights)


def attend_kernel(frames_per, lanes, turns, near, chunks, scalars, *refs):
    count = len(turns)
    blocks, refs = refs[:count], refs[count:]
    gain, w_query, w_key, w_value, w_out = refs[:5]
    waiting, outs = refs[5 : 5 + near * (chunks - 1)], refs[5 + near * (chunks - 1) :]
    for index, block in enumerate(waiting):
        outs[1 + index % near][index // near] = block[...]
    channels = gain.shape[-1]
    flat = len(blocks[0].shape) == 2
    groups = 1 if flat else blocks[0].shape[1] // lanes
    each = frames_per * lanes
    size = count * each

    def piece(j, g):
        if flat:
            return blocks[0][...]
        return blocks[j][:, g * lanes : (g + 1) * lanes].reshape(each, channels)

    def place(index):
        block = index // each
        time = index // lanes % frames_per
        for j in range(count):
            level = 0 if flat else scalars[2] ^ turns[j]
            time = time + jnp.where(block == j, level * frames_per, 0)
        return time, index % lanes

    row_time, row_lane = place(lax.broadcasted_iota(jnp.int32, (size, 1), 0))
    col_time, col_lane = place(lax.broadcasted_iota(jnp.int32, (1, size), 1))
    allowed = (row_lane == col_lane) & (col_time <= row_time)
    x = jnp.concatenate([piece(j, g) for g in range(groups) for j in range(count)], axis=0)
    wide = x.astype(jnp.float32)
    scale = lax.rsqrt(jnp.mean(wide * wide, axis=-1, keepdims=True) + epsilon)
    normed = (wide * scale * gain[...]).astype(jnp.bfloat16)
    query = dot32(normed, w_query[...]).astype(jnp.bfloat16)
    key = dot32(normed, w_key[...]).astype(jnp.bfloat16)
    value = dot32(normed, w_value[...]).astype(jnp.bfloat16)
    contexts = []
    for g in range(groups):
        part = slice(g * size, (g + 1) * size)
        scores = lax.dot_general(
            query[part], key[part], (((1,), (1,)), ((), ())), preferred_element_type=jnp.float32
        )
        scores = jnp.where(allowed, scores * channels ** (-0.5), -1e30)
        largest = jnp.max(scores, axis=-1, keepdims=True)
        probs = jnp.exp(scores - largest)
        probs = (probs / jnp.sum(probs, axis=-1, keepdims=True)).astype(jnp.bfloat16)
        contexts.append(dot32(probs, value[part]).astype(jnp.bfloat16))
    mixed = dot32(jnp.concatenate(contexts, axis=0), w_out[...])
    result = (wide + mixed).astype(jnp.bfloat16)
    if flat:
        outs[0][...] = result
        return
    short = frames_per // pair
    for g in range(groups):
        for j in range(count):
            begin = g * size + j * each
            rows = result[begin : begin + each].reshape(pair, short, lanes, channels)
            for side in range(pair):

                @pl.when(scalars[0] == side)
                def _():
                    part = slice(g * lanes, (g + 1) * lanes)
                    for x in range(pair):
                        m = pair * turns[j] + x
                        if 0 < m <= near:
                            outs[m][chunks - 1, :, part] = rows[side ^ x]
                        else:
                            outs[m][:, part] = rows[side ^ x]


def attend(scalars, blocks, turns, near, waiting, gain, w_query, w_key, w_value, w_out):
    frames_per, pixels, channels = blocks[0].shape
    flat = pixels % 16 != 0
    lanes = pixels if flat else 16
    if flat:
        blocks = [b.reshape(frames_per * pixels, channels) for b in blocks]
    count = len(blocks)
    size = frames_per * count * lanes
    block = (frames_per // pair, pixels, channels)
    chunks = 1 + len(waiting) // near if near else 1
    shapes = [
        (chunks,) + block if 0 < m <= near else block for m in range(pair * count)
    ]
    if flat:
        shapes = [blocks[0].shape]
    flops = 2 * frames_per * pixels * count * channels * (4 * channels + 2 * size)
    outs = pl.pallas_call(
        partial(attend_kernel, frames_per, lanes, turns, near, chunks),
        out_shape=[jax.ShapeDtypeStruct(shape, jnp.bfloat16) for shape in shapes],
        in_specs=[SMEM] + [VMEM] * (count + 5 + len(waiting)),
        out_specs=[VMEM] * len(shapes),
        compiler_params=params(20 if 16 * size * size < 20 * mebibyte else 56),
        cost_estimate=cost(flops, *blocks, w_query, w_key, w_value, w_out),
        name="attend",
    )(scalars, *blocks, gain, w_query, w_key, w_value, w_out, *waiting)
    return [o.reshape(frames_per, pixels, channels) for o in outs] if flat else outs


def collect_kernel(entries, levels, chunks, scalars, *refs):
    out, sems = refs[-2:]
    copies = []
    for index, (ref, sub, k, m) in enumerate(entries):
        block = refs[ref] if sub is None else refs[ref].at[sub]
        place = ((scalars[0] ^ m % pair) * chunks + k) * levels + (scalars[2] ^ m // pair)
        copies.append(pltpu.make_async_copy(block, out.at[:, place], sems.at[index]))
    run(copies)


def collect(scalars, blocks, entries, levels, chunks, whole):
    halves, pixels, channels = blocks[0].shape[-3:]
    given = [] if whole is None else [whole]
    shape = (halves, chunks * pair * levels, pixels, channels)
    return pl.pallas_call(
        partial(collect_kernel, entries, levels, chunks),
        out_shape=jax.ShapeDtypeStruct(shape, jnp.bfloat16),
        in_specs=[SMEM] + [ANY] * (len(blocks) + len(given)),
        out_specs=ANY,
        input_output_aliases={len(blocks) + 1: 0} if given else {},
        scratch_shapes=[pltpu.SemaphoreType.DMA((len(entries),))],
        compiler_params=params(16),
        name="collect",
    )(scalars, *blocks, *given)


def after(value, other):
    return lax.optimization_barrier((value, other))[0]


def per_device(
    video, w_time, b_time, w_down, b_down, w_space, b_space, gain, w_query, w_key, w_value, w_out
):
    frames, height, width, channels = video.shape
    devices = lax.axis_size("tm")
    levels = devices // pair
    columns = lax.axis_size("cols")
    assert columns == 2 and devices % pair == 0 and height % pair == 0 and frames >= taps
    place = lax.axis_index("tm").astype(jnp.int32)
    column = lax.axis_index("cols").astype(jnp.int32)
    side, level = place % pair, place // pair
    scalars = jnp.stack([side, column, level])
    half = height // pair
    gain = gain.reshape(1, -1)
    w_space = jnp.where(after(place, video) >= 0, w_space, 0)
    weights = [
        w_time.reshape(-1, channels), b_time.reshape(1, -1), w_down.reshape(-1, channels),
        b_down.reshape(1, -1), w_space, b_space.reshape(1, -1),
    ]
    attention = [gain, w_query, w_key, w_value, w_out]
    chunks = parts if half % parts == 0 and half // parts * width % levels == 0 else 1
    size = half // chunks
    each = size * width // levels
    direct = devices <= most_direct and levels & (levels - 1) == 0 and each % 16 == 0
    spans = [
        (k * size + (2 if k else 0), (k + 1) * size + 2) for k in range(chunks)
    ]

    def tm_permute(value, move):
        return lax.ppermute(value, "tm", [(i, move(i)) for i in range(devices) if move(i) < devices])

    sent = send(scalars, video, spans, half)
    received = [tm_permute(value, lambda i: i ^ 1) for value in sent]
    border = jnp.where(column == 0, video[:, :, -1], video[:, :, 0])
    border = jnp.pad(after(border, sent[0]), ((0, 0), (1, 1), (0, 0)))
    own_edge, other_edge = (
        lax.dynamic_slice_in_dim(border, s * half, half + 2, axis=1) for s in (side, 1 - side)
    )
    own_edge = lax.ppermute(own_edge, "cols", [(0, 1), (1, 0)])
    aslant = [
        (i * columns + c, (i ^ 1) * columns + 1 - c)
        for i in range(devices)
        for c in range(columns)
    ]
    other_edge = lax.ppermute(other_edge, ("tm", "cols"), aslant)

    def edge_rows(edge, begin, end):
        cut = jnp.pad(edge[:, begin:end], ((0, 0), (0, -(end - begin) % width), (0, 0)))
        return cut.reshape(frames, -1, width, channels)

    owners = levels if direct else 1
    edges = [[edge_rows(e, begin, end) for e in (own_edge, other_edge)] for begin, end in spans]
    lasts, firsts, halos = [], [], []
    newest = w_space
    for k, (begin, end) in enumerate(spans):
        span = (begin, end, half, scalars, video)
        arrived = after(received[2 * k], newest)
        last = join(join_last_kernel, taps, "join_last", *span, arrived, *edges[k])
        lasts.append(last)
        halos.append(tm_permute(last, lambda i: (i + pair) % devices))
        if k == 0:
            others = after(received[1], last)
            firsts.append(join(
                join_first_kernel, pair * frames - taps, "join_first", *span, arrived, others,
                *edges[k]
            ))
            part, spatial, *kept = early(
                scalars, firsts[0], last, chunks == 1, size, end - begin, *weights
            )
            newest = part

    spatials = []
    for k, (begin, end) in enumerate(spans):
        rows, final = end - begin, k == chunks - 1
        if k == 0:
            part = after(part, lasts[-1])
            made = late(
                owners, scalars, halos[k], firsts[0], part, spatial, final, rows, *weights
            )
            kept = [*made[owners:], *kept]
        else:
            span = (begin, end, half, scalars, video)
            others = after(received[2 * k + 1], spatials[-1][0])
            first = join(
                join_first_kernel, pair * frames - taps, "join_first", *span, received[2 * k],
                others, *edges[k]
            )
            made = full(
                owners, scalars, halos[k], first, lasts[k], kept, final, size, rows, *weights
            )
            kept = made[owners:]
        spatials.append(made[:owners])

    newest = spatials[-1][0]
    if direct:
        gathers = [
            [blocks[0]]
            + [tm_permute(blocks[j], lambda i: i ^ (pair * j)) for j in range(1, levels)]
            for blocks in spatials
        ]
        far = devices // 2
        near = far - 1
        whole, waiting = None, []
        for k, gathered in enumerate(gathers):
            gathered[0] = after(gathered[0], newest)
            final = k == chunks - 1
            turns = tuple(range(levels))
            if final:
                turns = turns[levels // 2 :] + turns[: levels // 2][::-1]
            results = attend(
                scalars, [gathered[j] for j in turns], turns, near if final else 0,
                waiting if final else [], *attention
            )
            newest = results[0]
            blocks = [tm_permute(results[m], lambda i: i ^ m) for m in range(far, devices)]
            entries = [(m - far, None, k, m) for m in range(far, devices)]
            if final:
                for m in range(1, far):
                    entries += [(len(blocks), c, c, m) for c in range(chunks)]
                    blocks.append(tm_permute(results[m], lambda i: i ^ m))
            else:
                waiting += results[1:far]
            entries.append((len(blocks), None, k, 0))
            blocks.append(results[0])
            whole = collect(scalars, blocks, entries, levels, chunks, whole)
        return whole.reshape(frames // 2, height, width, channels)
    sets = [[pair * z + s for z in range(levels)] for s in range(pair)]
    returns = []
    for (block,) in spatials:
        gathered = lax.all_to_all(block, "tm", 1, 0, axis_index_groups=sets, tiled=True)
        (result,) = attend(scalars, [gathered], (0,), 0, [], *attention)
        result = lax.all_to_all(result, "tm", 0, 1, tiled=True)
        result = result.reshape(frames // 2, levels, pair, each, channels)
        returns.append(result.transpose(0, 2, 1, 3, 4).reshape(frames // 2, pair, -1, channels))
    return jnp.concatenate(returns, axis=2).reshape(frames // 2, height, width, channels)


def solution(mesh):
    spread = P(("clips", "tm"), None, "cols", None)
    return jax.shard_map(
        per_device,
        mesh=mesh,
        in_specs=(spread,) + (P(),) * 11,
        out_specs=spread,
        check_vma=False,
    )
```

```python
from functools import partial

import jax
import jax.numpy as jnp
from jax import lax
from jax.experimental import pallas as pl
from jax.experimental.pallas import tpu as pltpu
from jax.sharding import PartitionSpec as P

epsilon = 1e-06
parts = 2
pair = 2
taps = 3
most_direct = 8
mebibyte = 1024 * 1024

VMEM = pl.BlockSpec(memory_space=pltpu.VMEM)
SMEM = pl.BlockSpec(memory_space=pltpu.SMEM)
ANY = pl.BlockSpec(memory_space=pl.ANY)


def silu(v):
    return 0.5 * v * (1.0 + jnp.tanh(0.5 * v))


def dot32(a, b):
    return jnp.dot(a, b, preferred_element_type=jnp.float32)


def cost(flops, *arrays):
    size = sum(a.size * a.dtype.itemsize for a in arrays)
    return pl.CostEstimate(flops=flops, bytes_accessed=size, transcendentals=0)


def params(mebibytes):
    return pltpu.CompilerParams(vmem_limit_bytes=mebibytes * mebibyte)


def rows_of(owner, begin, end, half, height):
    low, high = max(begin, 1), min(end, half + 1)
    pieces = [(owner * half + low - 1, low - begin, high - low)]
    if begin == 0:
        pieces.append((jnp.maximum(owner * half - 1, 0), 0, 1))
    if end == half + 2:
        pieces.append((jnp.minimum((owner + 1) * half, height - 1), end - 1 - begin, 1))
    return pieces


def run(copies):
    for copy in copies:
        copy.start()
    for copy in copies:
        copy.wait()


def cut(target, video, frame, owner, begin, end, half):
    for source, here, count in rows_of(owner, begin, end, half, video.shape[1]):
        target[here : here + count] = video[frame, pl.ds(source, count)]


def send_kernel(spans, pieces, half, scalars, video, *outs):
    for out, (k, low, high) in zip(outs, pieces):
        begin, end = spans[k]
        for t in range(low, high):
            cut(out.at[t - low], video, t, 1 - scalars[0], begin, end, half)


def send(scalars, video, spans, pieces, half):
    width, channels = video.shape[2:]
    shapes = [
        (high - low, spans[k][1] - spans[k][0], width, channels) for k, low, high in pieces
    ]
    return pl.pallas_call(
        partial(send_kernel, spans, pieces, half),
        out_shape=[jax.ShapeDtypeStruct(shape, video.dtype) for shape in shapes],
        in_specs=[SMEM, VMEM],
        out_specs=[VMEM] * len(shapes),
        compiler_params=params(12),
        name="send",
    )(scalars, video)


def join_last_kernel(begin, end, half, scalars, video, received, own_edge, other_edge, out):
    frames, rows = video.shape[0], end - begin

    @pl.when(scalars[0] == 0)
    def _():
        out[:, :rows] = received[...]
        out[:, rows:] = other_edge[frames - taps :]

    @pl.when(scalars[0] == 1)
    def _():
        for t in range(taps):
            cut(out.at[t], video, frames - taps + t, 1, begin, end, half)
        out[:, rows:] = own_edge[frames - taps :]


def join_first_kernel(
    begin, end, half, scalars, video, received, others, own_edge, other_edge, out
):
    frames, rows = video.shape[0], end - begin
    rest = frames - taps

    @pl.when(scalars[0] == 0)
    def _():
        for t in range(frames):
            cut(out.at[t], video, t, 0, begin, end, half)
        out[:frames, rows:] = own_edge[...]
        out[frames:, :rows] = others[...]
        out[frames:, rows:] = other_edge[:rest]

    @pl.when(scalars[0] == 1)
    def _():
        out[:rest, :rows] = others[...]
        out[rest:frames, :rows] = received[...]
        out[:frames, rows:] = other_edge[...]
        for t in range(rest):
            cut(out.at[frames + t], video, t, 1, begin, end, half)
        out[frames:, rows:] = own_edge[:rest]


def join(kernel, count, name, begin, end, half, scalars, video, *parts):
    _, _, width, channels = video.shape
    rows = end - begin + parts[-1].shape[1]
    return pl.pallas_call(
        partial(kernel, begin, end, half),
        out_shape=jax.ShapeDtypeStruct((count, rows, width, channels), jnp.bfloat16),
        in_specs=[SMEM] + [VMEM] * (1 + len(parts)),
        out_specs=VMEM,
        compiler_params=params(12),
        name=name,
    )(scalars, video, *parts)


def place_rows(buffers, index, top, reduced, rows, width, column):
    pixels, channels = rows * width, reduced.shape[-1]
    edges = reduced.shape[0] - pixels
    row_of = lax.broadcasted_iota(jnp.int32, (pixels, edges), 0) // width
    spread = (row_of == lax.broadcasted_iota(jnp.int32, (pixels, edges), 1)).astype(jnp.bfloat16)
    across = lax.broadcasted_iota(jnp.int32, (pixels, channels), 0) % width
    wide = reduced[:pixels].astype(jnp.float32)
    beside = dot32(spread, reduced[pixels:])
    before = jnp.where(column == 1, beside, 0.0)
    behind = jnp.where(column == 0, beside, 0.0)
    shifted = (
        jnp.where(across == 0, before, pltpu.roll(wide, 1, 0)),
        wide,
        jnp.where(across == width - 1, behind, pltpu.roll(wide, pixels - 1, 0)),
    )
    for b in range(3):
        value = shifted[b].astype(jnp.bfloat16).reshape(rows, width, channels)
        buffers[b, index, top : top + rows] = value


def convolve(buffers, fresh, last, side, kept, keeps, w_space, b_space):
    _, frames, rows, width, channels = buffers.shape
    size = rows - 2
    if fresh:

        @pl.when(side == 0)
        def _():
            buffers[:, :, :1] = jnp.zeros((3, frames, 1, width, channels), jnp.bfloat16)

    else:
        buffers[:, :, :2] = kept
    if last:

        @pl.when(side == pair - 1)
        def _():
            buffers[:, :, size + 1 :] = jnp.zeros((3, frames, 1, width, channels), jnp.bfloat16)

    else:
        keeps(buffers[:, :, size:])

    def window(b, a):
        return buffers[b, :, a : a + size].reshape(frames * size * width, channels)

    lhs = jnp.concatenate([window(b, a) for a in range(3) for b in range(3)], axis=1)
    acc = dot32(lhs, w_space[...].reshape(-1, channels)) + b_space[...]
    value = window(1, 1).astype(jnp.float32) + silu(acc)
    return value.astype(jnp.bfloat16).reshape(frames, size * width, channels)


def early_kernel(
    final, rows, scalars, first, last, w_time, b_time, w_down, b_down, w_space, b_space, *refs
):
    part, spatial = refs[:2]
    lifted, buffers = refs[-2:]
    keeps = None if final else (lambda value: refs[2].__setitem__(..., value))
    split, depth, width, channels = first.shape
    count = split + taps
    halves = count // 2
    pixels = depth * width

    def frame(t):
        return (first[t] if t < split else last[t - split]).reshape(pixels, channels)

    starts = list(range(taps - 1, count))
    for low in range(0, len(starts), 3):
        group = starts[low : low + 3]
        lhs = jnp.concatenate(
            [jnp.concatenate([frame(t - k) for t in group], axis=0) for k in range(taps)], axis=1
        )
        acc = dot32(lhs, w_time[...]) + b_time[...]
        held = jnp.concatenate([frame(t) for t in group], axis=0).astype(jnp.float32)
        value = (held + silu(acc)).astype(jnp.bfloat16)
        for g, t in enumerate(group):
            lifted[t] = value[g * pixels : (g + 1) * pixels]
    lhs = jnp.concatenate([lifted[3], lifted[2]], axis=1)
    part[...] = dot32(lhs, w_down[: 2 * channels]) + b_down[...]
    whole = range(2, halves)
    lhs = jnp.concatenate(
        [jnp.concatenate([lifted[2 * s + 1 - k] for s in whole], axis=0) for k in range(taps)],
        axis=1,
    )
    reduced = (dot32(lhs, w_down[...]) + b_down[...]).astype(jnp.bfloat16)
    for index in range(len(whole)):
        value = reduced[index * pixels : (index + 1) * pixels]
        place_rows(buffers, index, 0, value, rows, width, scalars[1])
    spatial[...] = convolve(buffers, True, final, scalars[0], None, keeps, w_space, b_space)


def early(scalars, first, last, final, size, rows, *weights):
    split, depth, width, channels = first.shape
    halves = (split + taps) // 2
    pixels = depth * width
    later = halves - 2
    shapes = [
        jax.ShapeDtypeStruct((pixels, channels), jnp.float32),
        jax.ShapeDtypeStruct((later, size * width, channels), jnp.bfloat16),
    ]
    if not final:
        shapes.append(jax.ShapeDtypeStruct((3, later, 2, width, channels), jnp.bfloat16))
    flops = 2 * channels * channels * (pixels * 26 + 9 * later * size * width)
    return pl.pallas_call(
        partial(early_kernel, final, rows),
        out_shape=shapes,
        in_specs=[SMEM] + [VMEM] * (2 + len(weights)),
        out_specs=[VMEM] * len(shapes),
        scratch_shapes=[
            pltpu.VMEM((2 * halves, pixels, channels), jnp.bfloat16),
            pltpu.VMEM((3, later, size + 2, width, channels), jnp.bfloat16),
        ],
        compiler_params=params(24),
        cost_estimate=cost(flops, first, last, *weights),
        name="early",
    )(scalars, first, last, *weights)


def full_kernel(
    owners, final, rows, scalars, halo, first, last, kept_late, kept_early, w_time, b_time, w_down,
    b_down, w_space, b_space, *refs
):
    outs = refs[:owners]
    keeps = None if final else refs[owners : owners + 2]
    lifted, buffers = refs[-2:]
    split, depth, width, channels = first.shape
    count = split + taps
    halves = count // 2
    pixels = depth * width

    def frame(t):
        if t < 0:
            value = halo[t + taps].reshape(pixels, channels)
            return jnp.where(scalars[2] > 0, value, jnp.zeros_like(value))
        return (first[t] if t < split else last[t - split]).reshape(pixels, channels)

    starts = list(range(-1, count))
    for low in range(0, len(starts), 3):
        group = starts[low : low + 3]
        lhs = jnp.concatenate(
            [jnp.concatenate([frame(t - k) for t in group], axis=0) for k in range(taps)], axis=1
        )
        acc = dot32(lhs, w_time[...]) + b_time[...]
        held = jnp.concatenate([frame(t) for t in group], axis=0).astype(jnp.float32)
        value = held + silu(acc)
        for g, t in enumerate(group):
            piece = value[g * pixels : (g + 1) * pixels]
            if t < 0:
                piece = jnp.where(scalars[2] > 0, piece, 0.0)
            lifted[t + 1] = piece.astype(jnp.bfloat16)
    lhs = jnp.concatenate(
        [
            jnp.concatenate([lifted[2 * s + 2 - k] for s in range(halves)], axis=0)
            for k in range(taps)
        ],
        axis=1,
    )
    reduced = (dot32(lhs, w_down[...]) + b_down[...]).astype(jnp.bfloat16)
    for index in range(halves):
        value = reduced[index * pixels : (index + 1) * pixels]
        place_rows(buffers, index, 2, value, rows, width, scalars[1])
    kept = jnp.concatenate([kept_late[...], kept_early[...]], axis=1)
    keep = None if final else (lambda value: keep_both(keeps, value))
    result = convolve(buffers, False, final, scalars[0], kept, keep, w_space, b_space)
    each = result.shape[1] // owners
    if owners == 1:
        outs[0][...] = result
    else:
        for j in range(owners):
            part = result[:, j * each : (j + 1) * each]
            for m in range(owners):

                @pl.when((scalars[2] ^ m) == j)
                def _():
                    outs[m][...] = part


def keep_both(keeps, value):
    keeps[0][...] = value[:, :2]
    keeps[1][...] = value[:, 2:]


def full(owners, scalars, halo, first, last, kept, final, size, rows, *weights):
    split, depth, width, channels = first.shape
    halves = (split + taps) // 2
    pixels = depth * width
    shapes = [(halves, size * width // owners, channels)] * owners
    if not final:
        shapes += [(3, count, 2, width, channels) for count in (2, halves - 2)]
    flops = 2 * channels * channels * (pixels * 39 + 9 * halves * size * width)
    return pl.pallas_call(
        partial(full_kernel, owners, final, rows),
        out_shape=[jax.ShapeDtypeStruct(shape, jnp.bfloat16) for shape in shapes],
        in_specs=[SMEM] + [VMEM] * (5 + len(weights)),
        out_specs=[VMEM] * len(shapes),
        scratch_shapes=[
            pltpu.VMEM((2 * halves + 1, pixels, channels), jnp.bfloat16),
            pltpu.VMEM((3, halves, size + 2, width, channels), jnp.bfloat16),
        ],
        compiler_params=params(28),
        cost_estimate=cost(flops, halo, first, last, *weights),
        name="full",
    )(scalars, halo, first, last, *kept, *weights)


def late_kernel(
    owners, final, rows, scalars, halo, first, part, spatial, w_time, b_time, w_down, b_down,
    w_space, b_space, *refs
):
    outs = refs[:owners]
    keeps = None if final else (lambda value: refs[owners].__setitem__(..., value))
    lifted, buffers, result = refs[-3:]
    _, depth, width, channels = first.shape
    pixels = depth * width

    def frame(t):
        if t < 0:
            value = halo[t + taps].reshape(pixels, channels)
            return jnp.where(scalars[2] > 0, value, jnp.zeros_like(value))
        return first[t].reshape(pixels, channels)

    group = range(-1, taps - 1)
    lhs = jnp.concatenate(
        [jnp.concatenate([frame(t - k) for t in group], axis=0) for k in range(taps)], axis=1
    )
    acc = dot32(lhs, w_time[...]) + b_time[...]
    held = jnp.concatenate([frame(t) for t in group], axis=0).astype(jnp.float32)
    value = held + silu(acc)
    for index in range(taps):
        piece = value[index * pixels : (index + 1) * pixels]
        if index == 0:
            piece = jnp.where(scalars[2] > 0, piece, 0.0)
        lifted[index] = piece.astype(jnp.bfloat16)
    lhs = jnp.concatenate([lifted[2], lifted[1], lifted[0]], axis=1)
    reduced = (
        dot32(lhs, w_down[...]) + b_down[...],
        dot32(lifted[2], w_down[2 * channels :]) + part[...],
    )
    for index, value in enumerate(reduced):
        value = value.astype(jnp.bfloat16)
        place_rows(buffers, index, 0, value, rows, width, scalars[1])
    result[:2] = convolve(buffers, True, final, scalars[0], None, keeps, w_space, b_space)
    result[2:] = spatial[...]
    each = result.shape[1] // owners
    if owners == 1:
        outs[0][...] = result[...]
    else:
        for j, out in enumerate(outs):
            begin = pl.multiple_of((scalars[2] ^ j) * each, each)
            out[...] = result[:, pl.ds(begin, each)]


def late(owners, scalars, halo, first, part, spatial, final, rows, *weights):
    _, depth, width, channels = first.shape
    later, pixels = spatial.shape[:2]
    halves = later + 2
    size = pixels // width
    shapes = [(halves, pixels // owners, channels)] * owners
    if not final:
        shapes.append((3, 2, 2, width, channels))
    flops = 2 * channels * channels * (depth * width * 13 + 18 * pixels)
    return pl.pallas_call(
        partial(late_kernel, owners, final, rows),
        out_shape=[jax.ShapeDtypeStruct(shape, jnp.bfloat16) for shape in shapes],
        in_specs=[SMEM] + [VMEM] * (4 + len(weights)),
        out_specs=[VMEM] * len(shapes),
        scratch_shapes=[
            pltpu.VMEM((taps, depth * width, channels), jnp.bfloat16),
            pltpu.VMEM((3, 2, size + 2, width, channels), jnp.bfloat16),
            pltpu.VMEM((halves, pixels, channels), jnp.bfloat16),
        ],
        compiler_params=params(24),
        cost_estimate=cost(flops, halo, first, part, *weights),
        name="late",
    )(scalars, halo, first, part, spatial, *weights)


def attend_kernel(frames_per, lanes, turns, near, chunks, scalars, *refs):
    count = len(turns)
    blocks, refs = refs[:count], refs[count:]
    gain, w_query, w_key, w_value, w_out = refs[:5]
    waiting, outs = refs[5 : 5 + near * (chunks - 1)], refs[5 + near * (chunks - 1) :]
    for index, block in enumerate(waiting):
        outs[1 + index % near][index // near] = block[...]
    channels = gain.shape[-1]
    flat = len(blocks[0].shape) == 2
    groups = 1 if flat else blocks[0].shape[1] // lanes
    each = frames_per * lanes
    size = count * each

    def piece(j, g):
        if flat:
            return blocks[0][...]
        return blocks[j][:, g * lanes : (g + 1) * lanes].reshape(each, channels)

    def place(index):
        block = index // each
        time = index // lanes % frames_per
        for j in range(count):
            level = 0 if flat else scalars[2] ^ turns[j]
            time = time + jnp.where(block == j, level * frames_per, 0)
        return time, index % lanes

    row_time, row_lane = place(lax.broadcasted_iota(jnp.int32, (size, 1), 0))
    col_time, col_lane = place(lax.broadcasted_iota(jnp.int32, (1, size), 1))
    allowed = (row_lane == col_lane) & (col_time <= row_time)
    x = jnp.concatenate([piece(j, g) for g in range(groups) for j in range(count)], axis=0)
    wide = x.astype(jnp.float32)
    scale = lax.rsqrt(jnp.mean(wide * wide, axis=-1, keepdims=True) + epsilon)
    normed = (wide * scale * gain[...]).astype(jnp.bfloat16)
    query = dot32(normed, w_query[...]).astype(jnp.bfloat16)
    key = dot32(normed, w_key[...]).astype(jnp.bfloat16)
    value = dot32(normed, w_value[...]).astype(jnp.bfloat16)
    contexts = []
    for g in range(groups):
        part = slice(g * size, (g + 1) * size)
        scores = lax.dot_general(
            query[part], key[part], (((1,), (1,)), ((), ())), preferred_element_type=jnp.float32
        )
        scores = jnp.where(allowed, scores * channels ** (-0.5), -1e30)
        largest = jnp.max(scores, axis=-1, keepdims=True)
        probs = jnp.exp(scores - largest)
        probs = (probs / jnp.sum(probs, axis=-1, keepdims=True)).astype(jnp.bfloat16)
        contexts.append(dot32(probs, value[part]).astype(jnp.bfloat16))
    mixed = dot32(jnp.concatenate(contexts, axis=0), w_out[...])
    result = (wide + mixed).astype(jnp.bfloat16)
    if flat:
        outs[0][...] = result
        return
    short = frames_per // pair
    for g in range(groups):
        for j in range(count):
            begin = g * size + j * each
            rows = result[begin : begin + each].reshape(pair, short, lanes, channels)
            for side in range(pair):

                @pl.when(scalars[0] == side)
                def _():
                    part = slice(g * lanes, (g + 1) * lanes)
                    for x in range(pair):
                        m = pair * turns[j] + x
                        if 0 < m <= near:
                            outs[m][chunks - 1, :, part] = rows[side ^ x]
                        else:
                            outs[m][:, part] = rows[side ^ x]


def attend(scalars, blocks, turns, near, waiting, gain, w_query, w_key, w_value, w_out):
    frames_per, pixels, channels = blocks[0].shape
    flat = pixels % 16 != 0
    lanes = pixels if flat else 16
    if flat:
        blocks = [b.reshape(frames_per * pixels, channels) for b in blocks]
    count = len(blocks)
    size = frames_per * count * lanes
    block = (frames_per // pair, pixels, channels)
    chunks = 1 + len(waiting) // near if near else 1
    shapes = [
        (chunks,) + block if 0 < m <= near else block for m in range(pair * count)
    ]
    if flat:
        shapes = [blocks[0].shape]
    flops = 2 * frames_per * pixels * count * channels * (4 * channels + 2 * size)
    outs = pl.pallas_call(
        partial(attend_kernel, frames_per, lanes, turns, near, chunks),
        out_shape=[jax.ShapeDtypeStruct(shape, jnp.bfloat16) for shape in shapes],
        in_specs=[SMEM] + [VMEM] * (count + 5 + len(waiting)),
        out_specs=[VMEM] * len(shapes),
        compiler_params=params(20 if 16 * size * size < 20 * mebibyte else 56),
        cost_estimate=cost(flops, *blocks, w_query, w_key, w_value, w_out),
        name="attend",
    )(scalars, *blocks, gain, w_query, w_key, w_value, w_out, *waiting)
    return [o.reshape(frames_per, pixels, channels) for o in outs] if flat else outs


def collect_kernel(entries, levels, chunks, scalars, *refs):
    out, sems = refs[-2:]
    copies = []
    for index, (ref, sub, k, m) in enumerate(entries):
        block = refs[ref] if sub is None else refs[ref].at[sub]
        place = ((scalars[0] ^ m % pair) * chunks + k) * levels + (scalars[2] ^ m // pair)
        copies.append(pltpu.make_async_copy(block, out.at[:, place], sems.at[index]))
    run(copies)


def collect(scalars, blocks, entries, levels, chunks, whole):
    halves, pixels, channels = blocks[0].shape[-3:]
    given = [] if whole is None else [whole]
    shape = (halves, chunks * pair * levels, pixels, channels)
    return pl.pallas_call(
        partial(collect_kernel, entries, levels, chunks),
        out_shape=jax.ShapeDtypeStruct(shape, jnp.bfloat16),
        in_specs=[SMEM] + [ANY] * (len(blocks) + len(given)),
        out_specs=ANY,
        input_output_aliases={len(blocks) + 1: 0} if given else {},
        scratch_shapes=[pltpu.SemaphoreType.DMA((len(entries),))],
        compiler_params=params(16),
        name="collect",
    )(scalars, *blocks, *given)


def after(value, other):
    return lax.optimization_barrier((value, other))[0]


def per_device(
    video, w_time, b_time, w_down, b_down, w_space, b_space, gain, w_query, w_key, w_value, w_out
):
    frames, height, width, channels = video.shape
    devices = lax.axis_size("tm")
    levels = devices // pair
    columns = lax.axis_size("cols")
    assert columns == 2 and devices % pair == 0 and height % pair == 0 and frames >= taps
    place = lax.axis_index("tm").astype(jnp.int32)
    column = lax.axis_index("cols").astype(jnp.int32)
    side, level = place % pair, place // pair
    scalars = jnp.stack([side, column, level])
    half = height // pair
    gain = gain.reshape(1, -1)
    w_space = jnp.where(after(place, video) >= 0, w_space, 0)
    weights = [
        w_time.reshape(-1, channels), b_time.reshape(1, -1), w_down.reshape(-1, channels),
        b_down.reshape(1, -1), w_space, b_space.reshape(1, -1),
    ]
    attention = [gain, w_query, w_key, w_value, w_out]
    chunks = parts if half % parts == 0 and half // parts * width % levels == 0 else 1
    size = half // chunks
    each = size * width // levels
    direct = devices <= most_direct and levels & (levels - 1) == 0 and each % 16 == 0
    spans = [
        (k * size + (2 if k else 0), (k + 1) * size + 2) for k in range(chunks)
    ]

    def tm_permute(value, move):
        return lax.ppermute(value, "tm", [(i, move(i)) for i in range(devices) if move(i) < devices])

    rest = frames - taps
    pieces = [(k,) + cut for k in range(chunks) for cut in ((rest, frames), (0, rest))]
    sent = send(scalars, video, spans, pieces[:1], half)
    sent = [*sent, *send(after(scalars, sent[0]), video, spans, pieces[1:], half)]
    received = [tm_permute(value, lambda i: i ^ 1) for value in sent]
    border = jnp.where(column == 0, video[:, :, -1], video[:, :, 0])
    border = jnp.pad(after(border, sent[0]), ((0, 0), (1, 1), (0, 0)))
    own_edge, other_edge = (
        lax.dynamic_slice_in_dim(border, s * half, half + 2, axis=1) for s in (side, 1 - side)
    )
    own_edge = lax.ppermute(own_edge, "cols", [(0, 1), (1, 0)])
    aslant = [
        (i * columns + c, (i ^ 1) * columns + 1 - c)
        for i in range(devices)
        for c in range(columns)
    ]
    other_edge = lax.ppermute(other_edge, ("tm", "cols"), aslant)

    def edge_rows(edge, begin, end):
        cut = jnp.pad(edge[:, begin:end], ((0, 0), (0, -(end - begin) % width), (0, 0)))
        return cut.reshape(frames, -1, width, channels)

    owners = levels if direct else 1
    edges = [[edge_rows(e, begin, end) for e in (own_edge, other_edge)] for begin, end in spans]
    lasts, firsts, halos = [], [], []
    newest = w_space
    for k, (begin, end) in enumerate(spans):
        span = (begin, end, half, scalars, video)
        arrived = after(received[2 * k], newest)
        last = join(join_last_kernel, taps, "join_last", *span, arrived, *edges[k])
        lasts.append(last)
        halos.append(tm_permute(last, lambda i: (i + pair) % devices))
        if k == 0:
            others = after(received[1], last)
            firsts.append(join(
                join_first_kernel, pair * frames - taps, "join_first", *span, arrived, others,
                *edges[k]
            ))
            part, spatial, *kept = early(
                scalars, firsts[0], last, chunks == 1, size, end - begin, *weights
            )
            newest = part

    spatials = []
    for k, (begin, end) in enumerate(spans):
        rows, final = end - begin, k == chunks - 1
        if k == 0:
            part = after(part, lasts[-1])
            made = late(
                owners, scalars, halos[k], firsts[0], part, spatial, final, rows, *weights
            )
            kept = [*made[owners:], *kept]
        else:
            span = (begin, end, half, scalars, video)
            others = after(received[2 * k + 1], spatials[-1][0])
            first = join(
                join_first_kernel, pair * frames - taps, "join_first", *span, received[2 * k],
                others, *edges[k]
            )
            made = full(
                owners, scalars, halos[k], first, lasts[k], kept, final, size, rows, *weights
            )
            kept = made[owners:]
        spatials.append(made[:owners])

    newest = spatials[-1][0]
    if direct:
        gathers = [
            [blocks[0]]
            + [tm_permute(blocks[j], lambda i: i ^ (pair * j)) for j in range(1, levels)]
            for blocks in spatials
        ]
        far = devices // 2
        near = far - 1
        whole, waiting = None, []
        for k, gathered in enumerate(gathers):
            gathered[0] = after(gathered[0], newest)
            final = k == chunks - 1
            turns = tuple(range(levels))
            if final:
                turns = turns[levels // 2 :] + turns[: levels // 2][::-1]
            results = attend(
                scalars, [gathered[j] for j in turns], turns, near if final else 0,
                waiting if final else [], *attention
            )
            newest = results[0]
            blocks = [tm_permute(results[m], lambda i: i ^ m) for m in range(far, devices)]
            entries = [(m - far, None, k, m) for m in range(far, devices)]
            if final:
                for m in range(1, far):
                    entries += [(len(blocks), c, c, m) for c in range(chunks)]
                    blocks.append(tm_permute(results[m], lambda i: i ^ m))
            else:
                waiting += results[1:far]
            entries.append((len(blocks), None, k, 0))
            blocks.append(results[0])
            whole = collect(scalars, blocks, entries, levels, chunks, whole)
        return whole.reshape(frames // 2, height, width, channels)
    sets = [[pair * z + s for z in range(levels)] for s in range(pair)]
    returns = []
    for (block,) in spatials:
        gathered = lax.all_to_all(block, "tm", 1, 0, axis_index_groups=sets, tiled=True)
        (result,) = attend(scalars, [gathered], (0,), 0, [], *attention)
        result = lax.all_to_all(result, "tm", 0, 1, tiled=True)
        result = result.reshape(frames // 2, levels, pair, each, channels)
        returns.append(result.transpose(0, 2, 1, 3, 4).reshape(frames // 2, pair, -1, channels))
    return jnp.concatenate(returns, axis=2).reshape(frames // 2, height, width, channels)


def solution(mesh):
    spread = P(("clips", "tm"), None, "cols", None)
    return jax.shard_map(
        per_device,
        mesh=mesh,
        in_specs=(spread,) + (P(),) * 11,
        out_specs=spread,
        check_vma=False,
    )
```

```python
from functools import partial

import jax
import jax.numpy as jnp
from jax import lax
from jax.experimental import pallas as pl
from jax.experimental.pallas import tpu as pltpu
from jax.sharding import PartitionSpec as P

epsilon = 1e-06
parts = 2
pair = 2
taps = 3
most_direct = 8
mebibyte = 1024 * 1024

VMEM = pl.BlockSpec(memory_space=pltpu.VMEM)
SMEM = pl.BlockSpec(memory_space=pltpu.SMEM)
ANY = pl.BlockSpec(memory_space=pl.ANY)


def silu(v):
    return 0.5 * v * (1.0 + jnp.tanh(0.5 * v))


def dot32(a, b):
    return jnp.dot(a, b, preferred_element_type=jnp.float32)


def cost(flops, *arrays):
    size = sum(a.size * a.dtype.itemsize for a in arrays)
    return pl.CostEstimate(flops=flops, bytes_accessed=size, transcendentals=0)


def params(mebibytes):
    return pltpu.CompilerParams(vmem_limit_bytes=mebibytes * mebibyte)


def rows_of(owner, begin, end, half, height):
    low, high = max(begin, 1), min(end, half + 1)
    pieces = [(owner * half + low - 1, low - begin, high - low)]
    if begin == 0:
        pieces.append((jnp.maximum(owner * half - 1, 0), 0, 1))
    if end == half + 2:
        pieces.append((jnp.minimum((owner + 1) * half, height - 1), end - 1 - begin, 1))
    return pieces


def run(copies):
    for copy in copies:
        copy.start()
    for copy in copies:
        copy.wait()


def cut(target, video, frame, owner, begin, end, half):
    for source, here, count in rows_of(owner, begin, end, half, video.shape[1]):
        target[here : here + count] = video[frame, pl.ds(source, count)]


def send_kernel(spans, half, scalars, video, *outs):
    frames = video.shape[0]
    rest = frames - taps
    for k, (begin, end) in enumerate(spans):
        for t in range(frames):
            target = outs[2 * k].at[t - rest] if t >= rest else outs[2 * k + 1].at[t]
            cut(target, video, t, 1 - scalars[0], begin, end, half)


def send(scalars, video, spans, half):
    frames, _, width, channels = video.shape
    shapes = [
        (count, end - begin, width, channels)
        for begin, end in spans
        for count in (taps, frames - taps)
    ]
    return pl.pallas_call(
        partial(send_kernel, spans, half),
        out_shape=[jax.ShapeDtypeStruct(shape, video.dtype) for shape in shapes],
        in_specs=[SMEM, VMEM],
        out_specs=[VMEM] * len(shapes),
        compiler_params=params(12),
        name="send",
    )(scalars, video)


def join_last_kernel(begin, end, half, scalars, video, received, own_edge, other_edge, out):
    frames, rows = video.shape[0], end - begin

    @pl.when(scalars[0] == 0)
    def _():
        out[:, :rows] = received[...]
        out[:, rows:] = other_edge[frames - taps :]

    @pl.when(scalars[0] == 1)
    def _():
        for t in range(taps):
            cut(out.at[t], video, frames - taps + t, 1, begin, end, half)
        out[:, rows:] = own_edge[frames - taps :]


def join_first_kernel(
    begin, end, half, scalars, video, received, others, own_edge, other_edge, out
):
    frames, rows = video.shape[0], end - begin
    rest = frames - taps

    @pl.when(scalars[0] == 0)
    def _():
        for t in range(frames):
            cut(out.at[t], video, t, 0, begin, end, half)
        out[:frames, rows:] = own_edge[...]
        out[frames:, :rows] = others[...]
        out[frames:, rows:] = other_edge[:rest]

    @pl.when(scalars[0] == 1)
    def _():
        out[:rest, :rows] = others[...]
        out[rest:frames, :rows] = received[...]
        out[:frames, rows:] = other_edge[...]
        for t in range(rest):
            cut(out.at[frames + t], video, t, 1, begin, end, half)
        out[frames:, rows:] = own_edge[:rest]


def join(kernel, count, name, begin, end, half, scalars, video, *parts):
    _, _, width, channels = video.shape
    rows = end - begin + parts[-1].shape[1]
    return pl.pallas_call(
        partial(kernel, begin, end, half),
        out_shape=jax.ShapeDtypeStruct((count, rows, width, channels), jnp.bfloat16),
        in_specs=[SMEM] + [VMEM] * (1 + len(parts)),
        out_specs=VMEM,
        compiler_params=params(12),
        name=name,
    )(scalars, video, *parts)


def place_rows(buffers, index, top, reduced, rows, width, column):
    pixels, channels = rows * width, reduced.shape[-1]
    edges = reduced.shape[0] - pixels
    row_of = lax.broadcasted_iota(jnp.int32, (pixels, edges), 0) // width
    spread = (row_of == lax.broadcasted_iota(jnp.int32, (pixels, edges), 1)).astype(jnp.bfloat16)
    across = lax.broadcasted_iota(jnp.int32, (pixels, channels), 0) % width
    wide = reduced[:pixels].astype(jnp.float32)
    beside = dot32(spread, reduced[pixels:])
    before = jnp.where(column == 1, beside, 0.0)
    behind = jnp.where(column == 0, beside, 0.0)
    shifted = (
        jnp.where(across == 0, before, pltpu.roll(wide, 1, 0)),
        wide,
        jnp.where(across == width - 1, behind, pltpu.roll(wide, pixels - 1, 0)),
    )
    for b in range(3):
        value = shifted[b].astype(jnp.bfloat16).reshape(rows, width, channels)
        buffers[b, index, top : top + rows] = value


def convolve(buffers, fresh, last, side, kept, keeps, w_space, b_space):
    _, frames, rows, width, channels = buffers.shape
    size = rows - 2
    if fresh:

        @pl.when(side == 0)
        def _():
            buffers[:, :, :1] = jnp.zeros((3, frames, 1, width, channels), jnp.bfloat16)

    else:
        buffers[:, :, :2] = kept
    if last:

        @pl.when(side == pair - 1)
        def _():
            buffers[:, :, size + 1 :] = jnp.zeros((3, frames, 1, width, channels), jnp.bfloat16)

    else:
        keeps(buffers[:, :, size:])

    def window(b, a):
        return buffers[b, :, a : a + size].reshape(frames * size * width, channels)

    lhs = jnp.concatenate([window(b, a) for a in range(3) for b in range(3)], axis=1)
    acc = dot32(lhs, w_space[...].reshape(-1, channels)) + b_space[...]
    value = window(1, 1).astype(jnp.float32) + silu(acc)
    return value.astype(jnp.bfloat16).reshape(frames, size * width, channels)


def early_kernel(
    final, rows, scalars, first, last, w_time, b_time, w_down, b_down, w_space, b_space, *refs
):
    part, spatial = refs[:2]
    lifted, buffers = refs[-2:]
    keeps = None if final else (lambda value: refs[2].__setitem__(..., value))
    split, depth, width, channels = first.shape
    count = split + taps
    halves = count // 2
    pixels = depth * width

    def frame(t):
        return (first[t] if t < split else last[t - split]).reshape(pixels, channels)

    starts = list(range(taps - 1, count))
    for low in range(0, len(starts), 3):
        group = starts[low : low + 3]
        lhs = jnp.concatenate(
            [jnp.concatenate([frame(t - k) for t in group], axis=0) for k in range(taps)], axis=1
        )
        acc = dot32(lhs, w_time[...]) + b_time[...]
        held = jnp.concatenate([frame(t) for t in group], axis=0).astype(jnp.float32)
        value = (held + silu(acc)).astype(jnp.bfloat16)
        for g, t in enumerate(group):
            lifted[t] = value[g * pixels : (g + 1) * pixels]
    lhs = jnp.concatenate([lifted[3], lifted[2]], axis=1)
    part[...] = dot32(lhs, w_down[: 2 * channels]) + b_down[...]
    whole = range(2, halves)
    lhs = jnp.concatenate(
        [jnp.concatenate([lifted[2 * s + 1 - k] for s in whole], axis=0) for k in range(taps)],
        axis=1,
    )
    reduced = (dot32(lhs, w_down[...]) + b_down[...]).astype(jnp.bfloat16)
    for index in range(len(whole)):
        value = reduced[index * pixels : (index + 1) * pixels]
        place_rows(buffers, index, 0, value, rows, width, scalars[1])
    spatial[...] = convolve(buffers, True, final, scalars[0], None, keeps, w_space, b_space)


def early(scalars, first, last, final, size, rows, *weights):
    split, depth, width, channels = first.shape
    halves = (split + taps) // 2
    pixels = depth * width
    later = halves - 2
    shapes = [
        jax.ShapeDtypeStruct((pixels, channels), jnp.float32),
        jax.ShapeDtypeStruct((later, size * width, channels), jnp.bfloat16),
    ]
    if not final:
        shapes.append(jax.ShapeDtypeStruct((3, later, 2, width, channels), jnp.bfloat16))
    flops = 2 * channels * channels * (pixels * 26 + 9 * later * size * width)
    return pl.pallas_call(
        partial(early_kernel, final, rows),
        out_shape=shapes,
        in_specs=[SMEM] + [VMEM] * (2 + len(weights)),
        out_specs=[VMEM] * len(shapes),
        scratch_shapes=[
            pltpu.VMEM((2 * halves, pixels, channels), jnp.bfloat16),
            pltpu.VMEM((3, later, size + 2, width, channels), jnp.bfloat16),
        ],
        compiler_params=params(24),
        cost_estimate=cost(flops, first, last, *weights),
        name="early",
    )(scalars, first, last, *weights)


def full_kernel(
    owners, final, rows, scalars, halo, first, last, kept_late, kept_early, w_time, b_time, w_down,
    b_down, w_space, b_space, *refs
):
    outs = refs[:owners]
    keeps = None if final else refs[owners : owners + 2]
    lifted, buffers = refs[-2:]
    split, depth, width, channels = first.shape
    count = split + taps
    halves = count // 2
    pixels = depth * width

    def frame(t):
        if t < 0:
            value = halo[t + taps].reshape(pixels, channels)
            return jnp.where(scalars[2] > 0, value, jnp.zeros_like(value))
        return (first[t] if t < split else last[t - split]).reshape(pixels, channels)

    starts = list(range(-1, count))
    for low in range(0, len(starts), 3):
        group = starts[low : low + 3]
        lhs = jnp.concatenate(
            [jnp.concatenate([frame(t - k) for t in group], axis=0) for k in range(taps)], axis=1
        )
        acc = dot32(lhs, w_time[...]) + b_time[...]
        held = jnp.concatenate([frame(t) for t in group], axis=0).astype(jnp.float32)
        value = held + silu(acc)
        for g, t in enumerate(group):
            piece = value[g * pixels : (g + 1) * pixels]
            if t < 0:
                piece = jnp.where(scalars[2] > 0, piece, 0.0)
            lifted[t + 1] = piece.astype(jnp.bfloat16)
    lhs = jnp.concatenate(
        [
            jnp.concatenate([lifted[2 * s + 2 - k] for s in range(halves)], axis=0)
            for k in range(taps)
        ],
        axis=1,
    )
    reduced = (dot32(lhs, w_down[...]) + b_down[...]).astype(jnp.bfloat16)
    for index in range(halves):
        value = reduced[index * pixels : (index + 1) * pixels]
        place_rows(buffers, index, 2, value, rows, width, scalars[1])
    kept = jnp.concatenate([kept_late[...], kept_early[...]], axis=1)
    keep = None if final else (lambda value: keep_both(keeps, value))
    result = convolve(buffers, False, final, scalars[0], kept, keep, w_space, b_space)
    each = result.shape[1] // owners
    if owners == 1:
        outs[0][...] = result
    else:
        for j in range(owners):
            part = result[:, j * each : (j + 1) * each]
            for m in range(owners):

                @pl.when((scalars[2] ^ m) == j)
                def _():
                    outs[m][...] = part


def keep_both(keeps, value):
    keeps[0][...] = value[:, :2]
    keeps[1][...] = value[:, 2:]


def full(owners, scalars, halo, first, last, kept, final, size, rows, *weights):
    split, depth, width, channels = first.shape
    halves = (split + taps) // 2
    pixels = depth * width
    shapes = [(halves, size * width // owners, channels)] * owners
    if not final:
        shapes += [(3, count, 2, width, channels) for count in (2, halves - 2)]
    flops = 2 * channels * channels * (pixels * 39 + 9 * halves * size * width)
    return pl.pallas_call(
        partial(full_kernel, owners, final, rows),
        out_shape=[jax.ShapeDtypeStruct(shape, jnp.bfloat16) for shape in shapes],
        in_specs=[SMEM] + [VMEM] * (5 + len(weights)),
        out_specs=[VMEM] * len(shapes),
        scratch_shapes=[
            pltpu.VMEM((2 * halves + 1, pixels, channels), jnp.bfloat16),
            pltpu.VMEM((3, halves, size + 2, width, channels), jnp.bfloat16),
        ],
        compiler_params=params(28),
        cost_estimate=cost(flops, halo, first, last, *weights),
        name="full",
    )(scalars, halo, first, last, *kept, *weights)


def late_kernel(
    owners, final, rows, scalars, halo, first, part, spatial, w_time, b_time, w_down, b_down,
    w_space, b_space, *refs
):
    outs = refs[:owners]
    keeps = None if final else (lambda value: refs[owners].__setitem__(..., value))
    lifted, buffers, result = refs[-3:]
    _, depth, width, channels = first.shape
    pixels = depth * width

    def frame(t):
        if t < 0:
            value = halo[t + taps].reshape(pixels, channels)
            return jnp.where(scalars[2] > 0, value, jnp.zeros_like(value))
        return first[t].reshape(pixels, channels)

    group = range(-1, taps - 1)
    lhs = jnp.concatenate(
        [jnp.concatenate([frame(t - k) for t in group], axis=0) for k in range(taps)], axis=1
    )
    acc = dot32(lhs, w_time[...]) + b_time[...]
    held = jnp.concatenate([frame(t) for t in group], axis=0).astype(jnp.float32)
    value = held + silu(acc)
    for index in range(taps):
        piece = value[index * pixels : (index + 1) * pixels]
        if index == 0:
            piece = jnp.where(scalars[2] > 0, piece, 0.0)
        lifted[index] = piece.astype(jnp.bfloat16)
    lhs = jnp.concatenate([lifted[2], lifted[1], lifted[0]], axis=1)
    reduced = (
        dot32(lhs, w_down[...]) + b_down[...],
        dot32(lifted[2], w_down[2 * channels :]) + part[...],
    )
    for index, value in enumerate(reduced):
        value = value.astype(jnp.bfloat16)
        place_rows(buffers, index, 0, value, rows, width, scalars[1])
    result[:2] = convolve(buffers, True, final, scalars[0], None, keeps, w_space, b_space)
    result[2:] = spatial[...]
    each = result.shape[1] // owners
    if owners == 1:
        outs[0][...] = result[...]
    else:
        for j, out in enumerate(outs):
            begin = pl.multiple_of((scalars[2] ^ j) * each, each)
            out[...] = result[:, pl.ds(begin, each)]


def late(owners, scalars, halo, first, part, spatial, final, rows, *weights):
    _, depth, width, channels = first.shape
    later, pixels = spatial.shape[:2]
    halves = later + 2
    size = pixels // width
    shapes = [(halves, pixels // owners, channels)] * owners
    if not final:
        shapes.append((3, 2, 2, width, channels))
    flops = 2 * channels * channels * (depth * width * 13 + 18 * pixels)
    return pl.pallas_call(
        partial(late_kernel, owners, final, rows),
        out_shape=[jax.ShapeDtypeStruct(shape, jnp.bfloat16) for shape in shapes],
        in_specs=[SMEM] + [VMEM] * (4 + len(weights)),
        out_specs=[VMEM] * len(shapes),
        scratch_shapes=[
            pltpu.VMEM((taps, depth * width, channels), jnp.bfloat16),
            pltpu.VMEM((3, 2, size + 2, width, channels), jnp.bfloat16),
            pltpu.VMEM((halves, pixels, channels), jnp.bfloat16),
        ],
        compiler_params=params(24),
        cost_estimate=cost(flops, halo, first, part, *weights),
        name="late",
    )(scalars, halo, first, part, spatial, *weights)


def attend_kernel(frames_per, lanes, turns, near, chunks, scalars, *refs):
    count = len(turns)
    blocks, refs = refs[:count], refs[count:]
    gain, w_query, w_key, w_value, w_out = refs[:5]
    waiting, outs = refs[5 : 5 + near * (chunks - 1)], refs[5 + near * (chunks - 1) :]
    for index, block in enumerate(waiting):
        outs[1 + index % near][index // near] = block[...]
    channels = gain.shape[-1]
    flat = len(blocks[0].shape) == 2
    groups = 1 if flat else blocks[0].shape[1] // lanes
    each = frames_per * lanes
    size = count * each

    def piece(j, g):
        if flat:
            return blocks[0][...]
        return blocks[j][:, g * lanes : (g + 1) * lanes].reshape(each, channels)

    def place(index):
        block = index // each
        time = index // lanes % frames_per
        for j in range(count):
            level = 0 if flat else scalars[2] ^ turns[j]
            time = time + jnp.where(block == j, level * frames_per, 0)
        return time, index % lanes

    row_time, row_lane = place(lax.broadcasted_iota(jnp.int32, (size, 1), 0))
    col_time, col_lane = place(lax.broadcasted_iota(jnp.int32, (1, size), 1))
    allowed = (row_lane == col_lane) & (col_time <= row_time)
    x = jnp.concatenate([piece(j, g) for g in range(groups) for j in range(count)], axis=0)
    wide = x.astype(jnp.float32)
    scale = lax.rsqrt(jnp.mean(wide * wide, axis=-1, keepdims=True) + epsilon)
    normed = (wide * scale * gain[...]).astype(jnp.bfloat16)
    query = dot32(normed, w_query[...]).astype(jnp.bfloat16)
    key = dot32(normed, w_key[...]).astype(jnp.bfloat16)
    value = dot32(normed, w_value[...]).astype(jnp.bfloat16)
    contexts = []
    for g in range(groups):
        part = slice(g * size, (g + 1) * size)
        scores = lax.dot_general(
            query[part], key[part], (((1,), (1,)), ((), ())), preferred_element_type=jnp.float32
        )
        scores = jnp.where(allowed, scores * channels ** (-0.5), -1e30)
        largest = jnp.max(scores, axis=-1, keepdims=True)
        probs = jnp.exp(scores - largest)
        probs = (probs / jnp.sum(probs, axis=-1, keepdims=True)).astype(jnp.bfloat16)
        contexts.append(dot32(probs, value[part]).astype(jnp.bfloat16))
    mixed = dot32(jnp.concatenate(contexts, axis=0), w_out[...])
    result = (wide + mixed).astype(jnp.bfloat16)
    if flat:
        outs[0][...] = result
        return
    short = frames_per // pair
    for g in range(groups):
        for j in range(count):
            begin = g * size + j * each
            rows = result[begin : begin + each].reshape(pair, short, lanes, channels)
            for side in range(pair):

                @pl.when(scalars[0] == side)
                def _():
                    part = slice(g * lanes, (g + 1) * lanes)
                    for x in range(pair):
                        m = pair * turns[j] + x
                        if 0 < m <= near:
                            outs[m][chunks - 1, :, part] = rows[side ^ x]
                        else:
                            outs[m][:, part] = rows[side ^ x]


def attend(scalars, blocks, turns, near, waiting, gain, w_query, w_key, w_value, w_out):
    frames_per, pixels, channels = blocks[0].shape
    flat = pixels % 16 != 0
    lanes = pixels if flat else 16
    if flat:
        blocks = [b.reshape(frames_per * pixels, channels) for b in blocks]
    count = len(blocks)
    size = frames_per * count * lanes
    block = (frames_per // pair, pixels, channels)
    chunks = 1 + len(waiting) // near if near else 1
    shapes = [
        (chunks,) + block if 0 < m <= near else block for m in range(pair * count)
    ]
    if flat:
        shapes = [blocks[0].shape]
    flops = 2 * frames_per * pixels * count * channels * (4 * channels + 2 * size)
    outs = pl.pallas_call(
        partial(attend_kernel, frames_per, lanes, turns, near, chunks),
        out_shape=[jax.ShapeDtypeStruct(shape, jnp.bfloat16) for shape in shapes],
        in_specs=[SMEM] + [VMEM] * (count + 5 + len(waiting)),
        out_specs=[VMEM] * len(shapes),
        compiler_params=params(20 if 16 * size * size < 20 * mebibyte else 56),
        cost_estimate=cost(flops, *blocks, w_query, w_key, w_value, w_out),
        name="attend",
    )(scalars, *blocks, gain, w_query, w_key, w_value, w_out, *waiting)
    return [o.reshape(frames_per, pixels, channels) for o in outs] if flat else outs


def collect_kernel(entries, levels, chunks, scalars, *refs):
    out, sems = refs[-2:]
    copies = []
    for index, (ref, sub, k, m) in enumerate(entries):
        block = refs[ref] if sub is None else refs[ref].at[sub]
        place = ((scalars[0] ^ m % pair) * chunks + k) * levels + (scalars[2] ^ m // pair)
        copies.append(pltpu.make_async_copy(block, out.at[:, place], sems.at[index]))
    run(copies)


def collect(scalars, blocks, entries, levels, chunks, whole):
    halves, pixels, channels = blocks[0].shape[-3:]
    given = [] if whole is None else [whole]
    shape = (halves, chunks * pair * levels, pixels, channels)
    return pl.pallas_call(
        partial(collect_kernel, entries, levels, chunks),
        out_shape=jax.ShapeDtypeStruct(shape, jnp.bfloat16),
        in_specs=[SMEM] + [ANY] * (len(blocks) + len(given)),
        out_specs=ANY,
        input_output_aliases={len(blocks) + 1: 0} if given else {},
        scratch_shapes=[pltpu.SemaphoreType.DMA((len(entries),))],
        compiler_params=params(16),
        name="collect",
    )(scalars, *blocks, *given)


def after(value, other):
    return lax.optimization_barrier((value, other))[0]


def per_device(
    video, w_time, b_time, w_down, b_down, w_space, b_space, gain, w_query, w_key, w_value, w_out
):
    frames, height, width, channels = video.shape
    devices = lax.axis_size("tm")
    levels = devices // pair
    columns = lax.axis_size("cols")
    assert columns == 2 and devices % pair == 0 and height % pair == 0 and frames >= taps
    place = lax.axis_index("tm").astype(jnp.int32)
    column = lax.axis_index("cols").astype(jnp.int32)
    side, level = place % pair, place // pair
    scalars = jnp.stack([side, column, level])
    half = height // pair
    gain = gain.reshape(1, -1)
    w_space = jnp.where(after(place, video) >= 0, w_space, 0)
    weights = [
        w_time.reshape(-1, channels), b_time.reshape(1, -1), w_down.reshape(-1, channels),
        b_down.reshape(1, -1), w_space, b_space.reshape(1, -1),
    ]
    attention = [gain, w_query, w_key, w_value, w_out]
    chunks = parts if half % parts == 0 and half // parts * width % levels == 0 else 1
    size = half // chunks
    each = size * width // levels
    direct = devices <= most_direct and levels & (levels - 1) == 0 and each % 16 == 0
    spans = [
        (k * size + (2 if k else 0), (k + 1) * size + 2) for k in range(chunks)
    ]

    def tm_permute(value, move):
        return lax.ppermute(value, "tm", [(i, move(i)) for i in range(devices) if move(i) < devices])

    sent = send(scalars, video, spans, half)
    received = [tm_permute(value, lambda i: i ^ 1) for value in sent]
    border = jnp.where(column == 0, video[:, :, -1], video[:, :, 0])
    border = jnp.pad(after(border, sent[0]), ((0, 0), (1, 1), (0, 0)))
    own_edge, other_edge = (
        lax.dynamic_slice_in_dim(border, s * half, half + 2, axis=1) for s in (side, 1 - side)
    )
    own_edge = lax.ppermute(own_edge, "cols", [(0, 1), (1, 0)])
    aslant = [
        (i * columns + c, (i ^ 1) * columns + 1 - c)
        for i in range(devices)
        for c in range(columns)
    ]
    other_edges = []
    for k, (begin, end) in enumerate(spans):
        cut_edge = other_edge[:, begin:end]
        if k:
            cut_edge = after(cut_edge, received[1])
        other_edges.append(lax.ppermute(cut_edge, ("tm", "cols"), aslant))

    def edge_rows(edge, begin, end):
        cut = jnp.pad(edge[:, begin:end], ((0, 0), (0, -(end - begin) % width), (0, 0)))
        return cut.reshape(frames, -1, width, channels)

    owners = levels if direct else 1
    edges = [
        [edge_rows(own_edge, begin, end), edge_rows(other, 0, end - begin)]
        for other, (begin, end) in zip(other_edges, spans)
    ]
    lasts, firsts, halos = [], [], []
    newest = w_space
    for k, (begin, end) in enumerate(spans):
        span = (begin, end, half, scalars, video)
        arrived = after(received[2 * k], newest)
        last = join(join_last_kernel, taps, "join_last", *span, arrived, *edges[k])
        lasts.append(last)
        halos.append(tm_permute(last, lambda i: (i + pair) % devices))
        if k == 0:
            others = after(received[1], last)
            firsts.append(join(
                join_first_kernel, pair * frames - taps, "join_first", *span, arrived, others,
                *edges[k]
            ))
            part, spatial, *kept = early(
                scalars, firsts[0], last, chunks == 1, size, end - begin, *weights
            )
            newest = part

    spatials = []
    for k, (begin, end) in enumerate(spans):
        rows, final = end - begin, k == chunks - 1
        if k == 0:
            part = after(part, lasts[-1])
            made = late(
                owners, scalars, halos[k], firsts[0], part, spatial, final, rows, *weights
            )
            kept = [*made[owners:], *kept]
        else:
            span = (begin, end, half, scalars, video)
            others = after(received[2 * k + 1], spatials[-1][0])
            first = join(
                join_first_kernel, pair * frames - taps, "join_first", *span, received[2 * k],
                others, *edges[k]
            )
            made = full(
                owners, scalars, halos[k], first, lasts[k], kept, final, size, rows, *weights
            )
            kept = made[owners:]
        spatials.append(made[:owners])

    newest = spatials[-1][0]
    if direct:
        gathers = [
            [blocks[0]]
            + [tm_permute(blocks[j], lambda i: i ^ (pair * j)) for j in range(1, levels)]
            for blocks in spatials
        ]
        far = devices // 2
        near = far - 1
        whole, waiting = None, []
        for k, gathered in enumerate(gathers):
            gathered[0] = after(gathered[0], newest)
            final = k == chunks - 1
            turns = tuple(range(levels))
            if final:
                turns = turns[levels // 2 :] + turns[: levels // 2][::-1]
            results = attend(
                scalars, [gathered[j] for j in turns], turns, near if final else 0,
                waiting if final else [], *attention
            )
            newest = results[0]
            blocks = [tm_permute(results[m], lambda i: i ^ m) for m in range(far, devices)]
            entries = [(m - far, None, k, m) for m in range(far, devices)]
            if final:
                for m in range(1, far):
                    entries += [(len(blocks), c, c, m) for c in range(chunks)]
                    blocks.append(tm_permute(results[m], lambda i: i ^ m))
            else:
                waiting += results[1:far]
            entries.append((len(blocks), None, k, 0))
            blocks.append(results[0])
            whole = collect(scalars, blocks, entries, levels, chunks, whole)
        return whole.reshape(frames // 2, height, width, channels)
    sets = [[pair * z + s for z in range(levels)] for s in range(pair)]
    returns = []
    for (block,) in spatials:
        gathered = lax.all_to_all(block, "tm", 1, 0, axis_index_groups=sets, tiled=True)
        (result,) = attend(scalars, [gathered], (0,), 0, [], *attention)
        result = lax.all_to_all(result, "tm", 0, 1, tiled=True)
        result = result.reshape(frames // 2, levels, pair, each, channels)
        returns.append(result.transpose(0, 2, 1, 3, 4).reshape(frames // 2, pair, -1, channels))
    return jnp.concatenate(returns, axis=2).reshape(frames // 2, height, width, channels)


def solution(mesh):
    spread = P(("clips", "tm"), None, "cols", None)
    return jax.shard_map(
        per_device,
        mesh=mesh,
        in_specs=(spread,) + (P(),) * 11,
        out_specs=spread,
        check_vma=False,
    )
```

```python
from functools import partial

import jax
import jax.numpy as jnp
from jax import lax
from jax.experimental import pallas as pl
from jax.experimental.pallas import tpu as pltpu
from jax.sharding import PartitionSpec as P

epsilon = 1e-06
parts = 2
pair = 2
taps = 3
most_direct = 8
mebibyte = 1024 * 1024

VMEM = pl.BlockSpec(memory_space=pltpu.VMEM)
SMEM = pl.BlockSpec(memory_space=pltpu.SMEM)
ANY = pl.BlockSpec(memory_space=pl.ANY)


def silu(v):
    return 0.5 * v * (1.0 + jnp.tanh(0.5 * v))


def dot32(a, b):
    return jnp.dot(a, b, preferred_element_type=jnp.float32)


def cost(flops, *arrays):
    size = sum(a.size * a.dtype.itemsize for a in arrays)
    return pl.CostEstimate(flops=flops, bytes_accessed=size, transcendentals=0)


def params(mebibytes):
    return pltpu.CompilerParams(vmem_limit_bytes=mebibytes * mebibyte)


def rows_of(owner, begin, end, half, height):
    low, high = max(begin, 1), min(end, half + 1)
    pieces = [(owner * half + low - 1, low - begin, high - low)]
    if begin == 0:
        pieces.append((jnp.maximum(owner * half - 1, 0), 0, 1))
    if end == half + 2:
        pieces.append((jnp.minimum((owner + 1) * half, height - 1), end - 1 - begin, 1))
    return pieces


def run(copies):
    for copy in copies:
        copy.start()
    for copy in copies:
        copy.wait()


def cut(target, video, frame, owner, begin, end, half):
    for source, here, count in rows_of(owner, begin, end, half, video.shape[1]):
        target[here : here + count] = video[frame, pl.ds(source, count)]


def send_kernel(spans, half, scalars, video, *outs):
    frames = video.shape[0]
    rest = frames - taps
    for k, (begin, end) in enumerate(spans):
        for t in range(frames):
            target = outs[2 * k].at[t - rest] if t >= rest else outs[2 * k + 1].at[t]
            cut(target, video, t, 1 - scalars[0], begin, end, half)


def send(scalars, video, spans, half):
    frames, _, width, channels = video.shape
    shapes = [
        (count, end - begin, width, channels)
        for begin, end in spans
        for count in (taps, frames - taps)
    ]
    return pl.pallas_call(
        partial(send_kernel, spans, half),
        out_shape=[jax.ShapeDtypeStruct(shape, video.dtype) for shape in shapes],
        in_specs=[SMEM, VMEM],
        out_specs=[VMEM] * len(shapes),
        compiler_params=params(12),
        name="send",
    )(scalars, video)


def join_last_kernel(begin, end, half, scalars, video, received, own_edge, other_edge, out):
    frames, rows = video.shape[0], end - begin

    @pl.when(scalars[0] == 0)
    def _():
        out[:, :rows] = received[...]
        out[:, rows:] = other_edge[frames - taps :]

    @pl.when(scalars[0] == 1)
    def _():
        for t in range(taps):
            cut(out.at[t], video, frames - taps + t, 1, begin, end, half)
        out[:, rows:] = own_edge[frames - taps :]


def join_first_kernel(
    begin, end, half, scalars, video, received, others, own_edge, other_edge, out
):
    frames, rows = video.shape[0], end - begin
    rest = frames - taps

    @pl.when(scalars[0] == 0)
    def _():
        for t in range(frames):
            cut(out.at[t], video, t, 0, begin, end, half)
        out[:frames, rows:] = own_edge[...]
        out[frames:, :rows] = others[...]
        out[frames:, rows:] = other_edge[:rest]

    @pl.when(scalars[0] == 1)
    def _():
        out[:rest, :rows] = others[...]
        out[rest:frames, :rows] = received[...]
        out[:frames, rows:] = other_edge[...]
        for t in range(rest):
            cut(out.at[frames + t], video, t, 1, begin, end, half)
        out[frames:, rows:] = own_edge[:rest]


def join(kernel, count, name, begin, end, half, scalars, video, *parts):
    _, _, width, channels = video.shape
    rows = end - begin + parts[-1].shape[1]
    return pl.pallas_call(
        partial(kernel, begin, end, half),
        out_shape=jax.ShapeDtypeStruct((count, rows, width, channels), jnp.bfloat16),
        in_specs=[SMEM] + [VMEM] * (1 + len(parts)),
        out_specs=VMEM,
        compiler_params=params(12),
        name=name,
    )(scalars, video, *parts)


def place_rows(buffers, index, top, reduced, rows, width, column):
    pixels, channels = rows * width, reduced.shape[-1]
    edges = reduced.shape[0] - pixels
    row_of = lax.broadcasted_iota(jnp.int32, (pixels, edges), 0) // width
    spread = (row_of == lax.broadcasted_iota(jnp.int32, (pixels, edges), 1)).astype(jnp.bfloat16)
    across = lax.broadcasted_iota(jnp.int32, (pixels, channels), 0) % width
    wide = reduced[:pixels].astype(jnp.float32)
    beside = dot32(spread, reduced[pixels:])
    before = jnp.where(column == 1, beside, 0.0)
    behind = jnp.where(column == 0, beside, 0.0)
    shifted = (
        jnp.where(across == 0, before, pltpu.roll(wide, 1, 0)),
        wide,
        jnp.where(across == width - 1, behind, pltpu.roll(wide, pixels - 1, 0)),
    )
    for b in range(3):
        value = shifted[b].astype(jnp.bfloat16).reshape(rows, width, channels)
        buffers[b, index, top : top + rows] = value


def convolve(buffers, fresh, last, side, kept, keeps, w_space, b_space):
    _, frames, rows, width, channels = buffers.shape
    size = rows - 2
    if fresh:

        @pl.when(side == 0)
        def _():
            buffers[:, :, :1] = jnp.zeros((3, frames, 1, width, channels), jnp.bfloat16)

    else:
        buffers[:, :, :2] = kept
    if last:

        @pl.when(side == pair - 1)
        def _():
            buffers[:, :, size + 1 :] = jnp.zeros((3, frames, 1, width, channels), jnp.bfloat16)

    else:
        keeps(buffers[:, :, size:])

    def window(b, a):
        return buffers[b, :, a : a + size].reshape(frames * size * width, channels)

    lhs = jnp.concatenate([window(b, a) for a in range(3) for b in range(3)], axis=1)
    acc = dot32(lhs, w_space[...].reshape(-1, channels)) + b_space[...]
    value = window(1, 1).astype(jnp.float32) + silu(acc)
    return value.astype(jnp.bfloat16).reshape(frames, size * width, channels)


def early_kernel(
    final, rows, scalars, first, last, w_time, b_time, w_down, b_down, w_space, b_space, *refs
):
    part, spatial = refs[:2]
    lifted, buffers = refs[-2:]
    keeps = None if final else (lambda value: refs[2].__setitem__(..., value))
    split, depth, width, channels = first.shape
    count = split + taps
    halves = count // 2
    pixels = depth * width

    def frame(t):
        return (first[t] if t < split else last[t - split]).reshape(pixels, channels)

    starts = list(range(taps - 1, count))
    for low in range(0, len(starts), 3):
        group = starts[low : low + 3]
        lhs = jnp.concatenate(
            [jnp.concatenate([frame(t - k) for t in group], axis=0) for k in range(taps)], axis=1
        )
        acc = dot32(lhs, w_time[...]) + b_time[...]
        held = jnp.concatenate([frame(t) for t in group], axis=0).astype(jnp.float32)
        value = (held + silu(acc)).astype(jnp.bfloat16)
        for g, t in enumerate(group):
            lifted[t] = value[g * pixels : (g + 1) * pixels]
    lhs = jnp.concatenate([lifted[3], lifted[2]], axis=1)
    part[...] = dot32(lhs, w_down[: 2 * channels]) + b_down[...]
    whole = range(2, halves)
    lhs = jnp.concatenate(
        [jnp.concatenate([lifted[2 * s + 1 - k] for s in whole], axis=0) for k in range(taps)],
        axis=1,
    )
    reduced = (dot32(lhs, w_down[...]) + b_down[...]).astype(jnp.bfloat16)
    for index in range(len(whole)):
        value = reduced[index * pixels : (index + 1) * pixels]
        place_rows(buffers, index, 0, value, rows, width, scalars[1])
    spatial[...] = convolve(buffers, True, final, scalars[0], None, keeps, w_space, b_space)


def early(scalars, first, last, final, size, rows, *weights):
    split, depth, width, channels = first.shape
    halves = (split + taps) // 2
    pixels = depth * width
    later = halves - 2
    shapes = [
        jax.ShapeDtypeStruct((pixels, channels), jnp.float32),
        jax.ShapeDtypeStruct((later, size * width, channels), jnp.bfloat16),
    ]
    if not final:
        shapes.append(jax.ShapeDtypeStruct((3, later, 2, width, channels), jnp.bfloat16))
    flops = 2 * channels * channels * (pixels * 26 + 9 * later * size * width)
    return pl.pallas_call(
        partial(early_kernel, final, rows),
        out_shape=shapes,
        in_specs=[SMEM] + [VMEM] * (2 + len(weights)),
        out_specs=[VMEM] * len(shapes),
        scratch_shapes=[
            pltpu.VMEM((2 * halves, pixels, channels), jnp.bfloat16),
            pltpu.VMEM((3, later, size + 2, width, channels), jnp.bfloat16),
        ],
        compiler_params=params(24),
        cost_estimate=cost(flops, first, last, *weights),
        name="early",
    )(scalars, first, last, *weights)


def full_kernel(
    owners, final, rows, scalars, halo, first, last, kept_late, kept_early, w_time, b_time, w_down,
    b_down, w_space, b_space, *refs
):
    outs = refs[:owners]
    keeps = None if final else refs[owners : owners + 2]
    lifted, buffers = refs[-2:]
    split, depth, width, channels = first.shape
    count = split + taps
    halves = count // 2
    pixels = depth * width

    def frame(t):
        if t < 0:
            value = halo[t + taps].reshape(pixels, channels)
            return jnp.where(scalars[2] > 0, value, jnp.zeros_like(value))
        return (first[t] if t < split else last[t - split]).reshape(pixels, channels)

    starts = list(range(-1, count))
    for low in range(0, len(starts), 3):
        group = starts[low : low + 3]
        lhs = jnp.concatenate(
            [jnp.concatenate([frame(t - k) for t in group], axis=0) for k in range(taps)], axis=1
        )
        acc = dot32(lhs, w_time[...]) + b_time[...]
        held = jnp.concatenate([frame(t) for t in group], axis=0).astype(jnp.float32)
        value = held + silu(acc)
        for g, t in enumerate(group):
            piece = value[g * pixels : (g + 1) * pixels]
            if t < 0:
                piece = jnp.where(scalars[2] > 0, piece, 0.0)
            lifted[t + 1] = piece.astype(jnp.bfloat16)
    lhs = jnp.concatenate(
        [
            jnp.concatenate([lifted[2 * s + 2 - k] for s in range(halves)], axis=0)
            for k in range(taps)
        ],
        axis=1,
    )
    reduced = (dot32(lhs, w_down[...]) + b_down[...]).astype(jnp.bfloat16)
    for index in range(halves):
        value = reduced[index * pixels : (index + 1) * pixels]
        place_rows(buffers, index, 2, value, rows, width, scalars[1])
    kept = jnp.concatenate([kept_late[...], kept_early[...]], axis=1)
    keep = None if final else (lambda value: keep_both(keeps, value))
    result = convolve(buffers, False, final, scalars[0], kept, keep, w_space, b_space)
    each = result.shape[1] // owners
    if owners == 1:
        outs[0][...] = result
    else:
        for j in range(owners):
            part = result[:, j * each : (j + 1) * each]
            for m in range(owners):

                @pl.when((scalars[2] ^ m) == j)
                def _():
                    outs[m][...] = part


def keep_both(keeps, value):
    keeps[0][...] = value[:, :2]
    keeps[1][...] = value[:, 2:]


def full(owners, scalars, halo, first, last, kept, final, size, rows, *weights):
    split, depth, width, channels = first.shape
    halves = (split + taps) // 2
    pixels = depth * width
    shapes = [(halves, size * width // owners, channels)] * owners
    if not final:
        shapes += [(3, count, 2, width, channels) for count in (2, halves - 2)]
    flops = 2 * channels * channels * (pixels * 39 + 9 * halves * size * width)
    return pl.pallas_call(
        partial(full_kernel, owners, final, rows),
        out_shape=[jax.ShapeDtypeStruct(shape, jnp.bfloat16) for shape in shapes],
        in_specs=[SMEM] + [VMEM] * (5 + len(weights)),
        out_specs=[VMEM] * len(shapes),
        scratch_shapes=[
            pltpu.VMEM((2 * halves + 1, pixels, channels), jnp.bfloat16),
            pltpu.VMEM((3, halves, size + 2, width, channels), jnp.bfloat16),
        ],
        compiler_params=params(28),
        cost_estimate=cost(flops, halo, first, last, *weights),
        name="full",
    )(scalars, halo, first, last, *kept, *weights)


def late_kernel(
    owners, final, rows, scalars, halo, first, part, spatial, w_time, b_time, w_down, b_down,
    w_space, b_space, *refs
):
    outs = refs[:owners]
    keeps = None if final else (lambda value: refs[owners].__setitem__(..., value))
    lifted, buffers, result = refs[-3:]
    _, depth, width, channels = first.shape
    pixels = depth * width

    def frame(t):
        if t < 0:
            value = halo[t + taps].reshape(pixels, channels)
            return jnp.where(scalars[2] > 0, value, jnp.zeros_like(value))
        return first[t].reshape(pixels, channels)

    group = range(-1, taps - 1)
    lhs = jnp.concatenate(
        [jnp.concatenate([frame(t - k) for t in group], axis=0) for k in range(taps)], axis=1
    )
    acc = dot32(lhs, w_time[...]) + b_time[...]
    held = jnp.concatenate([frame(t) for t in group], axis=0).astype(jnp.float32)
    value = held + silu(acc)
    for index in range(taps):
        piece = value[index * pixels : (index + 1) * pixels]
        if index == 0:
            piece = jnp.where(scalars[2] > 0, piece, 0.0)
        lifted[index] = piece.astype(jnp.bfloat16)
    lhs = jnp.concatenate([lifted[2], lifted[1], lifted[0]], axis=1)
    reduced = (
        dot32(lhs, w_down[...]) + b_down[...],
        dot32(lifted[2], w_down[2 * channels :]) + part[...],
    )
    for index, value in enumerate(reduced):
        value = value.astype(jnp.bfloat16)
        place_rows(buffers, index, 0, value, rows, width, scalars[1])
    result[:2] = convolve(buffers, True, final, scalars[0], None, keeps, w_space, b_space)
    result[2:] = spatial[...]
    each = result.shape[1] // owners
    if owners == 1:
        outs[0][...] = result[...]
    else:
        for j, out in enumerate(outs):
            begin = pl.multiple_of((scalars[2] ^ j) * each, each)
            out[...] = result[:, pl.ds(begin, each)]


def late(owners, scalars, halo, first, part, spatial, final, rows, *weights):
    _, depth, width, channels = first.shape
    later, pixels = spatial.shape[:2]
    halves = later + 2
    size = pixels // width
    shapes = [(halves, pixels // owners, channels)] * owners
    if not final:
        shapes.append((3, 2, 2, width, channels))
    flops = 2 * channels * channels * (depth * width * 13 + 18 * pixels)
    return pl.pallas_call(
        partial(late_kernel, owners, final, rows),
        out_shape=[jax.ShapeDtypeStruct(shape, jnp.bfloat16) for shape in shapes],
        in_specs=[SMEM] + [VMEM] * (4 + len(weights)),
        out_specs=[VMEM] * len(shapes),
        scratch_shapes=[
            pltpu.VMEM((taps, depth * width, channels), jnp.bfloat16),
            pltpu.VMEM((3, 2, size + 2, width, channels), jnp.bfloat16),
            pltpu.VMEM((halves, pixels, channels), jnp.bfloat16),
        ],
        compiler_params=params(24),
        cost_estimate=cost(flops, halo, first, part, *weights),
        name="late",
    )(scalars, halo, first, part, spatial, *weights)


def attend_kernel(frames_per, lanes, turns, near, chunks, scalars, *refs):
    count = len(turns)
    blocks, refs = refs[:count], refs[count:]
    gain, w_query, w_key, w_value, w_out = refs[:5]
    waiting, outs = refs[5 : 5 + near * (chunks - 1)], refs[5 + near * (chunks - 1) :]
    for index, block in enumerate(waiting):
        outs[1 + index % near][index // near] = block[...]
    channels = gain.shape[-1]
    flat = len(blocks[0].shape) == 2
    groups = 1 if flat else blocks[0].shape[1] // lanes
    each = frames_per * lanes
    size = count * each

    def piece(j, g):
        if flat:
            return blocks[0][...]
        return blocks[j][:, g * lanes : (g + 1) * lanes].reshape(each, channels)

    def place(index):
        block = index // each
        time = index // lanes % frames_per
        for j in range(count):
            level = 0 if flat else scalars[2] ^ turns[j]
            time = time + jnp.where(block == j, level * frames_per, 0)
        return time, index % lanes

    row_time, row_lane = place(lax.broadcasted_iota(jnp.int32, (size, 1), 0))
    col_time, col_lane = place(lax.broadcasted_iota(jnp.int32, (1, size), 1))
    allowed = (row_lane == col_lane) & (col_time <= row_time)
    x = jnp.concatenate([piece(j, g) for g in range(groups) for j in range(count)], axis=0)
    wide = x.astype(jnp.float32)
    scale = lax.rsqrt(jnp.mean(wide * wide, axis=-1, keepdims=True) + epsilon)
    normed = (wide * scale * gain[...]).astype(jnp.bfloat16)
    query = dot32(normed, w_query[...]).astype(jnp.bfloat16)
    key = dot32(normed, w_key[...]).astype(jnp.bfloat16)
    value = dot32(normed, w_value[...]).astype(jnp.bfloat16)
    contexts = []
    for g in range(groups):
        part = slice(g * size, (g + 1) * size)
        scores = lax.dot_general(
            query[part], key[part], (((1,), (1,)), ((), ())), preferred_element_type=jnp.float32
        )
        scores = jnp.where(allowed, scores * channels ** (-0.5), -1e30)
        largest = jnp.max(scores, axis=-1, keepdims=True)
        probs = jnp.exp(scores - largest)
        probs = (probs / jnp.sum(probs, axis=-1, keepdims=True)).astype(jnp.bfloat16)
        contexts.append(dot32(probs, value[part]).astype(jnp.bfloat16))
    mixed = dot32(jnp.concatenate(contexts, axis=0), w_out[...])
    result = (wide + mixed).astype(jnp.bfloat16)
    if flat:
        outs[0][...] = result
        return
    short = frames_per // pair
    for g in range(groups):
        for j in range(count):
            begin = g * size + j * each
            rows = result[begin : begin + each].reshape(pair, short, lanes, channels)
            for side in range(pair):

                @pl.when(scalars[0] == side)
                def _():
                    part = slice(g * lanes, (g + 1) * lanes)
                    for x in range(pair):
                        m = pair * turns[j] + x
                        if 0 < m <= near:
                            outs[m][chunks - 1, :, part] = rows[side ^ x]
                        else:
                            outs[m][:, part] = rows[side ^ x]


def attend(scalars, blocks, turns, near, waiting, gain, w_query, w_key, w_value, w_out):
    frames_per, pixels, channels = blocks[0].shape
    flat = pixels % 16 != 0
    lanes = pixels if flat else 16
    if flat:
        blocks = [b.reshape(frames_per * pixels, channels) for b in blocks]
    count = len(blocks)
    size = frames_per * count * lanes
    block = (frames_per // pair, pixels, channels)
    chunks = 1 + len(waiting) // near if near else 1
    shapes = [
        (chunks,) + block if 0 < m <= near else block for m in range(pair * count)
    ]
    if flat:
        shapes = [blocks[0].shape]
    flops = 2 * frames_per * pixels * count * channels * (4 * channels + 2 * size)
    outs = pl.pallas_call(
        partial(attend_kernel, frames_per, lanes, turns, near, chunks),
        out_shape=[jax.ShapeDtypeStruct(shape, jnp.bfloat16) for shape in shapes],
        in_specs=[SMEM] + [VMEM] * (count + 5 + len(waiting)),
        out_specs=[VMEM] * len(shapes),
        compiler_params=params(20 if 16 * size * size < 20 * mebibyte else 56),
        cost_estimate=cost(flops, *blocks, w_query, w_key, w_value, w_out),
        name="attend",
    )(scalars, *blocks, gain, w_query, w_key, w_value, w_out, *waiting)
    return [o.reshape(frames_per, pixels, channels) for o in outs] if flat else outs


def collect_kernel(entries, levels, chunks, scalars, *refs):
    out, sems = refs[-2:]
    copies = []
    for index, (ref, sub, k, m) in enumerate(entries):
        block = refs[ref] if sub is None else refs[ref].at[sub]
        place = ((scalars[0] ^ m % pair) * chunks + k) * levels + (scalars[2] ^ m // pair)
        copies.append(pltpu.make_async_copy(block, out.at[:, place], sems.at[index]))
    run(copies)


def collect(scalars, blocks, entries, levels, chunks, whole):
    halves, pixels, channels = blocks[0].shape[-3:]
    given = [] if whole is None else [whole]
    shape = (halves, chunks * pair * levels, pixels, channels)
    return pl.pallas_call(
        partial(collect_kernel, entries, levels, chunks),
        out_shape=jax.ShapeDtypeStruct(shape, jnp.bfloat16),
        in_specs=[SMEM] + [ANY] * (len(blocks) + len(given)),
        out_specs=ANY,
        input_output_aliases={len(blocks) + 1: 0} if given else {},
        scratch_shapes=[pltpu.SemaphoreType.DMA((len(entries),))],
        compiler_params=params(16),
        name="collect",
    )(scalars, *blocks, *given)


def after(value, other):
    return lax.optimization_barrier((value, other))[0]


def per_device(
    video, w_time, b_time, w_down, b_down, w_space, b_space, gain, w_query, w_key, w_value, w_out
):
    frames, height, width, channels = video.shape
    devices = lax.axis_size("tm")
    levels = devices // pair
    columns = lax.axis_size("cols")
    assert columns == 2 and devices % pair == 0 and height % pair == 0 and frames >= taps
    place = lax.axis_index("tm").astype(jnp.int32)
    column = lax.axis_index("cols").astype(jnp.int32)
    side, level = place % pair, place // pair
    scalars = jnp.stack([side, column, level])
    half = height // pair
    gain = gain.reshape(1, -1)
    w_space = jnp.where(after(place, video) >= 0, w_space, 0)
    weights = [
        w_time.reshape(-1, channels), b_time.reshape(1, -1), w_down.reshape(-1, channels),
        b_down.reshape(1, -1), w_space, b_space.reshape(1, -1),
    ]
    attention = [gain, w_query, w_key, w_value, w_out]
    chunks = parts if half % parts == 0 and half // parts * width % levels == 0 else 1
    size = half // chunks
    each = size * width // levels
    direct = devices <= most_direct and levels & (levels - 1) == 0 and each % 16 == 0
    spans = [
        (k * size + (2 if k else 0), (k + 1) * size + 2) for k in range(chunks)
    ]

    def tm_permute(value, move):
        return lax.ppermute(value, "tm", [(i, move(i)) for i in range(devices) if move(i) < devices])

    sent = send(scalars, video, spans, half)
    received = [tm_permute(value, lambda i: i ^ 1) for value in sent]
    border = jnp.where(column == 0, video[:, :, -1], video[:, :, 0])
    border = jnp.pad(after(border, sent[0]), ((0, 0), (1, 1), (0, 0)))
    own_edge, other_edge = (
        lax.dynamic_slice_in_dim(border, s * half, half + 2, axis=1) for s in (side, 1 - side)
    )
    own_edge = lax.ppermute(own_edge, "cols", [(0, 1), (1, 0)])
    aslant = [
        (i * columns + c, (i ^ 1) * columns + 1 - c)
        for i in range(devices)
        for c in range(columns)
    ]
    other_edge = lax.ppermute(other_edge, ("tm", "cols"), aslant)

    def edge_rows(edge, begin, end):
        cut = jnp.pad(edge[:, begin:end], ((0, 0), (0, -(end - begin) % width), (0, 0)))
        return cut.reshape(frames, -1, width, channels)

    owners = levels if direct else 1
    edges = [[edge_rows(e, begin, end) for e in (own_edge, other_edge)] for begin, end in spans]
    lasts, firsts, halos = [], [], []
    newest = w_space
    for k, (begin, end) in enumerate(spans):
        span = (begin, end, half, scalars, video)
        arrived = after(received[2 * k], newest)
        last = join(join_last_kernel, taps, "join_last", *span, arrived, *edges[k])
        lasts.append(last)
        halos.append(tm_permute(last, lambda i: (i + pair) % devices))
        if k == 0:
            others = after(received[1], last)
            firsts.append(join(
                join_first_kernel, pair * frames - taps, "join_first", *span, arrived, others,
                *edges[k]
            ))
            part, spatial, *kept = early(
                scalars, firsts[0], last, chunks == 1, size, end - begin, *weights
            )
            newest = part

    spatials = []
    for k, (begin, end) in enumerate(spans):
        rows, final = end - begin, k == chunks - 1
        if k == 0:
            part = after(part, lasts[-1])
            made = late(
                owners, scalars, halos[k], firsts[0], part, spatial, final, rows, *weights
            )
            kept = [*made[owners:], *kept]
        else:
            span = (begin, end, half, scalars, video)
            others = after(received[2 * k + 1], spatials[-1][0])
            first = join(
                join_first_kernel, pair * frames - taps, "join_first", *span, received[2 * k],
                others, *edges[k]
            )
            made = full(
                owners, scalars, halos[k], first, lasts[k], kept, final, size, rows, *weights
            )
            kept = made[owners:]
        spatials.append(made[:owners])

    newest = spatials[-1][0]
    if direct:
        gathers = [
            [blocks[0]]
            + [tm_permute(blocks[j], lambda i: i ^ (pair * j)) for j in range(1, levels)]
            for blocks in spatials
        ]
        far = devices // 2
        near = far - 1
        whole, waiting = None, []
        for k, gathered in enumerate(gathers):
            gathered[0] = after(gathered[0], newest)
            final = k == chunks - 1
            turns = tuple(range(levels))
            turns = turns[levels // 2 :] + turns[: levels // 2][::-1]
            results = attend(
                scalars, [gathered[j] for j in turns], turns, near if final else 0,
                waiting if final else [], *attention
            )
            newest = results[0]
            blocks = [tm_permute(results[m], lambda i: i ^ m) for m in range(far, devices)]
            entries = [(m - far, None, k, m) for m in range(far, devices)]
            if final:
                for m in range(1, far):
                    entries += [(len(blocks), c, c, m) for c in range(chunks)]
                    blocks.append(tm_permute(results[m], lambda i: i ^ m))
            else:
                waiting += results[1:far]
            entries.append((len(blocks), None, k, 0))
            blocks.append(results[0])
            whole = collect(scalars, blocks, entries, levels, chunks, whole)
        return whole.reshape(frames // 2, height, width, channels)
    sets = [[pair * z + s for z in range(levels)] for s in range(pair)]
    returns = []
    for (block,) in spatials:
        gathered = lax.all_to_all(block, "tm", 1, 0, axis_index_groups=sets, tiled=True)
        (result,) = attend(scalars, [gathered], (0,), 0, [], *attention)
        result = lax.all_to_all(result, "tm", 0, 1, tiled=True)
        result = result.reshape(frames // 2, levels, pair, each, channels)
        returns.append(result.transpose(0, 2, 1, 3, 4).reshape(frames // 2, pair, -1, channels))
    return jnp.concatenate(returns, axis=2).reshape(frames // 2, height, width, channels)


def solution(mesh):
    spread = P(("clips", "tm"), None, "cols", None)
    return jax.shard_map(
        per_device,
        mesh=mesh,
        in_specs=(spread,) + (P(),) * 11,
        out_specs=spread,
        check_vma=False,
    )
```
